32 devices in a mesh: dp: 8 (over z, x), tp: 4 (over y, core).
Axes of the slice: x: 2, y: 2, z: 4, core: 2. Of those that a mesh axis runs over, the one named last changes fastest.
Arguments:
- query_stream: bfloat16 [32, 1024, 512], P('dp', 'tp'), may hold values from -6 to 6
- token_embed: bfloat16 [32, 1024, 512], P('dp', 'tp'), may hold values from -6 to 6
- encoder_out: bfloat16 [32, 1024, 512], P('dp', 'tp'), may hold values from -6 to 6
- out_grad: bfloat16 [32, 1024, 512], P('dp', 'tp'), may hold values from -6 to 6
- attn_q: bfloat16 [512, 512], P('dp', 'tp'), may hold values from -0.25 to 0.25
- attn_k: bfloat16 [512, 512], P('dp', 'tp'), may hold values from -0.25 to 0.25
- attn_v: bfloat16 [512, 512], P('dp', 'tp'), may hold values from -0.25 to 0.25
- attn_o: bfloat16 [512, 512], P('tp', 'dp'), may hold values from -1 to 1
- cross_q: bfloat16 [512, 512], P('dp', 'tp'), may hold values from -0.25 to 0.25
- cross_k: bfloat16 [512, 512], P('dp', 'tp'), may hold values from -0.25 to 0.25
- cross_v: bfloat16 [512, 512], P('dp', 'tp'), may hold values from -0.25 to 0.25
- cross_o: bfloat16 [512, 512], P('tp', 'dp'), may hold values from -1 to 1
- ffn_in: bfloat16 [512, 2048], P('dp', 'tp'), may hold values from -0.25 to 0.25
- ffn_bias_in: bfloat16 [2048], P(('tp', 'dp')), may hold values from -3 to 3
- ffn_out: bfloat16 [2048, 512], P('tp', 'dp'), may hold values from -0.125 to 0.125
- ffn_bias_out: float32 [512], replicated, may hold values from -3 to 3
- norm_gain: float32 [3, 512], replicated, may hold values from 0.1 to 1.9
- norm_bias: float32 [3, 512], replicated, may hold values from -2 to 2
- doc_lengths: int32 [32, 8], P('dp'), may hold values from 1 to 1017, as said below
- src_lengths: int32 [32, 8], P('dp'), may hold values from 1 to 1017, as said below
- ctx_rank: int32 [32, 1024], P('dp'), may hold values from 0 to 1023
- ctx_limit: int32 [32, 1024], P('dp'), may hold values from 1 to 1024
Outputs:
- mixed: bfloat16 [32, 1024, 512], P('dp', 'tp')
- grad_query: float32 [32, 1024, 512], P('dp', 'tp')
- grad_embed: float32 [32, 1024, 512], P('dp', 'tp')
- grad_encoder: float32 [32, 1024, 512], P('dp', 'tp')
- grad_attn_q: float32 [512, 512], P('dp', 'tp')
- grad_attn_k: float32 [512, 512], P('dp', 'tp')
- grad_attn_v: float32 [512, 512], P('dp', 'tp')
- grad_attn_o: float32 [512, 512], P('tp', 'dp')
- grad_cross_q: float32 [512, 512], P('dp', 'tp')
- grad_cross_k: float32 [512, 512], P('dp', 'tp')
- grad_cross_v: float32 [512, 512], P('dp', 'tp')
- grad_cross_o: float32 [512, 512], P('tp', 'dp')
- grad_ffn_in: float32 [512, 2048], P('dp', 'tp')
- grad_ffn_bias_in: float32 [2048], P(('tp', 'dp'))
- grad_ffn_out: float32 [2048, 512], P('tp', 'dp')
- grad_ffn_bias_out: float32 [512], replicated
- grad_norm_gain: float32 [3, 512], replicated
- grad_norm_bias: float32 [3, 512], replicated
The draws below stay inside these ranges and needn't reach their ends.
Inputs may be any that keep to these rules, and one draw needn't show every extreme that they name: `doc_lengths`: in every row the 8 lengths sum to 1024; one of them, at a slot drawn from the seed, is a document that takes the rest of the row, the others are sentences of at most 32 tokens; in one row drawn from the seed all those sentences have one token. `src_lengths`: in every row the 8 lengths sum to 1024; one of them, at a slot drawn from the seed, is a source document that takes the rest of the row, the others are sentences of at most 32 tokens; in one row drawn from the seed all those sentences have one token.
All inputs are finite; a program needn't handle non-finite values.
Results may differ from the reference program's by a relative error of at most 0.025.
Values may be sent and summed in bfloat16 or wider, within the bound.
A program may use at most 192 MiB of HBM per device.

```python
import jax
import jax.numpy as jnp
from jax import lax

D = 512
HEADS = 8
FF = 2048
HEAD = 64
L = 1024
ENC_L = 1024
DOCS = 8
NROWS = 32
SHORT_MOST = 32
SRC_MOST = 32


def packed_lengths(key, total, longest_short):
    sentences = jax.random.randint(key, (NROWS, DOCS), 1, longest_short + 1)
    single_row = jax.random.randint(jax.random.fold_in(key, 7), (), 0, NROWS)
    sentences = jnp.where(jnp.arange(NROWS)[:, None] == single_row, 1, sentences)
    long_slot = jax.random.randint(jax.random.fold_in(key, 5), (NROWS, 1), 0, DOCS)
    is_long = jnp.arange(DOCS)[None, :] == long_slot
    remaining = jnp.sum(jnp.where(is_long, 0, sentences), axis=1, keepdims=True)
    return jnp.where(is_long, total - remaining, sentences).astype(jnp.int32)


def draw_doc_lengths(key, part):
    key = jax.random.fold_in(key, 11)
    return packed_lengths(key, L, SHORT_MOST)


def draw_src_lengths(key, part):
    key = jax.random.fold_in(key, 12)
    return packed_lengths(key, ENC_L, SRC_MOST)


def place_ends(drawn, rng, least, top_value):
    extent = drawn.shape
    spot = [jax.random.randint(jax.random.fold_in(rng, axis), (), 0, extent[axis]) for axis in range(len(extent))]
    drawn = drawn.at[tuple(spot)].set(least)
    longest = extent.index(max(extent))
    spot[longest] = (spot[longest] + 1) % extent[longest]
    return drawn.at[tuple(spot)].set(top_value)


def levels(key, extent, split, low, top_value):
    def one(dim, shards_of):
        steps = jax.random.uniform(jax.random.fold_in(jax.random.fold_in(key, 6), dim), (shards_of,), jnp.float32, low / len(split), top_value / len(split))
        return jnp.repeat(jnp.exp(steps), extent[dim] // shards_of).reshape((-1,) + (1,) * (len(extent) - dim - 1))

    loudness = one(*split[0])
    for cut in split[1:]:
        loudness = loudness * one(*cut)
    return loudness


def scatter_about(own_key, extent, width, reach, shards=(), kind=jnp.bfloat16):
    entries = width * jax.random.normal(own_key, extent, jnp.float32)
    if shards:
        entries = entries * levels(own_key, extent, shards, -0.22, 0.18)
    return jnp.clip(entries, -reach, reach).astype(kind)


def setup_inputs(seed: int = 0) -> dict:
    seeds = jax.random.split(jax.random.key(seed), 23)
    query_stream = scatter_about(seeds[0], (NROWS, L, D), 1.0, 6.0, ((0, 8), (1, 4)))
    token_embed = scatter_about(seeds[1], (NROWS, L, D), 1.0, 6.0, ((0, 8), (1, 4)))
    encoder_out = scatter_about(seeds[2], (NROWS, ENC_L, D), 1.0, 6.0, ((0, 8), (1, 4)))
    out_grad = scatter_about(seeds[3], (NROWS, L, D), 1.0, 6.0, ((0, 8), (1, 4)))
    attn_q = scatter_about(seeds[4], (D, D), D ** -0.5, 0.25, ((0, 8), (1, 4)))
    attn_k = scatter_about(seeds[5], (D, D), D ** -0.5, 0.25, ((0, 8), (1, 4)))
    attn_v = scatter_about(seeds[6], (D, D), D ** -0.5, 0.25, ((0, 8), (1, 4)))
    attn_o = scatter_about(seeds[7], (D, D), (D // 16) ** -0.5, 1.0, ((0, 4), (1, 8)))
    cross_q = scatter_about(seeds[8], (D, D), D ** -0.5, 0.25, ((0, 8), (1, 4)))
    cross_k = scatter_about(seeds[9], (D, D), D ** -0.5, 0.25, ((0, 8), (1, 4)))
    cross_v = scatter_about(seeds[10], (D, D), D ** -0.5, 0.25, ((0, 8), (1, 4)))
    cross_o = scatter_about(seeds[11], (D, D), (D // 16) ** -0.5, 1.0, ((0, 4), (1, 8)))
    ffn_in = scatter_about(seeds[12], (D, FF), D ** -0.5, 0.25, ((0, 8), (1, 4)))
    ffn_bias_in = scatter_about(seeds[13], (FF,), 0.5, 3.0, ((0, 32),))
    ffn_out = scatter_about(seeds[14], (FF, D), FF ** -0.5, 0.125, ((0, 4), (1, 8)))
    ffn_bias_out = scatter_about(seeds[15], (D,), 0.5, 3.0, (), jnp.float32)
    norm_gain = jnp.clip(1.0 + 0.18 * jax.random.normal(seeds[16], (3, D), jnp.float32), 0.1, 1.9)
    norm_bias = scatter_about(seeds[17], (3, D), 0.3, 2.0, (), jnp.float32)
    doc_lengths = draw_doc_lengths(jax.random.fold_in(seeds[22], 71), 0)
    src_lengths = draw_src_lengths(jax.random.fold_in(seeds[22], 71), 0)
    ctx_rank = place_ends(jax.random.randint(seeds[20], (NROWS, L), 0, L), jax.random.fold_in(seeds[20], 1), 0, L - 1).astype(jnp.int32)
    ctx_limit = place_ends(jax.random.randint(seeds[21], (NROWS, L), 1, L + 1), jax.random.fold_in(seeds[21], 1), 1, L).astype(jnp.int32)
    return {"query_stream": query_stream, "token_embed": token_embed, "encoder_out": encoder_out, "out_grad": out_grad, "attn_q": attn_q, "attn_k": attn_k, "attn_v": attn_v, "attn_o": attn_o, "cross_q": cross_q, "cross_k": cross_k, "cross_v": cross_v, "cross_o": cross_o, "ffn_in": ffn_in, "ffn_bias_in": ffn_bias_in, "ffn_out": ffn_out, "ffn_bias_out": ffn_bias_out, "norm_gain": norm_gain, "norm_bias": norm_bias, "doc_lengths": doc_lengths, "src_lengths": src_lengths, "ctx_rank": ctx_rank, "ctx_limit": ctx_limit}


EPSILON = 1e-05
HIGHEST = lax.Precision.HIGHEST

@jax.custom_vjp
def low(v):
    return lax.optimization_barrier(v.astype(jnp.bfloat16)).astype(jnp.float32)

@jax.custom_vjp
def low_back(v):
    return v

def low_keep(v):
    return (low(v), None)

def low_pass(kept, grad):
    return (grad,)

def back_keep(v):
    return (v, None)

def back_low(kept, grad):
    return (low(grad),)
low.defvjp(low_keep, low_pass)
low_back.defvjp(back_keep, back_low)

def round_both(values):
    return low(low_back(values))

def layer_norm(values, scale_vec, shift_vec):
    average = lax.optimization_barrier(jnp.mean(values, axis=-1, keepdims=True))
    centred = values - average
    spread = lax.optimization_barrier(jnp.mean(centred * centred, axis=-1, keepdims=True))
    return centred * lax.rsqrt(spread + EPSILON) * scale_vec + shift_vec

def gelu_exact(values):
    return 0.5 * values * (1.0 + lax.erf(values * 0.7071067811865476))

def product(left, right):
    return jnp.matmul(left, right, precision=HIGHEST)

def layout(lengths, length):
    lengths = lengths.astype(jnp.int32)
    offsets = (jnp.cumsum(lengths) - lengths).astype(jnp.int32)
    positions = jnp.arange(length, dtype=jnp.int32)
    passed = positions[:, None] >= offsets[None, :]
    document = (lax.optimization_barrier(jnp.sum(passed.astype(jnp.int32), axis=1)) - 1).astype(jnp.int32)
    doc_start = lax.optimization_barrier(jnp.max(jnp.where(passed, offsets[None, :], 0), axis=1)).astype(jnp.int32)
    return (document, doc_start)

def self_visible(lengths, rank_row, limit_row, length, first_row, block_rows):
    document, doc_start = layout(lengths, length)
    positions = jnp.arange(length, dtype=jnp.int32)
    rows_pos = positions[first_row:first_row + block_rows]
    same_text = document[first_row:first_row + block_rows, None] == document[None, :]
    chosen = (rank_row[None, :] < limit_row[first_row:first_row + block_rows, None]) & (rows_pos[:, None] != positions[None, :])
    opener = positions[None, :] == doc_start[first_row:first_row + block_rows, None]
    return same_text & (chosen | opener)

def cross_visible(lengths, src_lengths, length, src_length, first_row, block_rows):
    document, _ = layout(lengths, length)
    source_doc, _ = layout(src_lengths, src_length)
    return document[first_row:first_row + block_rows, None] == source_doc[None, :]

def attend(queries, keys_all, values_all, visible):
    query_count = queries.shape[0]
    queries = queries.reshape(query_count, HEADS, HEAD)
    keys_all = keys_all.reshape(keys_all.shape[0], HEADS, HEAD)
    values_all = values_all.reshape(values_all.shape[0], HEADS, HEAD)
    scores = jnp.einsum('qhd,khd->hqk', queries, keys_all, precision=HIGHEST) * HEAD ** (-0.5)
    scores = low_back(scores)
    scores = jnp.where(visible[None], scores, -1e+30)
    highest = lax.optimization_barrier(jnp.max(scores, axis=-1, keepdims=True))
    exponent = jnp.exp(scores - highest)
    weights = low(exponent / lax.optimization_barrier(jnp.sum(exponent, axis=-1, keepdims=True)))
    context = jnp.einsum('hqk,khd->qhd', weights, values_all, precision=HIGHEST)
    return context.reshape(query_count, HEADS * HEAD)

def row_layer(params, row_items):
    attn_q, attn_k, attn_v, attn_o, cross_q, cross_k, cross_v, cross_o, ffn_in, ffn_bias_in, ffn_out, ffn_bias_out, norm_gain, norm_bias = params
    query_row, embed_row, source_row, lengths, src_lengths, rank_row, limit_row = row_items
    own_mask = self_visible(lengths, rank_row, limit_row, L, 0, L)
    other_mask = cross_visible(lengths, src_lengths, L, ENC_L, 0, L)
    self_queries = round_both(product(query_row, attn_q))
    self_keys = round_both(product(embed_row, attn_k))
    self_values = round_both(product(embed_row, attn_v))
    self_context = round_both(attend(self_queries, self_keys, self_values, own_mask))
    attn_branch = low_back(product(self_context, attn_o))
    hidden_one = layer_norm(query_row + attn_branch, norm_gain[0], norm_bias[0])
    hidden_low = low(hidden_one)
    cross_queries = round_both(product(hidden_low, cross_q))
    cross_keys = round_both(product(source_row, cross_k))
    cross_values = round_both(product(source_row, cross_v))
    cross_context = round_both(attend(cross_queries, cross_keys, cross_values, other_mask))
    cross_branch = low_back(product(cross_context, cross_o))
    hidden_two = layer_norm(hidden_one + cross_branch, norm_gain[1], norm_bias[1])
    ffn_pre = low_back(product(low(hidden_two), ffn_in) + ffn_bias_in)
    ffn_act = low(gelu_exact(ffn_pre))
    ffn_branch = low_back(product(ffn_act, ffn_out) + ffn_bias_out)
    return layer_norm(hidden_two + ffn_branch, norm_gain[2], norm_bias[2])

def reference(query_stream, token_embed, encoder_out, out_grad, attn_q, attn_k, attn_v, attn_o, cross_q, cross_k, cross_v, cross_o, ffn_in, ffn_bias_in, ffn_out, ffn_bias_out, norm_gain, norm_bias, doc_lengths, src_lengths, ctx_rank, ctx_limit):
    params = tuple((weight.astype(jnp.float32) for weight in (attn_q, attn_k, attn_v, attn_o, cross_q, cross_k, cross_v, cross_o, ffn_in, ffn_bias_in, ffn_out, ffn_bias_out, norm_gain, norm_bias)))

    def forward(params, queries, embeds, sources):

        def one_row(row_items):
            return row_layer(params, row_items)
        return lax.map(jax.checkpoint(one_row), (queries, embeds, sources, doc_lengths, src_lengths, ctx_rank, ctx_limit))
    outputs, pullback = jax.vjp(forward, params, query_stream.astype(jnp.float32), token_embed.astype(jnp.float32), encoder_out.astype(jnp.float32))
    weight_grads, grad_query, grad_embed, grad_encoder = pullback(out_grad.astype(jnp.float32))
    g_attn_q, g_attn_k, g_attn_v, g_attn_o, g_cross_q, g_cross_k, g_cross_v, g_cross_o, g_ffn_in, g_bias_in, g_ffn_out, g_bias_out, g_gain, g_shift = weight_grads
    return (outputs.astype(jnp.bfloat16), grad_query, grad_embed, grad_encoder, g_attn_q, g_attn_k, g_attn_v, g_attn_o, g_cross_q, g_cross_k, g_cross_v, g_cross_o, g_ffn_in, g_bias_in, g_ffn_out, g_bias_out, g_gain, g_shift)
```

```python
import jax
import jax.numpy as jnp
from jax import lax
from jax.sharding import PartitionSpec as P

HEADS = 8


EPSILON = 1e-05
score_tile = 512


def layer_norm(values, scale_vec, shift_vec):
    average = jnp.mean(values, axis=-1, keepdims=True)
    centred = values - average
    spread = jnp.mean(centred * centred, axis=-1, keepdims=True)
    return centred * lax.rsqrt(spread + EPSILON) * scale_vec + shift_vec


def gelu_exact(values):
    return 0.5 * values * (1.0 + lax.erf(values * 0.7071067811865476))


def project(inputs, matrix):
    return jnp.einsum("rld,de->rle", inputs, matrix, preferred_element_type=jnp.float32)


def project_back(cotangent, matrix):
    return jnp.einsum("rle,de->rld", cotangent, matrix, preferred_element_type=jnp.float32)


def outer_sum(inputs, cotangent):
    return jnp.einsum("rld,rle->de", inputs, cotangent, preferred_element_type=jnp.float32)


def layout(lengths, length):
    offsets = jnp.cumsum(lengths) - lengths
    positions = jnp.arange(length, dtype=jnp.int32)
    passed = positions[:, None] >= offsets[None, :]
    document = jnp.sum(passed.astype(jnp.int32), axis=1) - 1
    doc_start = jnp.max(jnp.where(passed, offsets[None, :], 0), axis=1)
    return (document, doc_start)


def self_visible(lengths, rank_row, limit_row, length, first_row, block_rows):
    document, doc_start = layout(lengths, length)
    positions = jnp.arange(length, dtype=jnp.int32)
    rows_pos = positions[first_row : first_row + block_rows]
    same_text = document[first_row : first_row + block_rows, None] == document[None, :]
    chosen = (rank_row[None, :] < limit_row[first_row : first_row + block_rows, None]) & (
        rows_pos[:, None] != positions[None, :]
    )
    opener = positions[None, :] == doc_start[first_row : first_row + block_rows, None]
    return same_text & (chosen | opener)


def cross_visible(lengths, src_lengths, length, src_length, first_row, block_rows):
    document, _ = layout(lengths, length)
    source_doc, _ = layout(src_lengths, src_length)
    return document[first_row : first_row + block_rows, None] == source_doc[None, :]


def attend_forward(queries, keys_all, values_all, visible_of, head_count):
    query_count = queries.shape[0]
    head_size = queries.shape[1] // head_count
    factor = head_size ** (-0.5)
    queries = queries.reshape(query_count, head_count, head_size)
    keys_all = keys_all.reshape(keys_all.shape[0], head_count, head_size)
    values_all = values_all.reshape(values_all.shape[0], head_count, head_size)
    block_rows = min(score_tile, query_count)
    outputs = []
    totals = []
    for first_row in range(0, query_count, block_rows):
        query_part = queries[first_row : first_row + block_rows]
        scores = (
            jnp.einsum("qhd,khd->hqk", query_part, keys_all, preferred_element_type=jnp.float32)
            * factor
        )
        scores = jnp.where(visible_of(first_row, block_rows)[None], scores, -1e30)
        highest = jnp.max(scores, axis=-1, keepdims=True)
        exponent = jnp.exp(scores - highest)
        denominator = jnp.sum(exponent, axis=-1, keepdims=True)
        weights_low = (exponent / denominator).astype(jnp.bfloat16)
        outputs.append(
            jnp.einsum("hqk,khd->qhd", weights_low, values_all, preferred_element_type=jnp.float32)
        )
        totals.append(highest[..., 0] + jnp.log(denominator[..., 0]))
    context = jnp.concatenate(outputs, axis=0).reshape(query_count, head_count * head_size)
    return (context, jnp.concatenate(totals, axis=1))


def attend_backward(queries, keys_all, values_all, visible_of, totals, grad_context, head_count):
    query_count = queries.shape[0]
    key_count = keys_all.shape[0]
    head_size = queries.shape[1] // head_count
    factor = head_size ** (-0.5)
    queries = queries.reshape(query_count, head_count, head_size)
    keys_all = keys_all.reshape(key_count, head_count, head_size)
    values_all = values_all.reshape(key_count, head_count, head_size)
    grad_context = grad_context.reshape(query_count, head_count, head_size)
    grad_keys = jnp.zeros((key_count, head_count, head_size), jnp.float32)
    grad_values = jnp.zeros((key_count, head_count, head_size), jnp.float32)
    grad_queries = []
    block_rows = min(score_tile, query_count)
    for first_row in range(0, query_count, block_rows):
        query_part = queries[first_row : first_row + block_rows]
        grad_part = grad_context[first_row : first_row + block_rows]
        scores = (
            jnp.einsum("qhd,khd->hqk", query_part, keys_all, preferred_element_type=jnp.float32)
            * factor
        )
        scores = jnp.where(visible_of(first_row, block_rows)[None], scores, -1e30)
        weights_full = jnp.exp(scores - totals[:, first_row : first_row + block_rows, None])
        grad_weights = jnp.einsum(
            "qhd,khd->hqk", grad_part, values_all, preferred_element_type=jnp.float32
        )
        inner = jnp.sum(grad_weights * weights_full, axis=-1, keepdims=True)
        grad_scores = (weights_full * (grad_weights - inner)).astype(jnp.bfloat16)
        grad_queries.append(
            jnp.einsum("hqk,khd->qhd", grad_scores, keys_all, preferred_element_type=jnp.float32)
            * factor
        )
        grad_keys = (
            grad_keys
            + jnp.einsum(
                "hqk,qhd->khd", grad_scores, query_part, preferred_element_type=jnp.float32
            )
            * factor
        )
        grad_values = grad_values + jnp.einsum(
            "hqk,qhd->khd",
            weights_full.astype(jnp.bfloat16),
            grad_part,
            preferred_element_type=jnp.float32,
        )
    grad_queries = jnp.concatenate(grad_queries, axis=0).reshape(
        query_count, head_count * head_size
    )
    return (
        grad_queries.astype(jnp.bfloat16),
        grad_keys.reshape(key_count, -1).astype(jnp.bfloat16),
        grad_values.reshape(key_count, -1).astype(jnp.bfloat16),
    )


def collect(piece):
    return lax.all_gather(piece, "tp", axis=1, tiled=True)


def spread_sum(partial_sum):
    return lax.psum_scatter(partial_sum, "tp", scatter_dimension=1, tiled=True)


def collect_grad(piece):
    return lax.all_gather(piece, "tp", axis=1, tiled=True)


def send_back(partial_sum):
    return lax.psum_scatter(partial_sum, "tp", scatter_dimension=1, tiled=True)


def local_split(
    query_stream,
    token_embed,
    encoder_out,
    out_grad,
    attn_q,
    attn_k,
    attn_v,
    attn_o,
    cross_q,
    cross_k,
    cross_v,
    cross_o,
    ffn_in,
    ffn_bias_in,
    ffn_out,
    ffn_bias_out,
    norm_gain,
    norm_bias,
    doc_lengths,
    src_lengths,
    ctx_rank,
    ctx_limit,
):
    head_count = HEADS // lax.axis_size("tp")
    (
        self_query,
        self_key,
        self_value,
        self_out,
        other_query,
        other_key,
        other_value,
        other_out,
        hidden_in,
        hidden_bias,
        hidden_out,
    ) = (
        lax.all_gather(attn_q, "dp", axis=0, tiled=True),
        lax.all_gather(attn_k, "dp", axis=0, tiled=True),
        lax.all_gather(attn_v, "dp", axis=0, tiled=True),
        lax.all_gather(attn_o, "dp", axis=1, tiled=True),
        lax.all_gather(cross_q, "dp", axis=0, tiled=True),
        lax.all_gather(cross_k, "dp", axis=0, tiled=True),
        lax.all_gather(cross_v, "dp", axis=0, tiled=True),
        lax.all_gather(cross_o, "dp", axis=1, tiled=True),
        lax.all_gather(ffn_in, "dp", axis=0, tiled=True),
        lax.all_gather(ffn_bias_in, "dp", axis=0, tiled=True),
        lax.all_gather(ffn_out, "dp", axis=1, tiled=True),
    )

    def self_forward(row_items):
        queries, keys_all, values_all, lengths, rank_row, limit_row = row_items

        def visible_of(first_row, block_rows):
            return self_visible(
                lengths, rank_row, limit_row, keys_all.shape[0], first_row, block_rows
            )

        return attend_forward(queries, keys_all, values_all, visible_of, head_count)

    def self_backward(row_items):
        queries, keys_all, values_all, lengths, rank_row, limit_row, totals, grad_context = (
            row_items
        )

        def visible_of(first_row, block_rows):
            return self_visible(
                lengths, rank_row, limit_row, keys_all.shape[0], first_row, block_rows
            )

        return attend_backward(
            queries, keys_all, values_all, visible_of, totals, grad_context, head_count
        )

    def cross_forward(row_items):
        queries, keys_all, values_all, lengths, source_lengths = row_items

        def visible_of(first_row, block_rows):
            return cross_visible(
                lengths, source_lengths, queries.shape[0], keys_all.shape[0], first_row, block_rows
            )

        return attend_forward(queries, keys_all, values_all, visible_of, head_count)

    def cross_backward(row_items):
        queries, keys_all, values_all, lengths, source_lengths, totals, grad_context = row_items

        def visible_of(first_row, block_rows):
            return cross_visible(
                lengths, source_lengths, queries.shape[0], keys_all.shape[0], first_row, block_rows
            )

        return attend_backward(
            queries, keys_all, values_all, visible_of, totals, grad_context, head_count
        )

    query_all = collect(query_stream)
    embed_all = collect(token_embed)
    source_all = collect(encoder_out)
    self_queries = project(query_all, self_query).astype(jnp.bfloat16)
    self_keys = project(embed_all, self_key).astype(jnp.bfloat16)
    self_values = project(embed_all, self_value).astype(jnp.bfloat16)
    self_context, self_totals = lax.map(
        self_forward, (self_queries, self_keys, self_values, doc_lengths, ctx_rank, ctx_limit)
    )
    self_low = self_context.astype(jnp.bfloat16)
    first_sum = query_stream.astype(jnp.float32) + spread_sum(project(self_low, self_out))
    hidden_one, first_back = jax.vjp(layer_norm, first_sum, norm_gain[0], norm_bias[0])
    hidden_one_all = collect(hidden_one.astype(jnp.bfloat16))
    cross_queries = project(hidden_one_all, other_query).astype(jnp.bfloat16)
    cross_keys = project(source_all, other_key).astype(jnp.bfloat16)
    cross_values = project(source_all, other_value).astype(jnp.bfloat16)
    cross_context, cross_totals = lax.map(
        cross_forward, (cross_queries, cross_keys, cross_values, doc_lengths, src_lengths)
    )
    cross_low = cross_context.astype(jnp.bfloat16)
    second_sum = hidden_one + spread_sum(project(cross_low, other_out))
    hidden_two, second_back = jax.vjp(layer_norm, second_sum, norm_gain[1], norm_bias[1])
    hidden_two_low = hidden_two.astype(jnp.bfloat16)
    ffn_inputs = lax.all_gather(hidden_two_low, "tp", axis=1, tiled=True)
    ffn_pre = project(ffn_inputs, hidden_in) + hidden_bias.astype(jnp.float32)
    ffn_gate, gelu_back = jax.vjp(gelu_exact, ffn_pre)
    ffn_act = ffn_gate.astype(jnp.bfloat16)
    ffn_branch = (
        lax.psum_scatter(project(ffn_act, hidden_out), "tp", scatter_dimension=1, tiled=True)
        + ffn_bias_out
    )
    third_sum = hidden_two + ffn_branch
    mixed_full, third_back = jax.vjp(layer_norm, third_sum, norm_gain[2], norm_bias[2])
    grad_third, gain_two, shift_two = third_back(out_grad.astype(jnp.float32))
    grad_ffn = grad_third.astype(jnp.bfloat16)
    grad_bias_out = jnp.sum(grad_ffn.astype(jnp.float32), axis=(0, 1))
    grad_ffn_all = lax.all_gather(grad_ffn, "tp", axis=1, tiled=True)
    grad_act = project_back(grad_ffn_all, hidden_out)
    grad_down = outer_sum(ffn_act, grad_ffn_all)
    grad_pre = gelu_back(grad_act)[0].astype(jnp.bfloat16)
    grad_up = outer_sum(ffn_inputs, grad_pre)
    grad_bias_in = jnp.sum(grad_pre.astype(jnp.float32), axis=(0, 1))
    grad_two = grad_third + lax.psum_scatter(
        project_back(grad_pre, hidden_in), "tp", scatter_dimension=1, tiled=True
    )
    grad_second, gain_one, shift_one = second_back(grad_two)
    grad_cross_all = collect_grad(grad_second.astype(jnp.bfloat16))
    grad_other_out = outer_sum(cross_low, grad_cross_all)
    grad_cross_ctx = project_back(grad_cross_all, other_out).astype(jnp.bfloat16)
    cross_dq, cross_dk, cross_dv = lax.map(
        cross_backward,
        (
            cross_queries,
            cross_keys,
            cross_values,
            doc_lengths,
            src_lengths,
            cross_totals,
            grad_cross_ctx,
        ),
    )
    grad_other_query = outer_sum(hidden_one_all, cross_dq)
    grad_other_key = outer_sum(source_all, cross_dk)
    grad_other_value = outer_sum(source_all, cross_dv)
    grad_encoder = send_back(
        project_back(cross_dk, other_key) + project_back(cross_dv, other_value)
    )
    grad_one = grad_second + send_back(project_back(cross_dq, other_query))
    grad_first, gain_zero, shift_zero = first_back(grad_one)
    grad_attn_all = collect_grad(grad_first.astype(jnp.bfloat16))
    grad_self_out = outer_sum(self_low, grad_attn_all)
    grad_self_ctx = project_back(grad_attn_all, self_out).astype(jnp.bfloat16)
    self_dq, self_dk, self_dv = lax.map(
        self_backward,
        (
            self_queries,
            self_keys,
            self_values,
            doc_lengths,
            ctx_rank,
            ctx_limit,
            self_totals,
            grad_self_ctx,
        ),
    )
    grad_self_query = outer_sum(query_all, self_dq)
    grad_self_key = outer_sum(embed_all, self_dk)
    grad_self_value = outer_sum(embed_all, self_dv)
    grad_embed = send_back(project_back(self_dk, self_key) + project_back(self_dv, self_value))
    grad_query = grad_first + send_back(project_back(self_dq, self_query))
    (
        grad_self_query,
        grad_self_key,
        grad_self_value,
        grad_self_out,
        grad_other_query,
        grad_other_key,
        grad_other_value,
        grad_other_out,
        grad_up,
        grad_bias_in,
        grad_down,
    ) = (
        lax.psum_scatter(
            grad_self_query.astype(jnp.bfloat16), "dp", scatter_dimension=0, tiled=True
        ).astype(jnp.float32),
        lax.psum_scatter(
            grad_self_key.astype(jnp.bfloat16), "dp", scatter_dimension=0, tiled=True
        ).astype(jnp.float32),
        lax.psum_scatter(
            grad_self_value.astype(jnp.bfloat16), "dp", scatter_dimension=0, tiled=True
        ).astype(jnp.float32),
        lax.psum_scatter(
            grad_self_out.astype(jnp.bfloat16), "dp", scatter_dimension=1, tiled=True
        ).astype(jnp.float32),
        lax.psum_scatter(
            grad_other_query.astype(jnp.bfloat16), "dp", scatter_dimension=0, tiled=True
        ).astype(jnp.float32),
        lax.psum_scatter(
            grad_other_key.astype(jnp.bfloat16), "dp", scatter_dimension=0, tiled=True
        ).astype(jnp.float32),
        lax.psum_scatter(
            grad_other_value.astype(jnp.bfloat16), "dp", scatter_dimension=0, tiled=True
        ).astype(jnp.float32),
        lax.psum_scatter(
            grad_other_out.astype(jnp.bfloat16), "dp", scatter_dimension=1, tiled=True
        ).astype(jnp.float32),
        lax.psum_scatter(
            grad_up.astype(jnp.bfloat16), "dp", scatter_dimension=0, tiled=True
        ).astype(jnp.float32),
        lax.psum_scatter(
            grad_bias_in.astype(jnp.bfloat16), "dp", scatter_dimension=0, tiled=True
        ).astype(jnp.float32),
        lax.psum_scatter(
            grad_down.astype(jnp.bfloat16), "dp", scatter_dimension=1, tiled=True
        ).astype(jnp.float32),
    )
    gain_grads = jnp.stack([gain_zero, gain_one, gain_two])
    shift_grads = jnp.stack([shift_zero, shift_one, shift_two])
    gain_grads, shift_grads, grad_bias_out = lax.psum(
        (gain_grads, shift_grads, grad_bias_out), ("dp", "tp")
    )
    return (
        mixed_full.astype(jnp.bfloat16),
        grad_query,
        grad_embed,
        grad_encoder,
        grad_self_query,
        grad_self_key,
        grad_self_value,
        grad_self_out,
        grad_other_query,
        grad_other_key,
        grad_other_value,
        grad_other_out,
        grad_up,
        grad_bias_in,
        grad_down,
        grad_bias_out,
        gain_grads,
        shift_grads,
    )


def to_row(piece):
    return lax.all_to_all(piece, "tp", split_axis=0, concat_axis=1, tiled=True)


def from_row(row):
    return lax.all_to_all(row, "tp", split_axis=1, concat_axis=0, tiled=True)


def own_row(per_row):
    return lax.dynamic_slice_in_dim(per_row, lax.axis_index("tp"), 1, axis=0)


def whole_weight(piece, rows_axis, cols_axis):
    gathered = lax.all_gather(piece, rows_axis, axis=0, tiled=True)
    return lax.all_gather(gathered, cols_axis, axis=1, tiled=True)


def own_weight(partial_sum, rows_axis, cols_axis):
    low = partial_sum.astype(jnp.bfloat16)
    low = lax.psum_scatter(low, cols_axis, scatter_dimension=1, tiled=True)
    return lax.psum_scatter(low, rows_axis, scatter_dimension=0, tiled=True).astype(jnp.float32)


def local_rows(
    query_stream,
    token_embed,
    encoder_out,
    out_grad,
    attn_q,
    attn_k,
    attn_v,
    attn_o,
    cross_q,
    cross_k,
    cross_v,
    cross_o,
    ffn_in,
    ffn_bias_in,
    ffn_out,
    ffn_bias_out,
    norm_gain,
    norm_bias,
    doc_lengths,
    src_lengths,
    ctx_rank,
    ctx_limit,
):
    low = jnp.bfloat16
    query_row, embed_row, source_row = to_row(query_stream), to_row(token_embed), to_row(encoder_out)
    grad_row = to_row(out_grad)
    lengths, source_lengths = own_row(doc_lengths)[0], own_row(src_lengths)[0]
    rank_row, limit_row = own_row(ctx_rank)[0], own_row(ctx_limit)[0]
    self_query, self_key, self_value, other_query, other_key, other_value, hidden_in = [
        whole_weight(w, "dp", "tp")
        for w in (attn_q, attn_k, attn_v, cross_q, cross_k, cross_v, ffn_in)
    ]
    self_out, other_out, hidden_out = [
        whole_weight(w, "tp", "dp") for w in (attn_o, cross_o, ffn_out)
    ]
    hidden_bias = lax.all_gather(ffn_bias_in, ("tp", "dp"), axis=0, tiled=True)

    def own_mask(first_row, block_rows):
        return self_visible(
            lengths, rank_row, limit_row, query_row.shape[1], first_row, block_rows
        )

    def other_mask(first_row, block_rows):
        return cross_visible(
            lengths,
            source_lengths,
            query_row.shape[1],
            source_row.shape[1],
            first_row,
            block_rows,
        )

    self_queries = project(query_row, self_query).astype(low)
    self_keys = project(embed_row, self_key).astype(low)
    self_values = project(embed_row, self_value).astype(low)
    self_context, self_totals = attend_forward(
        self_queries[0], self_keys[0], self_values[0], own_mask, HEADS
    )
    self_low = self_context.astype(low)[None]
    first_sum = query_row.astype(jnp.float32) + project(self_low, self_out)
    hidden_one, first_back = jax.vjp(layer_norm, first_sum, norm_gain[0], norm_bias[0])
    hidden_one_low = hidden_one.astype(low)
    cross_queries = project(hidden_one_low, other_query).astype(low)
    cross_keys = project(source_row, other_key).astype(low)
    cross_values = project(source_row, other_value).astype(low)
    cross_context, cross_totals = attend_forward(
        cross_queries[0], cross_keys[0], cross_values[0], other_mask, HEADS
    )
    cross_low = cross_context.astype(low)[None]
    second_sum = hidden_one + project(cross_low, other_out)
    hidden_two, second_back = jax.vjp(layer_norm, second_sum, norm_gain[1], norm_bias[1])
    hidden_two_low = hidden_two.astype(low)
    ffn_pre = project(hidden_two_low, hidden_in) + hidden_bias.astype(jnp.float32)
    ffn_gate, gelu_back = jax.vjp(gelu_exact, ffn_pre)
    ffn_act = ffn_gate.astype(low)
    third_sum = hidden_two + project(ffn_act, hidden_out) + ffn_bias_out
    mixed, third_back = jax.vjp(layer_norm, third_sum, norm_gain[2], norm_bias[2])
    grad_third, gain_two, shift_two = third_back(grad_row.astype(jnp.float32))
    grad_ffn = grad_third.astype(low)
    grad_bias_out = jnp.sum(grad_ffn.astype(jnp.float32), axis=(0, 1))
    grad_down = outer_sum(ffn_act, grad_ffn)
    grad_pre = gelu_back(project_back(grad_ffn, hidden_out))[0].astype(low)
    grad_up = outer_sum(hidden_two_low, grad_pre)
    grad_bias_in = jnp.sum(grad_pre.astype(jnp.float32), axis=(0, 1))
    grad_two = grad_third + project_back(grad_pre, hidden_in)
    grad_second, gain_one, shift_one = second_back(grad_two)
    grad_cross = grad_second.astype(low)
    grad_other_out = outer_sum(cross_low, grad_cross)
    grad_cross_ctx = project_back(grad_cross, other_out).astype(low)
    cross_dq, cross_dk, cross_dv = [
        g[None]
        for g in attend_backward(
            cross_queries[0],
            cross_keys[0],
            cross_values[0],
            other_mask,
            cross_totals,
            grad_cross_ctx[0],
            HEADS,
        )
    ]
    grad_other_query = outer_sum(hidden_one_low, cross_dq)
    grad_other_key = outer_sum(source_row, cross_dk)
    grad_other_value = outer_sum(source_row, cross_dv)
    grad_encoder = project_back(cross_dk, other_key) + project_back(cross_dv, other_value)
    grad_one = grad_second + project_back(cross_dq, other_query)
    grad_first, gain_zero, shift_zero = first_back(grad_one)
    grad_attn = grad_first.astype(low)
    grad_self_out = outer_sum(self_low, grad_attn)
    grad_self_ctx = project_back(grad_attn, self_out).astype(low)
    self_dq, self_dk, self_dv = [
        g[None]
        for g in attend_backward(
            self_queries[0],
            self_keys[0],
            self_values[0],
            own_mask,
            self_totals,
            grad_self_ctx[0],
            HEADS,
        )
    ]
    grad_self_query = outer_sum(query_row, self_dq)
    grad_self_key = outer_sum(embed_row, self_dk)
    grad_self_value = outer_sum(embed_row, self_dv)
    grad_embed = project_back(self_dk, self_key) + project_back(self_dv, self_value)
    grad_query = grad_first + project_back(self_dq, self_query)
    gain_grads = jnp.stack([gain_zero, gain_one, gain_two])
    shift_grads = jnp.stack([shift_zero, shift_one, shift_two])
    gain_grads, shift_grads, grad_bias_out = lax.psum(
        (gain_grads, shift_grads, grad_bias_out), ("dp", "tp")
    )
    return (
        from_row(mixed.astype(low)),
        from_row(grad_query.astype(low)).astype(jnp.float32),
        from_row(grad_embed.astype(low)).astype(jnp.float32),
        from_row(grad_encoder.astype(low)).astype(jnp.float32),
        own_weight(grad_self_query, "dp", "tp"),
        own_weight(grad_self_key, "dp", "tp"),
        own_weight(grad_self_value, "dp", "tp"),
        own_weight(grad_self_out, "tp", "dp"),
        own_weight(grad_other_query, "dp", "tp"),
        own_weight(grad_other_key, "dp", "tp"),
        own_weight(grad_other_value, "dp", "tp"),
        own_weight(grad_other_out, "tp", "dp"),
        own_weight(grad_up, "dp", "tp"),
        lax.psum_scatter(
            grad_bias_in.astype(low), ("tp", "dp"), scatter_dimension=0, tiled=True
        ).astype(jnp.float32),
        own_weight(grad_down, "tp", "dp"),
        grad_bias_out,
        gain_grads,
        shift_grads,
    )


def local(*arrays):
    rows_here = arrays[0].shape[0]
    if rows_here == lax.axis_size("tp"):
        return local_rows(*arrays)
    return local_split(*arrays)


def solution(mesh):
    in_specs = (
        P("dp", "tp", None),
        P("dp", "tp", None),
        P("dp", "tp", None),
        P("dp", "tp", None),
        P("dp", "tp"),
        P("dp", "tp"),
        P("dp", "tp"),
        P("tp", "dp"),
        P("dp", "tp"),
        P("dp", "tp"),
        P("dp", "tp"),
        P("tp", "dp"),
        P("dp", "tp"),
        P(("tp", "dp")),
        P("tp", "dp"),
        P(),
        P(),
        P(),
        P("dp", None),
        P("dp", None),
        P("dp", None),
        P("dp", None),
    )
    out_specs = (
        P("dp", "tp", None),
        P("dp", "tp", None),
        P("dp", "tp", None),
        P("dp", "tp", None),
        P("dp", "tp"),
        P("dp", "tp"),
        P("dp", "tp"),
        P("tp", "dp"),
        P("dp", "tp"),
        P("dp", "tp"),
        P("dp", "tp"),
        P("tp", "dp"),
        P("dp", "tp"),
        P(("tp", "dp")),
        P("tp", "dp"),
        P(),
        P(),
        P(),
    )
    return jax.shard_map(local, mesh=mesh, in_specs=in_specs, out_specs=out_specs, check_vma=False)
```

```python
import jax
import jax.numpy as jnp
from jax import lax
from jax.experimental import pallas as pl
from jax.experimental.pallas import tpu as pltpu
from jax.sharding import PartitionSpec as P

HEADS = 8


EPSILON = 1e-05
score_tile = 512


def layer_norm(values, scale_vec, shift_vec):
    average = jnp.mean(values, axis=-1, keepdims=True)
    centred = values - average
    spread = jnp.mean(centred * centred, axis=-1, keepdims=True)
    return centred * lax.rsqrt(spread + EPSILON) * scale_vec + shift_vec


def gelu_exact(values):
    return 0.5 * values * (1.0 + lax.erf(values * 0.7071067811865476))


def project(inputs, matrix):
    return jnp.einsum("rld,de->rle", inputs, matrix, preferred_element_type=jnp.float32)


def project_back(cotangent, matrix):
    return jnp.einsum("rle,de->rld", cotangent, matrix, preferred_element_type=jnp.float32)


def outer_sum(inputs, cotangent):
    return jnp.einsum("rld,rle->de", inputs, cotangent, preferred_element_type=jnp.float32)


def layout(lengths, length):
    offsets = jnp.cumsum(lengths) - lengths
    positions = jnp.arange(length, dtype=jnp.int32)
    passed = positions[:, None] >= offsets[None, :]
    document = jnp.sum(passed.astype(jnp.int32), axis=1) - 1
    doc_start = jnp.max(jnp.where(passed, offsets[None, :], 0), axis=1)
    return (document, doc_start)


def self_visible(lengths, rank_row, limit_row, length, first_row, block_rows):
    document, doc_start = layout(lengths, length)
    positions = jnp.arange(length, dtype=jnp.int32)
    rows_pos = positions[first_row : first_row + block_rows]
    same_text = document[first_row : first_row + block_rows, None] == document[None, :]
    chosen = (rank_row[None, :] < limit_row[first_row : first_row + block_rows, None]) & (
        rows_pos[:, None] != positions[None, :]
    )
    opener = positions[None, :] == doc_start[first_row : first_row + block_rows, None]
    return same_text & (chosen | opener)


def cross_visible(lengths, src_lengths, length, src_length, first_row, block_rows):
    document, _ = layout(lengths, length)
    source_doc, _ = layout(src_lengths, src_length)
    return document[first_row : first_row + block_rows, None] == source_doc[None, :]


def attend_forward(queries, keys_all, values_all, visible_of, head_count):
    query_count = queries.shape[0]
    head_size = queries.shape[1] // head_count
    factor = head_size ** (-0.5)
    queries = queries.reshape(query_count, head_count, head_size)
    keys_all = keys_all.reshape(keys_all.shape[0], head_count, head_size)
    values_all = values_all.reshape(values_all.shape[0], head_count, head_size)
    block_rows = min(score_tile, query_count)
    outputs = []
    totals = []
    for first_row in range(0, query_count, block_rows):
        query_part = queries[first_row : first_row + block_rows]
        scores = (
            jnp.einsum("qhd,khd->hqk", query_part, keys_all, preferred_element_type=jnp.float32)
            * factor
        )
        scores = jnp.where(visible_of(first_row, block_rows)[None], scores, -1e30)
        highest = jnp.max(scores, axis=-1, keepdims=True)
        exponent = jnp.exp(scores - highest)
        denominator = jnp.sum(exponent, axis=-1, keepdims=True)
        weights_low = (exponent / denominator).astype(jnp.bfloat16)
        outputs.append(
            jnp.einsum("hqk,khd->qhd", weights_low, values_all, preferred_element_type=jnp.float32)
        )
        totals.append(highest[..., 0] + jnp.log(denominator[..., 0]))
    context = jnp.concatenate(outputs, axis=0).reshape(query_count, head_count * head_size)
    return (context, jnp.concatenate(totals, axis=1))


def attend_backward(queries, keys_all, values_all, visible_of, totals, grad_context, head_count):
    query_count = queries.shape[0]
    key_count = keys_all.shape[0]
    head_size = queries.shape[1] // head_count
    factor = head_size ** (-0.5)
    queries = queries.reshape(query_count, head_count, head_size)
    keys_all = keys_all.reshape(key_count, head_count, head_size)
    values_all = values_all.reshape(key_count, head_count, head_size)
    grad_context = grad_context.reshape(query_count, head_count, head_size)
    grad_keys = jnp.zeros((key_count, head_count, head_size), jnp.float32)
    grad_values = jnp.zeros((key_count, head_count, head_size), jnp.float32)
    grad_queries = []
    block_rows = min(score_tile, query_count)
    for first_row in range(0, query_count, block_rows):
        query_part = queries[first_row : first_row + block_rows]
        grad_part = grad_context[first_row : first_row + block_rows]
        scores = (
            jnp.einsum("qhd,khd->hqk", query_part, keys_all, preferred_element_type=jnp.float32)
            * factor
        )
        scores = jnp.where(visible_of(first_row, block_rows)[None], scores, -1e30)
        weights_full = jnp.exp(scores - totals[:, first_row : first_row + block_rows, None])
        grad_weights = jnp.einsum(
            "qhd,khd->hqk", grad_part, values_all, preferred_element_type=jnp.float32
        )
        inner = jnp.sum(grad_weights * weights_full, axis=-1, keepdims=True)
        grad_scores = (weights_full * (grad_weights - inner)).astype(jnp.bfloat16)
        grad_queries.append(
            jnp.einsum("hqk,khd->qhd", grad_scores, keys_all, preferred_element_type=jnp.float32)
            * factor
        )
        grad_keys = (
            grad_keys
            + jnp.einsum(
                "hqk,qhd->khd", grad_scores, query_part, preferred_element_type=jnp.float32
            )
            * factor
        )
        grad_values = grad_values + jnp.einsum(
            "hqk,qhd->khd",
            weights_full.astype(jnp.bfloat16),
            grad_part,
            preferred_element_type=jnp.float32,
        )
    grad_queries = jnp.concatenate(grad_queries, axis=0).reshape(
        query_count, head_count * head_size
    )
    return (
        grad_queries.astype(jnp.bfloat16),
        grad_keys.reshape(key_count, -1).astype(jnp.bfloat16),
        grad_values.reshape(key_count, -1).astype(jnp.bfloat16),
    )


def collect(piece):
    return lax.all_gather(piece, "tp", axis=1, tiled=True)


def spread_sum(partial_sum):
    return lax.psum_scatter(partial_sum, "tp", scatter_dimension=1, tiled=True)


def collect_grad(piece):
    return lax.all_gather(piece, "tp", axis=1, tiled=True)


def send_back(partial_sum):
    return lax.psum_scatter(partial_sum, "tp", scatter_dimension=1, tiled=True)


def local_split(
    query_stream,
    token_embed,
    encoder_out,
    out_grad,
    attn_q,
    attn_k,
    attn_v,
    attn_o,
    cross_q,
    cross_k,
    cross_v,
    cross_o,
    ffn_in,
    ffn_bias_in,
    ffn_out,
    ffn_bias_out,
    norm_gain,
    norm_bias,
    doc_lengths,
    src_lengths,
    ctx_rank,
    ctx_limit,
):
    head_count = HEADS // lax.axis_size("tp")
    (
        self_query,
        self_key,
        self_value,
        self_out,
        other_query,
        other_key,
        other_value,
        other_out,
        hidden_in,
        hidden_bias,
        hidden_out,
    ) = (
        lax.all_gather(attn_q, "dp", axis=0, tiled=True),
        lax.all_gather(attn_k, "dp", axis=0, tiled=True),
        lax.all_gather(attn_v, "dp", axis=0, tiled=True),
        lax.all_gather(attn_o, "dp", axis=1, tiled=True),
        lax.all_gather(cross_q, "dp", axis=0, tiled=True),
        lax.all_gather(cross_k, "dp", axis=0, tiled=True),
        lax.all_gather(cross_v, "dp", axis=0, tiled=True),
        lax.all_gather(cross_o, "dp", axis=1, tiled=True),
        lax.all_gather(ffn_in, "dp", axis=0, tiled=True),
        lax.all_gather(ffn_bias_in, "dp", axis=0, tiled=True),
        lax.all_gather(ffn_out, "dp", axis=1, tiled=True),
    )

    def self_forward(row_items):
        queries, keys_all, values_all, lengths, rank_row, limit_row = row_items

        def visible_of(first_row, block_rows):
            return self_visible(
                lengths, rank_row, limit_row, keys_all.shape[0], first_row, block_rows
            )

        return attend_forward(queries, keys_all, values_all, visible_of, head_count)

    def self_backward(row_items):
        queries, keys_all, values_all, lengths, rank_row, limit_row, totals, grad_context = (
            row_items
        )

        def visible_of(first_row, block_rows):
            return self_visible(
                lengths, rank_row, limit_row, keys_all.shape[0], first_row, block_rows
            )

        return attend_backward(
            queries, keys_all, values_all, visible_of, totals, grad_context, head_count
        )

    def cross_forward(row_items):
        queries, keys_all, values_all, lengths, source_lengths = row_items

        def visible_of(first_row, block_rows):
            return cross_visible(
                lengths, source_lengths, queries.shape[0], keys_all.shape[0], first_row, block_rows
            )

        return attend_forward(queries, keys_all, values_all, visible_of, head_count)

    def cross_backward(row_items):
        queries, keys_all, values_all, lengths, source_lengths, totals, grad_context = row_items

        def visible_of(first_row, block_rows):
            return cross_visible(
                lengths, source_lengths, queries.shape[0], keys_all.shape[0], first_row, block_rows
            )

        return attend_backward(
            queries, keys_all, values_all, visible_of, totals, grad_context, head_count
        )

    query_all = collect(query_stream)
    embed_all = collect(token_embed)
    source_all = collect(encoder_out)
    self_queries = project(query_all, self_query).astype(jnp.bfloat16)
    self_keys = project(embed_all, self_key).astype(jnp.bfloat16)
    self_values = project(embed_all, self_value).astype(jnp.bfloat16)
    self_context, self_totals = lax.map(
        self_forward, (self_queries, self_keys, self_values, doc_lengths, ctx_rank, ctx_limit)
    )
    self_low = self_context.astype(jnp.bfloat16)
    first_sum = query_stream.astype(jnp.float32) + spread_sum(project(self_low, self_out))
    hidden_one, first_back = jax.vjp(layer_norm, first_sum, norm_gain[0], norm_bias[0])
    hidden_one_all = collect(hidden_one.astype(jnp.bfloat16))
    cross_queries = project(hidden_one_all, other_query).astype(jnp.bfloat16)
    cross_keys = project(source_all, other_key).astype(jnp.bfloat16)
    cross_values = project(source_all, other_value).astype(jnp.bfloat16)
    cross_context, cross_totals = lax.map(
        cross_forward, (cross_queries, cross_keys, cross_values, doc_lengths, src_lengths)
    )
    cross_low = cross_context.astype(jnp.bfloat16)
    second_sum = hidden_one + spread_sum(project(cross_low, other_out))
    hidden_two, second_back = jax.vjp(layer_norm, second_sum, norm_gain[1], norm_bias[1])
    hidden_two_low = hidden_two.astype(jnp.bfloat16)
    ffn_inputs = lax.all_gather(hidden_two_low, "tp", axis=1, tiled=True)
    ffn_pre = project(ffn_inputs, hidden_in) + hidden_bias.astype(jnp.float32)
    ffn_gate, gelu_back = jax.vjp(gelu_exact, ffn_pre)
    ffn_act = ffn_gate.astype(jnp.bfloat16)
    ffn_branch = (
        lax.psum_scatter(project(ffn_act, hidden_out), "tp", scatter_dimension=1, tiled=True)
        + ffn_bias_out
    )
    third_sum = hidden_two + ffn_branch
    mixed_full, third_back = jax.vjp(layer_norm, third_sum, norm_gain[2], norm_bias[2])
    grad_third, gain_two, shift_two = third_back(out_grad.astype(jnp.float32))
    grad_ffn = grad_third.astype(jnp.bfloat16)
    grad_bias_out = jnp.sum(grad_ffn.astype(jnp.float32), axis=(0, 1))
    grad_ffn_all = lax.all_gather(grad_ffn, "tp", axis=1, tiled=True)
    grad_act = project_back(grad_ffn_all, hidden_out)
    grad_down = outer_sum(ffn_act, grad_ffn_all)
    grad_pre = gelu_back(grad_act)[0].astype(jnp.bfloat16)
    grad_up = outer_sum(ffn_inputs, grad_pre)
    grad_bias_in = jnp.sum(grad_pre.astype(jnp.float32), axis=(0, 1))
    grad_two = grad_third + lax.psum_scatter(
        project_back(grad_pre, hidden_in), "tp", scatter_dimension=1, tiled=True
    )
    grad_second, gain_one, shift_one = second_back(grad_two)
    grad_cross_all = collect_grad(grad_second.astype(jnp.bfloat16))
    grad_other_out = outer_sum(cross_low, grad_cross_all)
    grad_cross_ctx = project_back(grad_cross_all, other_out).astype(jnp.bfloat16)
    cross_dq, cross_dk, cross_dv = lax.map(
        cross_backward,
        (
            cross_queries,
            cross_keys,
            cross_values,
            doc_lengths,
            src_lengths,
            cross_totals,
            grad_cross_ctx,
        ),
    )
    grad_other_query = outer_sum(hidden_one_all, cross_dq)
    grad_other_key = outer_sum(source_all, cross_dk)
    grad_other_value = outer_sum(source_all, cross_dv)
    grad_encoder = send_back(
        project_back(cross_dk, other_key) + project_back(cross_dv, other_value)
    )
    grad_one = grad_second + send_back(project_back(cross_dq, other_query))
    grad_first, gain_zero, shift_zero = first_back(grad_one)
    grad_attn_all = collect_grad(grad_first.astype(jnp.bfloat16))
    grad_self_out = outer_sum(self_low, grad_attn_all)
    grad_self_ctx = project_back(grad_attn_all, self_out).astype(jnp.bfloat16)
    self_dq, self_dk, self_dv = lax.map(
        self_backward,
        (
            self_queries,
            self_keys,
            self_values,
            doc_lengths,
            ctx_rank,
            ctx_limit,
            self_totals,
            grad_self_ctx,
        ),
    )
    grad_self_query = outer_sum(query_all, self_dq)
    grad_self_key = outer_sum(embed_all, self_dk)
    grad_self_value = outer_sum(embed_all, self_dv)
    grad_embed = send_back(project_back(self_dk, self_key) + project_back(self_dv, self_value))
    grad_query = grad_first + send_back(project_back(self_dq, self_query))
    (
        grad_self_query,
        grad_self_key,
        grad_self_value,
        grad_self_out,
        grad_other_query,
        grad_other_key,
        grad_other_value,
        grad_other_out,
        grad_up,
        grad_bias_in,
        grad_down,
    ) = (
        lax.psum_scatter(
            grad_self_query.astype(jnp.bfloat16), "dp", scatter_dimension=0, tiled=True
        ).astype(jnp.float32),
        lax.psum_scatter(
            grad_self_key.astype(jnp.bfloat16), "dp", scatter_dimension=0, tiled=True
        ).astype(jnp.float32),
        lax.psum_scatter(
            grad_self_value.astype(jnp.bfloat16), "dp", scatter_dimension=0, tiled=True
        ).astype(jnp.float32),
        lax.psum_scatter(
            grad_self_out.astype(jnp.bfloat16), "dp", scatter_dimension=1, tiled=True
        ).astype(jnp.float32),
        lax.psum_scatter(
            grad_other_query.astype(jnp.bfloat16), "dp", scatter_dimension=0, tiled=True
        ).astype(jnp.float32),
        lax.psum_scatter(
            grad_other_key.astype(jnp.bfloat16), "dp", scatter_dimension=0, tiled=True
        ).astype(jnp.float32),
        lax.psum_scatter(
            grad_other_value.astype(jnp.bfloat16), "dp", scatter_dimension=0, tiled=True
        ).astype(jnp.float32),
        lax.psum_scatter(
            grad_other_out.astype(jnp.bfloat16), "dp", scatter_dimension=1, tiled=True
        ).astype(jnp.float32),
        lax.psum_scatter(
            grad_up.astype(jnp.bfloat16), "dp", scatter_dimension=0, tiled=True
        ).astype(jnp.float32),
        lax.psum_scatter(
            grad_bias_in.astype(jnp.bfloat16), "dp", scatter_dimension=0, tiled=True
        ).astype(jnp.float32),
        lax.psum_scatter(
            grad_down.astype(jnp.bfloat16), "dp", scatter_dimension=1, tiled=True
        ).astype(jnp.float32),
    )
    gain_grads = jnp.stack([gain_zero, gain_one, gain_two])
    shift_grads = jnp.stack([shift_zero, shift_one, shift_two])
    gain_grads, shift_grads, grad_bias_out = lax.psum(
        (gain_grads, shift_grads, grad_bias_out), ("dp", "tp")
    )
    return (
        mixed_full.astype(jnp.bfloat16),
        grad_query,
        grad_embed,
        grad_encoder,
        grad_self_query,
        grad_self_key,
        grad_self_value,
        grad_self_out,
        grad_other_query,
        grad_other_key,
        grad_other_value,
        grad_other_out,
        grad_up,
        grad_bias_in,
        grad_down,
        grad_bias_out,
        gain_grads,
        shift_grads,
    )


MESH = pl.DeviceIdType.MESH
LOW = jnp.bfloat16
WIDE = jnp.float32


class Place:
    def __init__(self):
        dp, tp = lax.axis_index("dp"), lax.axis_index("tp")
        self.dp, self.tp = dp, tp
        self.z, self.x = dp // 2, lax.rem(dp, 2)
        self.y, self.core = tp // 2, lax.rem(tp, 2)
        self.core_peer = (dp, 2 * self.y + 1 - self.core)
        self.y_peer = (dp, 2 * (1 - self.y) + self.core)
        self.far_peer = (dp, 2 * (1 - self.y) + 1 - self.core)
        self.x_peer = (2 * self.z + 1 - self.x, tp)

    def z_at(self, step):
        return lax.rem(self.z + step, 4)

    def z_peer(self, step):
        return (2 * self.z_at(step) + self.x, self.tp)

    def meet(self):
        peers = [self.core_peer, self.y_peer, self.far_peer, self.x_peer]
        peers += [self.z_peer(step) for step in (1, 2, 3)]
        barrier = pltpu.get_barrier_semaphore()
        for peer in peers:
            pl.semaphore_signal(barrier, inc=1, device_id=peer, device_id_type=MESH)
        pl.semaphore_wait(barrier, len(peers))


def send(source, target, send_sem, recv_sem, peer):
    copy = pltpu.make_async_remote_copy(
        src_ref=source,
        dst_ref=target,
        send_sem=send_sem,
        recv_sem=recv_sem,
        device_id=peer,
        device_id_type=MESH,
    )
    copy.start()
    return copy


def cols(index, width):
    return pl.ds(pl.multiple_of(index * width, width), width)


class Gather:
    def __init__(self, place, local, full, first, count, sends, recvs, own_sem):
        self.place, self.local, self.full = place, local, full
        self.items = pl.ds(first, count)
        self.width = local.shape[-1]
        self.sends, self.recvs, self.own_sem = sends, recvs, own_sem
        self.pending = []
        self.sent = []

    def _send(self, source, target, slot, peer):
        copy = send(source, target, self.sends.at[slot], self.recvs.at[slot], peer)
        self.pending.append(copy)
        self.sent.append(copy)

    def _arrive(self):
        for copy in self.pending:
            copy.wait_recv()
        self.pending = []

    def stage(self, number):
        p = self.place
        mine, other = cols(p.tp, self.width), cols(2 * (1 - p.y) + p.core, self.width)
        if number == 0:
            source = self.local.at[self.items]
            target = self.full.at[self.items, p.z, p.x, :, mine]
            self.own = pltpu.make_async_copy(source, target, self.own_sem)
            self.own.start()
            for step in (1, 2, 3):
                self._send(source, target, step - 1, p.z_peer(step))
            return
        self._arrive()
        if number == 1:
            self.own.wait()
            block = self.full.at[self.items, :, p.x, :, mine]
            self._send(block, block, 3, p.y_peer)
        elif number == 2:
            for slot, side in ((4, mine), (5, other)):
                block = self.full.at[self.items, :, p.x, :, side]
                self._send(block, block, slot, p.x_peer)
        elif number == 3:
            for slot, side in ((6, mine), (7, other)):
                block = self.full.at[self.items, :, :, :, side]
                self._send(block, block, slot, p.core_peer)
        else:
            for copy in self.sent:
                copy.wait_send()


GATHER_SLOTS = 8


class ToRow:
    def __init__(self, place, local, row, sends, recvs, own_sem):
        size = local.shape[1]
        p = place
        here = pl.ds(pl.multiple_of(p.tp * size, size), size)
        self.own = pltpu.make_async_copy(local.at[p.tp], row.at[here], own_sem)
        self.own.start()
        self.copies = [
            send(local.at[peer[1]], row.at[here], sends.at[slot], recvs.at[slot], peer)
            for slot, peer in enumerate((p.y_peer, p.far_peer, p.core_peer))
        ]

    def arrive(self):
        self.own.wait()
        for copy in self.copies:
            copy.wait_recv()

    def finish(self):
        for copy in self.copies:
            copy.wait_send()


class FromRow:
    def __init__(self, place, row, blocks, sends, recvs, own_sem):
        size = blocks.shape[1]
        p = place

        def part(tp):
            return row.at[pl.ds(pl.multiple_of(tp * size, size), size)]

        self.own = pltpu.make_async_copy(part(p.tp), blocks.at[p.tp], own_sem)
        self.own.start()
        self.copies = [
            send(part(peer[1]), blocks.at[p.tp], sends.at[slot], recvs.at[slot], peer)
            for slot, peer in enumerate((p.y_peer, p.far_peer, p.core_peer))
        ]

    def finish(self):
        self.own.wait()
        for copy in self.copies:
            copy.wait()


def gather_kernel(
    query, embed, source, cotangent, squares, wides, biases,
    query_row, embed_row, source_row, cotangent_row, all_squares, all_wides, all_biases,
    row_sends, row_recvs, row_own, sends, recvs, own,
):
    place = Place()
    place.meet()
    groups = [
        (squares, all_squares, 0, 2),
        (squares, all_squares, 2, 2),
        (squares, all_squares, 4, 4),
        (wides, all_wides, 0, 1),
        (biases, all_biases, 0, 1),
        (wides, all_wides, 1, 1),
    ]
    gathers = [
        Gather(place, *group, sends.at[i], recvs.at[i], own.at[i])
        for i, group in enumerate(groups)
    ]
    streams = [
        (embed, embed_row),
        (query, query_row),
        (source, source_row),
        (cotangent, cotangent_row),
    ]
    rows = []
    for tick in range(len(gathers) + 4):
        if tick < len(streams):
            rows.append(
                ToRow(place, *streams[tick], row_sends.at[tick], row_recvs.at[tick], row_own.at[tick])
            )
        for stage in range(5):
            if 0 <= tick - stage < len(gathers):
                gathers[tick - stage].stage(stage)
    for row in rows:
        row.arrive()
        row.finish()


def gather_all(query, embed, source, cotangent, squares, wides, biases):
    hbm = pl.BlockSpec(memory_space=pl.ANY)
    shape = jax.ShapeDtypeStruct
    row = shape((4 * query.shape[1], query.shape[2]), LOW)
    dma = pltpu.SemaphoreType.DMA
    full = [shape((n, 4, 2, h, 4 * w), LOW) for n, h, w in (a.shape for a in (squares, wides, biases))]
    outs = pl.pallas_call(
        gather_kernel,
        out_shape=[row] * 4 + full,
        in_specs=[hbm] * 7,
        out_specs=[hbm] * 7,
        scratch_shapes=[
            dma((4, 3)), dma((4, 3)), dma((4,)),
            dma((6, GATHER_SLOTS)), dma((6, GATHER_SLOTS)), dma((6,)),
        ],
        compiler_params=pltpu.CompilerParams(collective_id=0, has_side_effects=True),
        name="gather_all",
    )(query, embed, source, cotangent, squares, wides, biases)
    rows, full = outs[:4], outs[4:]
    return rows, [w.reshape(w.shape[0], -1, w.shape[-1]) for w in full]


class Scatter:
    def __init__(self, place, parts, half, quarter, eighth, last, out, first, count, sends, recvs):
        self.place, self.parts = place, parts
        self.half, self.quarter, self.eighth, self.last = half, quarter, eighth, last
        self.out = out
        self.first, self.count = first, count
        self.items = pl.ds(first, count)
        self.width = out.shape[-1]
        self.sends, self.recvs = sends, recvs
        self.pending = []
        self.sent = []

    def _send(self, source, target, slot, peer):
        copy = send(source, target, self.sends.at[slot], self.recvs.at[slot], peer)
        self.pending.append(copy)
        self.sent.append(copy)

    def _arrive(self):
        for copy in self.pending:
            copy.wait_recv()
        self.pending = []

    def stage(self, number):
        p = self.place
        width = self.width
        mine = cols(p.tp, width)
        other = cols(2 * (1 - p.y) + p.core, width)
        if number == 0:
            for side, column in ((0, p.core_peer[1]), (1, p.far_peer[1])):
                source = self.parts.at[self.items, :, :, :, cols(column, width)]
                self._send(source, self.half.at[self.items, side], side, p.core_peer)
            return
        self._arrive()
        if number == 1:
            for item in range(self.first, self.first + self.count):
                for side, column in ((0, mine), (1, other)):

                    @pl.loop(0, 4)
                    def _(z):
                        total = self.parts[item, z, :, :, column].astype(WIDE)
                        total = total + self.half[item, side, z].astype(WIDE)
                        self.half[item, side, z] = total.astype(LOW)

            for side in (0, 1):
                source = self.half.at[self.items, side, :, 1 - p.x]
                self._send(source, self.quarter.at[self.items, side], 2 + side, p.x_peer)
        elif number == 2:
            for item in range(self.first, self.first + self.count):
                for side in (0, 1):

                    @pl.loop(0, 4)
                    def _(z):
                        total = self.half[item, side, z, p.x].astype(WIDE)
                        total = total + self.quarter[item, side, z].astype(WIDE)
                        self.quarter[item, side, z] = total.astype(LOW)

            self._send(self.quarter.at[self.items, 1], self.eighth.at[self.items], 4, p.y_peer)
        elif number == 3:
            for item in range(self.first, self.first + self.count):

                @pl.loop(0, 4)
                def _(z):
                    total = self.quarter[item, 0, z].astype(WIDE)
                    total = total + self.eighth[item, z].astype(WIDE)
                    self.eighth[item, z] = total.astype(LOW)

            for step in (1, 2, 3):
                source = self.eighth.at[self.items, p.z_at(step)]
                target = self.last.at[self.items, step - 1]
                self._send(source, target, 4 + step, p.z_peer(step))
        else:
            for item in range(self.first, self.first + self.count):
                total = self.eighth[item, p.z].astype(WIDE)
                for step in range(3):
                    total = total + self.last[item, step].astype(WIDE)
                self.out[item] = total
            for copy in self.sent:
                copy.wait_send()


SCATTER_SLOTS = 8


class SumAll:
    def __init__(self, place, values, arrived, sends, recvs):
        self.place, self.values, self.arrived = place, values, arrived
        self.sends, self.recvs = sends, recvs
        self.copy = None

    def stage(self, number):
        p = self.place
        if self.copy is not None:
            self.copy.wait()
            self.values[...] = self.values[...] + self.arrived[number - 1]
        if number < 5:
            z_one = (2 * (p.z + 1 - 2 * lax.rem(p.z, 2)) + p.x, p.tp)
            z_two = (2 * lax.rem(p.z + 2, 4) + p.x, p.tp)
            peer = (p.core_peer, p.x_peer, p.y_peer, z_one, z_two)[number]
            self.copy = send(
                self.values, self.arrived.at[number], self.sends.at[number], self.recvs.at[number], peer
            )


def scatter_kernel(
    squares, wides, small, mixed, grad_query, grad_embed, grad_encoder,
    own_squares, own_wides, small_sum, mixed_blocks, query_blocks, embed_blocks, encoder_blocks,
    half_s, quarter_s, eighth_s, last_s, half_w, quarter_w, eighth_w, last_w, arrived,
    row_sends, row_recvs, row_own, sends, recvs, small_sends, small_recvs,
):
    place = Place()
    place.meet()
    rows = [
        FromRow(place, row, blocks, row_sends.at[i], row_recvs.at[i], row_own.at[i])
        for i, (row, blocks) in enumerate(
            (
                (mixed, mixed_blocks),
                (grad_encoder, encoder_blocks),
                (grad_embed, embed_blocks),
                (grad_query, query_blocks),
            )
        )
    ]
    small_sum[...] = small[...]
    sum_all = SumAll(place, small_sum, arrived, small_sends, small_recvs)
    square = (squares, half_s, quarter_s, eighth_s, last_s, own_squares)
    wide = (wides, half_w, quarter_w, eighth_w, last_w, own_wides)
    groups = [(wide, 0, 1), (wide, 1, 1), (square, 4, 4), (square, 2, 2), (square, 0, 2)]
    scatters = [
        Scatter(place, *buffers, first, count, sends.at[i], recvs.at[i])
        for i, (buffers, first, count) in enumerate(groups)
    ]
    for tick in range(len(scatters) + 4):
        for stage in range(5):
            if 0 <= tick - stage < len(scatters):
                scatters[tick - stage].stage(stage)
        if tick < 6:
            sum_all.stage(tick)
    for row in rows:
        row.finish()


def scatter_all(squares, wides, small, rows):
    hbm = pl.BlockSpec(memory_space=pl.ANY)
    vmem = pl.BlockSpec(memory_space=pltpu.VMEM)
    shape = jax.ShapeDtypeStruct
    squares = squares.reshape(squares.shape[0], 4, 2, -1, squares.shape[-1])
    wides = wides.reshape(wides.shape[0], 4, 2, -1, wides.shape[-1])
    dma = pltpu.SemaphoreType.DMA
    length, features = rows[0].shape
    blocks = shape((4, length // 4, features), LOW)

    def steps(a):
        n, _, _, h, w = a.shape
        w = w // 4
        return [
            pltpu.VMEM((n, 2, 4, 2, h, w), LOW),
            pltpu.VMEM((n, 2, 4, h, w), LOW),
            pltpu.VMEM((n, 4, h, w), LOW),
            pltpu.VMEM((n, 3, h, w), LOW),
        ]

    def own(a):
        n, _, _, h, w = a.shape
        return shape((n, h, w // 4), WIDE)

    return pl.pallas_call(
        scatter_kernel,
        out_shape=[own(squares), own(wides), shape(small.shape, WIDE)] + [blocks] * 4,
        in_specs=[vmem] * 3 + [hbm] * 4,
        out_specs=[vmem] * 3 + [hbm] * 4,
        scratch_shapes=steps(squares)
        + steps(wides)
        + [
            pltpu.VMEM((5,) + small.shape, WIDE),
            dma((4, 3)), dma((4, 3)), dma((4,)),
            dma((5, SCATTER_SLOTS)), dma((5, SCATTER_SLOTS)), dma((5,)), dma((5,)),
        ],
        compiler_params=pltpu.CompilerParams(
            collective_id=1, has_side_effects=True, vmem_limit_bytes=56 * 2**20
        ),
        name="scatter_all",
    )(squares, wides, small, *rows)


def own_row(per_row):
    return lax.dynamic_slice_in_dim(per_row, lax.axis_index("tp"), 1, axis=0)


def local_rows(
    query_stream,
    token_embed,
    encoder_out,
    out_grad,
    attn_q,
    attn_k,
    attn_v,
    attn_o,
    cross_q,
    cross_k,
    cross_v,
    cross_o,
    ffn_in,
    ffn_bias_in,
    ffn_out,
    ffn_bias_out,
    norm_gain,
    norm_bias,
    doc_lengths,
    src_lengths,
    ctx_rank,
    ctx_limit,
):
    low = jnp.bfloat16
    squares = jnp.stack(
        [attn_q, attn_k, attn_v, attn_o.T, cross_q, cross_k, cross_v, cross_o.T]
    )
    wides = jnp.stack([ffn_in, ffn_out.T])
    biases = jnp.pad(ffn_bias_in[None, None], ((0, 0), (0, 15), (0, 64)))
    rows, (squares, wides, biases) = gather_all(
        query_stream, token_embed, encoder_out, out_grad, squares, wides, biases
    )
    query_row, embed_row, source_row, grad_row = [row[None] for row in rows]
    lengths, source_lengths = own_row(doc_lengths)[0], own_row(src_lengths)[0]
    rank_row, limit_row = own_row(ctx_rank)[0], own_row(ctx_limit)[0]
    self_query, self_key, self_value, other_query, other_key, other_value = (
        squares[i] for i in (0, 1, 2, 4, 5, 6)
    )
    self_out, other_out = squares[3].T, squares[7].T
    hidden_in, hidden_out = wides[0], wides[1].T
    hidden_bias = biases.reshape(8, 16, 4, 128)[:, 0, :, :64].transpose(1, 0, 2).reshape(-1)

    def own_mask(first_row, block_rows):
        return self_visible(
            lengths, rank_row, limit_row, query_row.shape[1], first_row, block_rows
        )

    def other_mask(first_row, block_rows):
        return cross_visible(
            lengths,
            source_lengths,
            query_row.shape[1],
            source_row.shape[1],
            first_row,
            block_rows,
        )

    self_queries = project(query_row, self_query).astype(low)
    self_keys = project(embed_row, self_key).astype(low)
    self_values = project(embed_row, self_value).astype(low)
    self_context, self_totals = attend_forward(
        self_queries[0], self_keys[0], self_values[0], own_mask, HEADS
    )
    self_low = self_context.astype(low)[None]
    first_sum = query_row.astype(jnp.float32) + project(self_low, self_out)
    hidden_one, first_back = jax.vjp(layer_norm, first_sum, norm_gain[0], norm_bias[0])
    hidden_one_low = hidden_one.astype(low)
    cross_queries = project(hidden_one_low, other_query).astype(low)
    cross_keys = project(source_row, other_key).astype(low)
    cross_values = project(source_row, other_value).astype(low)
    cross_context, cross_totals = attend_forward(
        cross_queries[0], cross_keys[0], cross_values[0], other_mask, HEADS
    )
    cross_low = cross_context.astype(low)[None]
    second_sum = hidden_one + project(cross_low, other_out)
    hidden_two, second_back = jax.vjp(layer_norm, second_sum, norm_gain[1], norm_bias[1])
    hidden_two_low = hidden_two.astype(low)
    ffn_pre = project(hidden_two_low, hidden_in) + hidden_bias.astype(jnp.float32)
    ffn_gate, gelu_back = jax.vjp(gelu_exact, ffn_pre)
    ffn_act = ffn_gate.astype(low)
    third_sum = hidden_two + project(ffn_act, hidden_out) + ffn_bias_out
    mixed, third_back = jax.vjp(layer_norm, third_sum, norm_gain[2], norm_bias[2])
    grad_third, gain_two, shift_two = third_back(grad_row.astype(jnp.float32))
    grad_ffn = grad_third.astype(low)
    grad_bias_out = jnp.sum(grad_ffn.astype(jnp.float32), axis=(0, 1))
    grad_down = outer_sum(ffn_act, grad_ffn)
    grad_pre = gelu_back(project_back(grad_ffn, hidden_out))[0].astype(low)
    grad_up = outer_sum(hidden_two_low, grad_pre)
    grad_bias_in = jnp.sum(grad_pre.astype(jnp.float32), axis=(0, 1))
    grad_two = grad_third + project_back(grad_pre, hidden_in)
    grad_second, gain_one, shift_one = second_back(grad_two)
    grad_cross = grad_second.astype(low)
    grad_other_out = outer_sum(cross_low, grad_cross)
    grad_cross_ctx = project_back(grad_cross, other_out).astype(low)
    cross_dq, cross_dk, cross_dv = [
        g[None]
        for g in attend_backward(
            cross_queries[0],
            cross_keys[0],
            cross_values[0],
            other_mask,
            cross_totals,
            grad_cross_ctx[0],
            HEADS,
        )
    ]
    grad_other_query = outer_sum(hidden_one_low, cross_dq)
    grad_other_key = outer_sum(source_row, cross_dk)
    grad_other_value = outer_sum(source_row, cross_dv)
    grad_encoder = project_back(cross_dk, other_key) + project_back(cross_dv, other_value)
    grad_one = grad_second + project_back(cross_dq, other_query)
    grad_first, gain_zero, shift_zero = first_back(grad_one)
    grad_attn = grad_first.astype(low)
    grad_self_out = outer_sum(self_low, grad_attn)
    grad_self_ctx = project_back(grad_attn, self_out).astype(low)
    self_dq, self_dk, self_dv = [
        g[None]
        for g in attend_backward(
            self_queries[0],
            self_keys[0],
            self_values[0],
            own_mask,
            self_totals,
            grad_self_ctx[0],
            HEADS,
        )
    ]
    grad_self_query = outer_sum(query_row, self_dq)
    grad_self_key = outer_sum(embed_row, self_dk)
    grad_self_value = outer_sum(embed_row, self_dv)
    grad_embed = project_back(self_dk, self_key) + project_back(self_dv, self_value)
    grad_query = grad_first + project_back(self_dq, self_query)
    small = jnp.concatenate(
        [grad_bias_in, gain_zero, gain_one, gain_two, shift_zero, shift_one, shift_two]
        + [grad_bias_out, jnp.zeros((8 * 2048 - 2048 - 7 * 512,), jnp.float32)]
    ).reshape(8, 2048)
    squares = jnp.stack(
        [grad_self_query, grad_self_key, grad_self_value, grad_self_out.T]
        + [grad_other_query, grad_other_key, grad_other_value, grad_other_out.T]
    ).astype(low)
    wides = jnp.stack([grad_up, grad_down.T]).astype(low)
    rows = [g[0].astype(low) for g in (mixed, grad_query, grad_embed, grad_encoder)]
    squares, wides, small, mixed, grad_query, grad_embed, grad_encoder = scatter_all(
        squares, wides, small, rows
    )
    small = small.reshape(-1)
    device = lax.axis_index("tp") * lax.axis_size("dp") + lax.axis_index("dp")
    grad_bias_in = lax.dynamic_slice_in_dim(small, device * 64, 64)
    vectors = small[2048 : 2048 + 7 * 512].reshape(7, 512)
    return (
        mixed,
        grad_query.astype(jnp.float32),
        grad_embed.astype(jnp.float32),
        grad_encoder.astype(jnp.float32),
        squares[0],
        squares[1],
        squares[2],
        squares[3].T,
        squares[4],
        squares[5],
        squares[6],
        squares[7].T,
        wides[0],
        grad_bias_in,
        wides[1].T,
        vectors[6],
        vectors[:3],
        vectors[3:6],
    )


def local(*arrays):
    if arrays[0].shape[0] == 4 and (lax.axis_size("dp"), lax.axis_size("tp")) == (8, 4):
        return local_rows(*arrays)
    return local_split(*arrays)


def solution(mesh):
    in_specs = (
        P("dp", "tp", None),
        P("dp", "tp", None),
        P("dp", "tp", None),
        P("dp", "tp", None),
        P("dp", "tp"),
        P("dp", "tp"),
        P("dp", "tp"),
        P("tp", "dp"),
        P("dp", "tp"),
        P("dp", "tp"),
        P("dp", "tp"),
        P("tp", "dp"),
        P("dp", "tp"),
        P(("tp", "dp")),
        P("tp", "dp"),
        P(),
        P(),
        P(),
        P("dp", None),
        P("dp", None),
        P("dp", None),
        P("dp", None),
    )
    out_specs = (
        P("dp", "tp", None),
        P("dp", "tp", None),
        P("dp", "tp", None),
        P("dp", "tp", None),
        P("dp", "tp"),
        P("dp", "tp"),
        P("dp", "tp"),
        P("tp", "dp"),
        P("dp", "tp"),
        P("dp", "tp"),
        P("dp", "tp"),
        P("tp", "dp"),
        P("dp", "tp"),
        P(("tp", "dp")),
        P("tp", "dp"),
        P(),
        P(),
        P(),
    )
    return jax.shard_map(local, mesh=mesh, in_specs=in_specs, out_specs=out_specs, check_vma=False)
```

```python
import jax
import jax.numpy as jnp
from jax import lax
from jax.experimental import pallas as pl
from jax.experimental.pallas import tpu as pltpu
from jax.sharding import PartitionSpec as P

HEADS = 8


EPSILON = 1e-05
score_tile = 512


def layer_norm(values, scale_vec, shift_vec):
    average = jnp.mean(values, axis=-1, keepdims=True)
    centred = values - average
    spread = jnp.mean(centred * centred, axis=-1, keepdims=True)
    return centred * lax.rsqrt(spread + EPSILON) * scale_vec + shift_vec


def gelu_exact(values):
    return 0.5 * values * (1.0 + lax.erf(values * 0.7071067811865476))


def project(inputs, matrix):
    return jnp.einsum("rld,de->rle", inputs, matrix, preferred_element_type=jnp.float32)


def project_back(cotangent, matrix):
    return jnp.einsum("rle,de->rld", cotangent, matrix, preferred_element_type=jnp.float32)


def outer_sum(inputs, cotangent):
    return jnp.einsum("rld,rle->de", inputs, cotangent, preferred_element_type=jnp.float32)


def layout(lengths, length):
    offsets = jnp.cumsum(lengths) - lengths
    positions = jnp.arange(length, dtype=jnp.int32)
    passed = positions[:, None] >= offsets[None, :]
    document = jnp.sum(passed.astype(jnp.int32), axis=1) - 1
    doc_start = jnp.max(jnp.where(passed, offsets[None, :], 0), axis=1)
    return (document, doc_start)


def self_visible(lengths, rank_row, limit_row, length, first_row, block_rows):
    document, doc_start = layout(lengths, length)
    positions = jnp.arange(length, dtype=jnp.int32)
    rows_pos = positions[first_row : first_row + block_rows]
    same_text = document[first_row : first_row + block_rows, None] == document[None, :]
    chosen = (rank_row[None, :] < limit_row[first_row : first_row + block_rows, None]) & (
        rows_pos[:, None] != positions[None, :]
    )
    opener = positions[None, :] == doc_start[first_row : first_row + block_rows, None]
    return same_text & (chosen | opener)


def cross_visible(lengths, src_lengths, length, src_length, first_row, block_rows):
    document, _ = layout(lengths, length)
    source_doc, _ = layout(src_lengths, src_length)
    return document[first_row : first_row + block_rows, None] == source_doc[None, :]


def attend_forward(queries, keys_all, values_all, visible_of, head_count):
    query_count = queries.shape[0]
    head_size = queries.shape[1] // head_count
    factor = head_size ** (-0.5)
    queries = queries.reshape(query_count, head_count, head_size)
    keys_all = keys_all.reshape(keys_all.shape[0], head_count, head_size)
    values_all = values_all.reshape(values_all.shape[0], head_count, head_size)
    block_rows = min(score_tile, query_count)
    outputs = []
    totals = []
    for first_row in range(0, query_count, block_rows):
        query_part = queries[first_row : first_row + block_rows]
        scores = (
            jnp.einsum("qhd,khd->hqk", query_part, keys_all, preferred_element_type=jnp.float32)
            * factor
        )
        scores = jnp.where(visible_of(first_row, block_rows)[None], scores, -1e30)
        highest = jnp.max(scores, axis=-1, keepdims=True)
        exponent = jnp.exp(scores - highest)
        denominator = jnp.sum(exponent, axis=-1, keepdims=True)
        weights_low = (exponent / denominator).astype(jnp.bfloat16)
        outputs.append(
            jnp.einsum("hqk,khd->qhd", weights_low, values_all, preferred_element_type=jnp.float32)
        )
        totals.append(highest[..., 0] + jnp.log(denominator[..., 0]))
    context = jnp.concatenate(outputs, axis=0).reshape(query_count, head_count * head_size)
    return (context, jnp.concatenate(totals, axis=1))


def attend_backward(queries, keys_all, values_all, visible_of, totals, grad_context, head_count):
    query_count = queries.shape[0]
    key_count = keys_all.shape[0]
    head_size = queries.shape[1] // head_count
    factor = head_size ** (-0.5)
    queries = queries.reshape(query_count, head_count, head_size)
    keys_all = keys_all.reshape(key_count, head_count, head_size)
    values_all = values_all.reshape(key_count, head_count, head_size)
    grad_context = grad_context.reshape(query_count, head_count, head_size)
    grad_keys = jnp.zeros((key_count, head_count, head_size), jnp.float32)
    grad_values = jnp.zeros((key_count, head_count, head_size), jnp.float32)
    grad_queries = []
    block_rows = min(score_tile, query_count)
    for first_row in range(0, query_count, block_rows):
        query_part = queries[first_row : first_row + block_rows]
        grad_part = grad_context[first_row : first_row + block_rows]
        scores = (
            jnp.einsum("qhd,khd->hqk", query_part, keys_all, preferred_element_type=jnp.float32)
            * factor
        )
        scores = jnp.where(visible_of(first_row, block_rows)[None], scores, -1e30)
        weights_full = jnp.exp(scores - totals[:, first_row : first_row + block_rows, None])
        grad_weights = jnp.einsum(
            "qhd,khd->hqk", grad_part, values_all, preferred_element_type=jnp.float32
        )
        inner = jnp.sum(grad_weights * weights_full, axis=-1, keepdims=True)
        grad_scores = (weights_full * (grad_weights - inner)).astype(jnp.bfloat16)
        grad_queries.append(
            jnp.einsum("hqk,khd->qhd", grad_scores, keys_all, preferred_element_type=jnp.float32)
            * factor
        )
        grad_keys = (
            grad_keys
            + jnp.einsum(
                "hqk,qhd->khd", grad_scores, query_part, preferred_element_type=jnp.float32
            )
            * factor
        )
        grad_values = grad_values + jnp.einsum(
            "hqk,qhd->khd",
            weights_full.astype(jnp.bfloat16),
            grad_part,
            preferred_element_type=jnp.float32,
        )
    grad_queries = jnp.concatenate(grad_queries, axis=0).reshape(
        query_count, head_count * head_size
    )
    return (
        grad_queries.astype(jnp.bfloat16),
        grad_keys.reshape(key_count, -1).astype(jnp.bfloat16),
        grad_values.reshape(key_count, -1).astype(jnp.bfloat16),
    )


def collect(piece):
    return lax.all_gather(piece, "tp", axis=1, tiled=True)


def spread_sum(partial_sum):
    return lax.psum_scatter(partial_sum, "tp", scatter_dimension=1, tiled=True)


def collect_grad(piece):
    return lax.all_gather(piece, "tp", axis=1, tiled=True)


def send_back(partial_sum):
    return lax.psum_scatter(partial_sum, "tp", scatter_dimension=1, tiled=True)


def local_split(
    query_stream,
    token_embed,
    encoder_out,
    out_grad,
    attn_q,
    attn_k,
    attn_v,
    attn_o,
    cross_q,
    cross_k,
    cross_v,
    cross_o,
    ffn_in,
    ffn_bias_in,
    ffn_out,
    ffn_bias_out,
    norm_gain,
    norm_bias,
    doc_lengths,
    src_lengths,
    ctx_rank,
    ctx_limit,
):
    head_count = HEADS // lax.axis_size("tp")
    (
        self_query,
        self_key,
        self_value,
        self_out,
        other_query,
        other_key,
        other_value,
        other_out,
        hidden_in,
        hidden_bias,
        hidden_out,
    ) = (
        lax.all_gather(attn_q, "dp", axis=0, tiled=True),
        lax.all_gather(attn_k, "dp", axis=0, tiled=True),
        lax.all_gather(attn_v, "dp", axis=0, tiled=True),
        lax.all_gather(attn_o, "dp", axis=1, tiled=True),
        lax.all_gather(cross_q, "dp", axis=0, tiled=True),
        lax.all_gather(cross_k, "dp", axis=0, tiled=True),
        lax.all_gather(cross_v, "dp", axis=0, tiled=True),
        lax.all_gather(cross_o, "dp", axis=1, tiled=True),
        lax.all_gather(ffn_in, "dp", axis=0, tiled=True),
        lax.all_gather(ffn_bias_in, "dp", axis=0, tiled=True),
        lax.all_gather(ffn_out, "dp", axis=1, tiled=True),
    )

    def self_forward(row_items):
        queries, keys_all, values_all, lengths, rank_row, limit_row = row_items

        def visible_of(first_row, block_rows):
            return self_visible(
                lengths, rank_row, limit_row, keys_all.shape[0], first_row, block_rows
            )

        return attend_forward(queries, keys_all, values_all, visible_of, head_count)

    def self_backward(row_items):
        queries, keys_all, values_all, lengths, rank_row, limit_row, totals, grad_context = (
            row_items
        )

        def visible_of(first_row, block_rows):
            return self_visible(
                lengths, rank_row, limit_row, keys_all.shape[0], first_row, block_rows
            )

        return attend_backward(
            queries, keys_all, values_all, visible_of, totals, grad_context, head_count
        )

    def cross_forward(row_items):
        queries, keys_all, values_all, lengths, source_lengths = row_items

        def visible_of(first_row, block_rows):
            return cross_visible(
                lengths, source_lengths, queries.shape[0], keys_all.shape[0], first_row, block_rows
            )

        return attend_forward(queries, keys_all, values_all, visible_of, head_count)

    def cross_backward(row_items):
        queries, keys_all, values_all, lengths, source_lengths, totals, grad_context = row_items

        def visible_of(first_row, block_rows):
            return cross_visible(
                lengths, source_lengths, queries.shape[0], keys_all.shape[0], first_row, block_rows
            )

        return attend_backward(
            queries, keys_all, values_all, visible_of, totals, grad_context, head_count
        )

    query_all = collect(query_stream)
    embed_all = collect(token_embed)
    source_all = collect(encoder_out)
    self_queries = project(query_all, self_query).astype(jnp.bfloat16)
    self_keys = project(embed_all, self_key).astype(jnp.bfloat16)
    self_values = project(embed_all, self_value).astype(jnp.bfloat16)
    self_context, self_totals = lax.map(
        self_forward, (self_queries, self_keys, self_values, doc_lengths, ctx_rank, ctx_limit)
    )
    self_low = self_context.astype(jnp.bfloat16)
    first_sum = query_stream.astype(jnp.float32) + spread_sum(project(self_low, self_out))
    hidden_one, first_back = jax.vjp(layer_norm, first_sum, norm_gain[0], norm_bias[0])
    hidden_one_all = collect(hidden_one.astype(jnp.bfloat16))
    cross_queries = project(hidden_one_all, other_query).astype(jnp.bfloat16)
    cross_keys = project(source_all, other_key).astype(jnp.bfloat16)
    cross_values = project(source_all, other_value).astype(jnp.bfloat16)
    cross_context, cross_totals = lax.map(
        cross_forward, (cross_queries, cross_keys, cross_values, doc_lengths, src_lengths)
    )
    cross_low = cross_context.astype(jnp.bfloat16)
    second_sum = hidden_one + spread_sum(project(cross_low, other_out))
    hidden_two, second_back = jax.vjp(layer_norm, second_sum, norm_gain[1], norm_bias[1])
    hidden_two_low = hidden_two.astype(jnp.bfloat16)
    ffn_inputs = lax.all_gather(hidden_two_low, "tp", axis=1, tiled=True)
    ffn_pre = project(ffn_inputs, hidden_in) + hidden_bias.astype(jnp.float32)
    ffn_gate, gelu_back = jax.vjp(gelu_exact, ffn_pre)
    ffn_act = ffn_gate.astype(jnp.bfloat16)
    ffn_branch = (
        lax.psum_scatter(project(ffn_act, hidden_out), "tp", scatter_dimension=1, tiled=True)
        + ffn_bias_out
    )
    third_sum = hidden_two + ffn_branch
    mixed_full, third_back = jax.vjp(layer_norm, third_sum, norm_gain[2], norm_bias[2])
    grad_third, gain_two, shift_two = third_back(out_grad.astype(jnp.float32))
    grad_ffn = grad_third.astype(jnp.bfloat16)
    grad_bias_out = jnp.sum(grad_ffn.astype(jnp.float32), axis=(0, 1))
    grad_ffn_all = lax.all_gather(grad_ffn, "tp", axis=1, tiled=True)
    grad_act = project_back(grad_ffn_all, hidden_out)
    grad_down = outer_sum(ffn_act, grad_ffn_all)
    grad_pre = gelu_back(grad_act)[0].astype(jnp.bfloat16)
    grad_up = outer_sum(ffn_inputs, grad_pre)
    grad_bias_in = jnp.sum(grad_pre.astype(jnp.float32), axis=(0, 1))
    grad_two = grad_third + lax.psum_scatter(
        project_back(grad_pre, hidden_in), "tp", scatter_dimension=1, tiled=True
    )
    grad_second, gain_one, shift_one = second_back(grad_two)
    grad_cross_all = collect_grad(grad_second.astype(jnp.bfloat16))
    grad_other_out = outer_sum(cross_low, grad_cross_all)
    grad_cross_ctx = project_back(grad_cross_all, other_out).astype(jnp.bfloat16)
    cross_dq, cross_dk, cross_dv = lax.map(
        cross_backward,
        (
            cross_queries,
            cross_keys,
            cross_values,
            doc_lengths,
            src_lengths,
            cross_totals,
            grad_cross_ctx,
        ),
    )
    grad_other_query = outer_sum(hidden_one_all, cross_dq)
    grad_other_key = outer_sum(source_all, cross_dk)
    grad_other_value = outer_sum(source_all, cross_dv)
    grad_encoder = send_back(
        project_back(cross_dk, other_key) + project_back(cross_dv, other_value)
    )
    grad_one = grad_second + send_back(project_back(cross_dq, other_query))
    grad_first, gain_zero, shift_zero = first_back(grad_one)
    grad_attn_all = collect_grad(grad_first.astype(jnp.bfloat16))
    grad_self_out = outer_sum(self_low, grad_attn_all)
    grad_self_ctx = project_back(grad_attn_all, self_out).astype(jnp.bfloat16)
    self_dq, self_dk, self_dv = lax.map(
        self_backward,
        (
            self_queries,
            self_keys,
            self_values,
            doc_lengths,
            ctx_rank,
            ctx_limit,
            self_totals,
            grad_self_ctx,
        ),
    )
    grad_self_query = outer_sum(query_all, self_dq)
    grad_self_key = outer_sum(embed_all, self_dk)
    grad_self_value = outer_sum(embed_all, self_dv)
    grad_embed = send_back(project_back(self_dk, self_key) + project_back(self_dv, self_value))
    grad_query = grad_first + send_back(project_back(self_dq, self_query))
    (
        grad_self_query,
        grad_self_key,
        grad_self_value,
        grad_self_out,
        grad_other_query,
        grad_other_key,
        grad_other_value,
        grad_other_out,
        grad_up,
        grad_bias_in,
        grad_down,
    ) = (
        lax.psum_scatter(
            grad_self_query.astype(jnp.bfloat16), "dp", scatter_dimension=0, tiled=True
        ).astype(jnp.float32),
        lax.psum_scatter(
            grad_self_key.astype(jnp.bfloat16), "dp", scatter_dimension=0, tiled=True
        ).astype(jnp.float32),
        lax.psum_scatter(
            grad_self_value.astype(jnp.bfloat16), "dp", scatter_dimension=0, tiled=True
        ).astype(jnp.float32),
        lax.psum_scatter(
            grad_self_out.astype(jnp.bfloat16), "dp", scatter_dimension=1, tiled=True
        ).astype(jnp.float32),
        lax.psum_scatter(
            grad_other_query.astype(jnp.bfloat16), "dp", scatter_dimension=0, tiled=True
        ).astype(jnp.float32),
        lax.psum_scatter(
            grad_other_key.astype(jnp.bfloat16), "dp", scatter_dimension=0, tiled=True
        ).astype(jnp.float32),
        lax.psum_scatter(
            grad_other_value.astype(jnp.bfloat16), "dp", scatter_dimension=0, tiled=True
        ).astype(jnp.float32),
        lax.psum_scatter(
            grad_other_out.astype(jnp.bfloat16), "dp", scatter_dimension=1, tiled=True
        ).astype(jnp.float32),
        lax.psum_scatter(
            grad_up.astype(jnp.bfloat16), "dp", scatter_dimension=0, tiled=True
        ).astype(jnp.float32),
        lax.psum_scatter(
            grad_bias_in.astype(jnp.bfloat16), "dp", scatter_dimension=0, tiled=True
        ).astype(jnp.float32),
        lax.psum_scatter(
            grad_down.astype(jnp.bfloat16), "dp", scatter_dimension=1, tiled=True
        ).astype(jnp.float32),
    )
    gain_grads = jnp.stack([gain_zero, gain_one, gain_two])
    shift_grads = jnp.stack([shift_zero, shift_one, shift_two])
    gain_grads, shift_grads, grad_bias_out = lax.psum(
        (gain_grads, shift_grads, grad_bias_out), ("dp", "tp")
    )
    return (
        mixed_full.astype(jnp.bfloat16),
        grad_query,
        grad_embed,
        grad_encoder,
        grad_self_query,
        grad_self_key,
        grad_self_value,
        grad_self_out,
        grad_other_query,
        grad_other_key,
        grad_other_value,
        grad_other_out,
        grad_up,
        grad_bias_in,
        grad_down,
        grad_bias_out,
        gain_grads,
        shift_grads,
    )


MESH = pl.DeviceIdType.MESH
LOW = jnp.bfloat16
WIDE = jnp.float32


class Place:
    def __init__(self):
        dp, tp = lax.axis_index("dp"), lax.axis_index("tp")
        self.dp, self.tp = dp, tp
        self.z, self.x = dp // 2, lax.rem(dp, 2)
        self.y, self.core = tp // 2, lax.rem(tp, 2)
        self.core_peer = (dp, 2 * self.y + 1 - self.core)
        self.y_peer = (dp, 2 * (1 - self.y) + self.core)
        self.far_peer = (dp, 2 * (1 - self.y) + 1 - self.core)
        self.x_peer = (2 * self.z + 1 - self.x, tp)

    def z_at(self, step):
        return lax.rem(self.z + step, 4)

    def z_peer(self, step):
        return (2 * self.z_at(step) + self.x, self.tp)

    def meet(self):
        peers = [self.core_peer, self.y_peer, self.far_peer, self.x_peer]
        peers += [self.z_peer(step) for step in (1, 2, 3)]
        barrier = pltpu.get_barrier_semaphore()
        for peer in peers:
            pl.semaphore_signal(barrier, inc=1, device_id=peer, device_id_type=MESH)
        pl.semaphore_wait(barrier, len(peers))


def send(source, target, send_sem, recv_sem, peer):
    copy = pltpu.make_async_remote_copy(
        src_ref=source,
        dst_ref=target,
        send_sem=send_sem,
        recv_sem=recv_sem,
        device_id=peer,
        device_id_type=MESH,
    )
    copy.start()
    return copy


def cols(index, width):
    return pl.ds(pl.multiple_of(index * width, width), width)


class Gather:
    def __init__(self, place, local, full, first, count, sends, recvs, own_sem):
        self.place, self.local, self.full = place, local, full
        self.items = pl.ds(first, count)
        self.width = local.shape[-1]
        self.sends, self.recvs, self.own_sem = sends, recvs, own_sem
        self.pending = []
        self.sent = []

    def _send(self, source, target, slot, peer):
        copy = send(source, target, self.sends.at[slot], self.recvs.at[slot], peer)
        self.pending.append(copy)
        self.sent.append(copy)

    def _arrive(self):
        for copy in self.pending:
            copy.wait_recv()
        self.pending = []

    def stage(self, number):
        p = self.place
        mine, other = cols(p.tp, self.width), cols(2 * (1 - p.y) + p.core, self.width)
        if number == 0:
            source = self.local.at[self.items]
            target = self.full.at[self.items, p.z, p.x, :, mine]
            self.own = pltpu.make_async_copy(source, target, self.own_sem)
            self.own.start()
            for step in (1, 2, 3):
                self._send(source, target, step - 1, p.z_peer(step))
            return
        self._arrive()
        if number == 1:
            self.own.wait()
            block = self.full.at[self.items, :, p.x, :, mine]
            self._send(block, block, 3, p.y_peer)
        elif number == 2:
            for slot, side in ((4, mine), (5, other)):
                block = self.full.at[self.items, :, p.x, :, side]
                self._send(block, block, slot, p.x_peer)
        elif number == 3:
            for slot, side in ((6, mine), (7, other)):
                block = self.full.at[self.items, :, :, :, side]
                self._send(block, block, slot, p.core_peer)
        else:
            for copy in self.sent:
                copy.wait_send()


GATHER_SLOTS = 8


class ToRow:
    def __init__(self, place, local, row, sends, recvs, own_sem):
        size = local.shape[1]
        p = place
        here = pl.ds(pl.multiple_of(p.tp * size, size), size)
        self.own = pltpu.make_async_copy(local.at[p.tp], row.at[here], own_sem)
        self.own.start()
        self.copies = [
            send(local.at[peer[1]], row.at[here], sends.at[slot], recvs.at[slot], peer)
            for slot, peer in enumerate((p.y_peer, p.far_peer, p.core_peer))
        ]

    def arrive(self):
        self.own.wait()
        for copy in self.copies:
            copy.wait_recv()

    def finish(self):
        for copy in self.copies:
            copy.wait_send()


class FromRow:
    def __init__(self, place, row, blocks, sends, recvs, own_sem):
        size = blocks.shape[1]
        p = place

        def part(tp):
            return row.at[pl.ds(pl.multiple_of(tp * size, size), size)]

        self.own = pltpu.make_async_copy(part(p.tp), blocks.at[p.tp], own_sem)
        self.own.start()
        self.copies = [
            send(part(peer[1]), blocks.at[p.tp], sends.at[slot], recvs.at[slot], peer)
            for slot, peer in enumerate((p.y_peer, p.far_peer, p.core_peer))
        ]

    def finish(self):
        self.own.wait()
        for copy in self.copies:
            copy.wait()


def gather_kernel(
    query, embed, source, cotangent, squares, wides, biases,
    query_row, embed_row, source_row, cotangent_row, all_squares, all_wides, all_biases,
    row_sends, row_recvs, row_own, sends, recvs, own,
):
    place = Place()
    place.meet()
    groups = [
        (squares, all_squares, 0, 2),
        (squares, all_squares, 2, 2),
        (squares, all_squares, 4, 4),
        (wides, all_wides, 0, 1),
        (biases, all_biases, 0, 1),
        (wides, all_wides, 1, 1),
    ]
    gathers = [
        Gather(place, *group, sends.at[i], recvs.at[i], own.at[i])
        for i, group in enumerate(groups)
    ]
    streams = [
        (embed, embed_row),
        (query, query_row),
        (source, source_row),
        (cotangent, cotangent_row),
    ]
    rows = []
    for tick in range(len(gathers) + 4):
        if tick < len(streams):
            rows.append(
                ToRow(place, *streams[tick], row_sends.at[tick], row_recvs.at[tick], row_own.at[tick])
            )
        for stage in range(5):
            if 0 <= tick - stage < len(gathers):
                gathers[tick - stage].stage(stage)
    for row in rows:
        row.arrive()
        row.finish()


def gather_all(query, embed, source, cotangent, squares, wides, biases):
    hbm = pl.BlockSpec(memory_space=pl.ANY)
    shape = jax.ShapeDtypeStruct
    row = shape((4 * query.shape[1], query.shape[2]), LOW)
    dma = pltpu.SemaphoreType.DMA
    full = [shape((n, 4, 2, h, 4 * w), LOW) for n, h, w in (a.shape for a in (squares, wides, biases))]
    outs = pl.pallas_call(
        gather_kernel,
        out_shape=[row] * 4 + full,
        in_specs=[hbm] * 7,
        out_specs=[hbm] * 7,
        scratch_shapes=[
            dma((4, 3)), dma((4, 3)), dma((4,)),
            dma((6, GATHER_SLOTS)), dma((6, GATHER_SLOTS)), dma((6,)),
        ],
        compiler_params=pltpu.CompilerParams(collective_id=0, has_side_effects=True),
        name="gather_all",
    )(query, embed, source, cotangent, squares, wides, biases)
    rows, full = outs[:4], outs[4:]
    return rows, [w.reshape(w.shape[0], -1, w.shape[-1]) for w in full]


class Scatter:
    def __init__(self, place, parts, half, quarter, eighth, last, out, first, count, sends, recvs):
        self.place, self.parts = place, parts
        self.half, self.quarter, self.eighth, self.last = half, quarter, eighth, last
        self.out = out
        self.first, self.count = first, count
        self.items = pl.ds(first, count)
        self.width = out.shape[-1]
        self.sends, self.recvs = sends, recvs
        self.pending = []
        self.sent = []

    def _send(self, source, target, slot, peer):
        copy = send(source, target, self.sends.at[slot], self.recvs.at[slot], peer)
        self.pending.append(copy)
        self.sent.append(copy)

    def _arrive(self):
        for copy in self.pending:
            copy.wait_recv()
        self.pending = []

    def stage(self, number):
        p = self.place
        width = self.width
        mine = cols(p.tp, width)
        other = cols(2 * (1 - p.y) + p.core, width)
        if number == 0:
            for side, column in ((0, p.core_peer[1]), (1, p.far_peer[1])):
                source = self.parts.at[self.items, :, :, :, cols(column, width)]
                self._send(source, self.half.at[self.items, side], side, p.core_peer)
            return
        self._arrive()
        if number == 1:
            for item in range(self.first, self.first + self.count):
                for side, column in ((0, mine), (1, other)):

                    @pl.loop(0, 4)
                    def _(z):
                        total = self.parts[item, z, :, :, column].astype(WIDE)
                        total = total + self.half[item, side, z].astype(WIDE)
                        self.half[item, side, z] = total.astype(LOW)

            for side in (0, 1):
                source = self.half.at[self.items, side, :, 1 - p.x]
                self._send(source, self.quarter.at[self.items, side], 2 + side, p.x_peer)
        elif number == 2:
            for item in range(self.first, self.first + self.count):
                for side in (0, 1):

                    @pl.loop(0, 4)
                    def _(z):
                        total = self.half[item, side, z, p.x].astype(WIDE)
                        total = total + self.quarter[item, side, z].astype(WIDE)
                        self.quarter[item, side, z] = total.astype(LOW)

            self._send(self.quarter.at[self.items, 1], self.eighth.at[self.items], 4, p.y_peer)
        elif number == 3:
            for item in range(self.first, self.first + self.count):

                @pl.loop(0, 4)
                def _(z):
                    total = self.quarter[item, 0, z].astype(WIDE)
                    total = total + self.eighth[item, z].astype(WIDE)
                    self.eighth[item, z] = total.astype(LOW)

            for step in (1, 2, 3):
                source = self.eighth.at[self.items, p.z_at(step)]
                target = self.last.at[self.items, step - 1]
                self._send(source, target, 4 + step, p.z_peer(step))
        else:
            for item in range(self.first, self.first + self.count):
                total = self.eighth[item, p.z].astype(WIDE)
                for step in range(3):
                    total = total + self.last[item, step].astype(WIDE)
                self.out[item] = total
            for copy in self.sent:
                copy.wait_send()


SCATTER_SLOTS = 8


class SumAll:
    def __init__(self, place, values, arrived, sends, recvs):
        self.place, self.values, self.arrived = place, values, arrived
        self.sends, self.recvs = sends, recvs
        self.copy = None

    def stage(self, number):
        p = self.place
        if self.copy is not None:
            self.copy.wait()
            self.values[...] = self.values[...] + self.arrived[number - 1]
        if number < 5:
            z_one = (2 * (p.z + 1 - 2 * lax.rem(p.z, 2)) + p.x, p.tp)
            z_two = (2 * lax.rem(p.z + 2, 4) + p.x, p.tp)
            peer = (p.core_peer, p.x_peer, p.y_peer, z_one, z_two)[number]
            self.copy = send(
                self.values, self.arrived.at[number], self.sends.at[number], self.recvs.at[number], peer
            )


def scatter_kernel(
    squares, wides, small, mixed, grad_query, grad_embed, grad_encoder,
    own_squares, own_wides, small_sum, mixed_blocks, query_blocks, embed_blocks, encoder_blocks,
    half_s, quarter_s, eighth_s, last_s, half_w, quarter_w, eighth_w, last_w, arrived,
    row_sends, row_recvs, row_own, sends, recvs, small_sends, small_recvs,
):
    place = Place()
    place.meet()
    rows = [
        FromRow(place, row, blocks, row_sends.at[i], row_recvs.at[i], row_own.at[i])
        for i, (row, blocks) in enumerate(
            (
                (mixed, mixed_blocks),
                (grad_encoder, encoder_blocks),
                (grad_embed, embed_blocks),
                (grad_query, query_blocks),
            )
        )
    ]
    small_sum[...] = small[...]
    sum_all = SumAll(place, small_sum, arrived, small_sends, small_recvs)
    square = (squares, half_s, quarter_s, eighth_s, last_s, own_squares)
    wide = (wides, half_w, quarter_w, eighth_w, last_w, own_wides)
    groups = [(wide, 0, 1), (wide, 1, 1), (square, 4, 4), (square, 2, 2), (square, 0, 2)]
    scatters = [
        Scatter(place, *buffers, first, count, sends.at[i], recvs.at[i])
        for i, (buffers, first, count) in enumerate(groups)
    ]
    for tick in range(len(scatters) + 4):
        for stage in range(5):
            if 0 <= tick - stage < len(scatters):
                scatters[tick - stage].stage(stage)
        if tick < 6:
            sum_all.stage(tick)
    for row in rows:
        row.finish()


def scatter_all(squares, wides, small, rows):
    hbm = pl.BlockSpec(memory_space=pl.ANY)
    vmem = pl.BlockSpec(memory_space=pltpu.VMEM)
    shape = jax.ShapeDtypeStruct
    squares = squares.reshape(squares.shape[0], 4, 2, -1, squares.shape[-1])
    wides = wides.reshape(wides.shape[0], 4, 2, -1, wides.shape[-1])
    dma = pltpu.SemaphoreType.DMA
    length, features = rows[0].shape
    blocks = shape((4, length // 4, features), LOW)

    def steps(a):
        n, _, _, h, w = a.shape
        w = w // 4
        return [
            pltpu.VMEM((n, 2, 4, 2, h, w), LOW),
            pltpu.VMEM((n, 2, 4, h, w), LOW),
            pltpu.VMEM((n, 4, h, w), LOW),
            pltpu.VMEM((n, 3, h, w), LOW),
        ]

    def own(a):
        n, _, _, h, w = a.shape
        return shape((n, h, w // 4), WIDE)

    return pl.pallas_call(
        scatter_kernel,
        out_shape=[own(squares), own(wides), shape(small.shape, WIDE)] + [blocks] * 4,
        in_specs=[vmem] * 3 + [hbm] * 4,
        out_specs=[vmem] * 3 + [hbm] * 4,
        scratch_shapes=steps(squares)
        + steps(wides)
        + [
            pltpu.VMEM((5,) + small.shape, WIDE),
            dma((4, 3)), dma((4, 3)), dma((4,)),
            dma((5, SCATTER_SLOTS)), dma((5, SCATTER_SLOTS)), dma((5,)), dma((5,)),
        ],
        compiler_params=pltpu.CompilerParams(
            collective_id=1, has_side_effects=True, vmem_limit_bytes=56 * 2**20
        ),
        name="scatter_all",
    )(squares, wides, small, *rows)


HIDDEN = -1e30
Q_TILE = 256


def product(left, right, left_axis, right_axis):
    return lax.dot_general(
        left, right, (((left_axis,), (right_axis,)), ((), ())), preferred_element_type=WIDE
    )


def nn(left, right):
    return product(left, right, 1, 0)


def nt(left, right):
    return product(left, right, 1, 1)


def tn(left, right):
    return product(left, right, 0, 0)


def rows_of(index, size):
    return pl.ds(pl.multiple_of(index * size, size), size)


def normalize(values):
    average = jnp.mean(values, axis=-1, keepdims=True)
    centred = values - average
    spread = jnp.mean(centred * centred, axis=-1, keepdims=True)
    inverse = lax.rsqrt(spread + EPSILON)
    return centred * inverse, inverse


def normalize_back(grad, normal, inverse, gain):
    scaled = grad * gain
    mean_one = jnp.mean(scaled, axis=-1, keepdims=True)
    mean_two = jnp.mean(scaled * normal, axis=-1, keepdims=True)
    return inverse * (scaled - mean_one - normal * mean_two)


def add_rows(target, grad):
    target[...] += jnp.sum(grad, axis=0, keepdims=True)


def documents(lengths, row, shape, axis):
    positions = lax.broadcasted_iota(jnp.int32, shape, axis)
    document = jnp.full(shape, -1, jnp.int32)
    start = jnp.zeros(shape, jnp.int32)
    offset = jnp.int32(0)
    for slot in range(lengths.shape[1]):
        passed = positions >= offset
        document = document + passed.astype(jnp.int32)
        start = jnp.where(passed, offset, start)
        offset = offset + lengths[row, slot]
    return positions, document, start


def fill_self_bias(bias, lengths, rank, limit, row):
    length = bias.shape[0]
    key_position, key_document, _ = documents(lengths, row, (length, 1), 0)
    position, document, start = documents(lengths, row, (1, length), 1)
    rank_row = rank[pl.ds(row, 1), :].astype(WIDE)
    key_rank = jnp.transpose(jnp.broadcast_to(rank_row, (128, length)))[:, :1]
    query_limit = limit[pl.ds(row, 1), :].astype(WIDE)
    for tile in range(length // Q_TILE):
        part = slice(tile * Q_TILE, (tile + 1) * Q_TILE)
        chosen = (key_rank < query_limit[:, part]) & (key_position != position[:, part])
        seen = (key_document == document[:, part]) & (chosen | (key_position == start[:, part]))
        bias[:, part] = jnp.where(seen, 0.0, HIDDEN).astype(bias.dtype)


def fill_cross_bias(bias, lengths, source_lengths, row):
    length = bias.shape[0]
    _, key_document, _ = documents(source_lengths, row, (length, 1), 0)
    _, document, _ = documents(lengths, row, (1, length), 1)
    for tile in range(length // Q_TILE):
        part = slice(tile * Q_TILE, (tile + 1) * Q_TILE)
        seen = key_document == document[:, part]
        bias[:, part] = jnp.where(seen, 0.0, HIDDEN).astype(bias.dtype)


def one_head(pair, side):
    lane = lax.broadcasted_iota(jnp.int32, pair.shape, 1)
    return jnp.where(lane // 64 == side, pair, jnp.zeros_like(pair))


def attend(keys, queries, values_t, bias, context, totals):
    length = keys.shape[0]

    @pl.loop(0, HEADS // 2)
    def _(pair):
        lanes = rows_of(pair, 128)

        @pl.loop(0, length // Q_TILE)
        def _(tile):
            part = rows_of(tile, Q_TILE)
            key_pair, query_pair = keys[:, lanes], queries[part, lanes]
            outs = []
            for side in (0, 1):
                head = 2 * pair + side
                scores = nt(key_pair, one_head(query_pair, side)) + bias[:, part].astype(WIDE)
                highest = jnp.max(scores, axis=0, keepdims=True)
                weights = jnp.exp(scores - highest).astype(LOW)
                out = nn(values_t[head], weights)
                total = out[64:65]
                outs.append(out[:64] * (1.0 / total))
                totals[pl.ds(head, 1), part] = highest + jnp.log(total)
            context[part, lanes] = jnp.transpose(jnp.concatenate(outs, axis=0)).astype(LOW)


def attend_back(keys, keys_t, queries, values, cotangent, bias, totals, inner, grads):
    grad_keys, grad_values, grad_queries, key_sum, value_sum = grads
    length = keys.shape[0]

    @pl.loop(0, HEADS // 2)
    def _(pair):
        lanes = rows_of(pair, 128)
        key_sum[...] = jnp.zeros_like(key_sum)
        value_sum[...] = jnp.zeros_like(value_sum)

        @pl.loop(0, length // Q_TILE)
        def _(tile):
            part = rows_of(tile, Q_TILE)
            key_pair, value_pair = keys[:, lanes], values[:, lanes]
            all_weights, all_scores, all_queries, all_cotangents, outs = [], [], [], [], []
            for side in (0, 1):
                head = 2 * pair + side
                query = one_head(queries[part, lanes], side)
                grad = one_head(cotangent[part, lanes], side)
                scores = nt(key_pair, query) + bias[:, part].astype(WIDE)
                weights = jnp.exp(scores - totals[pl.ds(head, 1), part])
                grad_weights = nt(value_pair, grad)
                grad_scores = (weights * (grad_weights - inner[pl.ds(head, 1), part])).astype(LOW)
                outs.append(nn(keys_t[head, :64], grad_scores) * 0.125)
                all_weights.append(weights.astype(LOW))
                all_scores.append(grad_scores)
                all_queries.append(query)
                all_cotangents.append(grad)
            grad_queries[part, lanes] = jnp.transpose(jnp.concatenate(outs, axis=0)).astype(LOW)
            value_sum[...] += nn(
                jnp.concatenate(all_weights, axis=1), jnp.concatenate(all_cotangents, axis=0)
            )
            key_sum[...] += nn(
                jnp.concatenate(all_scores, axis=1), jnp.concatenate(all_queries, axis=0)
            )

        grad_keys[:, lanes] = key_sum[...].astype(LOW)
        grad_values[:, lanes] = value_sum[...].astype(LOW)


def inner_products(cotangent, context, inner):
    products = cotangent[...].astype(WIDE) * context[...].astype(WIDE)
    high = products.astype(LOW)
    rest = (products - high.astype(WIDE)).astype(LOW)
    shape = (2 * HEADS, products.shape[1])
    head = lax.broadcasted_iota(jnp.int32, shape, 0)
    lane = lax.broadcasted_iota(jnp.int32, shape, 1)
    pick = jnp.where(lane // 64 == head, 1.0, 0.0).astype(LOW)
    inner[...] = (nt(pick, high) + nt(pick, rest))[:HEADS]


def flip_heads(values, flipped):
    turned = jnp.transpose(values[...])
    for head in range(HEADS):
        flipped[head, :64] = turned[64 * head : 64 * head + 64]
    flipped[:, 64:] = jnp.ones((HEADS, flipped.shape[1] - 64, flipped.shape[2]), LOW)


def layer_kernel(
    query_row, embed_row, source_row, cotangent_row, squares, wides, bias_in, bias_out, norm_gain,
    norm_bias, lengths, source_lengths, rank, limit,
    mixed, grad_query, grad_embed, grad_encoder, grad_squares, grad_wides, small,
    self_q, self_k, self_v, self_context, cross_q, cross_k, cross_v, cross_context,
    flipped, totals, cross_totals, inner, normal_one, normal_two, inverse_one, inverse_two,
    hidden_one, hidden_two, act, pre, grad_ffn, grad_second, bias, key_sum, value_sum,
):
    row = lax.axis_index("tp")
    length, features = query_row.shape
    small[...] = jnp.zeros_like(small)

    def vector(index):
        first = (index % 4) * features
        return small.at[1 + index // 4 : 2 + index // 4, first : first + features]

    def quarter(ref, index):
        return ref.at[:, index * features : (index + 1) * features]

    fill_self_bias(bias, lengths, rank, limit, row)
    self_k[...] = nn(embed_row[...], squares[1]).astype(LOW)
    self_v[...] = nn(embed_row[...], squares[2]).astype(LOW)
    self_q[...] = (nn(query_row[...], squares[0]) * 0.125).astype(LOW)
    flip_heads(self_v, flipped)
    attend(self_k, self_q, flipped, bias, self_context, totals)

    @pl.loop(0, length // 256)
    def _(tile):
        part = rows_of(tile, 256)
        branch = nt(self_context[part], squares[3])
        normal, inverse = normalize(query_row[part].astype(WIDE) + branch)
        normal_one[part] = normal
        inverse_one[part] = inverse
        hidden_one[part] = (normal * norm_gain[0:1] + norm_bias[0:1]).astype(LOW)

    fill_cross_bias(bias, lengths, source_lengths, row)
    cross_k[...] = nn(source_row[...], squares[5]).astype(LOW)
    cross_v[...] = nn(source_row[...], squares[6]).astype(LOW)
    cross_q[...] = (nn(hidden_one[...], squares[4]) * 0.125).astype(LOW)
    flip_heads(cross_v, flipped)
    attend(cross_k, cross_q, flipped, bias, cross_context, cross_totals)

    @pl.loop(0, length // 256)
    def _(tile):
        part = rows_of(tile, 256)
        branch = nt(cross_context[part], squares[7])
        before = normal_one[part] * norm_gain[0:1] + norm_bias[0:1]
        normal, inverse = normalize(before + branch)
        normal_two[part] = normal
        inverse_two[part] = inverse
        after = normal * norm_gain[1:2] + norm_bias[1:2]
        low = after.astype(LOW)
        hidden_two[part] = low
        before = nn(low, wides[0]) + bias_in[...]
        below = 0.5 * (1.0 + lax.erf(before * 0.7071067811865476))
        density = jnp.exp(-0.5 * before * before) * 0.3989422804014327
        slope = below + before * density
        gate = (before * below).astype(LOW)
        act[part] = gate
        after = after + nt(gate, wides[1]) + bias_out[...]
        normal, inverse = normalize(after)
        mixed[part] = (normal * norm_gain[2:3] + norm_bias[2:3]).astype(LOW)
        grad = cotangent_row[part].astype(WIDE)
        add_rows(vector(2), grad * normal)
        add_rows(vector(5), grad)
        grad = normalize_back(grad, normal, inverse, norm_gain[2:3])
        low = grad.astype(LOW)
        grad_ffn[part] = low
        add_rows(vector(6), low.astype(WIDE))
        grad_pre = (nn(low, wides[1]) * slope).astype(LOW)
        pre[part] = grad_pre
        add_rows(small.at[0:1], grad_pre.astype(WIDE))
        grad = grad + nt(grad_pre, wides[0])
        normal = normal_two[part]
        add_rows(vector(1), grad * normal)
        add_rows(vector(4), grad)
        grad_second[part] = normalize_back(grad, normal, inverse_two[part], norm_gain[1:2])

    grad_wides[0] = tn(hidden_two[...], pre[...]).astype(LOW)
    grad_wides[1] = tn(grad_ffn[...], act[...]).astype(LOW)

    cotangent, grad_k, grad_v, grad_q = (quarter(act, i) for i in range(4))

    def attention_back(first, grad_out, context, keys, queries, values, sums):
        grad_squares[first + 3] = tn(grad_out, context[...]).astype(LOW)
        cotangent[...] = nn(grad_out, squares[first + 3]).astype(LOW)
        flip_heads(keys, flipped)
        inner_products(cotangent, context, inner)
        attend_back(
            keys, flipped, queries, values, cotangent, bias, sums, inner,
            (grad_k, grad_v, grad_q, key_sum, value_sum),
        )

    attention_back(
        4, grad_second[...].astype(LOW), cross_context, cross_k, cross_q, cross_v, cross_totals
    )
    grad_squares[4] = tn(hidden_one[...], grad_q[...]).astype(LOW)
    grad_squares[5] = tn(source_row[...], grad_k[...]).astype(LOW)
    grad_squares[6] = tn(source_row[...], grad_v[...]).astype(LOW)
    grad_encoder[...] = (
        nt(grad_k[...], squares[5]) + nt(grad_v[...], squares[6])
    ).astype(LOW)

    @pl.loop(0, length // 256)
    def _(tile):
        part = rows_of(tile, 256)
        grad = grad_second[part] + nt(grad_q[part], squares[4])
        normal = normal_one[part]
        add_rows(vector(0), grad * normal)
        add_rows(vector(3), grad)
        grad_second[part] = normalize_back(grad, normal, inverse_one[part], norm_gain[0:1])

    fill_self_bias(bias, lengths, rank, limit, row)
    attention_back(
        0, grad_second[...].astype(LOW), self_context, self_k, self_q, self_v, totals
    )
    grad_squares[0] = tn(query_row[...], grad_q[...]).astype(LOW)
    grad_squares[1] = tn(embed_row[...], grad_k[...]).astype(LOW)
    grad_squares[2] = tn(embed_row[...], grad_v[...]).astype(LOW)
    grad_embed[...] = (nt(grad_k[...], squares[1]) + nt(grad_v[...], squares[2])).astype(LOW)
    grad_query[...] = (grad_second[...] + nt(grad_q[...], squares[0])).astype(LOW)


def layer_scratch(length, features, hidden):
    vmem = pltpu.VMEM
    row = vmem((length, features), LOW)
    wide_row = vmem((length, features), WIDE)
    per_head = vmem((HEADS, length), WIDE)
    return (
        [row] * 8
        + [vmem((HEADS, 80, length), LOW)]
        + [per_head] * 3
        + [wide_row] * 2
        + [vmem((length, 1), WIDE)] * 2
        + [row] * 2
        + [vmem((length, hidden), LOW)] * 2
        + [row, wide_row, vmem((length, length), LOW)]
        + [vmem((length, 128), WIDE)] * 2
    )


def run_layer(rows, squares, wides, bias_in, bias_out, norm_gain, norm_bias, lengths, source_lengths, rank, limit):
    length, features = rows[0].shape
    hidden = wides.shape[2]
    shape = jax.ShapeDtypeStruct
    vmem = pl.BlockSpec(memory_space=pltpu.VMEM)
    smem = pl.BlockSpec(memory_space=pltpu.SMEM)
    row = shape((length, features), LOW)
    return pl.pallas_call(
        layer_kernel,
        out_shape=[row] * 4
        + [shape(squares.shape, LOW), shape(wides.shape, LOW), shape((8, hidden), WIDE)],
        in_specs=[vmem] * 10 + [smem] * 2 + [vmem] * 2,
        out_specs=[vmem] * 7,
        scratch_shapes=layer_scratch(length, features, hidden),
        compiler_params=pltpu.CompilerParams(vmem_limit_bytes=63 * 2**20),
        name="layer",
    )(*rows, squares, wides, bias_in, bias_out, norm_gain, norm_bias, lengths, source_lengths, rank, limit)


def local_rows(
    query_stream,
    token_embed,
    encoder_out,
    out_grad,
    attn_q,
    attn_k,
    attn_v,
    attn_o,
    cross_q,
    cross_k,
    cross_v,
    cross_o,
    ffn_in,
    ffn_bias_in,
    ffn_out,
    ffn_bias_out,
    norm_gain,
    norm_bias,
    doc_lengths,
    src_lengths,
    ctx_rank,
    ctx_limit,
):
    squares = jnp.stack(
        [attn_q, attn_k, attn_v, attn_o.T, cross_q, cross_k, cross_v, cross_o.T]
    )
    wides = jnp.stack([ffn_in, ffn_out.T])
    biases = jnp.pad(ffn_bias_in[None, None], ((0, 0), (0, 15), (0, 64)))
    rows, (squares, wides, biases) = gather_all(
        query_stream, token_embed, encoder_out, out_grad, squares, wides, biases
    )
    hidden_bias = biases.reshape(8, 16, 4, 128)[:, 0, :, :64].transpose(1, 0, 2).reshape(1, -1)
    mixed, grad_query, grad_embed, grad_encoder, squares, wides, small = run_layer(
        rows,
        squares,
        wides,
        hidden_bias.astype(jnp.float32),
        ffn_bias_out[None],
        norm_gain,
        norm_bias,
        doc_lengths,
        src_lengths,
        ctx_rank,
        ctx_limit,
    )
    squares, wides, small, mixed, grad_query, grad_embed, grad_encoder = scatter_all(
        squares, wides, small, [mixed, grad_query, grad_embed, grad_encoder]
    )
    small = small.reshape(-1)
    device = lax.axis_index("tp") * lax.axis_size("dp") + lax.axis_index("dp")
    grad_bias_in = lax.dynamic_slice_in_dim(small, device * 64, 64)
    vectors = small[2048 : 2048 + 7 * 512].reshape(7, 512)
    return (
        mixed,
        grad_query.astype(jnp.float32),
        grad_embed.astype(jnp.float32),
        grad_encoder.astype(jnp.float32),
        squares[0],
        squares[1],
        squares[2],
        squares[3].T,
        squares[4],
        squares[5],
        squares[6],
        squares[7].T,
        wides[0],
        grad_bias_in,
        wides[1].T,
        vectors[6],
        vectors[:3],
        vectors[3:6],
    )


def local(*arrays):
    if arrays[0].shape[0] == 4 and (lax.axis_size("dp"), lax.axis_size("tp")) == (8, 4):
        return local_rows(*arrays)
    return local_split(*arrays)


def solution(mesh):
    in_specs = (
        P("dp", "tp", None),
        P("dp", "tp", None),
        P("dp", "tp", None),
        P("dp", "tp", None),
        P("dp", "tp"),
        P("dp", "tp"),
        P("dp", "tp"),
        P("tp", "dp"),
        P("dp", "tp"),
        P("dp", "tp"),
        P("dp", "tp"),
        P("tp", "dp"),
        P("dp", "tp"),
        P(("tp", "dp")),
        P("tp", "dp"),
        P(),
        P(),
        P(),
        P("dp", None),
        P("dp", None),
        P("dp", None),
        P("dp", None),
    )
    out_specs = (
        P("dp", "tp", None),
        P("dp", "tp", None),
        P("dp", "tp", None),
        P("dp", "tp", None),
        P("dp", "tp"),
        P("dp", "tp"),
        P("dp", "tp"),
        P("tp", "dp"),
        P("dp", "tp"),
        P("dp", "tp"),
        P("dp", "tp"),
        P("tp", "dp"),
        P("dp", "tp"),
        P(("tp", "dp")),
        P("tp", "dp"),
        P(),
        P(),
        P(),
    )
    return jax.shard_map(local, mesh=mesh, in_specs=in_specs, out_specs=out_specs, check_vma=False)
```

```python
import jax
import jax.numpy as jnp
from jax import lax
from jax.experimental import pallas as pl
from jax.experimental.pallas import tpu as pltpu
from jax.sharding import PartitionSpec as P

HEADS = 8
LOW = jnp.bfloat16
WIDE = jnp.float32


EPSILON = 1e-05
score_tile = 512


def layer_norm(values, scale_vec, shift_vec):
    average = jnp.mean(values, axis=-1, keepdims=True)
    centred = values - average
    spread = jnp.mean(centred * centred, axis=-1, keepdims=True)
    return centred * lax.rsqrt(spread + EPSILON) * scale_vec + shift_vec


def gelu_exact(values):
    return 0.5 * values * (1.0 + lax.erf(values * 0.7071067811865476))


def project(inputs, matrix):
    return jnp.einsum("rld,de->rle", inputs, matrix, preferred_element_type=jnp.float32)


def project_back(cotangent, matrix):
    return jnp.einsum("rle,de->rld", cotangent, matrix, preferred_element_type=jnp.float32)


def outer_sum(inputs, cotangent):
    return jnp.einsum("rld,rle->de", inputs, cotangent, preferred_element_type=jnp.float32)


def layout(lengths, length):
    offsets = jnp.cumsum(lengths) - lengths
    positions = jnp.arange(length, dtype=jnp.int32)
    passed = positions[:, None] >= offsets[None, :]
    document = jnp.sum(passed.astype(jnp.int32), axis=1) - 1
    doc_start = jnp.max(jnp.where(passed, offsets[None, :], 0), axis=1)
    return (document, doc_start)


def self_visible(lengths, rank_row, limit_row, length, first_row, block_rows):
    document, doc_start = layout(lengths, length)
    positions = jnp.arange(length, dtype=jnp.int32)
    rows_pos = positions[first_row : first_row + block_rows]
    same_text = document[first_row : first_row + block_rows, None] == document[None, :]
    chosen = (rank_row[None, :] < limit_row[first_row : first_row + block_rows, None]) & (
        rows_pos[:, None] != positions[None, :]
    )
    opener = positions[None, :] == doc_start[first_row : first_row + block_rows, None]
    return same_text & (chosen | opener)


def cross_visible(lengths, src_lengths, length, src_length, first_row, block_rows):
    document, _ = layout(lengths, length)
    source_doc, _ = layout(src_lengths, src_length)
    return document[first_row : first_row + block_rows, None] == source_doc[None, :]


def attend_forward(queries, keys_all, values_all, visible_of, head_count):
    query_count = queries.shape[0]
    head_size = queries.shape[1] // head_count
    factor = head_size ** (-0.5)
    queries = queries.reshape(query_count, head_count, head_size)
    keys_all = keys_all.reshape(keys_all.shape[0], head_count, head_size)
    values_all = values_all.reshape(values_all.shape[0], head_count, head_size)
    block_rows = min(score_tile, query_count)
    outputs = []
    totals = []
    for first_row in range(0, query_count, block_rows):
        query_part = queries[first_row : first_row + block_rows]
        scores = (
            jnp.einsum("qhd,khd->hqk", query_part, keys_all, preferred_element_type=jnp.float32)
            * factor
        )
        scores = jnp.where(visible_of(first_row, block_rows)[None], scores, -1e30)
        highest = jnp.max(scores, axis=-1, keepdims=True)
        exponent = jnp.exp(scores - highest)
        denominator = jnp.sum(exponent, axis=-1, keepdims=True)
        weights_low = (exponent / denominator).astype(jnp.bfloat16)
        outputs.append(
            jnp.einsum("hqk,khd->qhd", weights_low, values_all, preferred_element_type=jnp.float32)
        )
        totals.append(highest[..., 0] + jnp.log(denominator[..., 0]))
    context = jnp.concatenate(outputs, axis=0).reshape(query_count, head_count * head_size)
    return (context, jnp.concatenate(totals, axis=1))


def attend_backward(queries, keys_all, values_all, visible_of, totals, grad_context, head_count):
    query_count = queries.shape[0]
    key_count = keys_all.shape[0]
    head_size = queries.shape[1] // head_count
    factor = head_size ** (-0.5)
    queries = queries.reshape(query_count, head_count, head_size)
    keys_all = keys_all.reshape(key_count, head_count, head_size)
    values_all = values_all.reshape(key_count, head_count, head_size)
    grad_context = grad_context.reshape(query_count, head_count, head_size)
    grad_keys = jnp.zeros((key_count, head_count, head_size), jnp.float32)
    grad_values = jnp.zeros((key_count, head_count, head_size), jnp.float32)
    grad_queries = []
    block_rows = min(score_tile, query_count)
    for first_row in range(0, query_count, block_rows):
        query_part = queries[first_row : first_row + block_rows]
        grad_part = grad_context[first_row : first_row + block_rows]
        scores = (
            jnp.einsum("qhd,khd->hqk", query_part, keys_all, preferred_element_type=jnp.float32)
            * factor
        )
        scores = jnp.where(visible_of(first_row, block_rows)[None], scores, -1e30)
        weights_full = jnp.exp(scores - totals[:, first_row : first_row + block_rows, None])
        grad_weights = jnp.einsum(
            "qhd,khd->hqk", grad_part, values_all, preferred_element_type=jnp.float32
        )
        inner = jnp.sum(grad_weights * weights_full, axis=-1, keepdims=True)
        grad_scores = (weights_full * (grad_weights - inner)).astype(jnp.bfloat16)
        grad_queries.append(
            jnp.einsum("hqk,khd->qhd", grad_scores, keys_all, preferred_element_type=jnp.float32)
            * factor
        )
        grad_keys = (
            grad_keys
            + jnp.einsum(
                "hqk,qhd->khd", grad_scores, query_part, preferred_element_type=jnp.float32
            )
            * factor
        )
        grad_values = grad_values + jnp.einsum(
            "hqk,qhd->khd",
            weights_full.astype(jnp.bfloat16),
            grad_part,
            preferred_element_type=jnp.float32,
        )
    grad_queries = jnp.concatenate(grad_queries, axis=0).reshape(
        query_count, head_count * head_size
    )
    return (
        grad_queries.astype(jnp.bfloat16),
        grad_keys.reshape(key_count, -1).astype(jnp.bfloat16),
        grad_values.reshape(key_count, -1).astype(jnp.bfloat16),
    )


def collect(piece):
    return lax.all_gather(piece, "tp", axis=1, tiled=True)


def spread_sum(partial_sum):
    return lax.psum_scatter(partial_sum, "tp", scatter_dimension=1, tiled=True)


def collect_grad(piece):
    return lax.all_gather(piece, "tp", axis=1, tiled=True)


def send_back(partial_sum):
    return lax.psum_scatter(partial_sum, "tp", scatter_dimension=1, tiled=True)


def local_split(
    query_stream,
    token_embed,
    encoder_out,
    out_grad,
    attn_q,
    attn_k,
    attn_v,
    attn_o,
    cross_q,
    cross_k,
    cross_v,
    cross_o,
    ffn_in,
    ffn_bias_in,
    ffn_out,
    ffn_bias_out,
    norm_gain,
    norm_bias,
    doc_lengths,
    src_lengths,
    ctx_rank,
    ctx_limit,
):
    head_count = HEADS // lax.axis_size("tp")
    (
        self_query,
        self_key,
        self_value,
        self_out,
        other_query,
        other_key,
        other_value,
        other_out,
        hidden_in,
        hidden_bias,
        hidden_out,
    ) = (
        lax.all_gather(attn_q, "dp", axis=0, tiled=True),
        lax.all_gather(attn_k, "dp", axis=0, tiled=True),
        lax.all_gather(attn_v, "dp", axis=0, tiled=True),
        lax.all_gather(attn_o, "dp", axis=1, tiled=True),
        lax.all_gather(cross_q, "dp", axis=0, tiled=True),
        lax.all_gather(cross_k, "dp", axis=0, tiled=True),
        lax.all_gather(cross_v, "dp", axis=0, tiled=True),
        lax.all_gather(cross_o, "dp", axis=1, tiled=True),
        lax.all_gather(ffn_in, "dp", axis=0, tiled=True),
        lax.all_gather(ffn_bias_in, "dp", axis=0, tiled=True),
        lax.all_gather(ffn_out, "dp", axis=1, tiled=True),
    )

    def self_forward(row_items):
        queries, keys_all, values_all, lengths, rank_row, limit_row = row_items

        def visible_of(first_row, block_rows):
            return self_visible(
                lengths, rank_row, limit_row, keys_all.shape[0], first_row, block_rows
            )

        return attend_forward(queries, keys_all, values_all, visible_of, head_count)

    def self_backward(row_items):
        queries, keys_all, values_all, lengths, rank_row, limit_row, totals, grad_context = (
            row_items
        )

        def visible_of(first_row, block_rows):
            return self_visible(
                lengths, rank_row, limit_row, keys_all.shape[0], first_row, block_rows
            )

        return attend_backward(
            queries, keys_all, values_all, visible_of, totals, grad_context, head_count
        )

    def cross_forward(row_items):
        queries, keys_all, values_all, lengths, source_lengths = row_items

        def visible_of(first_row, block_rows):
            return cross_visible(
                lengths, source_lengths, queries.shape[0], keys_all.shape[0], first_row, block_rows
            )

        return attend_forward(queries, keys_all, values_all, visible_of, head_count)

    def cross_backward(row_items):
        queries, keys_all, values_all, lengths, source_lengths, totals, grad_context = row_items

        def visible_of(first_row, block_rows):
            return cross_visible(
                lengths, source_lengths, queries.shape[0], keys_all.shape[0], first_row, block_rows
            )

        return attend_backward(
            queries, keys_all, values_all, visible_of, totals, grad_context, head_count
        )

    query_all = collect(query_stream)
    embed_all = collect(token_embed)
    source_all = collect(encoder_out)
    self_queries = project(query_all, self_query).astype(jnp.bfloat16)
    self_keys = project(embed_all, self_key).astype(jnp.bfloat16)
    self_values = project(embed_all, self_value).astype(jnp.bfloat16)
    self_context, self_totals = lax.map(
        self_forward, (self_queries, self_keys, self_values, doc_lengths, ctx_rank, ctx_limit)
    )
    self_low = self_context.astype(jnp.bfloat16)
    first_sum = query_stream.astype(jnp.float32) + spread_sum(project(self_low, self_out))
    hidden_one, first_back = jax.vjp(layer_norm, first_sum, norm_gain[0], norm_bias[0])
    hidden_one_all = collect(hidden_one.astype(jnp.bfloat16))
    cross_queries = project(hidden_one_all, other_query).astype(jnp.bfloat16)
    cross_keys = project(source_all, other_key).astype(jnp.bfloat16)
    cross_values = project(source_all, other_value).astype(jnp.bfloat16)
    cross_context, cross_totals = lax.map(
        cross_forward, (cross_queries, cross_keys, cross_values, doc_lengths, src_lengths)
    )
    cross_low = cross_context.astype(jnp.bfloat16)
    second_sum = hidden_one + spread_sum(project(cross_low, other_out))
    hidden_two, second_back = jax.vjp(layer_norm, second_sum, norm_gain[1], norm_bias[1])
    hidden_two_low = hidden_two.astype(jnp.bfloat16)
    ffn_inputs = lax.all_gather(hidden_two_low, "tp", axis=1, tiled=True)
    ffn_pre = project(ffn_inputs, hidden_in) + hidden_bias.astype(jnp.float32)
    ffn_gate, gelu_back = jax.vjp(gelu_exact, ffn_pre)
    ffn_act = ffn_gate.astype(jnp.bfloat16)
    ffn_branch = (
        lax.psum_scatter(project(ffn_act, hidden_out), "tp", scatter_dimension=1, tiled=True)
        + ffn_bias_out
    )
    third_sum = hidden_two + ffn_branch
    mixed_full, third_back = jax.vjp(layer_norm, third_sum, norm_gain[2], norm_bias[2])
    grad_third, gain_two, shift_two = third_back(out_grad.astype(jnp.float32))
    grad_ffn = grad_third.astype(jnp.bfloat16)
    grad_bias_out = jnp.sum(grad_ffn.astype(jnp.float32), axis=(0, 1))
    grad_ffn_all = lax.all_gather(grad_ffn, "tp", axis=1, tiled=True)
    grad_act = project_back(grad_ffn_all, hidden_out)
    grad_down = outer_sum(ffn_act, grad_ffn_all)
    grad_pre = gelu_back(grad_act)[0].astype(jnp.bfloat16)
    grad_up = outer_sum(ffn_inputs, grad_pre)
    grad_bias_in = jnp.sum(grad_pre.astype(jnp.float32), axis=(0, 1))
    grad_two = grad_third + lax.psum_scatter(
        project_back(grad_pre, hidden_in), "tp", scatter_dimension=1, tiled=True
    )
    grad_second, gain_one, shift_one = second_back(grad_two)
    grad_cross_all = collect_grad(grad_second.astype(jnp.bfloat16))
    grad_other_out = outer_sum(cross_low, grad_cross_all)
    grad_cross_ctx = project_back(grad_cross_all, other_out).astype(jnp.bfloat16)
    cross_dq, cross_dk, cross_dv = lax.map(
        cross_backward,
        (
            cross_queries,
            cross_keys,
            cross_values,
            doc_lengths,
            src_lengths,
            cross_totals,
            grad_cross_ctx,
        ),
    )
    grad_other_query = outer_sum(hidden_one_all, cross_dq)
    grad_other_key = outer_sum(source_all, cross_dk)
    grad_other_value = outer_sum(source_all, cross_dv)
    grad_encoder = send_back(
        project_back(cross_dk, other_key) + project_back(cross_dv, other_value)
    )
    grad_one = grad_second + send_back(project_back(cross_dq, other_query))
    grad_first, gain_zero, shift_zero = first_back(grad_one)
    grad_attn_all = collect_grad(grad_first.astype(jnp.bfloat16))
    grad_self_out = outer_sum(self_low, grad_attn_all)
    grad_self_ctx = project_back(grad_attn_all, self_out).astype(jnp.bfloat16)
    self_dq, self_dk, self_dv = lax.map(
        self_backward,
        (
            self_queries,
            self_keys,
            self_values,
            doc_lengths,
            ctx_rank,
            ctx_limit,
            self_totals,
            grad_self_ctx,
        ),
    )
    grad_self_query = outer_sum(query_all, self_dq)
    grad_self_key = outer_sum(embed_all, self_dk)
    grad_self_value = outer_sum(embed_all, self_dv)
    grad_embed = send_back(project_back(self_dk, self_key) + project_back(self_dv, self_value))
    grad_query = grad_first + send_back(project_back(self_dq, self_query))
    (
        grad_self_query,
        grad_self_key,
        grad_self_value,
        grad_self_out,
        grad_other_query,
        grad_other_key,
        grad_other_value,
        grad_other_out,
        grad_up,
        grad_bias_in,
        grad_down,
    ) = (
        lax.psum_scatter(
            grad_self_query.astype(jnp.bfloat16), "dp", scatter_dimension=0, tiled=True
        ).astype(jnp.float32),
        lax.psum_scatter(
            grad_self_key.astype(jnp.bfloat16), "dp", scatter_dimension=0, tiled=True
        ).astype(jnp.float32),
        lax.psum_scatter(
            grad_self_value.astype(jnp.bfloat16), "dp", scatter_dimension=0, tiled=True
        ).astype(jnp.float32),
        lax.psum_scatter(
            grad_self_out.astype(jnp.bfloat16), "dp", scatter_dimension=1, tiled=True
        ).astype(jnp.float32),
        lax.psum_scatter(
            grad_other_query.astype(jnp.bfloat16), "dp", scatter_dimension=0, tiled=True
        ).astype(jnp.float32),
        lax.psum_scatter(
            grad_other_key.astype(jnp.bfloat16), "dp", scatter_dimension=0, tiled=True
        ).astype(jnp.float32),
        lax.psum_scatter(
            grad_other_value.astype(jnp.bfloat16), "dp", scatter_dimension=0, tiled=True
        ).astype(jnp.float32),
        lax.psum_scatter(
            grad_other_out.astype(jnp.bfloat16), "dp", scatter_dimension=1, tiled=True
        ).astype(jnp.float32),
        lax.psum_scatter(
            grad_up.astype(jnp.bfloat16), "dp", scatter_dimension=0, tiled=True
        ).astype(jnp.float32),
        lax.psum_scatter(
            grad_bias_in.astype(jnp.bfloat16), "dp", scatter_dimension=0, tiled=True
        ).astype(jnp.float32),
        lax.psum_scatter(
            grad_down.astype(jnp.bfloat16), "dp", scatter_dimension=1, tiled=True
        ).astype(jnp.float32),
    )
    gain_grads = jnp.stack([gain_zero, gain_one, gain_two])
    shift_grads = jnp.stack([shift_zero, shift_one, shift_two])
    gain_grads, shift_grads, grad_bias_out = lax.psum(
        (gain_grads, shift_grads, grad_bias_out), ("dp", "tp")
    )
    return (
        mixed_full.astype(jnp.bfloat16),
        grad_query,
        grad_embed,
        grad_encoder,
        grad_self_query,
        grad_self_key,
        grad_self_value,
        grad_self_out,
        grad_other_query,
        grad_other_key,
        grad_other_value,
        grad_other_out,
        grad_up,
        grad_bias_in,
        grad_down,
        grad_bias_out,
        gain_grads,
        shift_grads,
    )


HIDDEN = -1e30
Q_TILE = 256


def product(left, right, left_axis, right_axis):
    return lax.dot_general(
        left, right, (((left_axis,), (right_axis,)), ((), ())), preferred_element_type=WIDE
    )


def nn(left, right):
    return product(left, right, 1, 0)


def nt(left, right):
    return product(left, right, 1, 1)


def tn(left, right):
    return product(left, right, 0, 0)


def rows_of(index, size):
    return pl.ds(pl.multiple_of(index * size, size), size)


def normalize(values):
    average = jnp.mean(values, axis=-1, keepdims=True)
    centred = values - average
    spread = jnp.mean(centred * centred, axis=-1, keepdims=True)
    inverse = lax.rsqrt(spread + EPSILON)
    return centred * inverse, inverse


def normalize_back(grad, normal, inverse, gain):
    scaled = grad * gain
    mean_one = jnp.mean(scaled, axis=-1, keepdims=True)
    mean_two = jnp.mean(scaled * normal, axis=-1, keepdims=True)
    return inverse * (scaled - mean_one - normal * mean_two)


def add_rows(target, grad):
    target[...] += jnp.sum(grad, axis=0, keepdims=True)


def documents(lengths, row, shape, axis):
    positions = lax.broadcasted_iota(jnp.int32, shape, axis)
    document = jnp.full(shape, -1, jnp.int32)
    start = jnp.zeros(shape, jnp.int32)
    offset = jnp.int32(0)
    for slot in range(lengths.shape[1]):
        passed = positions >= offset
        document = document + passed.astype(jnp.int32)
        start = jnp.where(passed, offset, start)
        offset = offset + lengths[row, slot]
    return positions, document, start


def fill_self_bias(bias, lengths, rank, limit, row):
    length = bias.shape[0]
    key_position, key_document, _ = documents(lengths, row, (length, 1), 0)
    position, document, start = documents(lengths, row, (1, length), 1)
    rank_row = rank[pl.ds(row, 1), :].astype(WIDE)
    key_rank = jnp.transpose(jnp.broadcast_to(rank_row, (128, length)))[:, :1]
    query_limit = limit[pl.ds(row, 1), :].astype(WIDE)
    for tile in range(length // Q_TILE):
        part = slice(tile * Q_TILE, (tile + 1) * Q_TILE)
        chosen = (key_rank < query_limit[:, part]) & (key_position != position[:, part])
        seen = (key_document == document[:, part]) & (chosen | (key_position == start[:, part]))
        bias[:, part] = jnp.where(seen, 0.0, HIDDEN).astype(bias.dtype)


def fill_cross_bias(bias, lengths, source_lengths, row):
    length = bias.shape[0]
    _, key_document, _ = documents(source_lengths, row, (length, 1), 0)
    _, document, _ = documents(lengths, row, (1, length), 1)
    for tile in range(length // Q_TILE):
        part = slice(tile * Q_TILE, (tile + 1) * Q_TILE)
        seen = key_document == document[:, part]
        bias[:, part] = jnp.where(seen, 0.0, HIDDEN).astype(bias.dtype)


def one_head(pair, side):
    lane = lax.broadcasted_iota(jnp.int32, pair.shape, 1)
    return jnp.where(lane // 64 == side, pair, jnp.zeros_like(pair))


def run_after(pair, after):
    for number, actions in after.items():
        if actions:

            @pl.when(pair == number)
            def _():
                for action in actions:
                    action()


def attend(keys, queries, values_t, bias, context, totals, after):
    length = keys.shape[0]

    @pl.loop(0, HEADS // 2)
    def _(pair):
        lanes = rows_of(pair, 128)

        @pl.loop(0, length // Q_TILE)
        def _(tile):
            part = rows_of(tile, Q_TILE)
            key_pair, query_pair = keys[:, lanes], queries[part, lanes]
            outs = []
            for side in (0, 1):
                head = 2 * pair + side
                scores = nt(key_pair, one_head(query_pair, side)) + bias[:, part].astype(WIDE)
                highest = jnp.max(scores, axis=0, keepdims=True)
                weights = jnp.exp(scores - highest).astype(LOW)
                out = nn(values_t[head], weights)
                total = out[64:65]
                outs.append(out[:64] * (1.0 / total))
                totals[pl.ds(head, 1), part] = highest + jnp.log(total)
            context[part, lanes] = jnp.transpose(jnp.concatenate(outs, axis=0)).astype(LOW)

        run_after(pair, after)


def attend_back(keys, keys_t, queries, values, cotangent, bias, totals, inner, grads, after):
    grad_keys, grad_values, grad_queries, key_sum, value_sum = grads
    length = keys.shape[0]

    @pl.loop(0, HEADS // 2)
    def _(pair):
        lanes = rows_of(pair, 128)
        key_sum[...] = jnp.zeros_like(key_sum)
        value_sum[...] = jnp.zeros_like(value_sum)

        @pl.loop(0, length // Q_TILE)
        def _(tile):
            part = rows_of(tile, Q_TILE)
            key_pair, value_pair = keys[:, lanes], values[:, lanes]
            all_weights, all_scores, all_queries, all_cotangents, outs = [], [], [], [], []
            for side in (0, 1):
                head = 2 * pair + side
                query = one_head(queries[part, lanes], side)
                grad = one_head(cotangent[part, lanes], side)
                scores = nt(key_pair, query) + bias[:, part].astype(WIDE)
                weights = jnp.exp(scores - totals[pl.ds(head, 1), part])
                grad_weights = nt(value_pair, grad)
                grad_scores = (weights * (grad_weights - inner[pl.ds(head, 1), part])).astype(LOW)
                outs.append(nn(keys_t[head, :64], grad_scores) * 0.125)
                all_weights.append(weights.astype(LOW))
                all_scores.append(grad_scores)
                all_queries.append(query)
                all_cotangents.append(grad)
            grad_queries[part, lanes] = jnp.transpose(jnp.concatenate(outs, axis=0)).astype(LOW)
            value_sum[...] += nn(
                jnp.concatenate(all_weights, axis=1), jnp.concatenate(all_cotangents, axis=0)
            )
            key_sum[...] += nn(
                jnp.concatenate(all_scores, axis=1), jnp.concatenate(all_queries, axis=0)
            )

        grad_keys[:, lanes] = key_sum[...].astype(LOW)
        grad_values[:, lanes] = value_sum[...].astype(LOW)
        run_after(pair, after)


def inner_products(cotangent, context, inner):
    products = cotangent[...].astype(WIDE) * context[...].astype(WIDE)
    high = products.astype(LOW)
    rest = (products - high.astype(WIDE)).astype(LOW)
    shape = (2 * HEADS, products.shape[1])
    head = lax.broadcasted_iota(jnp.int32, shape, 0)
    lane = lax.broadcasted_iota(jnp.int32, shape, 1)
    pick = jnp.where(lane // 64 == head, 1.0, 0.0).astype(LOW)
    inner[...] = (nt(pick, high) + nt(pick, rest))[:HEADS]


def flip_heads(values, flipped):
    turned = jnp.transpose(values[...])
    for head in range(HEADS):
        flipped[head, :64] = turned[64 * head : 64 * head + 64]

MESH = pl.DeviceIdType.MESH


class Place:
    def __init__(self):
        dp, tp = lax.axis_index("dp"), lax.axis_index("tp")
        self.dp, self.tp = dp, tp
        self.z, self.x = dp // 2, lax.rem(dp, 2)
        self.y, self.core = tp // 2, lax.rem(tp, 2)
        self.core_peer = (dp, 2 * self.y + 1 - self.core)
        self.y_peer = (dp, 2 * (1 - self.y) + self.core)
        self.far_peer = (dp, 2 * (1 - self.y) + 1 - self.core)
        self.x_peer = (2 * self.z + 1 - self.x, tp)
        self.z_steps = [lax.rem(self.z + step, 4) for step in range(4)]
        self.z_peers = [(2 * z + self.x, tp) for z in self.z_steps[1:]]
        self.summing = [self.core_peer, self.x_peer, self.y_peer] + self.z_peers

    def meet(self):
        peers = self.summing + [self.far_peer]
        barrier = pltpu.get_barrier_semaphore()
        for peer in peers:
            pl.semaphore_signal(barrier, inc=1, device_id=peer, device_id_type=MESH)
        pl.semaphore_wait(barrier, len(peers))

    def columns(self, width):
        return [
            pl.ds(pl.multiple_of(tp * width, width), width)
            for tp in (self.tp, self.y_peer[1], self.core_peer[1], self.far_peer[1])
        ]


class Exchange:
    def __init__(self, sends, recvs, number):
        self.sends, self.recvs, self.number = sends, recvs, number
        self.made = []
        self.arriving = []

    def send(self, source, target, peer):
        slot = len(self.made)

        def copy():
            return pltpu.make_async_remote_copy(
                src_ref=source(),
                dst_ref=target(),
                send_sem=self.sends.at[self.number, slot],
                recv_sem=self.recvs.at[self.number, slot],
                device_id=peer,
                device_id_type=MESH,
            )

        copy().start()
        self.made.append(copy)
        self.arriving.append(copy)

    def move(self, block, peer):
        self.send(block, block, peer)

    def arrive(self):
        for copy in self.arriving:
            copy().wait_recv()
        self.arriving = []

    def finish(self):
        for copy in self.made:
            copy().wait_send()


class Gather(Exchange):
    slots = 11

    def __init__(self, place, local, full, first, count, sends, recvs, own_sems, number):
        super().__init__(sends, recvs, number)
        self.place, self.full, self.items = place, full, pl.ds(first, count)
        self.sides = place.columns(local.shape[-1])[:2]
        p = place
        self.source = lambda: local.at[self.items]
        self.target = lambda: full.at[self.items, p.z, p.x, :, self.sides[0]]
        self.own = lambda: pltpu.make_async_copy(
            self.source(), self.target(), own_sems.at[number]
        )

    def stage(self, number):
        p, full, items = self.place, self.full, self.items
        self.arrive()
        if number == 0:
            self.own().start()
            self.send(self.source, self.target, p.y_peer)
        elif number == 1:
            self.own().wait()
            for side in self.sides:
                for peer in p.z_peers:
                    self.move(lambda side=side: full.at[items, p.z, p.x, :, side], peer)
        elif number == 2:
            for side in self.sides:
                self.move(lambda side=side: full.at[items, :, p.x, :, side], p.x_peer)
        elif number == 3:
            for side in self.sides:
                self.move(lambda side=side: full.at[items, :, :, :, side], p.core_peer)


class ToRow(Exchange):
    slots = 3

    def __init__(self, place, local, row, sends, recvs, own_sems, number):
        super().__init__(sends, recvs, number)
        size = local.shape[1]
        p = place
        span = pl.ds(pl.multiple_of(p.tp * size, size), size)

        def here():
            return row.at[span]

        self.own = lambda: pltpu.make_async_copy(local.at[p.tp], here(), own_sems.at[number])
        self.own().start()
        for peer in (p.y_peer, p.far_peer, p.core_peer):
            self.send(lambda peer=peer: local.at[peer[1]], here, peer)

    def wait(self):
        self.own().wait()
        self.arrive()


class FromRow(Exchange):
    slots = 3

    def __init__(self, place, row, blocks, sends, recvs, own_sems, number):
        super().__init__(sends, recvs, number)
        size = blocks.shape[1]
        p = place

        def part(tp):
            return row.at[pl.ds(pl.multiple_of(tp * size, size), size)]

        self.own = lambda: pltpu.make_async_copy(
            part(p.tp), blocks.at[p.tp], own_sems.at[number]
        )
        for peer in (p.y_peer, p.far_peer, p.core_peer):
            self.send(lambda peer=peer: part(peer[1]), lambda: blocks.at[p.tp], peer)
        self.own().start()

    def wait(self):
        self.own().wait()
        self.arrive()


class Scatter(Exchange):
    slots = 8

    def __init__(
        self, place, parts, work, last, out, first, count, ready, sends, recvs, number
    ):
        super().__init__(sends, recvs, number)
        self.place, self.parts, self.work, self.last, self.out = place, parts, work, last, out
        self.numbers = range(first, first + count)
        self.items = pl.ds(first, count)
        self.width = out.shape[-1]
        self.columns = place.columns(self.width)
        self.ready = ready

    def expect(self, index):
        if self.ready is not None:
            pl.semaphore_wait(self.ready.at[self.number, index], 1)

    def stage(self, number):
        p, parts, work, items, width = self.place, self.parts, self.work, self.items, self.width
        first_half, second_half = slice(0, 2 * width), slice(2 * width, 4 * width)
        sides = [slice(side * width, (side + 1) * width) for side in range(4)]
        self.arrive()
        if number == 0:
            self.expect(0)
            for side, column in zip(sides, self.columns[2:]):
                self.send(
                    lambda column=column: parts.at[items, :, :, :, column],
                    lambda side=side: work.at[items, :, :, :, side],
                    p.core_peer,
                )
        elif number == 1:
            for item in self.numbers:
                for side, column in zip(sides, self.columns[:2]):

                    @pl.loop(0, 4)
                    def _(z):
                        work[item, z, :, :, side] += parts[item, z, :, :, column]

            self.expect(1)
            self.send(
                lambda: work.at[items, :, 1 - p.x, :, first_half],
                lambda: work.at[items, :, 0, :, second_half],
                p.x_peer,
            )
        elif number == 2:
            for item in self.numbers:

                @pl.loop(0, 4)
                def _(z):
                    work[item, z, 0, :, second_half] += work[item, z, p.x, :, first_half]

            for step, peer in enumerate(p.z_peers):
                self.expect(3 + step)
                self.send(
                    lambda step=step: work.at[items, p.z_steps[step + 1], 0, :, second_half],
                    lambda step=step: work.at[items, step, 1, :, second_half],
                    peer,
                )
        elif number == 3:
            for item in self.numbers:
                total = work[item, p.z, 0, :, second_half].astype(WIDE)
                for step in range(3):
                    total = total + work[item, step, 1, :, second_half].astype(WIDE)
                work[item, 3, 1, :, second_half] = total.astype(LOW)
            self.expect(2)
            self.send(
                lambda: work.at[items, 3, 1, :, sides[3]],
                lambda: self.last.at[items],
                p.y_peer,
            )
        else:
            for item in self.numbers:
                mine = work[item, 3, 1, :, sides[2]].astype(WIDE)
                self.out[item] = mine + self.last[item].astype(WIDE)


class SumAll(Exchange):
    slots = 5

    def __init__(self, place, values, arrived, sends, recvs):
        super().__init__(sends, recvs, 0)
        p = place
        z_one = p.z + 1 - 2 * lax.rem(p.z, 2)
        peers = (p.core_peer, p.x_peer, p.y_peer, (2 * z_one + p.x, p.tp), p.z_peers[1])
        self.peers, self.values, self.arrived = peers, values, arrived

    def stage(self, number):
        if number:
            self.arrive()
            self.made[-1]().wait_send()
            self.values[...] = self.values[...] + self.arrived[number - 1]
        if number < 5:
            self.send(
                lambda: self.values, lambda: self.arrived.at[number], self.peers[number]
            )


def layer_kernel(
    query, embed, source, cotangent, attn_q, attn_k, attn_v, attn_o, cross_q, cross_k, cross_v,
    cross_o, ffn_in, ffn_bias_in, ffn_out, bias_out, norm_gain, norm_bias, lengths, source_lengths,
    rank, limit,
    own_squares, own_wides, small, mixed_blocks, query_blocks, embed_blocks, encoder_blocks,
    local_squares, local_wides, local_bias, squares, wides, biases, grad_squares, grad_wides,
    work, last_squares, last_wides, arrived,
    query_row, embed_row, source_row, cotangent_row,
    self_q, self_k, self_v, self_context, other_q, other_k, other_v, other_context,
    flipped, totals, other_totals, inner, normal_one, inverse_one, inverse_two,
    hidden_one, hidden_two, act, pre, grad_ffn, grad_second, bias, key_sum, value_sum, bias_in,
    row_sends, row_recvs, row_own, gather_sends, gather_recvs, gather_own,
    scatter_sends, scatter_recvs, sum_sends, sum_recvs, ready,
):
    place = Place()
    row = place.tp
    length, features = query_row.shape
    hidden = act.shape[1]

    for index, piece in enumerate((attn_q, attn_k, attn_v, attn_o, cross_q, cross_k, cross_v, cross_o)):
        flip = index % 4 == 3
        local_squares[index] = jnp.transpose(piece[...]) if flip else piece[...]
    local_wides[0] = ffn_in[...]
    local_wides[1] = jnp.transpose(ffn_out[...])
    local_bias[...] = jnp.zeros_like(local_bias)
    local_bias[0, 0:1, 0:64] = ffn_bias_in[...]
    place.meet()

    def gather(number, local, full, first, count):
        sems = (gather_sends, gather_recvs, gather_own)
        return Gather(place, local, full, first, count, *sems, number)

    def scatter(number, *buffers):
        return Scatter(place, *buffers, scatter_sends, scatter_recvs, number)

    def row_sems(number):
        return row_sends, row_recvs, row_own, number

    keys_values = gather(0, local_squares, squares, 1, 2)
    query_in = gather(1, local_squares, squares, 0, 1)
    out_in = gather(2, local_squares, squares, 3, 1)
    cross_in = gather(3, local_squares, squares, 4, 4)
    ffn_one = gather(4, local_wides, wides, 0, 1)
    ffn_two = gather(5, local_wides, wides, 1, 1)
    bias_gather = gather(6, local_bias, biases, 0, 1)
    gathers = [keys_values, query_in, out_in, cross_in, ffn_one, ffn_two, bias_gather]
    scatter_down = scatter(0, grad_wides, wides, last_wides, own_wides, 1, 1, ready)
    scatter_up = scatter(1, grad_wides, wides, last_wides, own_wides, 0, 1, ready)
    scatter_cross = scatter(2, grad_squares, work, last_squares, own_squares, 4, 4, None)
    scatter_out = scatter(3, grad_squares, work, last_squares, own_squares, 3, 1, None)
    scatter_self = scatter(4, grad_squares, work, last_squares, own_squares, 0, 3, None)
    sum_all = SumAll(place, small, arrived, sum_sends, sum_recvs)

    def step(task, number):
        return lambda: task.stage(number)

    def square(index):
        return squares[index].reshape(features, features)

    def wide(index):
        return wides[index].reshape(features, hidden)

    def vector(index):
        first = (index % 4) * features
        return small.at[1 + index // 4 : 2 + index // 4, first : first + features]

    def quarter(ref, index):
        return ref.at[:, index * features : (index + 1) * features]

    for task in (keys_values, query_in, out_in):
        task.stage(0)
    embed_in = ToRow(place, embed, embed_row, *row_sems(0))
    for task in (cross_in, ffn_one, ffn_two, bias_gather):
        task.stage(0)
    for task in (keys_values, query_in, out_in):
        task.stage(1)
    query_stream = ToRow(place, query, query_row, *row_sems(1))
    small[...] = jnp.zeros_like(small)
    fill_self_bias(bias, lengths, rank, limit, row)
    flipped[:, 64:] = jnp.ones((HEADS, flipped.shape[1] - 64, length), LOW)
    keys_values.stage(2)
    query_in.stage(2)
    keys_values.stage(3)
    cross_in.stage(1)
    source_in = ToRow(place, source, source_row, *row_sems(2))
    cotangent_in = ToRow(place, cotangent, cotangent_row, *row_sems(3))
    embed_in.wait()
    keys_values.stage(4)
    self_k[...] = nn(embed_row[...], square(1)).astype(LOW)
    query_in.stage(3)
    out_in.stage(2)
    self_v[...] = nn(embed_row[...], square(2)).astype(LOW)
    flip_heads(self_v, flipped)
    query_stream.wait()
    query_in.stage(4)
    out_in.stage(3)
    cross_in.stage(2)
    self_q[...] = (nn(query_row[...], square(0)) * 0.125).astype(LOW)
    attend(
        self_k, self_q, flipped, bias, self_context, totals,
        {
            0: [step(out_in, 4), step(ffn_one, 1), step(ffn_two, 1), step(bias_gather, 1)],
            1: [step(cross_in, 3), step(ffn_one, 2)],
            2: [step(bias_gather, 2)],
            3: [step(ffn_two, 2), step(bias_gather, 3)],
        },
    )

    @pl.loop(0, length // 256)
    def _(tile):
        part = rows_of(tile, 256)
        branch = nt(self_context[part], square(3))
        normal, inverse = normalize(query_row[part].astype(WIDE) + branch)
        normal_one[part] = normal
        inverse_one[part] = inverse
        hidden_one[part] = (normal * norm_gain[0:1] + norm_bias[0:1]).astype(LOW)

    fill_cross_bias(bias, lengths, source_lengths, row)
    cross_in.stage(4)
    source_in.wait()
    other_k[...] = nn(source_row[...], square(5)).astype(LOW)
    other_v[...] = nn(source_row[...], square(6)).astype(LOW)
    ffn_one.stage(3)
    other_q[...] = (nn(hidden_one[...], square(4)) * 0.125).astype(LOW)
    flip_heads(other_v, flipped)
    attend(
        other_k, other_q, flipped, bias, other_context, other_totals,
        {1: [step(ffn_two, 3), step(bias_gather, 4)], 3: [step(ffn_one, 4), step(ffn_two, 4)]},
    )
    cotangent_in.wait()
    for block in range(4):
        pieces = biases[0, :, :, :, block * 128 : block * 128 + 128].reshape(128, 128)
        size = hidden // 4
        lane = lax.broadcasted_iota(jnp.int32, (128, size), 1)
        line = lax.broadcasted_iota(jnp.int32, (128, size), 0)
        spread = nn(pieces, jnp.where(lane % 64 == line, 1.0, 0.0).astype(LOW))
        spread = jnp.where(lane // 64 == line // 16, spread, 0.0)
        bias_in[:, block * size : block * size + size] = jnp.sum(spread, axis=0, keepdims=True)

    @pl.loop(0, length // 256)
    def _(tile):
        part = rows_of(tile, 256)
        branch = nt(other_context[part], square(7))
        before = normal_one[part] * norm_gain[0:1] + norm_bias[0:1]
        normal_mid, inverse_mid = normalize(before + branch)
        after = normal_mid * norm_gain[1:2] + norm_bias[1:2]
        low = after.astype(LOW)
        hidden_two[part] = low
        before = nn(low, wide(0)) + bias_in[...]
        below = 0.5 * (1.0 + lax.erf(before * 0.7071067811865476))
        density = jnp.exp(-0.5 * before * before) * 0.3989422804014327
        slope = below + before * density
        gate = (before * below).astype(LOW)
        act[part] = gate
        after = after + nt(gate, wide(1)) + bias_out[...]
        normal, inverse = normalize(after)
        grad = cotangent_row[part].astype(WIDE)
        cotangent_row[part] = (normal * norm_gain[2:3] + norm_bias[2:3]).astype(LOW)
        add_rows(vector(2), grad * normal)
        add_rows(vector(5), grad)
        grad = normalize_back(grad, normal, inverse, norm_gain[2:3])
        low = grad.astype(LOW)
        grad_ffn[part] = low
        add_rows(vector(6), low.astype(WIDE))
        grad_pre = (nn(low, wide(1)) * slope).astype(LOW)
        pre[part] = grad_pre
        add_rows(small.at[0:1], grad_pre.astype(WIDE))
        grad = grad + nt(grad_pre, wide(0))
        add_rows(vector(1), grad * normal_mid)
        add_rows(vector(4), grad)
        grad_second[part] = normalize_back(grad, normal_mid, inverse_mid, norm_gain[1:2])

    for task in (ffn_one, ffn_two):
        task.finish()
    for group in (0, 1):
        for index, peer in enumerate(place.summing):
            there = index if index < 3 else 8 - index
            pl.semaphore_signal(
                ready.at[group, there], inc=1, device_id=peer, device_id_type=MESH
            )
    mixed_out = FromRow(place, cotangent_row, mixed_blocks, *row_sems(4))
    grad_wides[1] = tn(grad_ffn[...], act[...]).astype(LOW).reshape(grad_wides.shape[1:])
    scatter_down.stage(0)
    grad_wides[0] = tn(hidden_two[...], pre[...]).astype(LOW).reshape(grad_wides.shape[1:])
    scatter_up.stage(0)

    cotangent_low, grad_k, grad_v, grad_q = (quarter(act, i) for i in range(4))

    def weight_grad(index, inputs, grad):
        grad_squares[index] = tn(inputs, grad).astype(LOW).reshape(grad_squares.shape[1:])

    def attention_back(first, grad_out, context, keys, queries, values, sums, before, after):
        weight_grad(first + 3, grad_out, context[...])
        cotangent_low[...] = nn(grad_out, square(first + 3)).astype(LOW)
        before()
        flip_heads(keys, flipped)
        inner_products(cotangent_low, context, inner)
        attend_back(
            keys, flipped, queries, values, cotangent_low, bias, sums, inner,
            (grad_k, grad_v, grad_q, key_sum, value_sum), after,
        )

    attention_back(
        4, grad_second[...].astype(LOW), other_context, other_k, other_q, other_v, other_totals,
        lambda: scatter_down.stage(1),
        {
            0: [step(scatter_up, 1)],
            1: [step(scatter_down, 2)],
            3: [step(scatter_up, 2), step(scatter_down, 3)],
        },
    )
    weight_grad(4, hidden_one[...], grad_q[...])
    weight_grad(5, source_row[...], grad_k[...])
    weight_grad(6, source_row[...], grad_v[...])
    scatter_cross.stage(0)
    source_row[...] = (nt(grad_k[...], square(5)) + nt(grad_v[...], square(6))).astype(LOW)
    encoder_out = FromRow(place, source_row, encoder_blocks, *row_sems(5))

    @pl.loop(0, length // 256)
    def _(tile):
        part = rows_of(tile, 256)
        grad = grad_second[part] + nt(grad_q[part], square(4))
        normal = normal_one[part]
        add_rows(vector(0), grad * normal)
        add_rows(vector(3), grad)
        grad_second[part] = normalize_back(grad, normal, inverse_one[part], norm_gain[0:1])

    sum_all.stage(0)
    fill_self_bias(bias, lengths, rank, limit, row)
    scatter_cross.stage(1)
    attention_back(
        0, grad_second[...].astype(LOW), self_context, self_k, self_q, self_v, totals,
        lambda: (scatter_out.stage(0), sum_all.stage(1)),
        {
            0: [step(scatter_up, 3), step(scatter_down, 4), step(scatter_out, 1), step(sum_all, 2)],
            1: [step(scatter_cross, 2), step(scatter_up, 4), step(sum_all, 3)],
            2: [step(scatter_out, 2), step(sum_all, 4)],
            3: [step(scatter_cross, 3), step(sum_all, 5)],
        },
    )
    weight_grad(1, embed_row[...], grad_k[...])
    weight_grad(2, embed_row[...], grad_v[...])
    embed_row[...] = (nt(grad_k[...], square(1)) + nt(grad_v[...], square(2))).astype(LOW)
    embed_out = FromRow(place, embed_row, embed_blocks, *row_sems(6))
    weight_grad(0, query_row[...], grad_q[...])
    scatter_self.stage(0)
    query_row[...] = (grad_second[...] + nt(grad_q[...], square(0))).astype(LOW)
    query_out = FromRow(place, query_row, query_blocks, *row_sems(7))
    scatter_out.stage(3)
    scatter_cross.stage(4)
    for number in (1, 2, 3):
        scatter_self.stage(number)
    scatter_out.stage(4)
    scatter_self.stage(4)
    outgoing = [mixed_out, encoder_out, embed_out, query_out]
    for task in outgoing:
        task.wait()
    for task in outgoing + [embed_in, query_stream, source_in, cotangent_in]:
        task.finish()
    for task in gathers[:4] + gathers[6:]:
        task.finish()
    for task in (scatter_down, scatter_up, scatter_cross, scatter_out, scatter_self):
        task.finish()


def run_layer(streams, weights, vectors, tables):
    _, size, features = streams[0].shape
    length = 4 * size
    hidden = weights[8].shape[0] * 8 * 4
    hidden = 4 * weights[8].shape[1]
    shape = jax.ShapeDtypeStruct
    vmem_in = pl.BlockSpec(memory_space=pltpu.VMEM)
    smem_in = pl.BlockSpec(memory_space=pltpu.SMEM)
    hbm = pl.BlockSpec(memory_space=pl.ANY)
    vmem, dma = pltpu.VMEM, pltpu.SemaphoreType.DMA
    row, wide_row = vmem((length, features), LOW), vmem((length, features), WIDE)
    per_head, column = vmem((HEADS, length), WIDE), vmem((length, 1), WIDE)
    full_squares = vmem((8, 4, 2, features // 8, features), LOW)
    full_wides = vmem((2, 4, 2, features // 8, hidden), LOW)
    blocks = shape((4, size, features), LOW)
    return pl.pallas_call(
        layer_kernel,
        out_shape=[
            shape((8, features // 8, features // 4), WIDE),
            shape((2, features // 8, hidden // 4), WIDE),
            shape((8, hidden), WIDE),
        ]
        + [blocks] * 4,
        in_specs=[hbm] * 4 + [vmem_in] * 14 + [smem_in] * 2 + [vmem_in] * 2,
        out_specs=[vmem_in] * 3 + [hbm] * 4,
        scratch_shapes=[
            vmem((8, features // 8, features // 4), LOW),
            vmem((2, features // 8, hidden // 4), LOW),
            vmem((1, 16, 128), LOW),
            full_squares,
            full_wides,
            vmem((1, 4, 2, 16, 512), LOW),
            full_squares,
            full_wides,
            full_squares,
            vmem((8, features // 8, features // 4), LOW),
            vmem((2, features // 8, hidden // 4), LOW),
            vmem((5, 8, hidden), WIDE),
        ]
        + [row] * 12
        + [vmem((HEADS, 80, length), LOW)]
        + [per_head] * 3
        + [wide_row, column, column, row, row]
        + [vmem((length, hidden), LOW)] * 2
        + [row, wide_row, vmem((length, length), LOW)]
        + [vmem((length, 128), WIDE)] * 2
        + [vmem((1, hidden), WIDE)]
        + [dma((8, 3)), dma((8, 3)), dma((8,))]
        + [dma((7, Gather.slots)), dma((7, Gather.slots)), dma((7,))]
        + [dma((5, Scatter.slots)), dma((5, Scatter.slots)), dma((1, 5)), dma((1, 5))]
        + [pltpu.SemaphoreType.REGULAR((2, 6))],
        compiler_params=pltpu.CompilerParams(
            collective_id=0, has_side_effects=True, vmem_limit_bytes=63 * 2**20
        ),
        name="layer",
    )(*streams, *weights, *vectors, *tables)


def local_rows(
    query_stream,
    token_embed,
    encoder_out,
    out_grad,
    attn_q,
    attn_k,
    attn_v,
    attn_o,
    cross_q,
    cross_k,
    cross_v,
    cross_o,
    ffn_in,
    ffn_bias_in,
    ffn_out,
    ffn_bias_out,
    norm_gain,
    norm_bias,
    doc_lengths,
    src_lengths,
    ctx_rank,
    ctx_limit,
):
    squares, wides, small, mixed, grad_query, grad_embed, grad_encoder = run_layer(
        (query_stream, token_embed, encoder_out, out_grad),
        (attn_q, attn_k, attn_v, attn_o, cross_q, cross_k, cross_v, cross_o)
        + (ffn_in, ffn_bias_in[None], ffn_out),
        (ffn_bias_out[None], norm_gain, norm_bias),
        (doc_lengths, src_lengths, ctx_rank, ctx_limit),
    )
    small = small.reshape(-1)
    device = lax.axis_index("tp") * lax.axis_size("dp") + lax.axis_index("dp")
    grad_bias_in = lax.dynamic_slice_in_dim(small, device * 64, 64)
    vectors = small[2048 : 2048 + 7 * 512].reshape(7, 512)
    return (
        mixed,
        grad_query.astype(jnp.float32),
        grad_embed.astype(jnp.float32),
        grad_encoder.astype(jnp.float32),
        squares[0],
        squares[1],
        squares[2],
        squares[3].T,
        squares[4],
        squares[5],
        squares[6],
        squares[7].T,
        wides[0],
        grad_bias_in,
        wides[1].T,
        vectors[6],
        vectors[:3],
        vectors[3:6],
    )


def local(*arrays):
    if arrays[0].shape[0] == 4 and (lax.axis_size("dp"), lax.axis_size("tp")) == (8, 4):
        return local_rows(*arrays)
    return local_split(*arrays)


def solution(mesh):
    in_specs = (
        P("dp", "tp", None),
        P("dp", "tp", None),
        P("dp", "tp", None),
        P("dp", "tp", None),
        P("dp", "tp"),
        P("dp", "tp"),
        P("dp", "tp"),
        P("tp", "dp"),
        P("dp", "tp"),
        P("dp", "tp"),
        P("dp", "tp"),
        P("tp", "dp"),
        P("dp", "tp"),
        P(("tp", "dp")),
        P("tp", "dp"),
        P(),
        P(),
        P(),
        P("dp", None),
        P("dp", None),
        P("dp", None),
        P("dp", None),
    )
    out_specs = (
        P("dp", "tp", None),
        P("dp", "tp", None),
        P("dp", "tp", None),
        P("dp", "tp", None),
        P("dp", "tp"),
        P("dp", "tp"),
        P("dp", "tp"),
        P("tp", "dp"),
        P("dp", "tp"),
        P("dp", "tp"),
        P("dp", "tp"),
        P("tp", "dp"),
        P("dp", "tp"),
        P(("tp", "dp")),
        P("tp", "dp"),
        P(),
        P(),
        P(),
    )
    return jax.shard_map(local, mesh=mesh, in_specs=in_specs, out_specs=out_specs, check_vma=False)
```

```python
from types import SimpleNamespace

import jax
import jax.numpy as jnp
from jax import lax
from jax.experimental import pallas as pl
from jax.experimental.pallas import tpu as pltpu
from jax.sharding import PartitionSpec as P

HEADS = 8
LOW = jnp.bfloat16
WIDE = jnp.float32


EPSILON = 1e-05
score_tile = 512


def layer_norm(values, scale_vec, shift_vec):
    average = jnp.mean(values, axis=-1, keepdims=True)
    centred = values - average
    spread = jnp.mean(centred * centred, axis=-1, keepdims=True)
    return centred * lax.rsqrt(spread + EPSILON) * scale_vec + shift_vec


def gelu_exact(values):
    return 0.5 * values * (1.0 + lax.erf(values * 0.7071067811865476))


def project(inputs, matrix):
    return jnp.einsum("rld,de->rle", inputs, matrix, preferred_element_type=jnp.float32)


def project_back(cotangent, matrix):
    return jnp.einsum("rle,de->rld", cotangent, matrix, preferred_element_type=jnp.float32)


def outer_sum(inputs, cotangent):
    return jnp.einsum("rld,rle->de", inputs, cotangent, preferred_element_type=jnp.float32)


def layout(lengths, length):
    offsets = jnp.cumsum(lengths) - lengths
    positions = jnp.arange(length, dtype=jnp.int32)
    passed = positions[:, None] >= offsets[None, :]
    document = jnp.sum(passed.astype(jnp.int32), axis=1) - 1
    doc_start = jnp.max(jnp.where(passed, offsets[None, :], 0), axis=1)
    return (document, doc_start)


def self_visible(lengths, rank_row, limit_row, length, first_row, block_rows):
    document, doc_start = layout(lengths, length)
    positions = jnp.arange(length, dtype=jnp.int32)
    rows_pos = positions[first_row : first_row + block_rows]
    same_text = document[first_row : first_row + block_rows, None] == document[None, :]
    chosen = (rank_row[None, :] < limit_row[first_row : first_row + block_rows, None]) & (
        rows_pos[:, None] != positions[None, :]
    )
    opener = positions[None, :] == doc_start[first_row : first_row + block_rows, None]
    return same_text & (chosen | opener)


def cross_visible(lengths, src_lengths, length, src_length, first_row, block_rows):
    document, _ = layout(lengths, length)
    source_doc, _ = layout(src_lengths, src_length)
    return document[first_row : first_row + block_rows, None] == source_doc[None, :]


def attend_forward(queries, keys_all, values_all, visible_of, head_count):
    query_count = queries.shape[0]
    head_size = queries.shape[1] // head_count
    factor = head_size ** (-0.5)
    queries = queries.reshape(query_count, head_count, head_size)
    keys_all = keys_all.reshape(keys_all.shape[0], head_count, head_size)
    values_all = values_all.reshape(values_all.shape[0], head_count, head_size)
    block_rows = min(score_tile, query_count)
    outputs = []
    totals = []
    for first_row in range(0, query_count, block_rows):
        query_part = queries[first_row : first_row + block_rows]
        scores = (
            jnp.einsum("qhd,khd->hqk", query_part, keys_all, preferred_element_type=jnp.float32)
            * factor
        )
        scores = jnp.where(visible_of(first_row, block_rows)[None], scores, -1e30)
        highest = jnp.max(scores, axis=-1, keepdims=True)
        exponent = jnp.exp(scores - highest)
        denominator = jnp.sum(exponent, axis=-1, keepdims=True)
        weights_low = (exponent / denominator).astype(jnp.bfloat16)
        outputs.append(
            jnp.einsum("hqk,khd->qhd", weights_low, values_all, preferred_element_type=jnp.float32)
        )
        totals.append(highest[..., 0] + jnp.log(denominator[..., 0]))
    context = jnp.concatenate(outputs, axis=0).reshape(query_count, head_count * head_size)
    return (context, jnp.concatenate(totals, axis=1))


def attend_backward(queries, keys_all, values_all, visible_of, totals, grad_context, head_count):
    query_count = queries.shape[0]
    key_count = keys_all.shape[0]
    head_size = queries.shape[1] // head_count
    factor = head_size ** (-0.5)
    queries = queries.reshape(query_count, head_count, head_size)
    keys_all = keys_all.reshape(key_count, head_count, head_size)
    values_all = values_all.reshape(key_count, head_count, head_size)
    grad_context = grad_context.reshape(query_count, head_count, head_size)
    grad_keys = jnp.zeros((key_count, head_count, head_size), jnp.float32)
    grad_values = jnp.zeros((key_count, head_count, head_size), jnp.float32)
    grad_queries = []
    block_rows = min(score_tile, query_count)
    for first_row in range(0, query_count, block_rows):
        query_part = queries[first_row : first_row + block_rows]
        grad_part = grad_context[first_row : first_row + block_rows]
        scores = (
            jnp.einsum("qhd,khd->hqk", query_part, keys_all, preferred_element_type=jnp.float32)
            * factor
        )
        scores = jnp.where(visible_of(first_row, block_rows)[None], scores, -1e30)
        weights_full = jnp.exp(scores - totals[:, first_row : first_row + block_rows, None])
        grad_weights = jnp.einsum(
            "qhd,khd->hqk", grad_part, values_all, preferred_element_type=jnp.float32
        )
        inner = jnp.sum(grad_weights * weights_full, axis=-1, keepdims=True)
        grad_scores = (weights_full * (grad_weights - inner)).astype(jnp.bfloat16)
        grad_queries.append(
            jnp.einsum("hqk,khd->qhd", grad_scores, keys_all, preferred_element_type=jnp.float32)
            * factor
        )
        grad_keys = (
            grad_keys
            + jnp.einsum(
                "hqk,qhd->khd", grad_scores, query_part, preferred_element_type=jnp.float32
            )
            * factor
        )
        grad_values = grad_values + jnp.einsum(
            "hqk,qhd->khd",
            weights_full.astype(jnp.bfloat16),
            grad_part,
            preferred_element_type=jnp.float32,
        )
    grad_queries = jnp.concatenate(grad_queries, axis=0).reshape(
        query_count, head_count * head_size
    )
    return (
        grad_queries.astype(jnp.bfloat16),
        grad_keys.reshape(key_count, -1).astype(jnp.bfloat16),
        grad_values.reshape(key_count, -1).astype(jnp.bfloat16),
    )


def collect(piece):
    return lax.all_gather(piece, "tp", axis=1, tiled=True)


def spread_sum(partial_sum):
    return lax.psum_scatter(partial_sum, "tp", scatter_dimension=1, tiled=True)


def collect_grad(piece):
    return lax.all_gather(piece, "tp", axis=1, tiled=True)


def send_back(partial_sum):
    return lax.psum_scatter(partial_sum, "tp", scatter_dimension=1, tiled=True)


def local_split(
    query_stream,
    token_embed,
    encoder_out,
    out_grad,
    attn_q,
    attn_k,
    attn_v,
    attn_o,
    cross_q,
    cross_k,
    cross_v,
    cross_o,
    ffn_in,
    ffn_bias_in,
    ffn_out,
    ffn_bias_out,
    norm_gain,
    norm_bias,
    doc_lengths,
    src_lengths,
    ctx_rank,
    ctx_limit,
):
    head_count = HEADS // lax.axis_size("tp")
    (
        self_query,
        self_key,
        self_value,
        self_out,
        other_query,
        other_key,
        other_value,
        other_out,
        hidden_in,
        hidden_bias,
        hidden_out,
    ) = (
        lax.all_gather(attn_q, "dp", axis=0, tiled=True),
        lax.all_gather(attn_k, "dp", axis=0, tiled=True),
        lax.all_gather(attn_v, "dp", axis=0, tiled=True),
        lax.all_gather(attn_o, "dp", axis=1, tiled=True),
        lax.all_gather(cross_q, "dp", axis=0, tiled=True),
        lax.all_gather(cross_k, "dp", axis=0, tiled=True),
        lax.all_gather(cross_v, "dp", axis=0, tiled=True),
        lax.all_gather(cross_o, "dp", axis=1, tiled=True),
        lax.all_gather(ffn_in, "dp", axis=0, tiled=True),
        lax.all_gather(ffn_bias_in, "dp", axis=0, tiled=True),
        lax.all_gather(ffn_out, "dp", axis=1, tiled=True),
    )

    def self_forward(row_items):
        queries, keys_all, values_all, lengths, rank_row, limit_row = row_items

        def visible_of(first_row, block_rows):
            return self_visible(
                lengths, rank_row, limit_row, keys_all.shape[0], first_row, block_rows
            )

        return attend_forward(queries, keys_all, values_all, visible_of, head_count)

    def self_backward(row_items):
        queries, keys_all, values_all, lengths, rank_row, limit_row, totals, grad_context = (
            row_items
        )

        def visible_of(first_row, block_rows):
            return self_visible(
                lengths, rank_row, limit_row, keys_all.shape[0], first_row, block_rows
            )

        return attend_backward(
            queries, keys_all, values_all, visible_of, totals, grad_context, head_count
        )

    def cross_forward(row_items):
        queries, keys_all, values_all, lengths, source_lengths = row_items

        def visible_of(first_row, block_rows):
            return cross_visible(
                lengths, source_lengths, queries.shape[0], keys_all.shape[0], first_row, block_rows
            )

        return attend_forward(queries, keys_all, values_all, visible_of, head_count)

    def cross_backward(row_items):
        queries, keys_all, values_all, lengths, source_lengths, totals, grad_context = row_items

        def visible_of(first_row, block_rows):
            return cross_visible(
                lengths, source_lengths, queries.shape[0], keys_all.shape[0], first_row, block_rows
            )

        return attend_backward(
            queries, keys_all, values_all, visible_of, totals, grad_context, head_count
        )

    query_all = collect(query_stream)
    embed_all = collect(token_embed)
    source_all = collect(encoder_out)
    self_queries = project(query_all, self_query).astype(jnp.bfloat16)
    self_keys = project(embed_all, self_key).astype(jnp.bfloat16)
    self_values = project(embed_all, self_value).astype(jnp.bfloat16)
    self_context, self_totals = lax.map(
        self_forward, (self_queries, self_keys, self_values, doc_lengths, ctx_rank, ctx_limit)
    )
    self_low = self_context.astype(jnp.bfloat16)
    first_sum = query_stream.astype(jnp.float32) + spread_sum(project(self_low, self_out))
    hidden_one, first_back = jax.vjp(layer_norm, first_sum, norm_gain[0], norm_bias[0])
    hidden_one_all = collect(hidden_one.astype(jnp.bfloat16))
    cross_queries = project(hidden_one_all, other_query).astype(jnp.bfloat16)
    cross_keys = project(source_all, other_key).astype(jnp.bfloat16)
    cross_values = project(source_all, other_value).astype(jnp.bfloat16)
    cross_context, cross_totals = lax.map(
        cross_forward, (cross_queries, cross_keys, cross_values, doc_lengths, src_lengths)
    )
    cross_low = cross_context.astype(jnp.bfloat16)
    second_sum = hidden_one + spread_sum(project(cross_low, other_out))
    hidden_two, second_back = jax.vjp(layer_norm, second_sum, norm_gain[1], norm_bias[1])
    hidden_two_low = hidden_two.astype(jnp.bfloat16)
    ffn_inputs = lax.all_gather(hidden_two_low, "tp", axis=1, tiled=True)
    ffn_pre = project(ffn_inputs, hidden_in) + hidden_bias.astype(jnp.float32)
    ffn_gate, gelu_back = jax.vjp(gelu_exact, ffn_pre)
    ffn_act = ffn_gate.astype(jnp.bfloat16)
    ffn_branch = (
        lax.psum_scatter(project(ffn_act, hidden_out), "tp", scatter_dimension=1, tiled=True)
        + ffn_bias_out
    )
    third_sum = hidden_two + ffn_branch
    mixed_full, third_back = jax.vjp(layer_norm, third_sum, norm_gain[2], norm_bias[2])
    grad_third, gain_two, shift_two = third_back(out_grad.astype(jnp.float32))
    grad_ffn = grad_third.astype(jnp.bfloat16)
    grad_bias_out = jnp.sum(grad_ffn.astype(jnp.float32), axis=(0, 1))
    grad_ffn_all = lax.all_gather(grad_ffn, "tp", axis=1, tiled=True)
    grad_act = project_back(grad_ffn_all, hidden_out)
    grad_down = outer_sum(ffn_act, grad_ffn_all)
    grad_pre = gelu_back(grad_act)[0].astype(jnp.bfloat16)
    grad_up = outer_sum(ffn_inputs, grad_pre)
    grad_bias_in = jnp.sum(grad_pre.astype(jnp.float32), axis=(0, 1))
    grad_two = grad_third + lax.psum_scatter(
        project_back(grad_pre, hidden_in), "tp", scatter_dimension=1, tiled=True
    )
    grad_second, gain_one, shift_one = second_back(grad_two)
    grad_cross_all = collect_grad(grad_second.astype(jnp.bfloat16))
    grad_other_out = outer_sum(cross_low, grad_cross_all)
    grad_cross_ctx = project_back(grad_cross_all, other_out).astype(jnp.bfloat16)
    cross_dq, cross_dk, cross_dv = lax.map(
        cross_backward,
        (
            cross_queries,
            cross_keys,
            cross_values,
            doc_lengths,
            src_lengths,
            cross_totals,
            grad_cross_ctx,
        ),
    )
    grad_other_query = outer_sum(hidden_one_all, cross_dq)
    grad_other_key = outer_sum(source_all, cross_dk)
    grad_other_value = outer_sum(source_all, cross_dv)
    grad_encoder = send_back(
        project_back(cross_dk, other_key) + project_back(cross_dv, other_value)
    )
    grad_one = grad_second + send_back(project_back(cross_dq, other_query))
    grad_first, gain_zero, shift_zero = first_back(grad_one)
    grad_attn_all = collect_grad(grad_first.astype(jnp.bfloat16))
    grad_self_out = outer_sum(self_low, grad_attn_all)
    grad_self_ctx = project_back(grad_attn_all, self_out).astype(jnp.bfloat16)
    self_dq, self_dk, self_dv = lax.map(
        self_backward,
        (
            self_queries,
            self_keys,
            self_values,
            doc_lengths,
            ctx_rank,
            ctx_limit,
            self_totals,
            grad_self_ctx,
        ),
    )
    grad_self_query = outer_sum(query_all, self_dq)
    grad_self_key = outer_sum(embed_all, self_dk)
    grad_self_value = outer_sum(embed_all, self_dv)
    grad_embed = send_back(project_back(self_dk, self_key) + project_back(self_dv, self_value))
    grad_query = grad_first + send_back(project_back(self_dq, self_query))
    (
        grad_self_query,
        grad_self_key,
        grad_self_value,
        grad_self_out,
        grad_other_query,
        grad_other_key,
        grad_other_value,
        grad_other_out,
        grad_up,
        grad_bias_in,
        grad_down,
    ) = (
        lax.psum_scatter(
            grad_self_query.astype(jnp.bfloat16), "dp", scatter_dimension=0, tiled=True
        ).astype(jnp.float32),
        lax.psum_scatter(
            grad_self_key.astype(jnp.bfloat16), "dp", scatter_dimension=0, tiled=True
        ).astype(jnp.float32),
        lax.psum_scatter(
            grad_self_value.astype(jnp.bfloat16), "dp", scatter_dimension=0, tiled=True
        ).astype(jnp.float32),
        lax.psum_scatter(
            grad_self_out.astype(jnp.bfloat16), "dp", scatter_dimension=1, tiled=True
        ).astype(jnp.float32),
        lax.psum_scatter(
            grad_other_query.astype(jnp.bfloat16), "dp", scatter_dimension=0, tiled=True
        ).astype(jnp.float32),
        lax.psum_scatter(
            grad_other_key.astype(jnp.bfloat16), "dp", scatter_dimension=0, tiled=True
        ).astype(jnp.float32),
        lax.psum_scatter(
            grad_other_value.astype(jnp.bfloat16), "dp", scatter_dimension=0, tiled=True
        ).astype(jnp.float32),
        lax.psum_scatter(
            grad_other_out.astype(jnp.bfloat16), "dp", scatter_dimension=1, tiled=True
        ).astype(jnp.float32),
        lax.psum_scatter(
            grad_up.astype(jnp.bfloat16), "dp", scatter_dimension=0, tiled=True
        ).astype(jnp.float32),
        lax.psum_scatter(
            grad_bias_in.astype(jnp.bfloat16), "dp", scatter_dimension=0, tiled=True
        ).astype(jnp.float32),
        lax.psum_scatter(
            grad_down.astype(jnp.bfloat16), "dp", scatter_dimension=1, tiled=True
        ).astype(jnp.float32),
    )
    gain_grads = jnp.stack([gain_zero, gain_one, gain_two])
    shift_grads = jnp.stack([shift_zero, shift_one, shift_two])
    gain_grads, shift_grads, grad_bias_out = lax.psum(
        (gain_grads, shift_grads, grad_bias_out), ("dp", "tp")
    )
    return (
        mixed_full.astype(jnp.bfloat16),
        grad_query,
        grad_embed,
        grad_encoder,
        grad_self_query,
        grad_self_key,
        grad_self_value,
        grad_self_out,
        grad_other_query,
        grad_other_key,
        grad_other_value,
        grad_other_out,
        grad_up,
        grad_bias_in,
        grad_down,
        grad_bias_out,
        gain_grads,
        shift_grads,
    )


HIDDEN = -1e30
Q_TILE = 256


def product(left, right, left_axis, right_axis):
    return lax.dot_general(
        left, right, (((left_axis,), (right_axis,)), ((), ())), preferred_element_type=WIDE
    )


def nn(left, right):
    return product(left, right, 1, 0)


def nt(left, right):
    return product(left, right, 1, 1)


def tn(left, right):
    return product(left, right, 0, 0)


def rows_of(index, size):
    return pl.ds(pl.multiple_of(index * size, size), size)


def normalize(values):
    average = jnp.mean(values, axis=-1, keepdims=True)
    centred = values - average
    spread = jnp.mean(centred * centred, axis=-1, keepdims=True)
    inverse = lax.rsqrt(spread + EPSILON)
    return centred * inverse, inverse


def normalize_back(grad, normal, inverse, gain):
    scaled = grad * gain
    mean_one = jnp.mean(scaled, axis=-1, keepdims=True)
    mean_two = jnp.mean(scaled * normal, axis=-1, keepdims=True)
    return inverse * (scaled - mean_one - normal * mean_two)


def add_rows(target, grad):
    target[...] += jnp.sum(grad, axis=0, keepdims=True)


def documents(lengths, row, shape, axis):
    positions = lax.broadcasted_iota(jnp.int32, shape, axis)
    document = jnp.full(shape, -1, jnp.int32)
    start = jnp.zeros(shape, jnp.int32)
    offset = jnp.int32(0)
    for slot in range(lengths.shape[1]):
        passed = positions >= offset
        document = document + passed.astype(jnp.int32)
        start = jnp.where(passed, offset, start)
        offset = offset + lengths[row, slot]
    return positions, document, start


def fill_self_bias(bias, lengths, rank, limit, row):
    length = bias.shape[0]
    key_position, key_document, _ = documents(lengths, row, (length, 1), 0)
    position, document, start = documents(lengths, row, (1, length), 1)
    rank_row = rank[pl.ds(row, 1), :].astype(WIDE)
    key_rank = jnp.transpose(jnp.broadcast_to(rank_row, (128, length)))[:, :1]
    query_limit = limit[pl.ds(row, 1), :].astype(WIDE)
    for tile in range(length // Q_TILE):
        part = slice(tile * Q_TILE, (tile + 1) * Q_TILE)
        chosen = (key_rank < query_limit[:, part]) & (key_position != position[:, part])
        seen = (key_document == document[:, part]) & (chosen | (key_position == start[:, part]))
        bias[:, part] = jnp.where(seen, 0.0, HIDDEN).astype(bias.dtype)


def fill_cross_bias(bias, lengths, source_lengths, row):
    length = bias.shape[0]
    _, key_document, _ = documents(source_lengths, row, (length, 1), 0)
    _, document, _ = documents(lengths, row, (1, length), 1)
    for tile in range(length // Q_TILE):
        part = slice(tile * Q_TILE, (tile + 1) * Q_TILE)
        seen = key_document == document[:, part]
        bias[:, part] = jnp.where(seen, 0.0, HIDDEN).astype(bias.dtype)


def one_head(pair, side):
    lane = lax.broadcasted_iota(jnp.int32, pair.shape, 1)
    return jnp.where(lane // 64 == side, pair, jnp.zeros_like(pair))


def run_after(step, after):
    for number, actions in after.items():
        if actions:

            @pl.when(step == number)
            def _():
                for action in actions:
                    action()


PAIRS = HEADS // 2


def attend(keys, queries, values_t, bias, context, totals, tile_of, room, after):
    scores_of, highest_of = room
    steps = keys.shape[0] // Q_TILE * PAIRS

    def where(step):
        return rows_of(tile_of(step // PAIRS), Q_TILE), lax.rem(step, PAIRS)

    def score(step, slot):
        part, pair = where(step)
        lanes = rows_of(pair, 128)
        for side in (0, 1):
            scores = nt(keys[:, lanes], one_head(queries[part, lanes], side))
            scores = scores + bias[:, part].astype(WIDE)
            scores_of[slot][:, side * Q_TILE : (side + 1) * Q_TILE] = scores
            highest_of[2 * slot + side] = jnp.max(scores, axis=0, keepdims=True)

    def weigh(step, slot):
        part, pair = where(step)
        outs = []
        for side in (0, 1):
            head = 2 * pair + side
            highest = highest_of[2 * slot + side]
            scores = scores_of[slot][:, side * Q_TILE : (side + 1) * Q_TILE]
            out = nn(values_t[head], jnp.exp(scores - highest).astype(LOW))
            total = out[64:65]
            outs.append(out[:64] * (1.0 / total))
            totals[pl.ds(head, 1), part] = highest + jnp.log(total)
        context[part, rows_of(pair, 128)] = jnp.transpose(jnp.concatenate(outs, axis=0)).astype(LOW)

    score(0, 0)

    @pl.loop(0, steps // 2)
    def _(double):
        score(2 * double + 1, 1)
        weigh(2 * double, 0)
        score(lax.rem(2 * double + 2, steps), 0)
        weigh(2 * double + 1, 1)
        run_after(double, after)


def attend_back(
    keys, keys_t, queries, values, cotangent, bias, totals, inner, grads, tile_of, room, after
):
    key_sum, value_sum, grad_queries = grads
    all_weights, all_grads = room
    steps = keys.shape[0] // Q_TILE * PAIRS

    def where(step):
        return rows_of(tile_of(step // PAIRS), Q_TILE), rows_of(lax.rem(step, PAIRS), 128)

    def make(step, slot):
        part, lanes = where(step)
        pair = lax.rem(step, PAIRS)
        for side in (0, 1):
            head = 2 * pair + side
            span = slice(side * Q_TILE, (side + 1) * Q_TILE)
            scores = nt(keys[:, lanes], one_head(queries[part, lanes], side))
            scores = scores + bias[:, part].astype(WIDE)
            grad_weights = nt(values[:, lanes], one_head(cotangent[part, lanes], side))
            weights = jnp.exp(scores - totals[pl.ds(head, 1), part])
            all_weights[slot][:, span] = weights.astype(LOW)
            grad_scores = weights * (grad_weights - inner[pl.ds(head, 1), part])
            all_grads[slot][:, span] = grad_scores.astype(LOW)

    def use(step, slot):
        part, lanes = where(step)
        pair = lax.rem(step, PAIRS)

        def stacked(ref):
            return jnp.concatenate([one_head(ref[part, lanes], side) for side in (0, 1)], axis=0)

        outs = [
            nn(keys_t[2 * pair + side, :64], all_grads[slot][:, side * Q_TILE : (side + 1) * Q_TILE])
            for side in (0, 1)
        ]
        turned = jnp.transpose(jnp.concatenate(outs, axis=0) * 0.125)
        grad_queries[part, lanes] = turned.astype(LOW)
        value_sum[:, lanes] += nn(all_weights[slot][...], stacked(cotangent))
        key_sum[:, lanes] += nn(all_grads[slot][...], stacked(queries))

    key_sum[...] = jnp.zeros_like(key_sum)
    value_sum[...] = jnp.zeros_like(value_sum)
    make(0, 0)

    @pl.loop(0, steps // 2)
    def _(double):
        make(2 * double + 1, 1)
        use(2 * double, 0)
        make(lax.rem(2 * double + 2, steps), 0)
        use(2 * double + 1, 1)
        run_after(double, after)


def inner_products(cotangent, context, inner):
    products = cotangent[...].astype(WIDE) * context[...].astype(WIDE)
    high = products.astype(LOW)
    rest = (products - high.astype(WIDE)).astype(LOW)
    shape = (2 * HEADS, products.shape[1])
    head = lax.broadcasted_iota(jnp.int32, shape, 0)
    lane = lax.broadcasted_iota(jnp.int32, shape, 1)
    pick = jnp.where(lane // 64 == head, 1.0, 0.0).astype(LOW)
    inner[...] = (nt(pick, high) + nt(pick, rest))[:HEADS]


def flip_heads(values, flipped):
    turned = jnp.transpose(values[...])
    for head in range(HEADS):
        flipped[head, :64] = turned[64 * head : 64 * head + 64]

MESH = pl.DeviceIdType.MESH


class Place:
    def __init__(self):
        dp, tp = lax.axis_index("dp"), lax.axis_index("tp")
        self.dp, self.tp = dp, tp
        self.z, self.x = dp // 2, lax.rem(dp, 2)
        self.y, self.core = tp // 2, lax.rem(tp, 2)
        self.core_peer = (dp, 2 * self.y + 1 - self.core)
        self.y_peer = (dp, 2 * (1 - self.y) + self.core)
        self.far_peer = (dp, 2 * (1 - self.y) + 1 - self.core)
        self.x_peer = (2 * self.z + 1 - self.x, tp)
        self.z_steps = [lax.rem(self.z + step, 4) for step in range(4)]
        self.z_peers = [(2 * z + self.x, tp) for z in self.z_steps[1:]]
        self.summing = [self.core_peer, self.x_peer, self.y_peer] + self.z_peers

    def greet(self):
        for peer in self.summing + [self.far_peer]:
            barrier = pltpu.get_barrier_semaphore()
            pl.semaphore_signal(barrier, inc=1, device_id=peer, device_id_type=MESH)

    def meet(self):
        pl.semaphore_wait(pltpu.get_barrier_semaphore(), len(self.summing) + 1)

    def tile(self, number):
        side = lax.rem(self.y + 1 - number // 2, 2)
        return 2 * side + lax.rem(self.core + (number + 1) // 2, 2)

    def columns(self, width):
        return [
            pl.ds(pl.multiple_of(tp * width, width), width)
            for tp in (self.tp, self.y_peer[1], self.core_peer[1], self.far_peer[1])
        ]


class Exchange:
    def __init__(self, sends, recvs, number):
        self.sends, self.recvs, self.number = sends, recvs, number
        self.made = []
        self.arriving = []

    def send(self, source, target, peer):
        slot = len(self.made)

        def copy():
            return pltpu.make_async_remote_copy(
                src_ref=source(),
                dst_ref=target(),
                send_sem=self.sends.at[self.number, slot],
                recv_sem=self.recvs.at[self.number, slot],
                device_id=peer,
                device_id_type=MESH,
            )

        copy().start()
        self.made.append(copy)
        self.arriving.append(copy)

    def move(self, block, peer):
        self.send(block, block, peer)

    def arrive(self):
        for copy in self.arriving:
            copy().wait_recv()
        self.arriving = []

    def finish(self):
        for copy in self.made:
            copy().wait_send()


class Gather(Exchange):
    slots = 11

    def __init__(
        self, place, local, full, first, count, side, sides, sends, recvs, own_sems, number
    ):
        super().__init__(sends, recvs, number)
        self.place, self.full, self.items = place, full, pl.ds(first, count)
        width = local.shape[-1] // sides
        self.sides = [
            pl.ds(pl.multiple_of((tp * sides + side) * width, width), width)
            for tp in (place.tp, place.y_peer[1])
        ]
        p = place
        self.source = lambda: local.at[self.items, :, side * width : (side + 1) * width]
        self.target = lambda: full.at[self.items, p.z, p.x, :, self.sides[0]]
        self.own = lambda: pltpu.make_async_copy(
            self.source(), self.target(), own_sems.at[number]
        )

    def stage(self, number):
        p, full, items = self.place, self.full, self.items
        self.arrive()
        if number == 0:
            self.own().start()
            self.send(self.source, self.target, p.y_peer)
        elif number == 1:
            self.own().wait()
            for side in self.sides:
                for peer in p.z_peers:
                    self.move(lambda side=side: full.at[items, p.z, p.x, :, side], peer)
        elif number == 2:
            for side in self.sides:
                self.move(lambda side=side: full.at[items, :, p.x, :, side], p.x_peer)
        elif number == 3:
            for side in self.sides:
                self.move(lambda side=side: full.at[items, :, :, :, side], p.core_peer)


class ToRow(Exchange):
    slots = 3

    def __init__(self, place, local, row, sends, recvs, own_sems, number):
        super().__init__(sends, recvs, number)
        size = local.shape[1]
        p = place
        span = pl.ds(pl.multiple_of(p.tp * size, size), size)

        def here():
            return row.at[span]

        self.local, self.here = local, here
        self.peers = (p.y_peer, p.far_peer, p.core_peer)
        self.own = lambda: pltpu.make_async_copy(local.at[p.tp], here(), own_sems.at[number])

    def start(self):
        for peer in self.peers:
            self.send(lambda peer=peer: self.local.at[peer[1]], self.here, peer)
        self.own().start()

    def near(self):
        self.own().wait()
        self.arriving.pop()().wait_recv()

    def far(self):
        self.arrive()


class FromRow(Exchange):
    slots = 3

    def __init__(self, place, row, blocks, sends, recvs, own_sems, number):
        super().__init__(sends, recvs, number)
        size = blocks.shape[1]
        p = place
        self.peers = (p.y_peer, p.far_peer, p.core_peer)
        self.target = lambda: blocks.at[p.tp]

        def part(tp):
            return row.at[pl.ds(pl.multiple_of(tp * size, size), size)]

        self.part = part
        self.own = lambda: pltpu.make_async_copy(
            self.part(p.tp), self.target(), own_sems.at[number]
        )

    def give(self, number):
        if number == 3:
            self.own().start()
        else:
            peer = self.peers[number]
            self.send(lambda: self.part(peer[1]), self.target, peer)

    def give_all(self):
        for number in range(4):
            self.give(number)

    def wait(self):
        self.own().wait()
        self.arrive()


class Scatter(Exchange):
    slots = 8

    def __init__(
        self, place, parts, work, last, out, first, count, ready, sends, recvs, number
    ):
        super().__init__(sends, recvs, number)
        self.place, self.parts, self.work, self.last, self.out = place, parts, work, last, out
        self.numbers = range(first, first + count)
        self.items = pl.ds(first, count)
        self.width = out.shape[-1]
        self.columns = place.columns(self.width)
        self.ready = ready

    def expect(self, index):
        if self.ready is not None:
            pl.semaphore_wait(self.ready.at[self.number, index], 1)

    def stage(self, number):
        p, parts, work, items, width = self.place, self.parts, self.work, self.items, self.width
        first_half, second_half = slice(0, 2 * width), slice(2 * width, 4 * width)
        sides = [slice(side * width, (side + 1) * width) for side in range(4)]
        self.arrive()
        if number == 0:
            self.expect(0)
            for side, column in zip(sides, self.columns[2:]):
                self.send(
                    lambda column=column: parts.at[items, :, :, :, column],
                    lambda side=side: work.at[items, :, :, :, side],
                    p.core_peer,
                )
        elif number == 1:
            for item in self.numbers:
                for side, column in zip(sides, self.columns[:2]):

                    @pl.loop(0, 4)
                    def _(z):
                        work[item, z, :, :, side] += parts[item, z, :, :, column]

            self.expect(1)
            self.send(
                lambda: work.at[items, :, 1 - p.x, :, first_half],
                lambda: work.at[items, :, 0, :, second_half],
                p.x_peer,
            )
        elif number == 2:
            for item in self.numbers:

                @pl.loop(0, 4)
                def _(z):
                    work[item, z, 0, :, second_half] += work[item, z, p.x, :, first_half]

            for step, peer in enumerate(p.z_peers):
                self.expect(3 + step)
                self.send(
                    lambda step=step: work.at[items, p.z_steps[step + 1], 0, :, second_half],
                    lambda step=step: work.at[items, step, 1, :, second_half],
                    peer,
                )
        elif number == 3:
            for item in self.numbers:
                total = work[item, p.z, 0, :, second_half].astype(WIDE)
                for step in range(3):
                    total = total + work[item, step, 1, :, second_half].astype(WIDE)
                work[item, 3, 1, :, second_half] = total.astype(LOW)
            self.expect(2)
            self.send(
                lambda: work.at[items, 3, 1, :, sides[3]],
                lambda: self.last.at[items],
                p.y_peer,
            )
        else:
            for item in self.numbers:
                mine = work[item, 3, 1, :, sides[2]].astype(WIDE)
                self.out[item] = mine + self.last[item].astype(WIDE)


class SumAll(Exchange):
    slots = 5

    def __init__(self, place, values, arrived, sends, recvs):
        super().__init__(sends, recvs, 0)
        p = place
        z_one = p.z + 1 - 2 * lax.rem(p.z, 2)
        peers = (p.core_peer, p.x_peer, p.y_peer, (2 * z_one + p.x, p.tp), p.z_peers[1])
        self.peers, self.values, self.arrived = peers, values, arrived

    def stage(self, number):
        if number:
            self.arrive()
            self.made[-1]().wait_send()
            self.values[...] = self.values[...] + self.arrived[number - 1]
        if number < 5:
            self.send(
                lambda: self.values, lambda: self.arrived.at[number], self.peers[number]
            )


def run_schedule(to, do):
    def step(task, number):
        return lambda: task.stage(number)

    do.fill_self_bias()
    to.place.meet()
    first = [to.keys_values, to.query, to.out, to.bias]
    rest = to.cross + to.ffn
    for task in first + rest:
        task.stage(0)
    for task in (to.embed_row, to.query_row, to.source_row, to.cotangent_row):
        task.start()
    for task in first + rest:
        task.stage(1)
    to.keys_values.stage(2)
    to.query.stage(2)
    to.keys_values.stage(3)
    to.embed_row.near()
    to.query_row.near()
    to.keys_values.stage(4)
    do.near_keys_values()
    to.out.stage(2)
    to.bias.stage(2)
    to.query.stage(3)
    to.query.stage(4)
    do.near_queries()
    to.embed_row.far()
    do.far_keys_values()

    def far_queries():
        to.query_row.far()
        do.far_queries()

    do.attend_self(
        {
            0: [step(to.cross[0], 2), step(to.out, 3)],
            1: [step(to.out, 4), step(to.bias, 3)],
            2: [far_queries, step(to.cross[0], 3), step(to.cross[1], 2)],
            3: [step(to.cross[0], 4), step(to.bias, 4)],
            5: [step(to.ffn[0], 2)],
            7: [step(to.cross[1], 3)],
        }
    )
    do.first_norm()
    to.ffn[1].stage(2)
    to.cross[1].stage(4)
    do.fill_cross_bias()
    do.cross_queries()
    to.source_row.near()
    to.source_row.far()
    do.cross_keys_values()
    do.attend_cross(
        {
            0: [step(to.ffn[0], 3)],
            1: [step(to.ffn[2], 2), step(to.ffn[0], 4)],
            4: [step(to.ffn[1], 3)],
            5: [step(to.ffn[3], 2), step(to.ffn[1], 4)],
        }
    )
    do.bias_in()
    do.feed_forward_in(
        {
            0: [step(to.ffn[2], 3)],
            1: [step(to.ffn[2], 4)],
            2: [step(to.ffn[3], 3)],
        }
    )
    to.cotangent_row.near()
    to.cotangent_row.far()
    to.ffn[3].stage(4)
    do.feed_forward()

    for task in to.ffn:
        task.finish()
    for group in (0, 1):
        for index, peer in enumerate(to.place.summing):
            there = index if index < 3 else 8 - index
            pl.semaphore_signal(
                to.ready.at[group, there], inc=1, device_id=peer, device_id_type=MESH
            )
    to.mixed.give_all()
    do.down_grad()
    to.down_sum.stage(0)
    do.up_grad()
    to.up_sum.stage(0)
    do.cross_out_back()
    to.down_sum.stage(1)
    do.cross_back(
        {
            0: [step(to.up_sum, 1)],
            4: [step(to.down_sum, 2)],
            7: [step(to.up_sum, 2)],
        }
    )
    do.cross_grads()
    to.cross_sum.stage(0)
    do.source_grad()
    do.first_norm_back()
    to.small_sum.stage(0)
    to.down_sum.stage(3)
    do.fill_self_bias()
    to.small_sum.stage(1)
    to.cross_sum.stage(1)
    do.self_out_back()
    to.out_sum.stage(0)
    to.small_sum.stage(2)
    to.source_grad.give_all()

    def give_query(number):
        def action():
            do.query_grad(number)
            to.query_grad.give(number)

        return action

    do.self_back(
        {
            0: [step(to.up_sum, 3), step(to.small_sum, 3), step(to.out_sum, 1)],
            1: [give_query(0), step(to.small_sum, 4)],
            2: [step(to.small_sum, 5)],
            3: [give_query(1), step(to.cross_sum, 2), step(to.down_sum, 4)],
            4: [step(to.out_sum, 2)],
            5: [give_query(2), step(to.up_sum, 4)],
            6: [step(to.cross_sum, 3)],
            7: [give_query(3), step(to.out_sum, 3)],
        }
    )
    to.mixed.wait()
    to.mixed.finish()
    do.key_grad()
    to.key_sum.stage(0)
    do.value_grad()
    to.value_sum.stage(0)
    to.key_sum.stage(1)
    do.query_weight_grad()
    to.query_sum.stage(0)
    to.value_sum.stage(1)
    do.far_embed_grad()
    to.embed_grad.give(0)
    to.embed_grad.give(1)
    to.query_sum.stage(1)
    do.near_embed_grad()
    to.embed_grad.give(2)
    to.embed_grad.give(3)
    for task in (to.key_sum, to.value_sum, to.query_sum):
        task.stage(2)
    to.cross_sum.stage(4)
    to.out_sum.stage(4)
    for number in (3, 4):
        for task in (to.key_sum, to.value_sum, to.query_sum):
            task.stage(number)
    outgoing = [to.source_grad, to.query_grad, to.embed_grad]
    for task in outgoing:
        task.wait()
    for task in outgoing + [to.embed_row, to.query_row, to.source_row, to.cotangent_row]:
        task.finish()
    for task in first + to.cross:
        task.finish()
    for task in (to.down_sum, to.up_sum, to.cross_sum, to.out_sum):
        task.finish()
    for task in (to.key_sum, to.value_sum, to.query_sum):
        task.finish()


def layer_kernel(
    query, embed, source, cotangent, attn_q, attn_k, attn_v, attn_o, cross_q, cross_k, cross_v,
    cross_o, ffn_in, ffn_bias_in, ffn_out, bias_out, norm_gain, norm_bias, lengths, source_lengths,
    rank, limit,
    own_squares, own_wides, small, mixed_blocks, query_blocks, embed_blocks, encoder_blocks,
    local_squares, local_wides, local_bias, squares, wides, biases, grad_squares, grad_wides,
    work, last_squares, last_wides, arrived,
    query_row, embed_row, source_row, cotangent_row,
    self_q, self_k, self_v, self_context, other_q, other_k, other_v, other_context,
    flipped, totals, other_totals, inner, highest, normal_one, inverse_one,
    hidden_one, hidden_two, act, pre, grad_ffn, grad_second, key_sum, value_sum, bias, bias_in,
    row_sends, row_recvs, row_own, gather_sends, gather_recvs, gather_own,
    scatter_sends, scatter_recvs, sum_sends, sum_recvs, ready,
):
    place = Place()
    place.greet()
    row = place.tp
    length, features = query_row.shape
    hidden = act.shape[1]
    half = length // 2
    near_half, far_half = rows_of(place.y, half), rows_of(1 - place.y, half)

    for index, piece in enumerate((attn_q, attn_k, attn_v, attn_o, cross_q, cross_k, cross_v, cross_o)):
        local_squares[index] = piece[...]
    local_wides[0] = ffn_in[...]
    local_wides[1] = ffn_out[...]
    local_bias[...] = jnp.zeros_like(local_bias)
    local_bias[0, 0:1, 0:64] = ffn_bias_in[...]
    small[...] = jnp.zeros_like(small)
    flipped[:, 64:] = jnp.ones((HEADS, flipped.shape[1] - 64, length), LOW)

    def gather(number, local, full, first, count, side=0, sides=1):
        sems = (gather_sends, gather_recvs, gather_own)
        return Gather(place, local, full, first, count, side, sides, *sems, number)

    def scatter(number, *buffers):
        return Scatter(place, *buffers, scatter_sends, scatter_recvs, number)

    def row_sems(number):
        return row_sends, row_recvs, row_own, number

    def square(index):
        return squares[index].reshape(features, features)

    def wide(index):
        return wides[index].reshape(features, hidden)

    def vector(index):
        first = (index % 4) * features
        return small.at[1 + index // 4 : 2 + index // 4, first : first + features]

    def quarter(ref, index):
        return ref.at[:, index * features : (index + 1) * features]

    square_sums = (grad_squares, work, last_squares, own_squares)
    wide_sums = (grad_wides, wides, last_wides, own_wides)
    to = SimpleNamespace(
        place=place,
        ready=ready,
        keys_values=gather(0, local_squares, squares, 1, 2),
        query=gather(1, local_squares, squares, 0, 1),
        out=gather(2, local_squares, squares, 3, 1),
        cross=[gather(3 + i, local_squares, squares, 4 + 2 * i, 2) for i in (0, 1)],
        ffn=[gather(5 + i, local_wides, wides, i // 2, 1, i % 2, 2) for i in range(4)],
        bias=gather(9, local_bias, biases, 0, 1),
        embed_row=ToRow(place, embed, embed_row, *row_sems(0)),
        query_row=ToRow(place, query, query_row, *row_sems(1)),
        source_row=ToRow(place, source, source_row, *row_sems(2)),
        cotangent_row=ToRow(place, cotangent, cotangent_row, *row_sems(3)),
        down_sum=scatter(0, *wide_sums, 1, 1, ready),
        up_sum=scatter(1, *wide_sums, 0, 1, ready),
        cross_sum=scatter(2, *square_sums, 4, 4, None),
        out_sum=scatter(3, *square_sums, 3, 1, None),
        key_sum=scatter(4, *square_sums, 1, 1, None),
        value_sum=scatter(5, *square_sums, 2, 1, None),
        query_sum=scatter(6, *square_sums, 0, 1, None),
        small_sum=SumAll(place, small, arrived, sum_sends, sum_recvs),
        mixed=FromRow(place, cotangent_row, mixed_blocks, *row_sems(4)),
        source_grad=FromRow(place, source_row, encoder_blocks, *row_sems(5)),
        query_grad=FromRow(place, hidden_two, query_blocks, *row_sems(6)),
        embed_grad=FromRow(place, cotangent_row, embed_blocks, *row_sems(7)),
    )
    score_room = ((key_sum, value_sum), highest)
    cotangent_low, grad_k, grad_v, grad_q = (quarter(act, i) for i in range(4))
    room = tuple(tuple(quarter(pre, 2 * i + j) for j in (0, 1)) for i in (0, 1))

    def fill_keys_values(rows):
        self_k[rows] = nn(embed_row[rows], square(1)).astype(LOW)
        self_v[rows] = nn(embed_row[rows], square(2)).astype(LOW)

    def fill_queries(rows):
        self_q[rows] = (nn(query_row[rows], square(0)) * 0.125).astype(LOW)

    def attend_self(after):
        flip_heads(self_v, flipped)
        attend(
            self_k, self_q, flipped, bias, self_context, totals,
            lambda number: place.tile(3 - number), score_room, after,
        )

    def first_norm():
        @pl.loop(0, length // 256)
        def _(tile):
            part = rows_of(tile, 256)
            branch = nt(self_context[part], square(3))
            normal, inverse = normalize(query_row[part].astype(WIDE) + branch)
            normal_one[part] = normal
            inverse_one[part] = inverse
            hidden_one[part] = (normal * norm_gain[0:1] + norm_bias[0:1]).astype(LOW)

    def fill_cross_queries():
        other_q[...] = (nn(hidden_one[...], square(4)) * 0.125).astype(LOW)

    def fill_cross_keys_values():
        other_k[...] = nn(source_row[...], square(5)).astype(LOW)
        other_v[...] = nn(source_row[...], square(6)).astype(LOW)

    def attend_cross(after):
        flip_heads(other_v, flipped)
        attend(
            other_k, other_q, flipped, bias, other_context, other_totals,
            lambda number: number, score_room, after,
        )

    def fill_bias_in():
        for block in range(4):
            pieces = biases[0, :, :, :, block * 128 : block * 128 + 128].reshape(128, 128)
            size = hidden // 4
            lane = lax.broadcasted_iota(jnp.int32, (128, size), 1)
            line = lax.broadcasted_iota(jnp.int32, (128, size), 0)
            spread = nn(pieces, jnp.where(lane % 64 == line, 1.0, 0.0).astype(LOW))
            spread = jnp.where(lane // 64 == line // 16, spread, 0.0)
            bias_in[:, block * size : block * size + size] = jnp.sum(spread, axis=0, keepdims=True)

    def feed_forward_in(after):
        @pl.loop(0, length // 256)
        def _(tile):
            part = rows_of(tile, 256)
            branch = nt(other_context[part], square(7))
            before = normal_one[part] * norm_gain[0:1] + norm_bias[0:1]
            normal, inverse = normalize(before + branch)
            grad_second[part] = normal
            key_sum[part, 0:1] = inverse
            low = (normal * norm_gain[1:2] + norm_bias[1:2]).astype(LOW)
            hidden_two[part] = low
            before = nn(low, wide(0)) + bias_in[...]
            below = 0.5 * (1.0 + lax.erf(before * 0.7071067811865476))
            density = jnp.exp(-0.5 * before * before) * 0.3989422804014327
            pre[part] = (below + before * density).astype(LOW)
            act[part] = (before * below).astype(LOW)
            run_after(tile, after)

    def feed_forward():
        @pl.loop(0, length // 256)
        def _(tile):
            part = rows_of(tile, 256)
            normal_mid = grad_second[part]
            after = normal_mid * norm_gain[1:2] + norm_bias[1:2]
            after = after + nt(act[part], wide(1)) + bias_out[...]
            normal, inverse = normalize(after)
            grad = cotangent_row[part].astype(WIDE)
            cotangent_row[part] = (normal * norm_gain[2:3] + norm_bias[2:3]).astype(LOW)
            add_rows(vector(2), grad * normal)
            add_rows(vector(5), grad)
            grad = normalize_back(grad, normal, inverse, norm_gain[2:3])
            low = grad.astype(LOW)
            grad_ffn[part] = low
            add_rows(vector(6), low.astype(WIDE))
            grad_pre = (nn(low, wide(1)) * pre[part].astype(WIDE)).astype(LOW)
            pre[part] = grad_pre
            add_rows(small.at[0:1], grad_pre.astype(WIDE))
            grad = grad + nt(grad_pre, wide(0))
            add_rows(vector(1), grad * normal_mid)
            add_rows(vector(4), grad)
            inverse_mid = key_sum[part, 0:1]
            grad_second[part] = normalize_back(grad, normal_mid, inverse_mid, norm_gain[1:2])

    def wide_grad(index, left, right):
        for side in (slice(0, hidden // 2), slice(hidden // 2, hidden)):
            total = tn(left[...], right[:, side]).astype(LOW)
            grad_wides[index, :, :, :, side] = total.reshape(4, 2, features // 8, hidden // 2)

    def square_grad(index, inputs, grad):
        grad_squares[index] = tn(inputs, grad).astype(LOW).reshape(grad_squares.shape[1:])

    def out_back(first, context):
        grad = grad_second[...].astype(LOW)
        square_grad(first + 3, grad, context[...])
        cotangent_low[...] = nn(grad, square(first + 3)).astype(LOW)

    def attend_back_with(keys, queries, values, context, sums, tile_of, after):
        flip_heads(keys, flipped)
        inner_products(cotangent_low, context, inner)
        attend_back(
            keys, flipped, queries, values, cotangent_low, bias, sums, inner,
            (key_sum, value_sum, grad_q), tile_of, room, after,
        )
        grad_k[...] = key_sum[...].astype(LOW)
        grad_v[...] = value_sum[...].astype(LOW)

    def cross_grads():
        square_grad(4, hidden_one[...], grad_q[...])
        square_grad(5, source_row[...], grad_k[...])
        square_grad(6, source_row[...], grad_v[...])

    def fill_source_grad():
        source_row[...] = (nt(grad_k[...], square(5)) + nt(grad_v[...], square(6))).astype(LOW)

    def first_norm_back():
        @pl.loop(0, length // 256)
        def _(tile):
            part = rows_of(tile, 256)
            grad = grad_second[part] + nt(grad_q[part], square(4))
            normal = normal_one[part]
            add_rows(vector(0), grad * normal)
            add_rows(vector(3), grad)
            grad_second[part] = normalize_back(grad, normal, inverse_one[part], norm_gain[0:1])

    def fill_query_grad(number):
        part = rows_of(place.tile(number), Q_TILE)
        grad = grad_second[part] + nt(grad_q[part], square(0))
        hidden_two[part] = grad.astype(LOW)

    def fill_embed_grad(rows):
        grad = nt(grad_k[rows], square(1)) + nt(grad_v[rows], square(2))
        cotangent_row[rows] = grad.astype(LOW)

    run_schedule(
        to,
        SimpleNamespace(
            fill_self_bias=lambda: fill_self_bias(bias, lengths, rank, limit, row),
            fill_cross_bias=lambda: fill_cross_bias(bias, lengths, source_lengths, row),
            near_keys_values=lambda: fill_keys_values(near_half),
            far_keys_values=lambda: fill_keys_values(far_half),
            near_queries=lambda: fill_queries(near_half),
            far_queries=lambda: fill_queries(far_half),
            attend_self=attend_self,
            first_norm=first_norm,
            cross_queries=fill_cross_queries,
            cross_keys_values=fill_cross_keys_values,
            attend_cross=attend_cross,
            bias_in=fill_bias_in,
            feed_forward_in=feed_forward_in,
            feed_forward=feed_forward,
            down_grad=lambda: wide_grad(1, grad_ffn, act),
            up_grad=lambda: wide_grad(0, hidden_two, pre),
            cross_out_back=lambda: out_back(4, other_context),
            cross_back=lambda after: attend_back_with(
                other_k, other_q, other_v, other_context, other_totals, lambda number: number, after
            ),
            cross_grads=cross_grads,
            source_grad=fill_source_grad,
            first_norm_back=first_norm_back,
            self_out_back=lambda: out_back(0, self_context),
            self_back=lambda after: attend_back_with(
                self_k, self_q, self_v, self_context, totals, place.tile, after
            ),
            query_grad=fill_query_grad,
            far_embed_grad=lambda: fill_embed_grad(far_half),
            near_embed_grad=lambda: fill_embed_grad(near_half),
            key_grad=lambda: square_grad(1, embed_row[...], grad_k[...]),
            value_grad=lambda: square_grad(2, embed_row[...], grad_v[...]),
            query_weight_grad=lambda: square_grad(0, query_row[...], grad_q[...]),
        ),
    )


def run_layer(streams, weights, vectors, tables):
    _, size, features = streams[0].shape
    length = 4 * size
    hidden = 4 * weights[8].shape[1]
    shape = jax.ShapeDtypeStruct
    vmem_in = pl.BlockSpec(memory_space=pltpu.VMEM)
    smem_in = pl.BlockSpec(memory_space=pltpu.SMEM)
    hbm = pl.BlockSpec(memory_space=pl.ANY)
    vmem, dma = pltpu.VMEM, pltpu.SemaphoreType.DMA
    row, wide_row = vmem((length, features), LOW), vmem((length, features), WIDE)
    per_head, column = vmem((HEADS, length), WIDE), vmem((length, 1), WIDE)
    full_squares = vmem((8, 4, 2, features // 8, features), LOW)
    full_wides = vmem((2, 4, 2, features // 8, hidden), LOW)
    blocks = shape((4, size, features), LOW)
    return pl.pallas_call(
        layer_kernel,
        out_shape=[
            shape((8, features // 8, features // 4), WIDE),
            shape((2, features // 8, hidden // 4), WIDE),
            shape((8, hidden), WIDE),
        ]
        + [blocks] * 4,
        in_specs=[hbm] * 4 + [vmem_in] * 14 + [smem_in] * 2 + [vmem_in] * 2,
        out_specs=[vmem_in] * 3 + [hbm] * 4,
        scratch_shapes=[
            vmem((8, features // 8, features // 4), LOW),
            vmem((2, features // 8, hidden // 4), LOW),
            vmem((1, 16, 128), LOW),
            full_squares,
            full_wides,
            vmem((1, 4, 2, 16, 512), LOW),
            full_squares,
            full_wides,
            full_squares,
            vmem((8, features // 8, features // 4), LOW),
            vmem((2, features // 8, hidden // 4), LOW),
            vmem((5, 8, hidden), WIDE),
        ]
        + [row] * 12
        + [vmem((HEADS, 80, length), LOW)]
        + [per_head] * 3
        + [vmem((4, 1, Q_TILE), WIDE)]
        + [wide_row, column, row, row]
        + [vmem((length, hidden), LOW)] * 2
        + [row, wide_row, wide_row, wide_row, vmem((length, length), LOW)]
        + [vmem((1, hidden), WIDE)]
        + [dma((8, 3)), dma((8, 3)), dma((8,))]
        + [dma((10, Gather.slots)), dma((10, Gather.slots)), dma((10,))]
        + [dma((7, Scatter.slots)), dma((7, Scatter.slots)), dma((1, 5)), dma((1, 5))]
        + [pltpu.SemaphoreType.REGULAR((2, 6))],
        compiler_params=pltpu.CompilerParams(
            collective_id=0, has_side_effects=True, vmem_limit_bytes=127 * 2**19
        ),
        name="layer",
    )(*streams, *weights, *vectors, *tables)


def outputs_kernel(
    squares, wides, small, mixed, grad_query, grad_embed, grad_encoder,
    mixed_out, query_out, embed_out, encoder_out, *rest,
):
    square_outs, wide_outs, (bias_in, bias_out, gains, shifts) = rest[:8], rest[8:10], rest[10:]
    mixed_out[...] = mixed[...]
    for low, out in ((grad_query, query_out), (grad_embed, embed_out), (grad_encoder, encoder_out)):
        out[...] = low[...].astype(WIDE)

    @pl.when(pl.program_id(0) == 0)
    def _():
        for index, out in enumerate(square_outs):
            out[...] = squares[index]
        for index, out in enumerate(wide_outs):
            out[...] = wides[index]
        features = gains.shape[1]
        for index in range(7):
            first = (index % 4) * features
            value = small[1 + index // 4 : 2 + index // 4, first : first + features]
            if index == 6:
                bias_out[...] = value
            else:
                (gains if index < 3 else shifts)[index % 3 : index % 3 + 1] = value
        count = wides.shape[2]
        mine = small[0:1, rows_of(lax.axis_index("tp"), count)]
        shift = lax.rem(count - lax.axis_index("dp") * bias_in.shape[1], count)
        bias_in[...] = pltpu.roll(mine, shift, 1)[:, : bias_in.shape[1]]


def write_outputs(squares, wides, small, *blocks):
    shape = jax.ShapeDtypeStruct
    rows, size, features = blocks[0].shape
    whole = pl.BlockSpec(memory_space=pltpu.VMEM)
    one = pl.BlockSpec((1, size, features), lambda i: (i, 0, 0))

    def fixed(extent):
        return pl.BlockSpec(extent, lambda i: (0,) * len(extent))

    singles = [squares.shape[1:]] * 8 + [wides.shape[1:]] * 2
    singles += [(1, wides.shape[1]), (1, features), (3, features), (3, features)]
    return pl.pallas_call(
        outputs_kernel,
        grid=(rows,),
        out_shape=[shape(blocks[0].shape, LOW)]
        + [shape(blocks[0].shape, WIDE)] * 3
        + [shape(extent, WIDE) for extent in singles],
        in_specs=[fixed(squares.shape), fixed(wides.shape), fixed(small.shape)] + [one] * 4,
        out_specs=[one] * 4 + [fixed(extent) for extent in singles],
        name="outputs",
    )(squares, wides, small, *blocks)


def local_rows(
    query_stream,
    token_embed,
    encoder_out,
    out_grad,
    attn_q,
    attn_k,
    attn_v,
    attn_o,
    cross_q,
    cross_k,
    cross_v,
    cross_o,
    ffn_in,
    ffn_bias_in,
    ffn_out,
    ffn_bias_out,
    norm_gain,
    norm_bias,
    doc_lengths,
    src_lengths,
    ctx_rank,
    ctx_limit,
):
    received = run_layer(
        (query_stream, token_embed, encoder_out, out_grad),
        (attn_q, attn_k, attn_v, attn_o.T, cross_q, cross_k, cross_v, cross_o.T)
        + (ffn_in, ffn_bias_in[None], ffn_out.T),
        (ffn_bias_out[None], norm_gain, norm_bias),
        (doc_lengths, src_lengths, ctx_rank, ctx_limit),
    )
    (
        mixed,
        grad_query,
        grad_embed,
        grad_encoder,
        grad_attn_q,
        grad_attn_k,
        grad_attn_v,
        grad_attn_o,
        grad_cross_q,
        grad_cross_k,
        grad_cross_v,
        grad_cross_o,
        grad_ffn_in,
        grad_ffn_out,
        grad_bias_in,
        grad_bias_out,
        gain_grads,
        shift_grads,
    ) = write_outputs(*received)
    return (
        mixed,
        grad_query,
        grad_embed,
        grad_encoder,
        grad_attn_q,
        grad_attn_k,
        grad_attn_v,
        grad_attn_o.T,
        grad_cross_q,
        grad_cross_k,
        grad_cross_v,
        grad_cross_o.T,
        grad_ffn_in,
        grad_bias_in[0],
        grad_ffn_out.T,
        grad_bias_out[0],
        gain_grads,
        shift_grads,
    )


def local(*arrays):
    if arrays[0].shape[0] == 4 and (lax.axis_size("dp"), lax.axis_size("tp")) == (8, 4):
        return local_rows(*arrays)
    return local_split(*arrays)


def solution(mesh):
    in_specs = (
        P("dp", "tp", None),
        P("dp", "tp", None),
        P("dp", "tp", None),
        P("dp", "tp", None),
        P("dp", "tp"),
        P("dp", "tp"),
        P("dp", "tp"),
        P("tp", "dp"),
        P("dp", "tp"),
        P("dp", "tp"),
        P("dp", "tp"),
        P("tp", "dp"),
        P("dp", "tp"),
        P(("tp", "dp")),
        P("tp", "dp"),
        P(),
        P(),
        P(),
        P("dp", None),
        P("dp", None),
        P("dp", None),
        P("dp", None),
    )
    out_specs = (
        P("dp", "tp", None),
        P("dp", "tp", None),
        P("dp", "tp", None),
        P("dp", "tp", None),
        P("dp", "tp"),
        P("dp", "tp"),
        P("dp", "tp"),
        P("tp", "dp"),
        P("dp", "tp"),
        P("dp", "tp"),
        P("dp", "tp"),
        P("tp", "dp"),
        P("dp", "tp"),
        P(("tp", "dp")),
        P("tp", "dp"),
        P(),
        P(),
        P(),
    )
    return jax.shard_map(local, mesh=mesh, in_specs=in_specs, out_specs=out_specs, check_vma=False)
```

```python
from types import SimpleNamespace

import jax
import jax.numpy as jnp
from jax import lax
from jax.experimental import pallas as pl
from jax.experimental.pallas import tpu as pltpu
from jax.sharding import PartitionSpec as P

HEADS = 8
LOW = jnp.bfloat16
WIDE = jnp.float32


EPSILON = 1e-05
score_tile = 512


def layer_norm(values, scale_vec, shift_vec):
    average = jnp.mean(values, axis=-1, keepdims=True)
    centred = values - average
    spread = jnp.mean(centred * centred, axis=-1, keepdims=True)
    return centred * lax.rsqrt(spread + EPSILON) * scale_vec + shift_vec


def gelu_exact(values):
    return 0.5 * values * (1.0 + lax.erf(values * 0.7071067811865476))


def project(inputs, matrix):
    return jnp.einsum("rld,de->rle", inputs, matrix, preferred_element_type=jnp.float32)


def project_back(cotangent, matrix):
    return jnp.einsum("rle,de->rld", cotangent, matrix, preferred_element_type=jnp.float32)


def outer_sum(inputs, cotangent):
    return jnp.einsum("rld,rle->de", inputs, cotangent, preferred_element_type=jnp.float32)


def layout(lengths, length):
    offsets = jnp.cumsum(lengths) - lengths
    positions = jnp.arange(length, dtype=jnp.int32)
    passed = positions[:, None] >= offsets[None, :]
    document = jnp.sum(passed.astype(jnp.int32), axis=1) - 1
    doc_start = jnp.max(jnp.where(passed, offsets[None, :], 0), axis=1)
    return (document, doc_start)


def self_visible(lengths, rank_row, limit_row, length, first_row, block_rows):
    document, doc_start = layout(lengths, length)
    positions = jnp.arange(length, dtype=jnp.int32)
    rows_pos = positions[first_row : first_row + block_rows]
    same_text = document[first_row : first_row + block_rows, None] == document[None, :]
    chosen = (rank_row[None, :] < limit_row[first_row : first_row + block_rows, None]) & (
        rows_pos[:, None] != positions[None, :]
    )
    opener = positions[None, :] == doc_start[first_row : first_row + block_rows, None]
    return same_text & (chosen | opener)


def cross_visible(lengths, src_lengths, length, src_length, first_row, block_rows):
    document, _ = layout(lengths, length)
    source_doc, _ = layout(src_lengths, src_length)
    return document[first_row : first_row + block_rows, None] == source_doc[None, :]


def attend_forward(queries, keys_all, values_all, visible_of, head_count):
    query_count = queries.shape[0]
    head_size = queries.shape[1] // head_count
    factor = head_size ** (-0.5)
    queries = queries.reshape(query_count, head_count, head_size)
    keys_all = keys_all.reshape(keys_all.shape[0], head_count, head_size)
    values_all = values_all.reshape(values_all.shape[0], head_count, head_size)
    block_rows = min(score_tile, query_count)
    outputs = []
    totals = []
    for first_row in range(0, query_count, block_rows):
        query_part = queries[first_row : first_row + block_rows]
        scores = (
            jnp.einsum("qhd,khd->hqk", query_part, keys_all, preferred_element_type=jnp.float32)
            * factor
        )
        scores = jnp.where(visible_of(first_row, block_rows)[None], scores, -1e30)
        highest = jnp.max(scores, axis=-1, keepdims=True)
        exponent = jnp.exp(scores - highest)
        denominator = jnp.sum(exponent, axis=-1, keepdims=True)
        weights_low = (exponent / denominator).astype(jnp.bfloat16)
        outputs.append(
            jnp.einsum("hqk,khd->qhd", weights_low, values_all, preferred_element_type=jnp.float32)
        )
        totals.append(highest[..., 0] + jnp.log(denominator[..., 0]))
    context = jnp.concatenate(outputs, axis=0).reshape(query_count, head_count * head_size)
    return (context, jnp.concatenate(totals, axis=1))


def attend_backward(queries, keys_all, values_all, visible_of, totals, grad_context, head_count):
    query_count = queries.shape[0]
    key_count = keys_all.shape[0]
    head_size = queries.shape[1] // head_count
    factor = head_size ** (-0.5)
    queries = queries.reshape(query_count, head_count, head_size)
    keys_all = keys_all.reshape(key_count, head_count, head_size)
    values_all = values_all.reshape(key_count, head_count, head_size)
    grad_context = grad_context.reshape(query_count, head_count, head_size)
    grad_keys = jnp.zeros((key_count, head_count, head_size), jnp.float32)
    grad_values = jnp.zeros((key_count, head_count, head_size), jnp.float32)
    grad_queries = []
    block_rows = min(score_tile, query_count)
    for first_row in range(0, query_count, block_rows):
        query_part = queries[first_row : first_row + block_rows]
        grad_part = grad_context[first_row : first_row + block_rows]
        scores = (
            jnp.einsum("qhd,khd->hqk", query_part, keys_all, preferred_element_type=jnp.float32)
            * factor
        )
        scores = jnp.where(visible_of(first_row, block_rows)[None], scores, -1e30)
        weights_full = jnp.exp(scores - totals[:, first_row : first_row + block_rows, None])
        grad_weights = jnp.einsum(
            "qhd,khd->hqk", grad_part, values_all, preferred_element_type=jnp.float32
        )
        inner = jnp.sum(grad_weights * weights_full, axis=-1, keepdims=True)
        grad_scores = (weights_full * (grad_weights - inner)).astype(jnp.bfloat16)
        grad_queries.append(
            jnp.einsum("hqk,khd->qhd", grad_scores, keys_all, preferred_element_type=jnp.float32)
            * factor
        )
        grad_keys = (
            grad_keys
            + jnp.einsum(
                "hqk,qhd->khd", grad_scores, query_part, preferred_element_type=jnp.float32
            )
            * factor
        )
        grad_values = grad_values + jnp.einsum(
            "hqk,qhd->khd",
            weights_full.astype(jnp.bfloat16),
            grad_part,
            preferred_element_type=jnp.float32,
        )
    grad_queries = jnp.concatenate(grad_queries, axis=0).reshape(
        query_count, head_count * head_size
    )
    return (
        grad_queries.astype(jnp.bfloat16),
        grad_keys.reshape(key_count, -1).astype(jnp.bfloat16),
        grad_values.reshape(key_count, -1).astype(jnp.bfloat16),
    )


def collect(piece):
    return lax.all_gather(piece, "tp", axis=1, tiled=True)


def spread_sum(partial_sum):
    return lax.psum_scatter(partial_sum, "tp", scatter_dimension=1, tiled=True)


def collect_grad(piece):
    return lax.all_gather(piece, "tp", axis=1, tiled=True)


def send_back(partial_sum):
    return lax.psum_scatter(partial_sum, "tp", scatter_dimension=1, tiled=True)


def local_split(
    query_stream,
    token_embed,
    encoder_out,
    out_grad,
    attn_q,
    attn_k,
    attn_v,
    attn_o,
    cross_q,
    cross_k,
    cross_v,
    cross_o,
    ffn_in,
    ffn_bias_in,
    ffn_out,
    ffn_bias_out,
    norm_gain,
    norm_bias,
    doc_lengths,
    src_lengths,
    ctx_rank,
    ctx_limit,
):
    head_count = HEADS // lax.axis_size("tp")
    (
        self_query,
        self_key,
        self_value,
        self_out,
        other_query,
        other_key,
        other_value,
        other_out,
        hidden_in,
        hidden_bias,
        hidden_out,
    ) = (
        lax.all_gather(attn_q, "dp", axis=0, tiled=True),
        lax.all_gather(attn_k, "dp", axis=0, tiled=True),
        lax.all_gather(attn_v, "dp", axis=0, tiled=True),
        lax.all_gather(attn_o, "dp", axis=1, tiled=True),
        lax.all_gather(cross_q, "dp", axis=0, tiled=True),
        lax.all_gather(cross_k, "dp", axis=0, tiled=True),
        lax.all_gather(cross_v, "dp", axis=0, tiled=True),
        lax.all_gather(cross_o, "dp", axis=1, tiled=True),
        lax.all_gather(ffn_in, "dp", axis=0, tiled=True),
        lax.all_gather(ffn_bias_in, "dp", axis=0, tiled=True),
        lax.all_gather(ffn_out, "dp", axis=1, tiled=True),
    )

    def self_forward(row_items):
        queries, keys_all, values_all, lengths, rank_row, limit_row = row_items

        def visible_of(first_row, block_rows):
            return self_visible(
                lengths, rank_row, limit_row, keys_all.shape[0], first_row, block_rows
            )

        return attend_forward(queries, keys_all, values_all, visible_of, head_count)

    def self_backward(row_items):
        queries, keys_all, values_all, lengths, rank_row, limit_row, totals, grad_context = (
            row_items
        )

        def visible_of(first_row, block_rows):
            return self_visible(
                lengths, rank_row, limit_row, keys_all.shape[0], first_row, block_rows
            )

        return attend_backward(
            queries, keys_all, values_all, visible_of, totals, grad_context, head_count
        )

    def cross_forward(row_items):
        queries, keys_all, values_all, lengths, source_lengths = row_items

        def visible_of(first_row, block_rows):
            return cross_visible(
                lengths, source_lengths, queries.shape[0], keys_all.shape[0], first_row, block_rows
            )

        return attend_forward(queries, keys_all, values_all, visible_of, head_count)

    def cross_backward(row_items):
        queries, keys_all, values_all, lengths, source_lengths, totals, grad_context = row_items

        def visible_of(first_row, block_rows):
            return cross_visible(
                lengths, source_lengths, queries.shape[0], keys_all.shape[0], first_row, block_rows
            )

        return attend_backward(
            queries, keys_all, values_all, visible_of, totals, grad_context, head_count
        )

    query_all = collect(query_stream)
    embed_all = collect(token_embed)
    source_all = collect(encoder_out)
    self_queries = project(query_all, self_query).astype(jnp.bfloat16)
    self_keys = project(embed_all, self_key).astype(jnp.bfloat16)
    self_values = project(embed_all, self_value).astype(jnp.bfloat16)
    self_context, self_totals = lax.map(
        self_forward, (self_queries, self_keys, self_values, doc_lengths, ctx_rank, ctx_limit)
    )
    self_low = self_context.astype(jnp.bfloat16)
    first_sum = query_stream.astype(jnp.float32) + spread_sum(project(self_low, self_out))
    hidden_one, first_back = jax.vjp(layer_norm, first_sum, norm_gain[0], norm_bias[0])
    hidden_one_all = collect(hidden_one.astype(jnp.bfloat16))
    cross_queries = project(hidden_one_all, other_query).astype(jnp.bfloat16)
    cross_keys = project(source_all, other_key).astype(jnp.bfloat16)
    cross_values = project(source_all, other_value).astype(jnp.bfloat16)
    cross_context, cross_totals = lax.map(
        cross_forward, (cross_queries, cross_keys, cross_values, doc_lengths, src_lengths)
    )
    cross_low = cross_context.astype(jnp.bfloat16)
    second_sum = hidden_one + spread_sum(project(cross_low, other_out))
    hidden_two, second_back = jax.vjp(layer_norm, second_sum, norm_gain[1], norm_bias[1])
    hidden_two_low = hidden_two.astype(jnp.bfloat16)
    ffn_inputs = lax.all_gather(hidden_two_low, "tp", axis=1, tiled=True)
    ffn_pre = project(ffn_inputs, hidden_in) + hidden_bias.astype(jnp.float32)
    ffn_gate, gelu_back = jax.vjp(gelu_exact, ffn_pre)
    ffn_act = ffn_gate.astype(jnp.bfloat16)
    ffn_branch = (
        lax.psum_scatter(project(ffn_act, hidden_out), "tp", scatter_dimension=1, tiled=True)
        + ffn_bias_out
    )
    third_sum = hidden_two + ffn_branch
    mixed_full, third_back = jax.vjp(layer_norm, third_sum, norm_gain[2], norm_bias[2])
    grad_third, gain_two, shift_two = third_back(out_grad.astype(jnp.float32))
    grad_ffn = grad_third.astype(jnp.bfloat16)
    grad_bias_out = jnp.sum(grad_ffn.astype(jnp.float32), axis=(0, 1))
    grad_ffn_all = lax.all_gather(grad_ffn, "tp", axis=1, tiled=True)
    grad_act = project_back(grad_ffn_all, hidden_out)
    grad_down = outer_sum(ffn_act, grad_ffn_all)
    grad_pre = gelu_back(grad_act)[0].astype(jnp.bfloat16)
    grad_up = outer_sum(ffn_inputs, grad_pre)
    grad_bias_in = jnp.sum(grad_pre.astype(jnp.float32), axis=(0, 1))
    grad_two = grad_third + lax.psum_scatter(
        project_back(grad_pre, hidden_in), "tp", scatter_dimension=1, tiled=True
    )
    grad_second, gain_one, shift_one = second_back(grad_two)
    grad_cross_all = collect_grad(grad_second.astype(jnp.bfloat16))
    grad_other_out = outer_sum(cross_low, grad_cross_all)
    grad_cross_ctx = project_back(grad_cross_all, other_out).astype(jnp.bfloat16)
    cross_dq, cross_dk, cross_dv = lax.map(
        cross_backward,
        (
            cross_queries,
            cross_keys,
            cross_values,
            doc_lengths,
            src_lengths,
            cross_totals,
            grad_cross_ctx,
        ),
    )
    grad_other_query = outer_sum(hidden_one_all, cross_dq)
    grad_other_key = outer_sum(source_all, cross_dk)
    grad_other_value = outer_sum(source_all, cross_dv)
    grad_encoder = send_back(
        project_back(cross_dk, other_key) + project_back(cross_dv, other_value)
    )
    grad_one = grad_second + send_back(project_back(cross_dq, other_query))
    grad_first, gain_zero, shift_zero = first_back(grad_one)
    grad_attn_all = collect_grad(grad_first.astype(jnp.bfloat16))
    grad_self_out = outer_sum(self_low, grad_attn_all)
    grad_self_ctx = project_back(grad_attn_all, self_out).astype(jnp.bfloat16)
    self_dq, self_dk, self_dv = lax.map(
        self_backward,
        (
            self_queries,
            self_keys,
            self_values,
            doc_lengths,
            ctx_rank,
            ctx_limit,
            self_totals,
            grad_self_ctx,
        ),
    )
    grad_self_query = outer_sum(query_all, self_dq)
    grad_self_key = outer_sum(embed_all, self_dk)
    grad_self_value = outer_sum(embed_all, self_dv)
    grad_embed = send_back(project_back(self_dk, self_key) + project_back(self_dv, self_value))
    grad_query = grad_first + send_back(project_back(self_dq, self_query))
    (
        grad_self_query,
        grad_self_key,
        grad_self_value,
        grad_self_out,
        grad_other_query,
        grad_other_key,
        grad_other_value,
        grad_other_out,
        grad_up,
        grad_bias_in,
        grad_down,
    ) = (
        lax.psum_scatter(
            grad_self_query.astype(jnp.bfloat16), "dp", scatter_dimension=0, tiled=True
        ).astype(jnp.float32),
        lax.psum_scatter(
            grad_self_key.astype(jnp.bfloat16), "dp", scatter_dimension=0, tiled=True
        ).astype(jnp.float32),
        lax.psum_scatter(
            grad_self_value.astype(jnp.bfloat16), "dp", scatter_dimension=0, tiled=True
        ).astype(jnp.float32),
        lax.psum_scatter(
            grad_self_out.astype(jnp.bfloat16), "dp", scatter_dimension=1, tiled=True
        ).astype(jnp.float32),
        lax.psum_scatter(
            grad_other_query.astype(jnp.bfloat16), "dp", scatter_dimension=0, tiled=True
        ).astype(jnp.float32),
        lax.psum_scatter(
            grad_other_key.astype(jnp.bfloat16), "dp", scatter_dimension=0, tiled=True
        ).astype(jnp.float32),
        lax.psum_scatter(
            grad_other_value.astype(jnp.bfloat16), "dp", scatter_dimension=0, tiled=True
        ).astype(jnp.float32),
        lax.psum_scatter(
            grad_other_out.astype(jnp.bfloat16), "dp", scatter_dimension=1, tiled=True
        ).astype(jnp.float32),
        lax.psum_scatter(
            grad_up.astype(jnp.bfloat16), "dp", scatter_dimension=0, tiled=True
        ).astype(jnp.float32),
        lax.psum_scatter(
            grad_bias_in.astype(jnp.bfloat16), "dp", scatter_dimension=0, tiled=True
        ).astype(jnp.float32),
        lax.psum_scatter(
            grad_down.astype(jnp.bfloat16), "dp", scatter_dimension=1, tiled=True
        ).astype(jnp.float32),
    )
    gain_grads = jnp.stack([gain_zero, gain_one, gain_two])
    shift_grads = jnp.stack([shift_zero, shift_one, shift_two])
    gain_grads, shift_grads, grad_bias_out = lax.psum(
        (gain_grads, shift_grads, grad_bias_out), ("dp", "tp")
    )
    return (
        mixed_full.astype(jnp.bfloat16),
        grad_query,
        grad_embed,
        grad_encoder,
        grad_self_query,
        grad_self_key,
        grad_self_value,
        grad_self_out,
        grad_other_query,
        grad_other_key,
        grad_other_value,
        grad_other_out,
        grad_up,
        grad_bias_in,
        grad_down,
        grad_bias_out,
        gain_grads,
        shift_grads,
    )


HIDDEN = -1e30
Q_TILE = 256


def product(left, right, left_axis, right_axis):
    return lax.dot_general(
        left, right, (((left_axis,), (right_axis,)), ((), ())), preferred_element_type=WIDE
    )


def nn(left, right):
    return product(left, right, 1, 0)


def nt(left, right):
    return product(left, right, 1, 1)


def tn(left, right):
    return product(left, right, 0, 0)


def rows_of(index, size):
    return pl.ds(pl.multiple_of(index * size, size), size)


def normalize(values):
    average = jnp.mean(values, axis=-1, keepdims=True)
    centred = values - average
    spread = jnp.mean(centred * centred, axis=-1, keepdims=True)
    inverse = lax.rsqrt(spread + EPSILON)
    return centred * inverse, inverse


def normalize_back(grad, normal, inverse, gain):
    scaled = grad * gain
    mean_one = jnp.mean(scaled, axis=-1, keepdims=True)
    mean_two = jnp.mean(scaled * normal, axis=-1, keepdims=True)
    return inverse * (scaled - mean_one - normal * mean_two)


def add_rows(target, grad):
    target[...] += jnp.sum(grad, axis=0, keepdims=True)


def documents(lengths, row, shape, axis):
    positions = lax.broadcasted_iota(jnp.int32, shape, axis)
    document = jnp.full(shape, -1, jnp.int32)
    start = jnp.zeros(shape, jnp.int32)
    offset = jnp.int32(0)
    for slot in range(lengths.shape[1]):
        passed = positions >= offset
        document = document + passed.astype(jnp.int32)
        start = jnp.where(passed, offset, start)
        offset = offset + lengths[row, slot]
    return positions, document, start


def fill_self_bias(bias, lengths, rank, limit, row):
    length = bias.shape[0]
    key_position, key_document, _ = documents(lengths, row, (length, 1), 0)
    position, document, start = documents(lengths, row, (1, length), 1)
    rank_row = rank[pl.ds(row, 1), :].astype(WIDE)
    key_rank = jnp.transpose(jnp.broadcast_to(rank_row, (128, length)))[:, :1]
    query_limit = limit[pl.ds(row, 1), :].astype(WIDE)
    for tile in range(length // Q_TILE):
        part = slice(tile * Q_TILE, (tile + 1) * Q_TILE)
        chosen = (key_rank < query_limit[:, part]) & (key_position != position[:, part])
        seen = (key_document == document[:, part]) & (chosen | (key_position == start[:, part]))
        bias[:, part] = jnp.where(seen, 0.0, HIDDEN).astype(bias.dtype)


def fill_cross_bias(bias, lengths, source_lengths, row):
    length = bias.shape[0]
    _, key_document, _ = documents(source_lengths, row, (length, 1), 0)
    _, document, _ = documents(lengths, row, (1, length), 1)
    for tile in range(length // Q_TILE):
        part = slice(tile * Q_TILE, (tile + 1) * Q_TILE)
        seen = key_document == document[:, part]
        bias[:, part] = jnp.where(seen, 0.0, HIDDEN).astype(bias.dtype)


def one_head(pair, side):
    lane = lax.broadcasted_iota(jnp.int32, pair.shape, 1)
    return jnp.where(lane // 64 == side, pair, jnp.zeros_like(pair))


def run_after(step, after):
    for number, actions in after.items():
        if actions:

            @pl.when(step == number)
            def _():
                for action in actions:
                    action()


PAIRS = HEADS // 2


class Kept:
    def __init__(self, kept, room, sems, place_of=lambda step: step):
        self.kept, self.room, self.sems, self.place_of = kept, room, sems, place_of

    def slot(self, step, side=None):
        place = lax.rem(step, 4)
        if side is None:
            return rows_of(place, 2 * Q_TILE)
        return rows_of(2 * place + side, Q_TILE)

    def store(self, step):
        room = self.room.at[:, self.slot(step)]
        return pltpu.make_async_copy(room, self.kept.at[self.place_of(step)], self.sems.at[lax.rem(step, 4)])

    def load(self, step):
        room = self.room.at[:, self.slot(step)]
        return pltpu.make_async_copy(self.kept.at[self.place_of(step)], room, self.sems.at[lax.rem(step, 4)])


def attend(keys, queries, values_t, bias, context, inverses, tile_of, room, kept, after):
    scores_of, highest_of = room
    steps = keys.shape[0] // Q_TILE * PAIRS

    def where(step):
        return rows_of(tile_of(step // PAIRS), Q_TILE), lax.rem(step, PAIRS)

    def score(step, slot):
        part, pair = where(step)
        lanes = rows_of(pair, 128)
        for side in (0, 1):
            scores = nt(keys[:, lanes], one_head(queries[part, lanes], side))
            scores = scores + bias[:, part].astype(WIDE)
            scores_of[slot][:, side * Q_TILE : (side + 1) * Q_TILE] = scores
            highest_of[2 * slot + side] = jnp.max(scores, axis=0, keepdims=True)

    def weigh(step, slot):
        part, pair = where(step)
        outs = []
        for side in (0, 1):
            head = 2 * pair + side
            scores = scores_of[slot][:, side * Q_TILE : (side + 1) * Q_TILE]
            weights = jnp.exp(scores - highest_of[2 * slot + side]).astype(LOW)
            kept.room[:, kept.slot(step, side)] = weights
            out = nn(values_t[head], weights)
            inverse = 1.0 / out[64:65]
            outs.append(out[:64] * inverse)
            inverses[pl.ds(head, 1), part] = inverse
        context[part, rows_of(pair, 128)] = jnp.transpose(jnp.concatenate(outs, axis=0)).astype(LOW)

    score(0, 0)

    @pl.loop(0, steps // 2)
    def _(double):
        @pl.when(double > 1)
        def _():
            kept.store(2 * double - 4).wait()
            kept.store(2 * double - 3).wait()

        score(2 * double + 1, 1)
        weigh(2 * double, 0)
        score(lax.rem(2 * double + 2, steps), 0)
        weigh(2 * double + 1, 1)
        kept.store(2 * double).start()
        kept.store(2 * double + 1).start()
        run_after(double, after)

    for step in range(steps - 4, steps):
        kept.store(step).wait()


def attend_back(keys_t, queries, values, cotangent, inner, grads, tile_of, room, kept, after):
    key_sum, value_sum, grad_queries = grads
    steps = values.shape[0] // Q_TILE * PAIRS

    def where(step):
        return rows_of(tile_of(step // PAIRS), Q_TILE), rows_of(lax.rem(step, PAIRS), 128)

    def make(step, slot):
        part, lanes = where(step)
        pair = lax.rem(step, PAIRS)
        for side in (0, 1):
            head = 2 * pair + side
            grad_weights = nt(values[:, lanes], one_head(cotangent[part, lanes], side))
            weights = kept.room[:, kept.slot(step, side)].astype(WIDE)
            grad_scores = weights * (grad_weights - inner[pl.ds(head, 1), part])
            room[slot][:, side * Q_TILE : (side + 1) * Q_TILE] = grad_scores.astype(LOW)

    def use(step, slot):
        part, lanes = where(step)
        pair = lax.rem(step, PAIRS)

        def stacked(ref):
            return jnp.concatenate([one_head(ref[part, lanes], side) for side in (0, 1)], axis=0)

        outs = [
            nn(keys_t[2 * pair + side, :64], room[slot][:, side * Q_TILE : (side + 1) * Q_TILE])
            for side in (0, 1)
        ]
        turned = jnp.transpose(jnp.concatenate(outs, axis=0) * 0.125)
        grad_queries[part, lanes] = turned.astype(LOW)
        value_sum[:, lanes] += nn(kept.room[:, kept.slot(step)], stacked(cotangent))
        key_sum[:, lanes] += nn(room[slot][...], stacked(queries))

    key_sum[...] = jnp.zeros_like(key_sum)
    value_sum[...] = jnp.zeros_like(value_sum)
    kept.load(0).wait()
    make(0, 0)

    @pl.loop(0, steps // 2)
    def _(double):
        kept.load(2 * double + 1).wait()
        make(2 * double + 1, 1)
        use(2 * double, 0)

        @pl.when(double < steps // 2 - 1)
        def _():
            kept.load(2 * double + 2).wait()

        make(lax.rem(2 * double + 2, steps), 0)
        use(2 * double + 1, 1)

        @pl.when(double < steps // 2 - 2)
        def _():
            kept.load(2 * double + 4).start()
            kept.load(2 * double + 5).start()

        run_after(double, after)


def inner_products(cotangent, context, inner):
    products = cotangent[...].astype(WIDE) * context[...].astype(WIDE)
    high = products.astype(LOW)
    rest = (products - high.astype(WIDE)).astype(LOW)
    shape = (2 * HEADS, products.shape[1])
    head = lax.broadcasted_iota(jnp.int32, shape, 0)
    lane = lax.broadcasted_iota(jnp.int32, shape, 1)
    pick = jnp.where(lane // 64 == head, 1.0, 0.0).astype(LOW)
    inner[...] = (nt(pick, high) + nt(pick, rest))[:HEADS]


def flip_heads(values, flipped):
    turned = jnp.transpose(values[...])
    for head in range(HEADS):
        flipped[head, :64] = turned[64 * head : 64 * head + 64]

MESH = pl.DeviceIdType.MESH


class Place:
    def __init__(self):
        dp, tp = lax.axis_index("dp"), lax.axis_index("tp")
        self.dp, self.tp = dp, tp
        self.z, self.x = dp // 2, lax.rem(dp, 2)
        self.y, self.core = tp // 2, lax.rem(tp, 2)
        self.core_peer = (dp, 2 * self.y + 1 - self.core)
        self.y_peer = (dp, 2 * (1 - self.y) + self.core)
        self.far_peer = (dp, 2 * (1 - self.y) + 1 - self.core)
        self.x_peer = (2 * self.z + 1 - self.x, tp)
        self.z_steps = [lax.rem(self.z + step, 4) for step in range(4)]
        self.z_peers = [(2 * z + self.x, tp) for z in self.z_steps[1:]]
        self.summing = [self.core_peer, self.x_peer, self.y_peer] + self.z_peers

    def greet(self):
        for peer in self.summing + [self.far_peer]:
            barrier = pltpu.get_barrier_semaphore()
            pl.semaphore_signal(barrier, inc=1, device_id=peer, device_id_type=MESH)

    def meet(self):
        pl.semaphore_wait(pltpu.get_barrier_semaphore(), len(self.summing) + 1)

    def tile(self, number):
        side = lax.rem(self.y + 1 - number // 2, 2)
        return 2 * side + lax.rem(self.core + (number + 1) // 2, 2)

    def columns(self, width):
        return [
            pl.ds(pl.multiple_of(tp * width, width), width)
            for tp in (self.tp, self.y_peer[1], self.core_peer[1], self.far_peer[1])
        ]


class Exchange:
    def __init__(self, sends, recvs, number):
        self.sends, self.recvs, self.number = sends, recvs, number
        self.made = []
        self.arriving = []

    def send(self, source, target, peer):
        slot = len(self.made)

        def copy():
            return pltpu.make_async_remote_copy(
                src_ref=source(),
                dst_ref=target(),
                send_sem=self.sends.at[self.number, slot],
                recv_sem=self.recvs.at[self.number, slot],
                device_id=peer,
                device_id_type=MESH,
            )

        copy().start()
        self.made.append(copy)
        self.arriving.append(copy)

    def move(self, block, peer):
        self.send(block, block, peer)

    def arrive(self):
        for copy in self.arriving:
            copy().wait_recv()
        self.arriving = []

    def finish(self):
        for copy in self.made:
            copy().wait_send()


class Gather(Exchange):
    slots = 11

    def __init__(
        self, place, local, full, first, count, side, sides, sends, recvs, own_sems, number
    ):
        super().__init__(sends, recvs, number)
        self.place, self.full, self.items = place, full, pl.ds(first, count)
        width = local.shape[-1] // sides
        self.sides = [
            pl.ds(pl.multiple_of((tp * sides + side) * width, width), width)
            for tp in (place.tp, place.y_peer[1])
        ]
        p = place
        self.source = lambda: local.at[self.items, :, side * width : (side + 1) * width]
        self.target = lambda: full.at[self.items, p.z, p.x, :, self.sides[0]]
        self.own = lambda: pltpu.make_async_copy(
            self.source(), self.target(), own_sems.at[number]
        )

    def stage(self, number):
        p, full, items = self.place, self.full, self.items
        self.arrive()
        if number == 0:
            self.own().start()
            self.send(self.source, self.target, p.y_peer)
        elif number == 1:
            self.own().wait()
            for side in self.sides:
                for peer in p.z_peers:
                    self.move(lambda side=side: full.at[items, p.z, p.x, :, side], peer)
        elif number == 2:
            for side in self.sides:
                self.move(lambda side=side: full.at[items, :, p.x, :, side], p.x_peer)
        elif number == 3:
            for side in self.sides:
                self.move(lambda side=side: full.at[items, :, :, :, side], p.core_peer)


class ToRow(Exchange):
    slots = 3

    def __init__(self, place, local, row, sends, recvs, own_sems, number):
        super().__init__(sends, recvs, number)
        size = local.shape[1]
        p = place
        span = pl.ds(pl.multiple_of(p.tp * size, size), size)

        def here():
            return row.at[span]

        self.local, self.here = local, here
        self.peers = (p.y_peer, p.far_peer, p.core_peer)
        self.own = lambda: pltpu.make_async_copy(local.at[p.tp], here(), own_sems.at[number])

    def start(self):
        for peer in self.peers:
            self.send(lambda peer=peer: self.local.at[peer[1]], self.here, peer)
        self.own().start()

    def near(self):
        self.own().wait()
        self.arriving.pop()().wait_recv()

    def far(self):
        self.arrive()


class FromRow(Exchange):
    slots = 3

    def __init__(self, place, row, blocks, sends, recvs, own_sems, number):
        super().__init__(sends, recvs, number)
        size = blocks.shape[1]
        p = place
        self.peers = (p.y_peer, p.far_peer, p.core_peer)
        self.target = lambda: blocks.at[p.tp]

        def part(tp):
            return row.at[pl.ds(pl.multiple_of(tp * size, size), size)]

        self.part = part
        self.own = lambda: pltpu.make_async_copy(
            self.part(p.tp), self.target(), own_sems.at[number]
        )

    def give(self, number):
        if number == 3:
            self.own().start()
        else:
            peer = self.peers[number]
            self.send(lambda: self.part(peer[1]), self.target, peer)

    def give_all(self):
        for number in range(4):
            self.give(number)

    def wait(self):
        self.own().wait()
        self.arrive()


class Scatter(Exchange):
    slots = 8

    def __init__(
        self, place, parts, work, last, out, first, count, ready, sends, recvs, number
    ):
        super().__init__(sends, recvs, number)
        self.place, self.parts, self.work, self.last, self.out = place, parts, work, last, out
        self.numbers = range(first, first + count)
        self.items = pl.ds(first, count)
        self.width = out.shape[-1]
        self.columns = place.columns(self.width)
        self.ready = ready

    def expect(self, index):
        if self.ready is not None:
            pl.semaphore_wait(self.ready.at[self.number, index], 1)

    def stage(self, number):
        p, parts, work, items, width = self.place, self.parts, self.work, self.items, self.width
        first_half, second_half = slice(0, 2 * width), slice(2 * width, 4 * width)
        sides = [slice(side * width, (side + 1) * width) for side in range(4)]
        self.arrive()
        if number == 0:
            self.expect(0)
            for side, column in zip(sides, self.columns[2:]):
                self.send(
                    lambda column=column: parts.at[items, :, :, :, column],
                    lambda side=side: work.at[items, :, :, :, side],
                    p.core_peer,
                )
        elif number == 1:
            for item in self.numbers:
                for side, column in zip(sides, self.columns[:2]):

                    @pl.loop(0, 4)
                    def _(z):
                        work[item, z, :, :, side] += parts[item, z, :, :, column]

            self.expect(1)
            self.send(
                lambda: work.at[items, :, 1 - p.x, :, first_half],
                lambda: work.at[items, :, 0, :, second_half],
                p.x_peer,
            )
        elif number == 2:
            for item in self.numbers:

                @pl.loop(0, 4)
                def _(z):
                    work[item, z, 0, :, second_half] += work[item, z, p.x, :, first_half]

            for step, peer in enumerate(p.z_peers):
                self.expect(3 + step)
                self.send(
                    lambda step=step: work.at[items, p.z_steps[step + 1], 0, :, second_half],
                    lambda step=step: work.at[items, step, 1, :, second_half],
                    peer,
                )
        elif number == 3:
            for item in self.numbers:
                total = work[item, p.z, 0, :, second_half].astype(WIDE)
                for step in range(3):
                    total = total + work[item, step, 1, :, second_half].astype(WIDE)
                work[item, 3, 1, :, second_half] = total.astype(LOW)
            self.expect(2)
            self.send(
                lambda: work.at[items, 3, 1, :, sides[3]],
                lambda: self.last.at[items],
                p.y_peer,
            )
        else:
            for item in self.numbers:
                mine = work[item, 3, 1, :, sides[2]].astype(WIDE)
                self.out[item] = mine + self.last[item].astype(WIDE)


class SumAll(Exchange):
    slots = 5

    def __init__(self, place, values, arrived, sends, recvs):
        super().__init__(sends, recvs, 0)
        p = place
        z_one = p.z + 1 - 2 * lax.rem(p.z, 2)
        peers = (p.core_peer, p.x_peer, p.y_peer, (2 * z_one + p.x, p.tp), p.z_peers[1])
        self.peers, self.values, self.arrived = peers, values, arrived

    def stage(self, number):
        if number:
            self.arrive()
            self.made[-1]().wait_send()
            self.values[...] = self.values[...] + self.arrived[number - 1]
        if number < 5:
            self.send(
                lambda: self.values, lambda: self.arrived.at[number], self.peers[number]
            )


def run_schedule(to, do):
    def step(task, number):
        return lambda: task.stage(number)

    do.fill_self_bias()
    to.place.meet()
    first = [to.keys_values, to.query, to.out, to.bias]
    rest = to.cross + to.ffn
    for task in first + rest:
        task.stage(0)
    for task in (to.embed_row, to.query_row, to.source_row, to.cotangent_row):
        task.start()
    for task in first + rest:
        task.stage(1)
    to.keys_values.stage(2)
    to.query.stage(2)
    to.keys_values.stage(3)
    to.embed_row.near()
    to.query_row.near()
    to.keys_values.stage(4)
    do.near_keys_values()
    to.out.stage(2)
    to.bias.stage(2)
    to.query.stage(3)
    to.query.stage(4)
    do.near_queries()
    to.embed_row.far()
    do.far_keys_values()

    def far_queries():
        to.query_row.far()
        do.far_queries()

    do.attend_self(
        {
            0: [step(to.cross[0], 2), step(to.out, 3)],
            1: [step(to.out, 4), step(to.bias, 3)],
            2: [far_queries, step(to.cross[0], 3), step(to.cross[1], 2)],
            3: [step(to.cross[0], 4), step(to.bias, 4)],
            5: [step(to.ffn[0], 2)],
            7: [step(to.cross[1], 3)],
        }
    )
    do.first_norm()
    to.ffn[1].stage(2)
    to.cross[1].stage(4)
    do.fill_cross_bias()
    do.cross_queries()
    to.source_row.near()
    to.source_row.far()
    do.cross_keys_values()
    do.attend_cross(
        {
            0: [step(to.ffn[0], 3)],
            1: [step(to.ffn[2], 2), step(to.ffn[0], 4)],
            4: [step(to.ffn[1], 3)],
            5: [step(to.ffn[3], 2), step(to.ffn[1], 4)],
        }
    )
    do.bias_in()
    do.feed_forward_in(
        {
            0: [step(to.ffn[2], 3)],
            1: [step(to.ffn[2], 4)],
            2: [step(to.ffn[3], 3)],
        }
    )
    to.cotangent_row.near()
    to.cotangent_row.far()
    to.ffn[3].stage(4)
    do.feed_forward()

    for task in to.ffn:
        task.finish()
    for group in (0, 1):
        for index, peer in enumerate(to.place.summing):
            there = index if index < 3 else 8 - index
            pl.semaphore_signal(
                to.ready.at[group, there], inc=1, device_id=peer, device_id_type=MESH
            )
    to.mixed.give_all()
    do.down_grad()
    to.down_sum.stage(0)
    do.up_grad()
    to.up_sum.stage(0)
    do.cross_out_back()
    to.down_sum.stage(1)
    to.up_sum.stage(1)
    do.cross_back({4: [step(to.down_sum, 2)]})
    do.cross_grads()
    to.cross_sum.stage(0)
    do.source_grad()
    to.source_grad.give_all()
    to.up_sum.stage(2)
    to.cross_sum.stage(1)
    do.first_norm_back()
    to.small_sum.stage(0)
    to.down_sum.stage(3)
    do.self_out_back()
    to.out_sum.stage(0)
    to.small_sum.stage(1)

    def give_query(number):
        def action():
            do.query_grad(number)
            to.query_grad.give(number)

        return action

    do.self_back(
        {
            0: [step(to.out_sum, 1)],
            1: [give_query(0)],
            3: [give_query(1), step(to.cross_sum, 2), step(to.small_sum, 2)],
            4: [step(to.up_sum, 3)],
            5: [give_query(2), step(to.out_sum, 2)],
            7: [give_query(3), step(to.small_sum, 3)],
        }
    )
    to.mixed.wait()
    to.mixed.finish()
    do.key_grad()
    to.key_sum.stage(0)
    do.value_grad()
    to.value_sum.stage(0)
    to.key_sum.stage(1)
    do.query_weight_grad()
    to.query_sum.stage(0)
    to.value_sum.stage(1)
    do.far_embed_grad()
    to.embed_grad.give(0)
    to.embed_grad.give(1)
    to.query_sum.stage(1)
    do.near_embed_grad()
    to.embed_grad.give(2)
    to.embed_grad.give(3)
    to.key_sum.stage(2)
    to.small_sum.stage(4)
    to.value_sum.stage(2)
    to.cross_sum.stage(3)
    to.out_sum.stage(3)
    to.query_sum.stage(2)
    to.down_sum.stage(4)
    to.up_sum.stage(4)
    to.key_sum.stage(3)
    to.value_sum.stage(3)
    to.small_sum.stage(5)
    to.query_sum.stage(3)
    for task in (to.cross_sum, to.out_sum, to.key_sum, to.value_sum, to.query_sum):
        task.stage(4)
    outgoing = [to.source_grad, to.query_grad, to.embed_grad]
    for task in outgoing:
        task.wait()
    for task in outgoing + [to.embed_row, to.query_row, to.source_row, to.cotangent_row]:
        task.finish()
    for task in first + to.cross:
        task.finish()
    for task in (to.down_sum, to.up_sum, to.cross_sum, to.out_sum):
        task.finish()
    for task in (to.key_sum, to.value_sum, to.query_sum):
        task.finish()


def layer_kernel(
    query, embed, source, cotangent, attn_q, attn_k, attn_v, attn_o, cross_q, cross_k, cross_v,
    cross_o, ffn_in, ffn_bias_in, ffn_out, bias_out, norm_gain, norm_bias, lengths, source_lengths,
    rank, limit,
    own_squares, own_wides, small, mixed_blocks, query_blocks, embed_blocks, encoder_blocks, kept_self, kept_cross,
    local_squares, local_wides, local_bias, squares, wides, biases, grad_squares, grad_wides,
    work, last_squares, last_wides, arrived,
    query_row, embed_row, source_row, cotangent_row,
    self_q, self_k, self_v, self_context, other_q, other_k, other_v, other_context,
    flipped, totals, other_totals, inner, highest, normal_one, inverse_one,
    hidden_one, hidden_two, act, pre, grad_ffn, grad_second, key_sum, value_sum, bias, bias_in,
    row_sends, row_recvs, row_own, gather_sends, gather_recvs, gather_own,
    scatter_sends, scatter_recvs, sum_sends, sum_recvs, kept_sems, ready,
):
    place = Place()
    place.greet()
    row = place.tp
    length, features = query_row.shape
    hidden = act.shape[1]
    half = length // 2
    near_half, far_half = rows_of(place.y, half), rows_of(1 - place.y, half)

    for index, piece in enumerate((attn_q, attn_k, attn_v, attn_o, cross_q, cross_k, cross_v, cross_o)):
        local_squares[index] = piece[...]
    local_wides[0] = ffn_in[...]
    local_wides[1] = ffn_out[...]
    local_bias[...] = jnp.zeros_like(local_bias)
    local_bias[0, 0:1, 0:64] = ffn_bias_in[...]
    small[...] = jnp.zeros_like(small)
    flipped[:, 64:] = jnp.ones((HEADS, flipped.shape[1] - 64, length), LOW)

    def gather(number, local, full, first, count, side=0, sides=1):
        sems = (gather_sends, gather_recvs, gather_own)
        return Gather(place, local, full, first, count, side, sides, *sems, number)

    def scatter(number, *buffers):
        return Scatter(place, *buffers, scatter_sends, scatter_recvs, number)

    def row_sems(number):
        return row_sends, row_recvs, row_own, number

    def square(index):
        return squares[index].reshape(features, features)

    def wide(index):
        return wides[index].reshape(features, hidden)

    def vector(index):
        first = (index % 4) * features
        return small.at[1 + index // 4 : 2 + index // 4, first : first + features]

    def quarter(ref, index):
        return ref.at[:, index * features : (index + 1) * features]

    square_sums = (grad_squares, work, last_squares, own_squares)
    wide_sums = (grad_wides, wides, last_wides, own_wides)
    to = SimpleNamespace(
        place=place,
        ready=ready,
        keys_values=gather(0, local_squares, squares, 1, 2),
        query=gather(1, local_squares, squares, 0, 1),
        out=gather(2, local_squares, squares, 3, 1),
        cross=[gather(3 + i, local_squares, squares, 4 + 2 * i, 2) for i in (0, 1)],
        ffn=[gather(5 + i, local_wides, wides, i // 2, 1, i % 2, 2) for i in range(4)],
        bias=gather(9, local_bias, biases, 0, 1),
        embed_row=ToRow(place, embed, embed_row, *row_sems(0)),
        query_row=ToRow(place, query, query_row, *row_sems(1)),
        source_row=ToRow(place, source, source_row, *row_sems(2)),
        cotangent_row=ToRow(place, cotangent, cotangent_row, *row_sems(3)),
        down_sum=scatter(0, *wide_sums, 1, 1, ready),
        up_sum=scatter(1, *wide_sums, 0, 1, ready),
        cross_sum=scatter(2, *square_sums, 4, 4, None),
        out_sum=scatter(3, *square_sums, 3, 1, None),
        key_sum=scatter(4, *square_sums, 1, 1, None),
        value_sum=scatter(5, *square_sums, 2, 1, None),
        query_sum=scatter(6, *square_sums, 0, 1, None),
        small_sum=SumAll(place, small, arrived, sum_sends, sum_recvs),
        mixed=FromRow(place, cotangent_row, mixed_blocks, *row_sems(4)),
        source_grad=FromRow(place, source_row, encoder_blocks, *row_sems(5)),
        query_grad=FromRow(place, hidden_two, query_blocks, *row_sems(6)),
        embed_grad=FromRow(place, cotangent_row, embed_blocks, *row_sems(7)),
    )
    score_room = ((key_sum, value_sum), highest)
    cotangent_low, grad_k, grad_v, grad_q = (quarter(act, i) for i in range(4))
    room = tuple(quarter(bias, i) for i in (0, 1))

    def fill_keys_values(rows):
        self_k[rows] = nn(embed_row[rows], square(1)).astype(LOW)
        self_v[rows] = nn(embed_row[rows], square(2)).astype(LOW)

    def fill_queries(rows):
        self_q[rows] = (nn(query_row[rows], square(0)) * 0.125).astype(LOW)

    def turned(step):
        return (length // Q_TILE - 1 - step // PAIRS) * PAIRS + lax.rem(step, PAIRS)

    def attend_self(after):
        flip_heads(self_v, flipped)
        attend(
            self_k, self_q, flipped, bias, self_context, totals,
            lambda number: place.tile(3 - number), score_room, Kept(kept_self, act, kept_sems, turned), after,
        )

    def first_norm():
        @pl.loop(0, length // 256)
        def _(tile):
            part = rows_of(tile, 256)
            branch = nt(self_context[part], square(3))
            normal, inverse = normalize(query_row[part].astype(WIDE) + branch)
            normal_one[part] = normal
            inverse_one[part] = inverse
            hidden_one[part] = (normal * norm_gain[0:1] + norm_bias[0:1]).astype(LOW)

    def fill_cross_queries():
        other_q[...] = (nn(hidden_one[...], square(4)) * 0.125).astype(LOW)

    def fill_cross_keys_values():
        other_k[...] = nn(source_row[...], square(5)).astype(LOW)
        other_v[...] = nn(source_row[...], square(6)).astype(LOW)

    def attend_cross(after):
        flip_heads(other_v, flipped)
        attend(
            other_k, other_q, flipped, bias, other_context, other_totals,
            lambda number: number, score_room, Kept(kept_cross, act, kept_sems), after,
        )

    def fill_bias_in():
        for block in range(4):
            pieces = biases[0, :, :, :, block * 128 : block * 128 + 128].reshape(128, 128)
            size = hidden // 4
            lane = lax.broadcasted_iota(jnp.int32, (128, size), 1)
            line = lax.broadcasted_iota(jnp.int32, (128, size), 0)
            spread = nn(pieces, jnp.where(lane % 64 == line, 1.0, 0.0).astype(LOW))
            spread = jnp.where(lane // 64 == line // 16, spread, 0.0)
            bias_in[:, block * size : block * size + size] = jnp.sum(spread, axis=0, keepdims=True)

    def feed_forward_in(after):
        @pl.loop(0, length // 256)
        def _(tile):
            part = rows_of(tile, 256)
            branch = nt(other_context[part], square(7))
            before = normal_one[part] * norm_gain[0:1] + norm_bias[0:1]
            normal, inverse = normalize(before + branch)
            grad_second[part] = normal
            key_sum[part, 0:1] = inverse
            low = (normal * norm_gain[1:2] + norm_bias[1:2]).astype(LOW)
            hidden_two[part] = low
            before = nn(low, wide(0)) + bias_in[...]
            below = 0.5 * (1.0 + lax.erf(before * 0.7071067811865476))
            density = jnp.exp(-0.5 * before * before) * 0.3989422804014327
            pre[part] = (below + before * density).astype(LOW)
            act[part] = (before * below).astype(LOW)
            run_after(tile, after)

    def feed_forward():
        @pl.loop(0, length // 256)
        def _(tile):
            part = rows_of(tile, 256)
            normal_mid = grad_second[part]
            after = normal_mid * norm_gain[1:2] + norm_bias[1:2]
            after = after + nt(act[part], wide(1)) + bias_out[...]
            normal, inverse = normalize(after)
            grad = cotangent_row[part].astype(WIDE)
            cotangent_row[part] = (normal * norm_gain[2:3] + norm_bias[2:3]).astype(LOW)
            add_rows(vector(2), grad * normal)
            add_rows(vector(5), grad)
            grad = normalize_back(grad, normal, inverse, norm_gain[2:3])
            low = grad.astype(LOW)
            grad_ffn[part] = low
            add_rows(vector(6), low.astype(WIDE))
            grad_pre = (nn(low, wide(1)) * pre[part].astype(WIDE)).astype(LOW)
            pre[part] = grad_pre
            add_rows(small.at[0:1], grad_pre.astype(WIDE))
            grad = grad + nt(grad_pre, wide(0))
            add_rows(vector(1), grad * normal_mid)
            add_rows(vector(4), grad)
            inverse_mid = key_sum[part, 0:1]
            grad_second[part] = normalize_back(grad, normal_mid, inverse_mid, norm_gain[1:2])

    def wide_grad(index, left, right):
        for side in (slice(0, hidden // 2), slice(hidden // 2, hidden)):
            total = tn(left[...], right[:, side]).astype(LOW)
            grad_wides[index, :, :, :, side] = total.reshape(4, 2, features // 8, hidden // 2)

    def square_grad(index, inputs, grad):
        grad_squares[index] = tn(inputs, grad).astype(LOW).reshape(grad_squares.shape[1:])

    def out_back(first, context, inverses, kept):
        for index in range(4):
            Kept(kept, pre, kept_sems).load(index).start()
        grad = grad_second[...].astype(LOW)
        square_grad(first + 3, grad, context[...])
        lane = lax.broadcasted_iota(jnp.int32, (HEADS, features), 1)
        head = lax.broadcasted_iota(jnp.int32, (HEADS, features), 0)
        spread = lax.dot_general(
            inverses[...],
            jnp.where(lane // 64 == head, 1.0, 0.0),
            (((0,), (0,)), ((), ())),
            precision=lax.Precision.HIGHEST,
            preferred_element_type=WIDE,
        )
        cotangent_low[...] = (nn(grad, square(first + 3)) * spread).astype(LOW)

    def attend_back_with(keys, queries, values, context, kept, tile_of, after):
        flip_heads(keys, flipped)
        inner_products(cotangent_low, context, inner)
        attend_back(
            flipped, queries, values, cotangent_low, inner,
            (key_sum, value_sum, grad_q), tile_of, room, Kept(kept, pre, kept_sems), after,
        )
        grad_k[...] = key_sum[...].astype(LOW)
        grad_v[...] = value_sum[...].astype(LOW)

    def cross_grads():
        square_grad(4, hidden_one[...], grad_q[...])
        square_grad(5, source_row[...], grad_k[...])
        square_grad(6, source_row[...], grad_v[...])

    def fill_source_grad():
        source_row[...] = (nt(grad_k[...], square(5)) + nt(grad_v[...], square(6))).astype(LOW)

    def first_norm_back():
        @pl.loop(0, length // 256)
        def _(tile):
            part = rows_of(tile, 256)
            grad = grad_second[part] + nt(grad_q[part], square(4))
            normal = normal_one[part]
            add_rows(vector(0), grad * normal)
            add_rows(vector(3), grad)
            grad_second[part] = normalize_back(grad, normal, inverse_one[part], norm_gain[0:1])

    def fill_query_grad(number):
        part = rows_of(place.tile(number), Q_TILE)
        grad = grad_second[part] + nt(grad_q[part], square(0))
        hidden_two[part] = grad.astype(LOW)

    def fill_embed_grad(rows):
        grad = nt(grad_k[rows], square(1)) + nt(grad_v[rows], square(2))
        cotangent_row[rows] = grad.astype(LOW)

    run_schedule(
        to,
        SimpleNamespace(
            fill_self_bias=lambda: fill_self_bias(bias, lengths, rank, limit, row),
            fill_cross_bias=lambda: fill_cross_bias(bias, lengths, source_lengths, row),
            near_keys_values=lambda: fill_keys_values(near_half),
            far_keys_values=lambda: fill_keys_values(far_half),
            near_queries=lambda: fill_queries(near_half),
            far_queries=lambda: fill_queries(far_half),
            attend_self=attend_self,
            first_norm=first_norm,
            cross_queries=fill_cross_queries,
            cross_keys_values=fill_cross_keys_values,
            attend_cross=attend_cross,
            bias_in=fill_bias_in,
            feed_forward_in=feed_forward_in,
            feed_forward=feed_forward,
            down_grad=lambda: wide_grad(1, grad_ffn, act),
            up_grad=lambda: wide_grad(0, hidden_two, pre),
            cross_out_back=lambda: out_back(4, other_context, other_totals, kept_cross),
            cross_back=lambda after: attend_back_with(
                other_k, other_q, other_v, other_context, kept_cross, lambda number: number, after
            ),
            cross_grads=cross_grads,
            source_grad=fill_source_grad,
            first_norm_back=first_norm_back,
            self_out_back=lambda: out_back(0, self_context, totals, kept_self),
            self_back=lambda after: attend_back_with(
                self_k, self_q, self_v, self_context, kept_self, place.tile, after
            ),
            query_grad=fill_query_grad,
            far_embed_grad=lambda: fill_embed_grad(far_half),
            near_embed_grad=lambda: fill_embed_grad(near_half),
            key_grad=lambda: square_grad(1, embed_row[...], grad_k[...]),
            value_grad=lambda: square_grad(2, embed_row[...], grad_v[...]),
            query_weight_grad=lambda: square_grad(0, query_row[...], grad_q[...]),
        ),
    )


def run_layer(streams, weights, vectors, tables):
    _, size, features = streams[0].shape
    length = 4 * size
    hidden = 4 * weights[8].shape[1]
    shape = jax.ShapeDtypeStruct
    vmem_in = pl.BlockSpec(memory_space=pltpu.VMEM)
    smem_in = pl.BlockSpec(memory_space=pltpu.SMEM)
    hbm = pl.BlockSpec(memory_space=pl.ANY)
    vmem, dma = pltpu.VMEM, pltpu.SemaphoreType.DMA
    row, wide_row = vmem((length, features), LOW), vmem((length, features), WIDE)
    per_head, column = vmem((HEADS, length), WIDE), vmem((length, 1), WIDE)
    full_squares = vmem((8, 4, 2, features // 8, features), LOW)
    full_wides = vmem((2, 4, 2, features // 8, hidden), LOW)
    blocks = shape((4, size, features), LOW)
    return pl.pallas_call(
        layer_kernel,
        out_shape=[
            shape((8, features // 8, features // 4), WIDE),
            shape((2, features // 8, hidden // 4), WIDE),
            shape((8, hidden), WIDE),
        ]
        + [blocks] * 4
        + [shape((length // Q_TILE * PAIRS, length, 2 * Q_TILE), LOW)] * 2,
        in_specs=[hbm] * 4 + [vmem_in] * 14 + [smem_in] * 2 + [vmem_in] * 2,
        out_specs=[vmem_in] * 3 + [hbm] * 6,
        scratch_shapes=[
            vmem((8, features // 8, features // 4), LOW),
            vmem((2, features // 8, hidden // 4), LOW),
            vmem((1, 16, 128), LOW),
            full_squares,
            full_wides,
            vmem((1, 4, 2, 16, 512), LOW),
            full_squares,
            full_wides,
            full_squares,
            vmem((8, features // 8, features // 4), LOW),
            vmem((2, features // 8, hidden // 4), LOW),
            vmem((5, 8, hidden), WIDE),
        ]
        + [row] * 12
        + [vmem((HEADS, 80, length), LOW)]
        + [per_head] * 3
        + [vmem((4, 1, Q_TILE), WIDE)]
        + [wide_row, column, row, row]
        + [vmem((length, hidden), LOW)] * 2
        + [row, wide_row, wide_row, wide_row, vmem((length, length), LOW)]
        + [vmem((1, hidden), WIDE)]
        + [dma((8, 3)), dma((8, 3)), dma((8,))]
        + [dma((10, Gather.slots)), dma((10, Gather.slots)), dma((10,))]
        + [dma((7, Scatter.slots)), dma((7, Scatter.slots)), dma((1, 5)), dma((1, 5)), dma((4,))]
        + [pltpu.SemaphoreType.REGULAR((2, 6))],
        compiler_params=pltpu.CompilerParams(
            collective_id=0, has_side_effects=True, vmem_limit_bytes=127 * 2**19
        ),
        name="layer",
    )(*streams, *weights, *vectors, *tables)[:7]


def outputs_kernel(
    squares, wides, small, mixed, grad_query, grad_embed, grad_encoder,
    mixed_out, query_out, embed_out, encoder_out, *rest,
):
    square_outs, wide_outs, (bias_in, bias_out, gains, shifts) = rest[:8], rest[8:10], rest[10:]
    mixed_out[...] = mixed[...]
    for low, out in ((grad_query, query_out), (grad_embed, embed_out), (grad_encoder, encoder_out)):
        out[...] = low[...].astype(WIDE)

    @pl.when(pl.program_id(0) == 0)
    def _():
        for index, out in enumerate(square_outs):
            out[...] = squares[index]
        for index, out in enumerate(wide_outs):
            out[...] = wides[index]
        features = gains.shape[1]
        for index in range(7):
            first = (index % 4) * features
            value = small[1 + index // 4 : 2 + index // 4, first : first + features]
            if index == 6:
                bias_out[...] = value
            else:
                (gains if index < 3 else shifts)[index % 3 : index % 3 + 1] = value
        count = wides.shape[2]
        mine = small[0:1, rows_of(lax.axis_index("tp"), count)]
        shift = lax.rem(count - lax.axis_index("dp") * bias_in.shape[1], count)
        bias_in[...] = pltpu.roll(mine, shift, 1)[:, : bias_in.shape[1]]


def write_outputs(squares, wides, small, *blocks):
    shape = jax.ShapeDtypeStruct
    rows, size, features = blocks[0].shape
    whole = pl.BlockSpec(memory_space=pltpu.VMEM)
    one = pl.BlockSpec((1, size, features), lambda i: (i, 0, 0))

    def fixed(extent):
        return pl.BlockSpec(extent, lambda i: (0,) * len(extent))

    singles = [squares.shape[1:]] * 8 + [wides.shape[1:]] * 2
    singles += [(1, wides.shape[1]), (1, features), (3, features), (3, features)]
    return pl.pallas_call(
        outputs_kernel,
        grid=(rows,),
        out_shape=[shape(blocks[0].shape, LOW)]
        + [shape(blocks[0].shape, WIDE)] * 3
        + [shape(extent, WIDE) for extent in singles],
        in_specs=[fixed(squares.shape), fixed(wides.shape), fixed(small.shape)] + [one] * 4,
        out_specs=[one] * 4 + [fixed(extent) for extent in singles],
        name="outputs",
    )(squares, wides, small, *blocks)


def local_rows(
    query_stream,
    token_embed,
    encoder_out,
    out_grad,
    attn_q,
    attn_k,
    attn_v,
    attn_o,
    cross_q,
    cross_k,
    cross_v,
    cross_o,
    ffn_in,
    ffn_bias_in,
    ffn_out,
    ffn_bias_out,
    norm_gain,
    norm_bias,
    doc_lengths,
    src_lengths,
    ctx_rank,
    ctx_limit,
):
    received = run_layer(
        (query_stream, token_embed, encoder_out, out_grad),
        (attn_q, attn_k, attn_v, attn_o.T, cross_q, cross_k, cross_v, cross_o.T)
        + (ffn_in, ffn_bias_in[None], ffn_out.T),
        (ffn_bias_out[None], norm_gain, norm_bias),
        (doc_lengths, src_lengths, ctx_rank, ctx_limit),
    )
    (
        mixed,
        grad_query,
        grad_embed,
        grad_encoder,
        grad_attn_q,
        grad_attn_k,
        grad_attn_v,
        grad_attn_o,
        grad_cross_q,
        grad_cross_k,
        grad_cross_v,
        grad_cross_o,
        grad_ffn_in,
        grad_ffn_out,
        grad_bias_in,
        grad_bias_out,
        gain_grads,
        shift_grads,
    ) = write_outputs(*received)
    return (
        mixed,
        grad_query,
        grad_embed,
        grad_encoder,
        grad_attn_q,
        grad_attn_k,
        grad_attn_v,
        grad_attn_o.T,
        grad_cross_q,
        grad_cross_k,
        grad_cross_v,
        grad_cross_o.T,
        grad_ffn_in,
        grad_bias_in[0],
        grad_ffn_out.T,
        grad_bias_out[0],
        gain_grads,
        shift_grads,
    )


def local(*arrays):
    if arrays[0].shape[0] == 4 and (lax.axis_size("dp"), lax.axis_size("tp")) == (8, 4):
        return local_rows(*arrays)
    return local_split(*arrays)


def solution(mesh):
    in_specs = (
        P("dp", "tp", None),
        P("dp", "tp", None),
        P("dp", "tp", None),
        P("dp", "tp", None),
        P("dp", "tp"),
        P("dp", "tp"),
        P("dp", "tp"),
        P("tp", "dp"),
        P("dp", "tp"),
        P("dp", "tp"),
        P("dp", "tp"),
        P("tp", "dp"),
        P("dp", "tp"),
        P(("tp", "dp")),
        P("tp", "dp"),
        P(),
        P(),
        P(),
        P("dp", None),
        P("dp", None),
        P("dp", None),
        P("dp", None),
    )
    out_specs = (
        P("dp", "tp", None),
        P("dp", "tp", None),
        P("dp", "tp", None),
        P("dp", "tp", None),
        P("dp", "tp"),
        P("dp", "tp"),
        P("dp", "tp"),
        P("tp", "dp"),
        P("dp", "tp"),
        P("dp", "tp"),
        P("dp", "tp"),
        P("tp", "dp"),
        P("dp", "tp"),
        P(("tp", "dp")),
        P("tp", "dp"),
        P(),
        P(),
        P(),
    )
    return jax.shard_map(local, mesh=mesh, in_specs=in_specs, out_specs=out_specs, check_vma=False)
```

```python
from types import SimpleNamespace

import jax
import jax.numpy as jnp
from jax import lax
from jax.experimental import pallas as pl
from jax.experimental.pallas import tpu as pltpu
from jax.sharding import PartitionSpec as P

HEADS = 8
LOW = jnp.bfloat16
WIDE = jnp.float32


EPSILON = 1e-05
score_tile = 512


def layer_norm(values, scale_vec, shift_vec):
    average = jnp.mean(values, axis=-1, keepdims=True)
    centred = values - average
    spread = jnp.mean(centred * centred, axis=-1, keepdims=True)
    return centred * lax.rsqrt(spread + EPSILON) * scale_vec + shift_vec


def gelu_exact(values):
    return 0.5 * values * (1.0 + lax.erf(values * 0.7071067811865476))


def project(inputs, matrix):
    return jnp.einsum("rld,de->rle", inputs, matrix, preferred_element_type=jnp.float32)


def project_back(cotangent, matrix):
    return jnp.einsum("rle,de->rld", cotangent, matrix, preferred_element_type=jnp.float32)


def outer_sum(inputs, cotangent):
    return jnp.einsum("rld,rle->de", inputs, cotangent, preferred_element_type=jnp.float32)


def layout(lengths, length):
    offsets = jnp.cumsum(lengths) - lengths
    positions = jnp.arange(length, dtype=jnp.int32)
    passed = positions[:, None] >= offsets[None, :]
    document = jnp.sum(passed.astype(jnp.int32), axis=1) - 1
    doc_start = jnp.max(jnp.where(passed, offsets[None, :], 0), axis=1)
    return (document, doc_start)


def self_visible(lengths, rank_row, limit_row, length, first_row, block_rows):
    document, doc_start = layout(lengths, length)
    positions = jnp.arange(length, dtype=jnp.int32)
    rows_pos = positions[first_row : first_row + block_rows]
    same_text = document[first_row : first_row + block_rows, None] == document[None, :]
    chosen = (rank_row[None, :] < limit_row[first_row : first_row + block_rows, None]) & (
        rows_pos[:, None] != positions[None, :]
    )
    opener = positions[None, :] == doc_start[first_row : first_row + block_rows, None]
    return same_text & (chosen | opener)


def cross_visible(lengths, src_lengths, length, src_length, first_row, block_rows):
    document, _ = layout(lengths, length)
    source_doc, _ = layout(src_lengths, src_length)
    return document[first_row : first_row + block_rows, None] == source_doc[None, :]


def attend_forward(queries, keys_all, values_all, visible_of, head_count):
    query_count = queries.shape[0]
    head_size = queries.shape[1] // head_count
    factor = head_size ** (-0.5)
    queries = queries.reshape(query_count, head_count, head_size)
    keys_all = keys_all.reshape(keys_all.shape[0], head_count, head_size)
    values_all = values_all.reshape(values_all.shape[0], head_count, head_size)
    block_rows = min(score_tile, query_count)
    outputs = []
    totals = []
    for first_row in range(0, query_count, block_rows):
        query_part = queries[first_row : first_row + block_rows]
        scores = (
            jnp.einsum("qhd,khd->hqk", query_part, keys_all, preferred_element_type=jnp.float32)
            * factor
        )
        scores = jnp.where(visible_of(first_row, block_rows)[None], scores, -1e30)
        highest = jnp.max(scores, axis=-1, keepdims=True)
        exponent = jnp.exp(scores - highest)
        denominator = jnp.sum(exponent, axis=-1, keepdims=True)
        weights_low = (exponent / denominator).astype(jnp.bfloat16)
        outputs.append(
            jnp.einsum("hqk,khd->qhd", weights_low, values_all, preferred_element_type=jnp.float32)
        )
        totals.append(highest[..., 0] + jnp.log(denominator[..., 0]))
    context = jnp.concatenate(outputs, axis=0).reshape(query_count, head_count * head_size)
    return (context, jnp.concatenate(totals, axis=1))


def attend_backward(queries, keys_all, values_all, visible_of, totals, grad_context, head_count):
    query_count = queries.shape[0]
    key_count = keys_all.shape[0]
    head_size = queries.shape[1] // head_count
    factor = head_size ** (-0.5)
    queries = queries.reshape(query_count, head_count, head_size)
    keys_all = keys_all.reshape(key_count, head_count, head_size)
    values_all = values_all.reshape(key_count, head_count, head_size)
    grad_context = grad_context.reshape(query_count, head_count, head_size)
    grad_keys = jnp.zeros((key_count, head_count, head_size), jnp.float32)
    grad_values = jnp.zeros((key_count, head_count, head_size), jnp.float32)
    grad_queries = []
    block_rows = min(score_tile, query_count)
    for first_row in range(0, query_count, block_rows):
        query_part = queries[first_row : first_row + block_rows]
        grad_part = grad_context[first_row : first_row + block_rows]
        scores = (
            jnp.einsum("qhd,khd->hqk", query_part, keys_all, preferred_element_type=jnp.float32)
            * factor
        )
        scores = jnp.where(visible_of(first_row, block_rows)[None], scores, -1e30)
        weights_full = jnp.exp(scores - totals[:, first_row : first_row + block_rows, None])
        grad_weights = jnp.einsum(
            "qhd,khd->hqk", grad_part, values_all, preferred_element_type=jnp.float32
        )
        inner = jnp.sum(grad_weights * weights_full, axis=-1, keepdims=True)
        grad_scores = (weights_full * (grad_weights - inner)).astype(jnp.bfloat16)
        grad_queries.append(
            jnp.einsum("hqk,khd->qhd", grad_scores, keys_all, preferred_element_type=jnp.float32)
            * factor
        )
        grad_keys = (
            grad_keys
            + jnp.einsum(
                "hqk,qhd->khd", grad_scores, query_part, preferred_element_type=jnp.float32
            )
            * factor
        )
        grad_values = grad_values + jnp.einsum(
            "hqk,qhd->khd",
            weights_full.astype(jnp.bfloat16),
            grad_part,
            preferred_element_type=jnp.float32,
        )
    grad_queries = jnp.concatenate(grad_queries, axis=0).reshape(
        query_count, head_count * head_size
    )
    return (
        grad_queries.astype(jnp.bfloat16),
        grad_keys.reshape(key_count, -1).astype(jnp.bfloat16),
        grad_values.reshape(key_count, -1).astype(jnp.bfloat16),
    )


def collect(piece):
    return lax.all_gather(piece, "tp", axis=1, tiled=True)


def spread_sum(partial_sum):
    return lax.psum_scatter(partial_sum, "tp", scatter_dimension=1, tiled=True)


def collect_grad(piece):
    return lax.all_gather(piece, "tp", axis=1, tiled=True)


def send_back(partial_sum):
    return lax.psum_scatter(partial_sum, "tp", scatter_dimension=1, tiled=True)


def local_split(
    query_stream,
    token_embed,
    encoder_out,
    out_grad,
    attn_q,
    attn_k,
    attn_v,
    attn_o,
    cross_q,
    cross_k,
    cross_v,
    cross_o,
    ffn_in,
    ffn_bias_in,
    ffn_out,
    ffn_bias_out,
    norm_gain,
    norm_bias,
    doc_lengths,
    src_lengths,
    ctx_rank,
    ctx_limit,
):
    head_count = HEADS // lax.axis_size("tp")
    (
        self_query,
        self_key,
        self_value,
        self_out,
        other_query,
        other_key,
        other_value,
        other_out,
        hidden_in,
        hidden_bias,
        hidden_out,
    ) = (
        lax.all_gather(attn_q, "dp", axis=0, tiled=True),
        lax.all_gather(attn_k, "dp", axis=0, tiled=True),
        lax.all_gather(attn_v, "dp", axis=0, tiled=True),
        lax.all_gather(attn_o, "dp", axis=1, tiled=True),
        lax.all_gather(cross_q, "dp", axis=0, tiled=True),
        lax.all_gather(cross_k, "dp", axis=0, tiled=True),
        lax.all_gather(cross_v, "dp", axis=0, tiled=True),
        lax.all_gather(cross_o, "dp", axis=1, tiled=True),
        lax.all_gather(ffn_in, "dp", axis=0, tiled=True),
        lax.all_gather(ffn_bias_in, "dp", axis=0, tiled=True),
        lax.all_gather(ffn_out, "dp", axis=1, tiled=True),
    )

    def self_forward(row_items):
        queries, keys_all, values_all, lengths, rank_row, limit_row = row_items

        def visible_of(first_row, block_rows):
            return self_visible(
                lengths, rank_row, limit_row, keys_all.shape[0], first_row, block_rows
            )

        return attend_forward(queries, keys_all, values_all, visible_of, head_count)

    def self_backward(row_items):
        queries, keys_all, values_all, lengths, rank_row, limit_row, totals, grad_context = (
            row_items
        )

        def visible_of(first_row, block_rows):
            return self_visible(
                lengths, rank_row, limit_row, keys_all.shape[0], first_row, block_rows
            )

        return attend_backward(
            queries, keys_all, values_all, visible_of, totals, grad_context, head_count
        )

    def cross_forward(row_items):
        queries, keys_all, values_all, lengths, source_lengths = row_items

        def visible_of(first_row, block_rows):
            return cross_visible(
                lengths, source_lengths, queries.shape[0], keys_all.shape[0], first_row, block_rows
            )

        return attend_forward(queries, keys_all, values_all, visible_of, head_count)

    def cross_backward(row_items):
        queries, keys_all, values_all, lengths, source_lengths, totals, grad_context = row_items

        def visible_of(first_row, block_rows):
            return cross_visible(
                lengths, source_lengths, queries.shape[0], keys_all.shape[0], first_row, block_rows
            )

        return attend_backward(
            queries, keys_all, values_all, visible_of, totals, grad_context, head_count
        )

    query_all = collect(query_stream)
    embed_all = collect(token_embed)
    source_all = collect(encoder_out)
    self_queries = project(query_all, self_query).astype(jnp.bfloat16)
    self_keys = project(embed_all, self_key).astype(jnp.bfloat16)
    self_values = project(embed_all, self_value).astype(jnp.bfloat16)
    self_context, self_totals = lax.map(
        self_forward, (self_queries, self_keys, self_values, doc_lengths, ctx_rank, ctx_limit)
    )
    self_low = self_context.astype(jnp.bfloat16)
    first_sum = query_stream.astype(jnp.float32) + spread_sum(project(self_low, self_out))
    hidden_one, first_back = jax.vjp(layer_norm, first_sum, norm_gain[0], norm_bias[0])
    hidden_one_all = collect(hidden_one.astype(jnp.bfloat16))
    cross_queries = project(hidden_one_all, other_query).astype(jnp.bfloat16)
    cross_keys = project(source_all, other_key).astype(jnp.bfloat16)
    cross_values = project(source_all, other_value).astype(jnp.bfloat16)
    cross_context, cross_totals = lax.map(
        cross_forward, (cross_queries, cross_keys, cross_values, doc_lengths, src_lengths)
    )
    cross_low = cross_context.astype(jnp.bfloat16)
    second_sum = hidden_one + spread_sum(project(cross_low, other_out))
    hidden_two, second_back = jax.vjp(layer_norm, second_sum, norm_gain[1], norm_bias[1])
    hidden_two_low = hidden_two.astype(jnp.bfloat16)
    ffn_inputs = lax.all_gather(hidden_two_low, "tp", axis=1, tiled=True)
    ffn_pre = project(ffn_inputs, hidden_in) + hidden_bias.astype(jnp.float32)
    ffn_gate, gelu_back = jax.vjp(gelu_exact, ffn_pre)
    ffn_act = ffn_gate.astype(jnp.bfloat16)
    ffn_branch = (
        lax.psum_scatter(project(ffn_act, hidden_out), "tp", scatter_dimension=1, tiled=True)
        + ffn_bias_out
    )
    third_sum = hidden_two + ffn_branch
    mixed_full, third_back = jax.vjp(layer_norm, third_sum, norm_gain[2], norm_bias[2])
    grad_third, gain_two, shift_two = third_back(out_grad.astype(jnp.float32))
    grad_ffn = grad_third.astype(jnp.bfloat16)
    grad_bias_out = jnp.sum(grad_ffn.astype(jnp.float32), axis=(0, 1))
    grad_ffn_all = lax.all_gather(grad_ffn, "tp", axis=1, tiled=True)
    grad_act = project_back(grad_ffn_all, hidden_out)
    grad_down = outer_sum(ffn_act, grad_ffn_all)
    grad_pre = gelu_back(grad_act)[0].astype(jnp.bfloat16)
    grad_up = outer_sum(ffn_inputs, grad_pre)
    grad_bias_in = jnp.sum(grad_pre.astype(jnp.float32), axis=(0, 1))
    grad_two = grad_third + lax.psum_scatter(
        project_back(grad_pre, hidden_in), "tp", scatter_dimension=1, tiled=True
    )
    grad_second, gain_one, shift_one = second_back(grad_two)
    grad_cross_all = collect_grad(grad_second.astype(jnp.bfloat16))
    grad_other_out = outer_sum(cross_low, grad_cross_all)
    grad_cross_ctx = project_back(grad_cross_all, other_out).astype(jnp.bfloat16)
    cross_dq, cross_dk, cross_dv = lax.map(
        cross_backward,
        (
            cross_queries,
            cross_keys,
            cross_values,
            doc_lengths,
            src_lengths,
            cross_totals,
            grad_cross_ctx,
        ),
    )
    grad_other_query = outer_sum(hidden_one_all, cross_dq)
    grad_other_key = outer_sum(source_all, cross_dk)
    grad_other_value = outer_sum(source_all, cross_dv)
    grad_encoder = send_back(
        project_back(cross_dk, other_key) + project_back(cross_dv, other_value)
    )
    grad_one = grad_second + send_back(project_back(cross_dq, other_query))
    grad_first, gain_zero, shift_zero = first_back(grad_one)
    grad_attn_all = collect_grad(grad_first.astype(jnp.bfloat16))
    grad_self_out = outer_sum(self_low, grad_attn_all)
    grad_self_ctx = project_back(grad_attn_all, self_out).astype(jnp.bfloat16)
    self_dq, self_dk, self_dv = lax.map(
        self_backward,
        (
            self_queries,
            self_keys,
            self_values,
            doc_lengths,
            ctx_rank,
            ctx_limit,
            self_totals,
            grad_self_ctx,
        ),
    )
    grad_self_query = outer_sum(query_all, self_dq)
    grad_self_key = outer_sum(embed_all, self_dk)
    grad_self_value = outer_sum(embed_all, self_dv)
    grad_embed = send_back(project_back(self_dk, self_key) + project_back(self_dv, self_value))
    grad_query = grad_first + send_back(project_back(self_dq, self_query))
    (
        grad_self_query,
        grad_self_key,
        grad_self_value,
        grad_self_out,
        grad_other_query,
        grad_other_key,
        grad_other_value,
        grad_other_out,
        grad_up,
        grad_bias_in,
        grad_down,
    ) = (
        lax.psum_scatter(
            grad_self_query.astype(jnp.bfloat16), "dp", scatter_dimension=0, tiled=True
        ).astype(jnp.float32),
        lax.psum_scatter(
            grad_self_key.astype(jnp.bfloat16), "dp", scatter_dimension=0, tiled=True
        ).astype(jnp.float32),
        lax.psum_scatter(
            grad_self_value.astype(jnp.bfloat16), "dp", scatter_dimension=0, tiled=True
        ).astype(jnp.float32),
        lax.psum_scatter(
            grad_self_out.astype(jnp.bfloat16), "dp", scatter_dimension=1, tiled=True
        ).astype(jnp.float32),
        lax.psum_scatter(
            grad_other_query.astype(jnp.bfloat16), "dp", scatter_dimension=0, tiled=True
        ).astype(jnp.float32),
        lax.psum_scatter(
            grad_other_key.astype(jnp.bfloat16), "dp", scatter_dimension=0, tiled=True
        ).astype(jnp.float32),
        lax.psum_scatter(
            grad_other_value.astype(jnp.bfloat16), "dp", scatter_dimension=0, tiled=True
        ).astype(jnp.float32),
        lax.psum_scatter(
            grad_other_out.astype(jnp.bfloat16), "dp", scatter_dimension=1, tiled=True
        ).astype(jnp.float32),
        lax.psum_scatter(
            grad_up.astype(jnp.bfloat16), "dp", scatter_dimension=0, tiled=True
        ).astype(jnp.float32),
        lax.psum_scatter(
            grad_bias_in.astype(jnp.bfloat16), "dp", scatter_dimension=0, tiled=True
        ).astype(jnp.float32),
        lax.psum_scatter(
            grad_down.astype(jnp.bfloat16), "dp", scatter_dimension=1, tiled=True
        ).astype(jnp.float32),
    )
    gain_grads = jnp.stack([gain_zero, gain_one, gain_two])
    shift_grads = jnp.stack([shift_zero, shift_one, shift_two])
    gain_grads, shift_grads, grad_bias_out = lax.psum(
        (gain_grads, shift_grads, grad_bias_out), ("dp", "tp")
    )
    return (
        mixed_full.astype(jnp.bfloat16),
        grad_query,
        grad_embed,
        grad_encoder,
        grad_self_query,
        grad_self_key,
        grad_self_value,
        grad_self_out,
        grad_other_query,
        grad_other_key,
        grad_other_value,
        grad_other_out,
        grad_up,
        grad_bias_in,
        grad_down,
        grad_bias_out,
        gain_grads,
        shift_grads,
    )


HIDDEN = -1e30
Q_TILE = 256


def product(left, right, left_axis, right_axis):
    return lax.dot_general(
        left, right, (((left_axis,), (right_axis,)), ((), ())), preferred_element_type=WIDE
    )


def nn(left, right):
    return product(left, right, 1, 0)


def nt(left, right):
    return product(left, right, 1, 1)


def tn(left, right):
    return product(left, right, 0, 0)


def rows_of(index, size):
    return pl.ds(pl.multiple_of(index * size, size), size)


def normalize(values):
    average = jnp.mean(values, axis=-1, keepdims=True)
    centred = values - average
    spread = jnp.mean(centred * centred, axis=-1, keepdims=True)
    inverse = lax.rsqrt(spread + EPSILON)
    return centred * inverse, inverse


def normalize_back(grad, normal, inverse, gain):
    scaled = grad * gain
    mean_one = jnp.mean(scaled, axis=-1, keepdims=True)
    mean_two = jnp.mean(scaled * normal, axis=-1, keepdims=True)
    return inverse * (scaled - mean_one - normal * mean_two)


def add_rows(target, grad):
    target[...] += jnp.sum(grad, axis=0, keepdims=True)


def documents(lengths, row, shape, axis):
    positions = lax.broadcasted_iota(jnp.int32, shape, axis)
    document = jnp.full(shape, -1, jnp.int32)
    start = jnp.zeros(shape, jnp.int32)
    offset = jnp.int32(0)
    for slot in range(lengths.shape[1]):
        passed = positions >= offset
        document = document + passed.astype(jnp.int32)
        start = jnp.where(passed, offset, start)
        offset = offset + lengths[row, slot]
    return positions, document, start


def fill_self_bias(bias, lengths, rank, limit, row):
    length = bias.shape[0]
    key_position, key_document, _ = documents(lengths, row, (length, 1), 0)
    position, document, start = documents(lengths, row, (1, length), 1)
    rank_row = rank[pl.ds(row, 1), :].astype(WIDE)
    key_rank = jnp.transpose(jnp.broadcast_to(rank_row, (128, length)))[:, :1]
    query_limit = limit[pl.ds(row, 1), :].astype(WIDE)
    for tile in range(length // Q_TILE):
        part = slice(tile * Q_TILE, (tile + 1) * Q_TILE)
        chosen = (key_rank < query_limit[:, part]) & (key_position != position[:, part])
        seen = (key_document == document[:, part]) & (chosen | (key_position == start[:, part]))
        bias[:, part] = jnp.where(seen, 0.0, HIDDEN).astype(bias.dtype)


def fill_cross_bias(bias, lengths, source_lengths, row):
    length = bias.shape[0]
    _, key_document, _ = documents(source_lengths, row, (length, 1), 0)
    _, document, _ = documents(lengths, row, (1, length), 1)
    for tile in range(length // Q_TILE):
        part = slice(tile * Q_TILE, (tile + 1) * Q_TILE)
        seen = key_document == document[:, part]
        bias[:, part] = jnp.where(seen, 0.0, HIDDEN).astype(bias.dtype)


def one_head(pair, side):
    lane = lax.broadcasted_iota(jnp.int32, pair.shape, 1)
    return jnp.where(lane // 64 == side, pair, jnp.zeros_like(pair))


def run_after(step, after):
    for number, actions in after.items():
        if actions:

            @pl.when(step == number)
            def _():
                for action in actions:
                    action()


PAIRS = HEADS // 2


class Kept:
    def __init__(self, kept, room, sems, place_of=lambda step: step):
        self.kept, self.room, self.sems, self.place_of = kept, room, sems, place_of

    def slot(self, step, side=None):
        place = lax.rem(step, 4)
        if side is None:
            return rows_of(place, 2 * Q_TILE)
        return rows_of(2 * place + side, Q_TILE)

    def store(self, step):
        room = self.room.at[:, self.slot(step)]
        return pltpu.make_async_copy(room, self.kept.at[self.place_of(step)], self.sems.at[lax.rem(step, 4)])

    def load(self, step):
        room = self.room.at[:, self.slot(step)]
        return pltpu.make_async_copy(self.kept.at[self.place_of(step)], room, self.sems.at[lax.rem(step, 4)])


def attend(keys, queries, values_t, bias, context, inverses, tile_of, room, kept, after):
    scores_of, highest_of = room
    steps = keys.shape[0] // Q_TILE * PAIRS

    def where(step):
        return rows_of(tile_of(step // PAIRS), Q_TILE), lax.rem(step, PAIRS)

    def score(step, slot):
        part, pair = where(step)
        lanes = rows_of(pair, 128)
        for side in (0, 1):
            scores = nt(keys[:, lanes], one_head(queries[part, lanes], side))
            scores = scores + bias[:, part].astype(WIDE)
            scores_of[slot][:, side * Q_TILE : (side + 1) * Q_TILE] = scores
            highest_of[2 * slot + side] = jnp.max(scores, axis=0, keepdims=True)

    def weigh(step, slot):
        part, pair = where(step)
        outs = []
        for side in (0, 1):
            head = 2 * pair + side
            scores = scores_of[slot][:, side * Q_TILE : (side + 1) * Q_TILE]
            weights = jnp.exp(scores - highest_of[2 * slot + side]).astype(LOW)
            kept.room[:, kept.slot(step, side)] = weights
            out = nn(values_t[head], weights)
            inverse = 1.0 / out[64:65]
            outs.append(out[:64] * inverse)
            inverses[pl.ds(head, 1), part] = inverse
        context[part, rows_of(pair, 128)] = jnp.transpose(jnp.concatenate(outs, axis=0)).astype(LOW)

    score(0, 0)

    @pl.loop(0, steps // 2)
    def _(double):
        @pl.when(double > 1)
        def _():
            kept.store(2 * double - 4).wait()
            kept.store(2 * double - 3).wait()

        score(2 * double + 1, 1)
        weigh(2 * double, 0)
        score(lax.rem(2 * double + 2, steps), 0)
        weigh(2 * double + 1, 1)
        kept.store(2 * double).start()
        kept.store(2 * double + 1).start()
        run_after(double, after)

    for step in range(steps - 4, steps):
        kept.store(step).wait()


def attend_back(keys_t, queries, values, cotangent, inner, grads, tile_of, room, kept, after):
    key_sum, value_sum, grad_queries = grads
    steps = values.shape[0] // Q_TILE * PAIRS

    def where(step):
        return rows_of(tile_of(step // PAIRS), Q_TILE), rows_of(lax.rem(step, PAIRS), 128)

    def make(step, slot):
        part, lanes = where(step)
        pair = lax.rem(step, PAIRS)
        for side in (0, 1):
            head = 2 * pair + side
            grad_weights = nt(values[:, lanes], one_head(cotangent[part, lanes], side))
            weights = kept.room[:, kept.slot(step, side)].astype(WIDE)
            grad_scores = weights * (grad_weights - inner[pl.ds(head, 1), part])
            room[slot][:, side * Q_TILE : (side + 1) * Q_TILE] = grad_scores.astype(LOW)

    def use(step, slot):
        part, lanes = where(step)
        pair = lax.rem(step, PAIRS)

        def stacked(ref):
            return jnp.concatenate([one_head(ref[part, lanes], side) for side in (0, 1)], axis=0)

        outs = [
            nn(keys_t[2 * pair + side, :64], room[slot][:, side * Q_TILE : (side + 1) * Q_TILE])
            for side in (0, 1)
        ]
        turned = jnp.transpose(jnp.concatenate(outs, axis=0) * 0.125)
        grad_queries[part, lanes] = turned.astype(LOW)
        value_sum[:, lanes] += nn(kept.room[:, kept.slot(step)], stacked(cotangent))
        key_sum[:, lanes] += nn(room[slot][...], stacked(queries))

    key_sum[...] = jnp.zeros_like(key_sum)
    value_sum[...] = jnp.zeros_like(value_sum)
    kept.load(0).wait()
    make(0, 0)

    @pl.loop(0, steps // 2)
    def _(double):
        kept.load(2 * double + 1).wait()
        make(2 * double + 1, 1)
        use(2 * double, 0)

        @pl.when(double < steps // 2 - 1)
        def _():
            kept.load(2 * double + 2).wait()

        make(lax.rem(2 * double + 2, steps), 0)
        use(2 * double + 1, 1)

        @pl.when(double < steps // 2 - 2)
        def _():
            kept.load(2 * double + 4).start()
            kept.load(2 * double + 5).start()

        run_after(double, after)


def inner_products(cotangent, context, inner):
    products = cotangent[...].astype(WIDE) * context[...].astype(WIDE)
    high = products.astype(LOW)
    rest = (products - high.astype(WIDE)).astype(LOW)
    shape = (2 * HEADS, products.shape[1])
    head = lax.broadcasted_iota(jnp.int32, shape, 0)
    lane = lax.broadcasted_iota(jnp.int32, shape, 1)
    pick = jnp.where(lane // 64 == head, 1.0, 0.0).astype(LOW)
    inner[...] = (nt(pick, high) + nt(pick, rest))[:HEADS]


def flip_heads(values, flipped):
    turned = jnp.transpose(values[...])
    for head in range(HEADS):
        flipped[head, :64] = turned[64 * head : 64 * head + 64]

MESH = pl.DeviceIdType.MESH


class Place:
    def __init__(self):
        dp, tp = lax.axis_index("dp"), lax.axis_index("tp")
        self.dp, self.tp = dp, tp
        self.z, self.x = dp // 2, lax.rem(dp, 2)
        self.y, self.core = tp // 2, lax.rem(tp, 2)
        self.core_peer = (dp, 2 * self.y + 1 - self.core)
        self.y_peer = (dp, 2 * (1 - self.y) + self.core)
        self.far_peer = (dp, 2 * (1 - self.y) + 1 - self.core)
        self.x_peer = (2 * self.z + 1 - self.x, tp)
        self.z_steps = [lax.rem(self.z + step, 4) for step in range(4)]
        self.z_peers = [(2 * z + self.x, tp) for z in self.z_steps[1:]]
        self.summing = [self.core_peer, self.x_peer, self.y_peer] + self.z_peers

    def greet(self):
        for peer in self.summing + [self.far_peer]:
            barrier = pltpu.get_barrier_semaphore()
            pl.semaphore_signal(barrier, inc=1, device_id=peer, device_id_type=MESH)

    def meet(self):
        pl.semaphore_wait(pltpu.get_barrier_semaphore(), len(self.summing) + 1)

    def tile(self, number):
        side = lax.rem(self.y + 1 - number // 2, 2)
        return 2 * side + lax.rem(self.core + (number + 1) // 2, 2)

    def columns(self, width):
        return [
            pl.ds(pl.multiple_of(tp * width, width), width)
            for tp in (self.tp, self.y_peer[1], self.core_peer[1], self.far_peer[1])
        ]


class Exchange:
    def __init__(self, sends, recvs, number):
        self.sends, self.recvs, self.number = sends, recvs, number
        self.made = []
        self.arriving = []

    def send(self, source, target, peer):
        slot = len(self.made)

        def copy():
            return pltpu.make_async_remote_copy(
                src_ref=source(),
                dst_ref=target(),
                send_sem=self.sends.at[self.number, slot],
                recv_sem=self.recvs.at[self.number, slot],
                device_id=peer,
                device_id_type=MESH,
            )

        copy().start()
        self.made.append(copy)
        self.arriving.append(copy)

    def move(self, block, peer):
        self.send(block, block, peer)

    def arrive(self):
        for copy in self.arriving:
            copy().wait_recv()
        self.arriving = []

    def finish(self):
        for copy in self.made:
            copy().wait_send()


class Gather(Exchange):
    slots = 11

    def __init__(
        self, place, local, full, first, count, side, sides, sends, recvs, own_sems, number
    ):
        super().__init__(sends, recvs, number)
        self.place, self.full, self.items = place, full, pl.ds(first, count)
        width = local.shape[-1] // sides
        self.sides = [
            pl.ds(pl.multiple_of((tp * sides + side) * width, width), width)
            for tp in (place.tp, place.y_peer[1])
        ]
        p = place
        self.source = lambda: local.at[self.items, :, side * width : (side + 1) * width]
        self.target = lambda: full.at[self.items, p.z, p.x, :, self.sides[0]]
        self.own = lambda: pltpu.make_async_copy(
            self.source(), self.target(), own_sems.at[number]
        )

    def stage(self, number):
        p, full, items = self.place, self.full, self.items
        self.arrive()
        if number == 0:
            self.own().start()
            self.send(self.source, self.target, p.y_peer)
        elif number == 1:
            self.own().wait()
            for side in self.sides:
                for peer in p.z_peers:
                    self.move(lambda side=side: full.at[items, p.z, p.x, :, side], peer)
        elif number == 2:
            for side in self.sides:
                self.move(lambda side=side: full.at[items, :, p.x, :, side], p.x_peer)
        elif number == 3:
            for side in self.sides:
                self.move(lambda side=side: full.at[items, :, :, :, side], p.core_peer)


class ToRow(Exchange):
    slots = 3

    def __init__(self, place, local, row, sends, recvs, own_sems, number):
        super().__init__(sends, recvs, number)
        size = local.shape[1]
        p = place
        span = pl.ds(pl.multiple_of(p.tp * size, size), size)

        def here():
            return row.at[span]

        self.local, self.here = local, here
        self.peers = (p.y_peer, p.far_peer, p.core_peer)
        self.own = lambda: pltpu.make_async_copy(local.at[p.tp], here(), own_sems.at[number])

    def start(self):
        for peer in self.peers:
            self.send(lambda peer=peer: self.local.at[peer[1]], self.here, peer)
        self.own().start()

    def near(self):
        self.own().wait()
        self.arriving.pop()().wait_recv()

    def far(self):
        self.arrive()


class FromRow(Exchange):
    slots = 3

    def __init__(self, place, row, blocks, sends, recvs, own_sems, number):
        super().__init__(sends, recvs, number)
        size = blocks.shape[1]
        p = place
        self.peers = (p.y_peer, p.far_peer, p.core_peer)
        self.target = lambda: blocks.at[p.tp]

        def part(tp):
            return row.at[pl.ds(pl.multiple_of(tp * size, size), size)]

        self.part = part
        self.own = lambda: pltpu.make_async_copy(
            self.part(p.tp), self.target(), own_sems.at[number]
        )

    def give(self, number):
        if number == 3:
            self.own().start()
        else:
            peer = self.peers[number]
            self.send(lambda: self.part(peer[1]), self.target, peer)

    def give_all(self):
        for number in range(4):
            self.give(number)

    def wait(self):
        self.own().wait()
        self.arrive()


class Scatter(Exchange):
    slots = 8

    def __init__(
        self, place, parts, work, last, out, first, count, ready, sends, recvs, number
    ):
        super().__init__(sends, recvs, number)
        self.place, self.parts, self.work, self.last, self.out = place, parts, work, last, out
        self.numbers = range(first, first + count)
        self.items = pl.ds(first, count)
        self.width = out.shape[-1]
        self.columns = place.columns(self.width)
        self.ready = ready

    def add_core(self):
        width = self.width
        for item in self.numbers:
            for side in (0, 1):

                @pl.loop(0, 4)
                def _(z):
                    mine = self.parts[item, z, :, :, self.columns[side]]
                    self.work[item, z, :, :, side * width : (side + 1) * width] += mine

    def expect(self, index):
        if self.ready is not None:
            pl.semaphore_wait(self.ready.at[self.number, index], 1)

    def stage(self, number):
        p, parts, work, items, width = self.place, self.parts, self.work, self.items, self.width
        first_half, second_half = slice(0, 2 * width), slice(2 * width, 4 * width)
        sides = [slice(side * width, (side + 1) * width) for side in range(4)]
        self.arrive()
        if number == 0:
            self.expect(0)
            for side, column in zip(sides, self.columns[2:]):
                self.send(
                    lambda column=column: parts.at[items, :, :, :, column],
                    lambda side=side: work.at[items, :, :, :, side],
                    p.core_peer,
                )
        elif number == 1:
            self.add_core()
            self.expect(1)
            self.send(
                lambda: work.at[items, :, 1 - p.x, :, first_half],
                lambda: work.at[items, :, 0, :, second_half],
                p.x_peer,
            )
        elif number == 2:
            for item in self.numbers:

                @pl.loop(0, 4)
                def _(z):
                    work[item, z, 0, :, second_half] += work[item, z, p.x, :, first_half]

            for step, peer in enumerate(p.z_peers):
                self.expect(3 + step)
                self.send(
                    lambda step=step: work.at[items, p.z_steps[step + 1], 0, :, second_half],
                    lambda step=step: work.at[items, step, 1, :, second_half],
                    peer,
                )
        elif number == 3:
            for item in self.numbers:
                total = work[item, p.z, 0, :, second_half].astype(WIDE)
                for step in range(3):
                    total = total + work[item, step, 1, :, second_half].astype(WIDE)
                work[item, 3, 1, :, second_half] = total.astype(LOW)
            self.expect(2)
            self.send(
                lambda: work.at[items, 3, 1, :, sides[3]],
                lambda: self.last.at[items],
                p.y_peer,
            )
        else:
            for item in self.numbers:
                mine = work[item, 3, 1, :, sides[2]].astype(WIDE)
                self.out[item] = mine + self.last[item].astype(WIDE)


class ScatterAcross(Scatter):
    def __init__(
        self, place, parts, work, last, out, first, count, ready, across, sends, recvs, number
    ):
        super().__init__(place, parts, work, last, out, first, count, ready, sends, recvs, number)
        self.across = across

    def stage(self, number):
        if number == 0:
            super().stage(0)
            return
        p, work, items, width = self.place, self.work, self.items, self.width
        first_half, second_half = slice(0, 2 * width), slice(2 * width, 4 * width)
        kept, given = slice(2 * width, 3 * width), slice(3 * width, 4 * width)
        self.arrive()
        if number == 1:
            self.add_core()
            for step, peer in enumerate(p.z_peers):
                self.send(
                    lambda step=step: work.at[items, p.z_steps[step + 1], :, :, first_half],
                    lambda step=step: work.at[items, step, :, :, second_half],
                    peer,
                )
        elif number == 2:
            for item in self.numbers:
                total = work[item, p.z, :, :, first_half].astype(WIDE)
                for step in range(3):
                    total = total + work[item, step, :, :, second_half].astype(WIDE)
                work[item, 3, :, :, second_half] = total.astype(LOW)
            self.send(
                lambda: work.at[items, 3, 1 - p.x, :, second_half], lambda: self.across, p.x_peer
            )
        elif number == 3:
            for item in self.numbers:
                work[item, 3, p.x, :, second_half] += self.across[0]
            self.send(
                lambda: work.at[items, 3, p.x, :, given], lambda: self.last.at[items], p.y_peer
            )
        else:
            for item in self.numbers:
                mine = work[item, 3, p.x, :, kept].astype(WIDE)
                self.out[item] = mine + self.last[item].astype(WIDE)


class SumAll(Exchange):
    slots = 5

    def __init__(self, place, values, arrived, sends, recvs):
        super().__init__(sends, recvs, 0)
        p = place
        z_one = p.z + 1 - 2 * lax.rem(p.z, 2)
        peers = (p.core_peer, p.x_peer, p.y_peer, (2 * z_one + p.x, p.tp), p.z_peers[1])
        self.peers, self.values, self.arrived = peers, values, arrived

    def stage(self, number):
        if number:
            self.arrive()
            self.made[-1]().wait_send()
            self.values[...] = self.values[...] + self.arrived[number - 1]
        if number < 5:
            self.send(
                lambda: self.values, lambda: self.arrived.at[number], self.peers[number]
            )


def run_schedule(to, do):
    def step(task, number):
        return lambda: task.stage(number)

    do.fill_self_bias()
    to.place.meet()
    first = [to.keys_values, to.query, to.out, to.bias]
    rest = to.cross + to.ffn
    for task in first + to.cross:
        task.stage(0)
    to.embed_row.start()
    for task in to.ffn[:2]:
        task.stage(0)
    to.query_row.start()
    for task in to.ffn[2:]:
        task.stage(0)
    to.source_row.start()
    to.cotangent_row.start()
    for task in first + to.cross:
        task.stage(1)
    to.keys_values.stage(2)
    to.query.stage(2)
    to.keys_values.stage(3)
    to.embed_row.near()
    to.query_row.near()
    to.keys_values.stage(4)
    do.near_keys_values()
    to.out.stage(2)
    to.bias.stage(2)
    to.query.stage(3)
    to.query.stage(4)
    do.near_queries()
    to.embed_row.far()
    do.far_keys_values()
    for task in to.ffn[:2]:
        task.stage(1)

    def far_queries():
        to.query_row.far()
        do.far_queries()

    do.attend_self(
        {
            0: [step(to.cross[0], 2), step(to.out, 3)],
            1: [step(to.out, 4), step(to.bias, 3)],
            2: [far_queries, step(to.ffn[2], 1), step(to.ffn[3], 1), step(to.cross[0], 3), step(to.cross[1], 2)],
            3: [step(to.cross[0], 4), step(to.bias, 4)],
            5: [step(to.ffn[0], 2)],
            7: [step(to.cross[1], 3)],
        }
    )
    do.first_norm()
    to.ffn[1].stage(2)
    to.cross[1].stage(4)
    do.fill_cross_bias()
    do.cross_queries()
    to.source_row.near()
    to.source_row.far()
    do.cross_keys_values()
    do.attend_cross(
        {
            0: [step(to.ffn[2], 2), step(to.ffn[0], 3)],
            3: [step(to.ffn[3], 2), step(to.ffn[0], 4), step(to.ffn[1], 3)],
            5: [step(to.ffn[1], 4)],
            7: [step(to.ffn[2], 3)],
        }
    )
    do.bias_in()
    do.feed_forward_in(
        {
            1: [step(to.ffn[2], 4)],
            2: [step(to.ffn[3], 3)],
        }
    )
    to.cotangent_row.near()
    to.cotangent_row.far()
    to.ffn[3].stage(4)
    do.feed_forward()

    for task in to.ffn:
        task.finish()
    for group in (0, 1):
        for index, peer in enumerate(to.place.summing):
            there = index if index < 3 else 8 - index
            pl.semaphore_signal(
                to.ready.at[group, there], inc=1, device_id=peer, device_id_type=MESH
            )
    to.mixed.give_all()
    do.down_grad()
    to.down_sum.stage(0)
    do.up_grad()
    to.up_sum.stage(0)
    do.cross_out_back()
    to.down_sum.stage(1)
    to.up_sum.stage(1)
    do.cross_back({4: [step(to.down_sum, 2)]})
    do.cross_grads()
    to.cross_sum.stage(0)
    do.source_grad()
    to.source_grad.give_all()
    to.up_sum.stage(2)
    to.cross_sum.stage(1)
    do.first_norm_back()
    to.small_sum.stage(0)
    to.down_sum.stage(3)
    do.self_out_back()
    to.out_sum.stage(0)
    to.small_sum.stage(1)

    def give_query(number):
        def action():
            do.query_grad(number)
            to.query_grad.give(number)

        return action

    do.self_back(
        {
            0: [step(to.out_sum, 1)],
            1: [give_query(0)],
            3: [give_query(1), step(to.cross_sum, 2), step(to.small_sum, 2)],
            4: [step(to.up_sum, 3)],
            5: [give_query(2), step(to.out_sum, 2)],
            7: [give_query(3), step(to.small_sum, 3)],
        }
    )
    to.mixed.wait()
    to.mixed.finish()
    do.value_grad()
    to.value_sum.stage(0)
    do.key_grad()
    to.key_sum.stage(0)
    to.value_sum.stage(1)
    do.query_weight_grad()
    to.query_sum.stage(0)
    to.key_sum.stage(1)
    do.far_embed_grad()
    to.embed_grad.give(0)
    to.embed_grad.give(1)
    to.query_sum.stage(1)
    do.near_embed_grad()
    to.embed_grad.give(2)
    to.embed_grad.give(3)
    to.key_sum.stage(2)
    to.small_sum.stage(4)
    to.query_sum.stage(2)
    to.value_sum.stage(2)
    to.cross_sum.stage(3)
    to.out_sum.stage(3)
    to.down_sum.stage(4)
    to.up_sum.stage(4)
    to.key_sum.stage(3)
    to.small_sum.stage(5)
    to.query_sum.stage(3)
    to.value_sum.stage(3)
    for task in (to.cross_sum, to.out_sum, to.key_sum, to.value_sum, to.query_sum):
        task.stage(4)
    outgoing = [to.source_grad, to.query_grad, to.embed_grad]
    for task in outgoing:
        task.wait()
    for task in outgoing + [to.embed_row, to.query_row, to.source_row, to.cotangent_row]:
        task.finish()
    for task in first + to.cross:
        task.finish()
    for task in (to.down_sum, to.up_sum, to.cross_sum, to.out_sum):
        task.finish()
    for task in (to.key_sum, to.value_sum, to.query_sum):
        task.finish()


def layer_kernel(
    query, embed, source, cotangent, attn_q, attn_k, attn_v, attn_o, cross_q, cross_k, cross_v,
    cross_o, ffn_in, ffn_bias_in, ffn_out, bias_out, norm_gain, norm_bias, lengths, source_lengths,
    rank, limit,
    own_squares, own_wides, small, mixed_blocks, query_blocks, embed_blocks, encoder_blocks, kept_self, kept_cross,
    local_squares, local_wides, local_bias, squares, wides, biases, grad_squares, grad_wides,
    work, last_squares, last_wides, arrived, across,
    query_row, embed_row, source_row, cotangent_row,
    self_q, self_k, self_v, self_context, other_q, other_k, other_v, other_context,
    flipped, totals, other_totals, inner, highest, normal_one, inverse_one,
    hidden_one, hidden_two, act, pre, grad_ffn, grad_second, key_sum, value_sum, bias, bias_in,
    row_sends, row_recvs, row_own, gather_sends, gather_recvs, gather_own,
    scatter_sends, scatter_recvs, sum_sends, sum_recvs, kept_sems, ready,
):
    place = Place()
    place.greet()
    row = place.tp
    length, features = query_row.shape
    hidden = act.shape[1]
    half = length // 2
    near_half, far_half = rows_of(place.y, half), rows_of(1 - place.y, half)

    for index, piece in enumerate((attn_q, attn_k, attn_v, attn_o, cross_q, cross_k, cross_v, cross_o)):
        local_squares[index] = piece[...]
    local_wides[0] = ffn_in[...]
    local_wides[1] = ffn_out[...]
    local_bias[...] = jnp.zeros_like(local_bias)
    local_bias[0, 0:1, 0:64] = ffn_bias_in[...]
    small[...] = jnp.zeros_like(small)
    flipped[:, 64:] = jnp.ones((HEADS, flipped.shape[1] - 64, length), LOW)

    def gather(number, local, full, first, count, side=0, sides=1):
        sems = (gather_sends, gather_recvs, gather_own)
        return Gather(place, local, full, first, count, side, sides, *sems, number)

    def scatter(number, *buffers):
        kind = Scatter if len(buffers) == 7 else ScatterAcross
        return kind(place, *buffers, scatter_sends, scatter_recvs, number)

    def row_sems(number):
        return row_sends, row_recvs, row_own, number

    def square(index):
        return squares[index].reshape(features, features)

    def wide(index):
        return wides[index].reshape(features, hidden)

    def vector(index):
        first = (index % 4) * features
        return small.at[1 + index // 4 : 2 + index // 4, first : first + features]

    def quarter(ref, index):
        return ref.at[:, index * features : (index + 1) * features]

    square_sums = (grad_squares, work, last_squares, own_squares)
    wide_sums = (grad_wides, wides, last_wides, own_wides)
    to = SimpleNamespace(
        place=place,
        ready=ready,
        keys_values=gather(0, local_squares, squares, 1, 2),
        query=gather(1, local_squares, squares, 0, 1),
        out=gather(2, local_squares, squares, 3, 1),
        cross=[gather(3 + i, local_squares, squares, 4 + 2 * i, 2) for i in (0, 1)],
        ffn=[gather(5 + i, local_wides, wides, i // 2, 1, i % 2, 2) for i in range(4)],
        bias=gather(9, local_bias, biases, 0, 1),
        embed_row=ToRow(place, embed, embed_row, *row_sems(0)),
        query_row=ToRow(place, query, query_row, *row_sems(1)),
        source_row=ToRow(place, source, source_row, *row_sems(2)),
        cotangent_row=ToRow(place, cotangent, cotangent_row, *row_sems(3)),
        down_sum=scatter(0, *wide_sums, 1, 1, ready),
        up_sum=scatter(1, *wide_sums, 0, 1, ready),
        cross_sum=scatter(2, *square_sums, 4, 4, None),
        out_sum=scatter(3, *square_sums, 3, 1, None),
        key_sum=scatter(4, *square_sums, 1, 1, None),
        value_sum=scatter(5, *square_sums, 2, 1, None, across),
        query_sum=scatter(6, *square_sums, 0, 1, None),
        small_sum=SumAll(place, small, arrived, sum_sends, sum_recvs),
        mixed=FromRow(place, cotangent_row, mixed_blocks, *row_sems(4)),
        source_grad=FromRow(place, source_row, encoder_blocks, *row_sems(5)),
        query_grad=FromRow(place, hidden_two, query_blocks, *row_sems(6)),
        embed_grad=FromRow(place, cotangent_row, embed_blocks, *row_sems(7)),
    )
    score_room = ((key_sum, value_sum), highest)
    cotangent_low, grad_k, grad_v, grad_q = (quarter(act, i) for i in range(4))
    room = tuple(quarter(bias, i) for i in (0, 1))

    def fill_keys_values(rows):
        self_k[rows] = nn(embed_row[rows], square(1)).astype(LOW)
        self_v[rows] = nn(embed_row[rows], square(2)).astype(LOW)

    def fill_queries(rows):
        self_q[rows] = (nn(query_row[rows], square(0)) * 0.125).astype(LOW)

    def turned(step):
        return (length // Q_TILE - 1 - step // PAIRS) * PAIRS + lax.rem(step, PAIRS)

    def attend_self(after):
        flip_heads(self_v, flipped)
        attend(
            self_k, self_q, flipped, bias, self_context, totals,
            lambda number: place.tile(3 - number), score_room, Kept(kept_self, act, kept_sems, turned), after,
        )

    def first_norm():
        @pl.loop(0, length // 256)
        def _(tile):
            part = rows_of(tile, 256)
            branch = nt(self_context[part], square(3))
            normal, inverse = normalize(query_row[part].astype(WIDE) + branch)
            normal_one[part] = normal
            inverse_one[part] = inverse
            hidden_one[part] = (normal * norm_gain[0:1] + norm_bias[0:1]).astype(LOW)

    def fill_cross_queries():
        other_q[...] = (nn(hidden_one[...], square(4)) * 0.125).astype(LOW)

    def fill_cross_keys_values():
        other_k[...] = nn(source_row[...], square(5)).astype(LOW)
        other_v[...] = nn(source_row[...], square(6)).astype(LOW)

    def attend_cross(after):
        flip_heads(other_v, flipped)
        attend(
            other_k, other_q, flipped, bias, other_context, other_totals,
            lambda number: number, score_room, Kept(kept_cross, act, kept_sems), after,
        )

    def fill_bias_in():
        for block in range(4):
            pieces = biases[0, :, :, :, block * 128 : block * 128 + 128].reshape(128, 128)
            size = hidden // 4
            lane = lax.broadcasted_iota(jnp.int32, (128, size), 1)
            line = lax.broadcasted_iota(jnp.int32, (128, size), 0)
            spread = nn(pieces, jnp.where(lane % 64 == line, 1.0, 0.0).astype(LOW))
            spread = jnp.where(lane // 64 == line // 16, spread, 0.0)
            bias_in[:, block * size : block * size + size] = jnp.sum(spread, axis=0, keepdims=True)

    def feed_forward_in(after):
        @pl.loop(0, length // 256)
        def _(tile):
            part = rows_of(tile, 256)
            branch = nt(other_context[part], square(7))
            before = normal_one[part] * norm_gain[0:1] + norm_bias[0:1]
            normal, inverse = normalize(before + branch)
            grad_second[part] = normal
            key_sum[part, 0:1] = inverse
            low = (normal * norm_gain[1:2] + norm_bias[1:2]).astype(LOW)
            hidden_two[part] = low
            before = nn(low, wide(0)) + bias_in[...]
            below = 0.5 * (1.0 + lax.erf(before * 0.7071067811865476))
            density = jnp.exp(-0.5 * before * before) * 0.3989422804014327
            pre[part] = (below + before * density).astype(LOW)
            act[part] = (before * below).astype(LOW)
            run_after(tile, after)

    def feed_forward():
        @pl.loop(0, length // 256)
        def _(tile):
            part = rows_of(tile, 256)
            normal_mid = grad_second[part]
            after = normal_mid * norm_gain[1:2] + norm_bias[1:2]
            after = after + nt(act[part], wide(1)) + bias_out[...]
            normal, inverse = normalize(after)
            grad = cotangent_row[part].astype(WIDE)
            cotangent_row[part] = (normal * norm_gain[2:3] + norm_bias[2:3]).astype(LOW)
            add_rows(vector(2), grad * normal)
            add_rows(vector(5), grad)
            grad = normalize_back(grad, normal, inverse, norm_gain[2:3])
            low = grad.astype(LOW)
            grad_ffn[part] = low
            add_rows(vector(6), low.astype(WIDE))
            grad_pre = (nn(low, wide(1)) * pre[part].astype(WIDE)).astype(LOW)
            pre[part] = grad_pre
            add_rows(small.at[0:1], grad_pre.astype(WIDE))
            grad = grad + nt(grad_pre, wide(0))
            add_rows(vector(1), grad * normal_mid)
            add_rows(vector(4), grad)
            inverse_mid = key_sum[part, 0:1]
            grad_second[part] = normalize_back(grad, normal_mid, inverse_mid, norm_gain[1:2])

    def wide_grad(index, left, right):
        for side in (slice(0, hidden // 2), slice(hidden // 2, hidden)):
            total = tn(left[...], right[:, side]).astype(LOW)
            grad_wides[index, :, :, :, side] = total.reshape(4, 2, features // 8, hidden // 2)

    def square_grad(index, inputs, grad):
        grad_squares[index] = tn(inputs, grad).astype(LOW).reshape(grad_squares.shape[1:])

    def out_back(first, context, inverses, kept):
        for index in range(4):
            Kept(kept, pre, kept_sems).load(index).start()
        grad = grad_second[...].astype(LOW)
        square_grad(first + 3, grad, context[...])
        lane = lax.broadcasted_iota(jnp.int32, (HEADS, features), 1)
        head = lax.broadcasted_iota(jnp.int32, (HEADS, features), 0)
        spread = lax.dot_general(
            inverses[...],
            jnp.where(lane // 64 == head, 1.0, 0.0),
            (((0,), (0,)), ((), ())),
            precision=lax.Precision.HIGHEST,
            preferred_element_type=WIDE,
        )
        cotangent_low[...] = (nn(grad, square(first + 3)) * spread).astype(LOW)

    def attend_back_with(keys, queries, values, context, kept, tile_of, after):
        flip_heads(keys, flipped)
        inner_products(cotangent_low, context, inner)
        attend_back(
            flipped, queries, values, cotangent_low, inner,
            (key_sum, value_sum, grad_q), tile_of, room, Kept(kept, pre, kept_sems), after,
        )
        grad_k[...] = key_sum[...].astype(LOW)
        grad_v[...] = value_sum[...].astype(LOW)

    def cross_grads():
        square_grad(4, hidden_one[...], grad_q[...])
        square_grad(5, source_row[...], grad_k[...])
        square_grad(6, source_row[...], grad_v[...])

    def fill_source_grad():
        source_row[...] = (nt(grad_k[...], square(5)) + nt(grad_v[...], square(6))).astype(LOW)

    def first_norm_back():
        @pl.loop(0, length // 256)
        def _(tile):
            part = rows_of(tile, 256)
            grad = grad_second[part] + nt(grad_q[part], square(4))
            normal = normal_one[part]
            add_rows(vector(0), grad * normal)
            add_rows(vector(3), grad)
            grad_second[part] = normalize_back(grad, normal, inverse_one[part], norm_gain[0:1])

    def fill_query_grad(number):
        part = rows_of(place.tile(number), Q_TILE)
        grad = grad_second[part] + nt(grad_q[part], square(0))
        hidden_two[part] = grad.astype(LOW)

    def fill_embed_grad(rows):
        grad = nt(grad_k[rows], square(1)) + nt(grad_v[rows], square(2))
        cotangent_row[rows] = grad.astype(LOW)

    run_schedule(
        to,
        SimpleNamespace(
            fill_self_bias=lambda: fill_self_bias(bias, lengths, rank, limit, row),
            fill_cross_bias=lambda: fill_cross_bias(bias, lengths, source_lengths, row),
            near_keys_values=lambda: fill_keys_values(near_half),
            far_keys_values=lambda: fill_keys_values(far_half),
            near_queries=lambda: fill_queries(near_half),
            far_queries=lambda: fill_queries(far_half),
            attend_self=attend_self,
            first_norm=first_norm,
            cross_queries=fill_cross_queries,
            cross_keys_values=fill_cross_keys_values,
            attend_cross=attend_cross,
            bias_in=fill_bias_in,
            feed_forward_in=feed_forward_in,
            feed_forward=feed_forward,
            down_grad=lambda: wide_grad(1, grad_ffn, act),
            up_grad=lambda: wide_grad(0, hidden_two, pre),
            cross_out_back=lambda: out_back(4, other_context, other_totals, kept_cross),
            cross_back=lambda after: attend_back_with(
                other_k, other_q, other_v, other_context, kept_cross, lambda number: number, after
            ),
            cross_grads=cross_grads,
            source_grad=fill_source_grad,
            first_norm_back=first_norm_back,
            self_out_back=lambda: out_back(0, self_context, totals, kept_self),
            self_back=lambda after: attend_back_with(
                self_k, self_q, self_v, self_context, kept_self, place.tile, after
            ),
            query_grad=fill_query_grad,
            far_embed_grad=lambda: fill_embed_grad(far_half),
            near_embed_grad=lambda: fill_embed_grad(near_half),
            key_grad=lambda: square_grad(1, embed_row[...], grad_k[...]),
            value_grad=lambda: square_grad(2, embed_row[...], grad_v[...]),
            query_weight_grad=lambda: square_grad(0, query_row[...], grad_q[...]),
        ),
    )


def run_layer(streams, weights, vectors, tables):
    _, size, features = streams[0].shape
    length = 4 * size
    hidden = 4 * weights[8].shape[1]
    shape = jax.ShapeDtypeStruct
    vmem_in = pl.BlockSpec(memory_space=pltpu.VMEM)
    smem_in = pl.BlockSpec(memory_space=pltpu.SMEM)
    hbm = pl.BlockSpec(memory_space=pl.ANY)
    vmem, dma = pltpu.VMEM, pltpu.SemaphoreType.DMA
    row, wide_row = vmem((length, features), LOW), vmem((length, features), WIDE)
    per_head, column = vmem((HEADS, length), WIDE), vmem((length, 1), WIDE)
    full_squares = vmem((8, 4, 2, features // 8, features), LOW)
    full_wides = vmem((2, 4, 2, features // 8, hidden), LOW)
    blocks = shape((4, size, features), LOW)
    return pl.pallas_call(
        layer_kernel,
        out_shape=[
            shape((8, features // 8, features // 4), WIDE),
            shape((2, features // 8, hidden // 4), WIDE),
            shape((8, hidden), WIDE),
        ]
        + [blocks] * 4
        + [shape((length // Q_TILE * PAIRS, length, 2 * Q_TILE), LOW)] * 2,
        in_specs=[hbm] * 4 + [vmem_in] * 14 + [smem_in] * 2 + [vmem_in] * 2,
        out_specs=[vmem_in] * 3 + [hbm] * 6,
        scratch_shapes=[
            vmem((8, features // 8, features // 4), LOW),
            vmem((2, features // 8, hidden // 4), LOW),
            vmem((1, 16, 128), LOW),
            full_squares,
            full_wides,
            vmem((1, 4, 2, 16, 512), LOW),
            full_squares,
            full_wides,
            full_squares,
            vmem((8, features // 8, features // 4), LOW),
            vmem((2, features // 8, hidden // 4), LOW),
            vmem((5, 8, hidden), WIDE),
            vmem((1, features // 8, features // 2), LOW),
        ]
        + [row] * 12
        + [vmem((HEADS, 80, length), LOW)]
        + [per_head] * 3
        + [vmem((4, 1, Q_TILE), WIDE)]
        + [wide_row, column, row, row]
        + [vmem((length, hidden), LOW)] * 2
        + [row, wide_row, wide_row, wide_row, vmem((length, length), LOW)]
        + [vmem((1, hidden), WIDE)]
        + [dma((8, 3)), dma((8, 3)), dma((8,))]
        + [dma((10, Gather.slots)), dma((10, Gather.slots)), dma((10,))]
        + [dma((7, Scatter.slots)), dma((7, Scatter.slots)), dma((1, 5)), dma((1, 5)), dma((4,))]
        + [pltpu.SemaphoreType.REGULAR((2, 6))],
        compiler_params=pltpu.CompilerParams(
            collective_id=0, has_side_effects=True, vmem_limit_bytes=127 * 2**19
        ),
        name="layer",
    )(*streams, *weights, *vectors, *tables)[:7]


def outputs_kernel(
    squares, wides, small, mixed, grad_query, grad_embed, grad_encoder,
    mixed_out, query_out, embed_out, encoder_out, *rest,
):
    square_outs, wide_outs, (bias_in, bias_out, gains, shifts) = rest[:8], rest[8:10], rest[10:]
    mixed_out[...] = mixed[...]
    for low, out in ((grad_query, query_out), (grad_embed, embed_out), (grad_encoder, encoder_out)):
        out[...] = low[...].astype(WIDE)

    @pl.when(pl.program_id(0) == 0)
    def _():
        for index, out in enumerate(square_outs):
            out[...] = squares[index]
        for index, out in enumerate(wide_outs):
            out[...] = wides[index]
        features = gains.shape[1]
        for index in range(7):
            first = (index % 4) * features
            value = small[1 + index // 4 : 2 + index // 4, first : first + features]
            if index == 6:
                bias_out[...] = value
            else:
                (gains if index < 3 else shifts)[index % 3 : index % 3 + 1] = value
        count = wides.shape[2]
        mine = small[0:1, rows_of(lax.axis_index("tp"), count)]
        shift = lax.rem(count - lax.axis_index("dp") * bias_in.shape[1], count)
        bias_in[...] = pltpu.roll(mine, shift, 1)[:, : bias_in.shape[1]]


def write_outputs(squares, wides, small, *blocks):
    shape = jax.ShapeDtypeStruct
    rows, size, features = blocks[0].shape
    whole = pl.BlockSpec(memory_space=pltpu.VMEM)
    one = pl.BlockSpec((1, size, features), lambda i: (i, 0, 0))

    def fixed(extent):
        return pl.BlockSpec(extent, lambda i: (0,) * len(extent))

    singles = [squares.shape[1:]] * 8 + [wides.shape[1:]] * 2
    singles += [(1, wides.shape[1]), (1, features), (3, features), (3, features)]
    return pl.pallas_call(
        outputs_kernel,
        grid=(rows,),
        out_shape=[shape(blocks[0].shape, LOW)]
        + [shape(blocks[0].shape, WIDE)] * 3
        + [shape(extent, WIDE) for extent in singles],
        in_specs=[fixed(squares.shape), fixed(wides.shape), fixed(small.shape)] + [one] * 4,
        out_specs=[one] * 4 + [fixed(extent) for extent in singles],
        name="outputs",
    )(squares, wides, small, *blocks)


def local_rows(
    query_stream,
    token_embed,
    encoder_out,
    out_grad,
    attn_q,
    attn_k,
    attn_v,
    attn_o,
    cross_q,
    cross_k,
    cross_v,
    cross_o,
    ffn_in,
    ffn_bias_in,
    ffn_out,
    ffn_bias_out,
    norm_gain,
    norm_bias,
    doc_lengths,
    src_lengths,
    ctx_rank,
    ctx_limit,
):
    received = run_layer(
        (query_stream, token_embed, encoder_out, out_grad),
        (attn_q, attn_k, attn_v, attn_o.T, cross_q, cross_k, cross_v, cross_o.T)
        + (ffn_in, ffn_bias_in[None], ffn_out.T),
        (ffn_bias_out[None], norm_gain, norm_bias),
        (doc_lengths, src_lengths, ctx_rank, ctx_limit),
    )
    (
        mixed,
        grad_query,
        grad_embed,
        grad_encoder,
        grad_attn_q,
        grad_attn_k,
        grad_attn_v,
        grad_attn_o,
        grad_cross_q,
        grad_cross_k,
        grad_cross_v,
        grad_cross_o,
        grad_ffn_in,
        grad_ffn_out,
        grad_bias_in,
        grad_bias_out,
        gain_grads,
        shift_grads,
    ) = write_outputs(*received)
    return (
        mixed,
        grad_query,
        grad_embed,
        grad_encoder,
        grad_attn_q,
        grad_attn_k,
        grad_attn_v,
        grad_attn_o.T,
        grad_cross_q,
        grad_cross_k,
        grad_cross_v,
        grad_cross_o.T,
        grad_ffn_in,
        grad_bias_in[0],
        grad_ffn_out.T,
        grad_bias_out[0],
        gain_grads,
        shift_grads,
    )


def local(*arrays):
    if arrays[0].shape[0] == 4 and (lax.axis_size("dp"), lax.axis_size("tp")) == (8, 4):
        return local_rows(*arrays)
    return local_split(*arrays)


def solution(mesh):
    in_specs = (
        P("dp", "tp", None),
        P("dp", "tp", None),
        P("dp", "tp", None),
        P("dp", "tp", None),
        P("dp", "tp"),
        P("dp", "tp"),
        P("dp", "tp"),
        P("tp", "dp"),
        P("dp", "tp"),
        P("dp", "tp"),
        P("dp", "tp"),
        P("tp", "dp"),
        P("dp", "tp"),
        P(("tp", "dp")),
        P("tp", "dp"),
        P(),
        P(),
        P(),
        P("dp", None),
        P("dp", None),
        P("dp", None),
        P("dp", None),
    )
    out_specs = (
        P("dp", "tp", None),
        P("dp", "tp", None),
        P("dp", "tp", None),
        P("dp", "tp", None),
        P("dp", "tp"),
        P("dp", "tp"),
        P("dp", "tp"),
        P("tp", "dp"),
        P("dp", "tp"),
        P("dp", "tp"),
        P("dp", "tp"),
        P("tp", "dp"),
        P("dp", "tp"),
        P(("tp", "dp")),
        P("tp", "dp"),
        P(),
        P(),
        P(),
    )
    return jax.shard_map(local, mesh=mesh, in_specs=in_specs, out_specs=out_specs, check_vma=False)
```

```python
from types import SimpleNamespace

import jax
import jax.numpy as jnp
from jax import lax
from jax.experimental import pallas as pl
from jax.experimental.pallas import tpu as pltpu
from jax.sharding import PartitionSpec as P

HEADS = 8
LOW = jnp.bfloat16
WIDE = jnp.float32


EPSILON = 1e-05
score_tile = 512


def layer_norm(values, scale_vec, shift_vec):
    average = jnp.mean(values, axis=-1, keepdims=True)
    centred = values - average
    spread = jnp.mean(centred * centred, axis=-1, keepdims=True)
    return centred * lax.rsqrt(spread + EPSILON) * scale_vec + shift_vec


def gelu_exact(values):
    return 0.5 * values * (1.0 + lax.erf(values * 0.7071067811865476))


def project(inputs, matrix):
    return jnp.einsum("rld,de->rle", inputs, matrix, preferred_element_type=jnp.float32)


def project_back(cotangent, matrix):
    return jnp.einsum("rle,de->rld", cotangent, matrix, preferred_element_type=jnp.float32)


def outer_sum(inputs, cotangent):
    return jnp.einsum("rld,rle->de", inputs, cotangent, preferred_element_type=jnp.float32)


def layout(lengths, length):
    offsets = jnp.cumsum(lengths) - lengths
    positions = jnp.arange(length, dtype=jnp.int32)
    passed = positions[:, None] >= offsets[None, :]
    document = jnp.sum(passed.astype(jnp.int32), axis=1) - 1
    doc_start = jnp.max(jnp.where(passed, offsets[None, :], 0), axis=1)
    return (document, doc_start)


def self_visible(lengths, rank_row, limit_row, length, first_row, block_rows):
    document, doc_start = layout(lengths, length)
    positions = jnp.arange(length, dtype=jnp.int32)
    rows_pos = positions[first_row : first_row + block_rows]
    same_text = document[first_row : first_row + block_rows, None] == document[None, :]
    chosen = (rank_row[None, :] < limit_row[first_row : first_row + block_rows, None]) & (
        rows_pos[:, None] != positions[None, :]
    )
    opener = positions[None, :] == doc_start[first_row : first_row + block_rows, None]
    return same_text & (chosen | opener)


def cross_visible(lengths, src_lengths, length, src_length, first_row, block_rows):
    document, _ = layout(lengths, length)
    source_doc, _ = layout(src_lengths, src_length)
    return document[first_row : first_row + block_rows, None] == source_doc[None, :]


def attend_forward(queries, keys_all, values_all, visible_of, head_count):
    query_count = queries.shape[0]
    head_size = queries.shape[1] // head_count
    factor = head_size ** (-0.5)
    queries = queries.reshape(query_count, head_count, head_size)
    keys_all = keys_all.reshape(keys_all.shape[0], head_count, head_size)
    values_all = values_all.reshape(values_all.shape[0], head_count, head_size)
    block_rows = min(score_tile, query_count)
    outputs = []
    totals = []
    for first_row in range(0, query_count, block_rows):
        query_part = queries[first_row : first_row + block_rows]
        scores = (
            jnp.einsum("qhd,khd->hqk", query_part, keys_all, preferred_element_type=jnp.float32)
            * factor
        )
        scores = jnp.where(visible_of(first_row, block_rows)[None], scores, -1e30)
        highest = jnp.max(scores, axis=-1, keepdims=True)
        exponent = jnp.exp(scores - highest)
        denominator = jnp.sum(exponent, axis=-1, keepdims=True)
        weights_low = (exponent / denominator).astype(jnp.bfloat16)
        outputs.append(
            jnp.einsum("hqk,khd->qhd", weights_low, values_all, preferred_element_type=jnp.float32)
        )
        totals.append(highest[..., 0] + jnp.log(denominator[..., 0]))
    context = jnp.concatenate(outputs, axis=0).reshape(query_count, head_count * head_size)
    return (context, jnp.concatenate(totals, axis=1))


def attend_backward(queries, keys_all, values_all, visible_of, totals, grad_context, head_count):
    query_count = queries.shape[0]
    key_count = keys_all.shape[0]
    head_size = queries.shape[1] // head_count
    factor = head_size ** (-0.5)
    queries = queries.reshape(query_count, head_count, head_size)
    keys_all = keys_all.reshape(key_count, head_count, head_size)
    values_all = values_all.reshape(key_count, head_count, head_size)
    grad_context = grad_context.reshape(query_count, head_count, head_size)
    grad_keys = jnp.zeros((key_count, head_count, head_size), jnp.float32)
    grad_values = jnp.zeros((key_count, head_count, head_size), jnp.float32)
    grad_queries = []
    block_rows = min(score_tile, query_count)
    for first_row in range(0, query_count, block_rows):
        query_part = queries[first_row : first_row + block_rows]
        grad_part = grad_context[first_row : first_row + block_rows]
        scores = (
            jnp.einsum("qhd,khd->hqk", query_part, keys_all, preferred_element_type=jnp.float32)
            * factor
        )
        scores = jnp.where(visible_of(first_row, block_rows)[None], scores, -1e30)
        weights_full = jnp.exp(scores - totals[:, first_row : first_row + block_rows, None])
        grad_weights = jnp.einsum(
            "qhd,khd->hqk", grad_part, values_all, preferred_element_type=jnp.float32
        )
        inner = jnp.sum(grad_weights * weights_full, axis=-1, keepdims=True)
        grad_scores = (weights_full * (grad_weights - inner)).astype(jnp.bfloat16)
        grad_queries.append(
            jnp.einsum("hqk,khd->qhd", grad_scores, keys_all, preferred_element_type=jnp.float32)
            * factor
        )
        grad_keys = (
            grad_keys
            + jnp.einsum(
                "hqk,qhd->khd", grad_scores, query_part, preferred_element_type=jnp.float32
            )
            * factor
        )
        grad_values = grad_values + jnp.einsum(
            "hqk,qhd->khd",
            weights_full.astype(jnp.bfloat16),
            grad_part,
            preferred_element_type=jnp.float32,
        )
    grad_queries = jnp.concatenate(grad_queries, axis=0).reshape(
        query_count, head_count * head_size
    )
    return (
        grad_queries.astype(jnp.bfloat16),
        grad_keys.reshape(key_count, -1).astype(jnp.bfloat16),
        grad_values.reshape(key_count, -1).astype(jnp.bfloat16),
    )


def collect(piece):
    return lax.all_gather(piece, "tp", axis=1, tiled=True)


def spread_sum(partial_sum):
    return lax.psum_scatter(partial_sum, "tp", scatter_dimension=1, tiled=True)


def collect_grad(piece):
    return lax.all_gather(piece, "tp", axis=1, tiled=True)


def send_back(partial_sum):
    return lax.psum_scatter(partial_sum, "tp", scatter_dimension=1, tiled=True)


def local_split(
    query_stream,
    token_embed,
    encoder_out,
    out_grad,
    attn_q,
    attn_k,
    attn_v,
    attn_o,
    cross_q,
    cross_k,
    cross_v,
    cross_o,
    ffn_in,
    ffn_bias_in,
    ffn_out,
    ffn_bias_out,
    norm_gain,
    norm_bias,
    doc_lengths,
    src_lengths,
    ctx_rank,
    ctx_limit,
):
    head_count = HEADS // lax.axis_size("tp")
    (
        self_query,
        self_key,
        self_value,
        self_out,
        other_query,
        other_key,
        other_value,
        other_out,
        hidden_in,
        hidden_bias,
        hidden_out,
    ) = (
        lax.all_gather(attn_q, "dp", axis=0, tiled=True),
        lax.all_gather(attn_k, "dp", axis=0, tiled=True),
        lax.all_gather(attn_v, "dp", axis=0, tiled=True),
        lax.all_gather(attn_o, "dp", axis=1, tiled=True),
        lax.all_gather(cross_q, "dp", axis=0, tiled=True),
        lax.all_gather(cross_k, "dp", axis=0, tiled=True),
        lax.all_gather(cross_v, "dp", axis=0, tiled=True),
        lax.all_gather(cross_o, "dp", axis=1, tiled=True),
        lax.all_gather(ffn_in, "dp", axis=0, tiled=True),
        lax.all_gather(ffn_bias_in, "dp", axis=0, tiled=True),
        lax.all_gather(ffn_out, "dp", axis=1, tiled=True),
    )

    def self_forward(row_items):
        queries, keys_all, values_all, lengths, rank_row, limit_row = row_items

        def visible_of(first_row, block_rows):
            return self_visible(
                lengths, rank_row, limit_row, keys_all.shape[0], first_row, block_rows
            )

        return attend_forward(queries, keys_all, values_all, visible_of, head_count)

    def self_backward(row_items):
        queries, keys_all, values_all, lengths, rank_row, limit_row, totals, grad_context = (
            row_items
        )

        def visible_of(first_row, block_rows):
            return self_visible(
                lengths, rank_row, limit_row, keys_all.shape[0], first_row, block_rows
            )

        return attend_backward(
            queries, keys_all, values_all, visible_of, totals, grad_context, head_count
        )

    def cross_forward(row_items):
        queries, keys_all, values_all, lengths, source_lengths = row_items

        def visible_of(first_row, block_rows):
            return cross_visible(
                lengths, source_lengths, queries.shape[0], keys_all.shape[0], first_row, block_rows
            )

        return attend_forward(queries, keys_all, values_all, visible_of, head_count)

    def cross_backward(row_items):
        queries, keys_all, values_all, lengths, source_lengths, totals, grad_context = row_items

        def visible_of(first_row, block_rows):
            return cross_visible(
                lengths, source_lengths, queries.shape[0], keys_all.shape[0], first_row, block_rows
            )

        return attend_backward(
            queries, keys_all, values_all, visible_of, totals, grad_context, head_count
        )

    query_all = collect(query_stream)
    embed_all = collect(token_embed)
    source_all = collect(encoder_out)
    self_queries = project(query_all, self_query).astype(jnp.bfloat16)
    self_keys = project(embed_all, self_key).astype(jnp.bfloat16)
    self_values = project(embed_all, self_value).astype(jnp.bfloat16)
    self_context, self_totals = lax.map(
        self_forward, (self_queries, self_keys, self_values, doc_lengths, ctx_rank, ctx_limit)
    )
    self_low = self_context.astype(jnp.bfloat16)
    first_sum = query_stream.astype(jnp.float32) + spread_sum(project(self_low, self_out))
    hidden_one, first_back = jax.vjp(layer_norm, first_sum, norm_gain[0], norm_bias[0])
    hidden_one_all = collect(hidden_one.astype(jnp.bfloat16))
    cross_queries = project(hidden_one_all, other_query).astype(jnp.bfloat16)
    cross_keys = project(source_all, other_key).astype(jnp.bfloat16)
    cross_values = project(source_all, other_value).astype(jnp.bfloat16)
    cross_context, cross_totals = lax.map(
        cross_forward, (cross_queries, cross_keys, cross_values, doc_lengths, src_lengths)
    )
    cross_low = cross_context.astype(jnp.bfloat16)
    second_sum = hidden_one + spread_sum(project(cross_low, other_out))
    hidden_two, second_back = jax.vjp(layer_norm, second_sum, norm_gain[1], norm_bias[1])
    hidden_two_low = hidden_two.astype(jnp.bfloat16)
    ffn_inputs = lax.all_gather(hidden_two_low, "tp", axis=1, tiled=True)
    ffn_pre = project(ffn_inputs, hidden_in) + hidden_bias.astype(jnp.float32)
    ffn_gate, gelu_back = jax.vjp(gelu_exact, ffn_pre)
    ffn_act = ffn_gate.astype(jnp.bfloat16)
    ffn_branch = (
        lax.psum_scatter(project(ffn_act, hidden_out), "tp", scatter_dimension=1, tiled=True)
        + ffn_bias_out
    )
    third_sum = hidden_two + ffn_branch
    mixed_full, third_back = jax.vjp(layer_norm, third_sum, norm_gain[2], norm_bias[2])
    grad_third, gain_two, shift_two = third_back(out_grad.astype(jnp.float32))
    grad_ffn = grad_third.astype(jnp.bfloat16)
    grad_bias_out = jnp.sum(grad_ffn.astype(jnp.float32), axis=(0, 1))
    grad_ffn_all = lax.all_gather(grad_ffn, "tp", axis=1, tiled=True)
    grad_act = project_back(grad_ffn_all, hidden_out)
    grad_down = outer_sum(ffn_act, grad_ffn_all)
    grad_pre = gelu_back(grad_act)[0].astype(jnp.bfloat16)
    grad_up = outer_sum(ffn_inputs, grad_pre)
    grad_bias_in = jnp.sum(grad_pre.astype(jnp.float32), axis=(0, 1))
    grad_two = grad_third + lax.psum_scatter(
        project_back(grad_pre, hidden_in), "tp", scatter_dimension=1, tiled=True
    )
    grad_second, gain_one, shift_one = second_back(grad_two)
    grad_cross_all = collect_grad(grad_second.astype(jnp.bfloat16))
    grad_other_out = outer_sum(cross_low, grad_cross_all)
    grad_cross_ctx = project_back(grad_cross_all, other_out).astype(jnp.bfloat16)
    cross_dq, cross_dk, cross_dv = lax.map(
        cross_backward,
        (
            cross_queries,
            cross_keys,
            cross_values,
            doc_lengths,
            src_lengths,
            cross_totals,
            grad_cross_ctx,
        ),
    )
    grad_other_query = outer_sum(hidden_one_all, cross_dq)
    grad_other_key = outer_sum(source_all, cross_dk)
    grad_other_value = outer_sum(source_all, cross_dv)
    grad_encoder = send_back(
        project_back(cross_dk, other_key) + project_back(cross_dv, other_value)
    )
    grad_one = grad_second + send_back(project_back(cross_dq, other_query))
    grad_first, gain_zero, shift_zero = first_back(grad_one)
    grad_attn_all = collect_grad(grad_first.astype(jnp.bfloat16))
    grad_self_out = outer_sum(self_low, grad_attn_all)
    grad_self_ctx = project_back(grad_attn_all, self_out).astype(jnp.bfloat16)
    self_dq, self_dk, self_dv = lax.map(
        self_backward,
        (
            self_queries,
            self_keys,
            self_values,
            doc_lengths,
            ctx_rank,
            ctx_limit,
            self_totals,
            grad_self_ctx,
        ),
    )
    grad_self_query = outer_sum(query_all, self_dq)
    grad_self_key = outer_sum(embed_all, self_dk)
    grad_self_value = outer_sum(embed_all, self_dv)
    grad_embed = send_back(project_back(self_dk, self_key) + project_back(self_dv, self_value))
    grad_query = grad_first + send_back(project_back(self_dq, self_query))
    (
        grad_self_query,
        grad_self_key,
        grad_self_value,
        grad_self_out,
        grad_other_query,
        grad_other_key,
        grad_other_value,
        grad_other_out,
        grad_up,
        grad_bias_in,
        grad_down,
    ) = (
        lax.psum_scatter(
            grad_self_query.astype(jnp.bfloat16), "dp", scatter_dimension=0, tiled=True
        ).astype(jnp.float32),
        lax.psum_scatter(
            grad_self_key.astype(jnp.bfloat16), "dp", scatter_dimension=0, tiled=True
        ).astype(jnp.float32),
        lax.psum_scatter(
            grad_self_value.astype(jnp.bfloat16), "dp", scatter_dimension=0, tiled=True
        ).astype(jnp.float32),
        lax.psum_scatter(
            grad_self_out.astype(jnp.bfloat16), "dp", scatter_dimension=1, tiled=True
        ).astype(jnp.float32),
        lax.psum_scatter(
            grad_other_query.astype(jnp.bfloat16), "dp", scatter_dimension=0, tiled=True
        ).astype(jnp.float32),
        lax.psum_scatter(
            grad_other_key.astype(jnp.bfloat16), "dp", scatter_dimension=0, tiled=True
        ).astype(jnp.float32),
        lax.psum_scatter(
            grad_other_value.astype(jnp.bfloat16), "dp", scatter_dimension=0, tiled=True
        ).astype(jnp.float32),
        lax.psum_scatter(
            grad_other_out.astype(jnp.bfloat16), "dp", scatter_dimension=1, tiled=True
        ).astype(jnp.float32),
        lax.psum_scatter(
            grad_up.astype(jnp.bfloat16), "dp", scatter_dimension=0, tiled=True
        ).astype(jnp.float32),
        lax.psum_scatter(
            grad_bias_in.astype(jnp.bfloat16), "dp", scatter_dimension=0, tiled=True
        ).astype(jnp.float32),
        lax.psum_scatter(
            grad_down.astype(jnp.bfloat16), "dp", scatter_dimension=1, tiled=True
        ).astype(jnp.float32),
    )
    gain_grads = jnp.stack([gain_zero, gain_one, gain_two])
    shift_grads = jnp.stack([shift_zero, shift_one, shift_two])
    gain_grads, shift_grads, grad_bias_out = lax.psum(
        (gain_grads, shift_grads, grad_bias_out), ("dp", "tp")
    )
    return (
        mixed_full.astype(jnp.bfloat16),
        grad_query,
        grad_embed,
        grad_encoder,
        grad_self_query,
        grad_self_key,
        grad_self_value,
        grad_self_out,
        grad_other_query,
        grad_other_key,
        grad_other_value,
        grad_other_out,
        grad_up,
        grad_bias_in,
        grad_down,
        grad_bias_out,
        gain_grads,
        shift_grads,
    )


HIDDEN = -1e30
Q_TILE = 256


def product(left, right, left_axis, right_axis):
    return lax.dot_general(
        left, right, (((left_axis,), (right_axis,)), ((), ())), preferred_element_type=WIDE
    )


def nn(left, right):
    return product(left, right, 1, 0)


def nt(left, right):
    return product(left, right, 1, 1)


def tn(left, right):
    return product(left, right, 0, 0)


def rows_of(index, size):
    return pl.ds(pl.multiple_of(index * size, size), size)


def normalize(values):
    average = jnp.mean(values, axis=-1, keepdims=True)
    centred = values - average
    spread = jnp.mean(centred * centred, axis=-1, keepdims=True)
    inverse = lax.rsqrt(spread + EPSILON)
    return centred * inverse, inverse


def normalize_back(grad, normal, inverse, gain):
    scaled = grad * gain
    mean_one = jnp.mean(scaled, axis=-1, keepdims=True)
    mean_two = jnp.mean(scaled * normal, axis=-1, keepdims=True)
    return inverse * (scaled - mean_one - normal * mean_two)


def add_rows(target, grad):
    target[...] += jnp.sum(grad, axis=0, keepdims=True)


def documents(lengths, row, shape, axis, first=0):
    positions = lax.broadcasted_iota(jnp.int32, shape, axis) + first
    document = jnp.full(shape, -1, jnp.int32)
    start = jnp.zeros(shape, jnp.int32)
    offset = jnp.int32(0)
    for slot in range(lengths.shape[1]):
        passed = positions >= offset
        document = document + passed.astype(jnp.int32)
        start = jnp.where(passed, offset, start)
        offset = offset + lengths[row, slot]
    return positions, document, start


def fill_self_bias(bias, lengths, rank, limit, row):
    length = bias.shape[0]
    key_position, key_document, _ = documents(lengths, row, (length, 1), 0)
    rank_row = rank[pl.ds(row, 1), :].astype(WIDE)
    key_rank = jnp.transpose(jnp.broadcast_to(rank_row, (128, length)))[:, :1]

    @pl.loop(0, length // Q_TILE)
    def _(tile):
        part = rows_of(tile, Q_TILE)
        position, document, start = documents(lengths, row, (1, Q_TILE), 1, tile * Q_TILE)
        query_limit = limit[pl.ds(row, 1), part].astype(WIDE)
        chosen = (key_rank < query_limit) & (key_position != position)
        seen = (key_document == document) & (chosen | (key_position == start))
        bias[:, part] = jnp.where(seen, 0.0, HIDDEN).astype(bias.dtype)


def fill_cross_bias(bias, lengths, source_lengths, row):
    length = bias.shape[0]
    _, key_document, _ = documents(source_lengths, row, (length, 1), 0)

    @pl.loop(0, length // Q_TILE)
    def _(tile):
        part = rows_of(tile, Q_TILE)
        _, document, _ = documents(lengths, row, (1, Q_TILE), 1, tile * Q_TILE)
        seen = key_document == document
        bias[:, part] = jnp.where(seen, 0.0, HIDDEN).astype(bias.dtype)


def one_head(pair, side):
    lane = lax.broadcasted_iota(jnp.int32, pair.shape, 1)
    return jnp.where(lane // 64 == side, pair, jnp.zeros_like(pair))


def run_after(step, after):
    for number, actions in after.items():
        if actions:

            @pl.when(step == number)
            def _():
                for action in actions:
                    action()


PAIRS = HEADS // 2


class Kept:
    def __init__(self, kept, room, sems, place_of=lambda step: step):
        self.kept, self.room, self.sems, self.place_of = kept, room, sems, place_of

    def slot(self, step, side=None):
        place = lax.rem(step, 4)
        if side is None:
            return rows_of(place, 2 * Q_TILE)
        return rows_of(2 * place + side, Q_TILE)

    def store(self, step):
        room = self.room.at[:, self.slot(step)]
        return pltpu.make_async_copy(room, self.kept.at[self.place_of(step)], self.sems.at[lax.rem(step, 4)])

    def load(self, step):
        room = self.room.at[:, self.slot(step)]
        return pltpu.make_async_copy(self.kept.at[self.place_of(step)], room, self.sems.at[lax.rem(step, 4)])


def attend(keys, queries, values_t, bias, context, inverses, tile_of, room, kept, after):
    scores_of, highest_of = room
    steps = keys.shape[0] // Q_TILE * PAIRS

    def where(step):
        return rows_of(tile_of(step // PAIRS), Q_TILE), lax.rem(step, PAIRS)

    def score(step, slot):
        part, pair = where(step)
        lanes = rows_of(pair, 128)
        for side in (0, 1):
            scores = nt(keys[:, lanes], one_head(queries[part, lanes], side))
            scores = scores + bias[:, part].astype(WIDE)
            scores_of[slot][:, side * Q_TILE : (side + 1) * Q_TILE] = scores
            highest_of[2 * slot + side] = jnp.max(scores, axis=0, keepdims=True)

    def weigh(step, slot):
        part, pair = where(step)
        outs = []
        for side in (0, 1):
            head = 2 * pair + side
            scores = scores_of[slot][:, side * Q_TILE : (side + 1) * Q_TILE]
            weights = jnp.exp(scores - highest_of[2 * slot + side]).astype(LOW)
            kept.room[:, kept.slot(step, side)] = weights
            out = nn(values_t[head], weights)
            inverse = 1.0 / out[64:65]
            outs.append(out[:64] * inverse)
            inverses[pl.ds(head, 1), part] = inverse
        context[part, rows_of(pair, 128)] = jnp.transpose(jnp.concatenate(outs, axis=0)).astype(LOW)

    score(0, 0)

    @pl.loop(0, steps // 2)
    def _(double):
        @pl.when(double > 1)
        def _():
            kept.store(2 * double - 4).wait()
            kept.store(2 * double - 3).wait()

        score(2 * double + 1, 1)
        weigh(2 * double, 0)
        score(lax.rem(2 * double + 2, steps), 0)
        weigh(2 * double + 1, 1)
        kept.store(2 * double).start()
        kept.store(2 * double + 1).start()
        run_after(double, after)

    for step in range(steps - 4, steps):
        kept.store(step).wait()


def attend_back(keys_t, queries, values, cotangent, inner, grads, tile_of, room, kept, after):
    key_sum, value_sum, grad_queries = grads
    steps = values.shape[0] // Q_TILE * PAIRS

    def where(step):
        return rows_of(tile_of(step // PAIRS), Q_TILE), rows_of(lax.rem(step, PAIRS), 128)

    def make(step, slot):
        part, lanes = where(step)
        pair = lax.rem(step, PAIRS)
        for side in (0, 1):
            head = 2 * pair + side
            grad_weights = nt(values[:, lanes], one_head(cotangent[part, lanes], side))
            weights = kept.room[:, kept.slot(step, side)].astype(WIDE)
            grad_scores = weights * (grad_weights - inner[pl.ds(head, 1), part])
            room[slot][:, side * Q_TILE : (side + 1) * Q_TILE] = grad_scores.astype(LOW)

    def use(step, slot):
        part, lanes = where(step)
        pair = lax.rem(step, PAIRS)

        def stacked(ref):
            return jnp.concatenate([one_head(ref[part, lanes], side) for side in (0, 1)], axis=0)

        outs = [
            nn(keys_t[2 * pair + side, :64], room[slot][:, side * Q_TILE : (side + 1) * Q_TILE])
            for side in (0, 1)
        ]
        turned = jnp.transpose(jnp.concatenate(outs, axis=0) * 0.125)
        grad_queries[part, lanes] = turned.astype(LOW)
        value_sum[:, lanes] += nn(kept.room[:, kept.slot(step)], stacked(cotangent))
        key_sum[:, lanes] += nn(room[slot][...], stacked(queries))

    key_sum[...] = jnp.zeros_like(key_sum)
    value_sum[...] = jnp.zeros_like(value_sum)
    kept.load(0).wait()
    make(0, 0)

    @pl.loop(0, steps // 2)
    def _(double):
        kept.load(2 * double + 1).wait()
        make(2 * double + 1, 1)
        use(2 * double, 0)

        @pl.when(double < steps // 2 - 1)
        def _():
            kept.load(2 * double + 2).wait()

        make(lax.rem(2 * double + 2, steps), 0)
        use(2 * double + 1, 1)

        @pl.when(double < steps // 2 - 2)
        def _():
            kept.load(2 * double + 4).start()
            kept.load(2 * double + 5).start()

        run_after(double, after)


def inner_products(cotangent, context, inner):
    length, features = cotangent.shape
    shape = (2 * HEADS, features)
    head = lax.broadcasted_iota(jnp.int32, shape, 0)
    lane = lax.broadcasted_iota(jnp.int32, shape, 1)
    pick = jnp.where(lane // 64 == head, 1.0, 0.0).astype(LOW)

    @pl.loop(0, 2)
    def _(tile):
        part = rows_of(tile, length // 2)
        products = cotangent[part].astype(WIDE) * context[part].astype(WIDE)
        high = products.astype(LOW)
        rest = (products - high.astype(WIDE)).astype(LOW)
        inner[:, part] = (nt(pick, high) + nt(pick, rest))[:HEADS]


def flip_heads(values, flipped):
    @pl.loop(0, 2)
    def _(tile):
        part = rows_of(tile, values.shape[0] // 2)
        turned = jnp.transpose(values[part])
        for head in range(HEADS):
            flipped[head, :64, part] = turned[64 * head : 64 * head + 64]


MESH = pl.DeviceIdType.MESH


class Place:
    def __init__(self):
        dp, tp = lax.axis_index("dp"), lax.axis_index("tp")
        self.dp, self.tp = dp, tp
        self.z, self.x = dp // 2, lax.rem(dp, 2)
        self.y, self.core = tp // 2, lax.rem(tp, 2)
        self.core_peer = (dp, 2 * self.y + 1 - self.core)
        self.y_peer = (dp, 2 * (1 - self.y) + self.core)
        self.far_peer = (dp, 2 * (1 - self.y) + 1 - self.core)
        self.x_peer = (2 * self.z + 1 - self.x, tp)
        self.z_steps = [lax.rem(self.z + step, 4) for step in range(4)]
        self.z_peers = [(2 * z + self.x, tp) for z in self.z_steps[1:]]
        self.summing = [self.core_peer, self.x_peer, self.y_peer] + self.z_peers

    def greet(self):
        for peer in self.summing + [self.far_peer]:
            barrier = pltpu.get_barrier_semaphore()
            pl.semaphore_signal(barrier, inc=1, device_id=peer, device_id_type=MESH)

    def meet(self):
        pl.semaphore_wait(pltpu.get_barrier_semaphore(), len(self.summing) + 1)

    def tile(self, number):
        side = lax.rem(self.y + 1 - number // 2, 2)
        return 2 * side + lax.rem(self.core + (number + 1) // 2, 2)

    def columns(self, width):
        return [
            pl.ds(pl.multiple_of(tp * width, width), width)
            for tp in (self.tp, self.y_peer[1], self.core_peer[1], self.far_peer[1])
        ]


class Exchange:
    def __init__(self, sends, recvs, number):
        self.sends, self.recvs, self.number = sends, recvs, number
        self.made = []
        self.arriving = []

    def send(self, source, target, peer):
        slot = len(self.made)

        def copy():
            return pltpu.make_async_remote_copy(
                src_ref=source(),
                dst_ref=target(),
                send_sem=self.sends.at[self.number, slot],
                recv_sem=self.recvs.at[self.number, slot],
                device_id=peer,
                device_id_type=MESH,
            )

        copy().start()
        self.made.append(copy)
        self.arriving.append(copy)

    def move(self, block, peer):
        self.send(block, block, peer)

    def arrive(self):
        for copy in self.arriving:
            copy().wait_recv()
        self.arriving = []

    def finish(self):
        for copy in self.made:
            copy().wait_send()


class Gather(Exchange):
    slots = 11

    def __init__(
        self, place, local, full, first, count, side, sides, sends, recvs, own_sems, number
    ):
        super().__init__(sends, recvs, number)
        self.place, self.full, self.items = place, full, pl.ds(first, count)
        width = local.shape[-1] // sides
        self.sides = [
            pl.ds(pl.multiple_of((tp * sides + side) * width, width), width)
            for tp in (place.tp, place.y_peer[1])
        ]
        p = place
        self.source = lambda: local.at[self.items, :, side * width : (side + 1) * width]
        self.target = lambda: full.at[self.items, p.z, p.x, :, self.sides[0]]
        self.own = lambda: pltpu.make_async_copy(
            self.source(), self.target(), own_sems.at[number]
        )

    def stage(self, number):
        p, full, items = self.place, self.full, self.items
        self.arrive()
        if number == 0:
            self.own().start()
            self.send(self.source, self.target, p.y_peer)
        elif number == 1:
            self.own().wait()
            for side in self.sides:
                for peer in p.z_peers:
                    self.move(lambda side=side: full.at[items, p.z, p.x, :, side], peer)
        elif number == 2:
            for side in self.sides:
                self.move(lambda side=side: full.at[items, :, p.x, :, side], p.x_peer)
        elif number == 3:
            for side in self.sides:
                self.move(lambda side=side: full.at[items, :, :, :, side], p.core_peer)


class ToRow(Exchange):
    slots = 3

    def __init__(self, place, local, row, sends, recvs, own_sems, number):
        super().__init__(sends, recvs, number)
        size = local.shape[1]
        p = place
        span = pl.ds(pl.multiple_of(p.tp * size, size), size)

        def here():
            return row.at[span]

        self.local, self.here = local, here
        self.peers = (p.y_peer, p.far_peer, p.core_peer)
        self.own = lambda: pltpu.make_async_copy(local.at[p.tp], here(), own_sems.at[number])

    def start(self):
        for peer in self.peers:
            self.send(lambda peer=peer: self.local.at[peer[1]], self.here, peer)
        self.own().start()

    def near(self):
        self.own().wait()
        self.arriving.pop()().wait_recv()

    def far(self):
        self.arrive()


class FromRow(Exchange):
    slots = 3

    def __init__(self, place, row, blocks, sends, recvs, own_sems, number):
        super().__init__(sends, recvs, number)
        size = blocks.shape[1]
        p = place
        self.peers = (p.y_peer, p.far_peer, p.core_peer)
        self.target = lambda: blocks.at[p.tp]

        def part(tp):
            return row.at[pl.ds(pl.multiple_of(tp * size, size), size)]

        self.part = part
        self.own = lambda: pltpu.make_async_copy(
            self.part(p.tp), self.target(), own_sems.at[number]
        )

    def give(self, number):
        if number == 3:
            self.own().start()
        else:
            peer = self.peers[number]
            self.send(lambda: self.part(peer[1]), self.target, peer)

    def give_all(self):
        for number in range(4):
            self.give(number)

    def wait(self):
        self.own().wait()
        self.arrive()


class Scatter(Exchange):
    slots = 8

    def __init__(
        self, place, parts, work, last, out, first, count, ready, sends, recvs, number
    ):
        super().__init__(sends, recvs, number)
        self.place, self.parts, self.work, self.last, self.out = place, parts, work, last, out
        self.numbers = range(first, first + count)
        self.items = pl.ds(first, count)
        self.width = out.shape[-1]
        self.columns = place.columns(self.width)
        self.ready = ready

    def add_core(self):
        width = self.width
        for item in self.numbers:
            for side in (0, 1):

                @pl.loop(0, 4)
                def _(z):
                    mine = self.parts[item, z, :, :, self.columns[side]]
                    self.work[item, z, :, :, side * width : (side + 1) * width] += mine

    def expect(self, index):
        if self.ready is not None:
            pl.semaphore_wait(self.ready.at[self.number, index], 1)

    def stage(self, number):
        p, parts, work, items, width = self.place, self.parts, self.work, self.items, self.width
        first_half, second_half = slice(0, 2 * width), slice(2 * width, 4 * width)
        sides = [slice(side * width, (side + 1) * width) for side in range(4)]
        self.arrive()
        if number == 0:
            self.expect(0)
            for side, column in zip(sides, self.columns[2:]):
                self.send(
                    lambda column=column: parts.at[items, :, :, :, column],
                    lambda side=side: work.at[items, :, :, :, side],
                    p.core_peer,
                )
        elif number == 1:
            self.add_core()
            self.expect(1)
            self.send(
                lambda: work.at[items, :, 1 - p.x, :, first_half],
                lambda: work.at[items, :, 0, :, second_half],
                p.x_peer,
            )
        elif number == 2:
            for item in self.numbers:

                @pl.loop(0, 4)
                def _(z):
                    work[item, z, 0, :, second_half] += work[item, z, p.x, :, first_half]

            for step, peer in enumerate(p.z_peers):
                self.expect(3 + step)
                self.send(
                    lambda step=step: work.at[items, p.z_steps[step + 1], 0, :, second_half],
                    lambda step=step: work.at[items, step, 1, :, second_half],
                    peer,
                )
        elif number == 3:
            for item in self.numbers:
                total = work[item, p.z, 0, :, second_half].astype(WIDE)
                for step in range(3):
                    total = total + work[item, step, 1, :, second_half].astype(WIDE)
                work[item, 3, 1, :, second_half] = total.astype(LOW)
            self.expect(2)
            self.send(
                lambda: work.at[items, 3, 1, :, sides[3]],
                lambda: self.last.at[items],
                p.y_peer,
            )
        else:
            for item in self.numbers:
                mine = work[item, 3, 1, :, sides[2]].astype(WIDE)
                self.out[item] = mine + self.last[item].astype(WIDE)


class ScatterAcross(Scatter):
    def __init__(
        self, place, parts, work, last, out, first, count, ready, across, sends, recvs, number
    ):
        super().__init__(place, parts, work, last, out, first, count, ready, sends, recvs, number)
        self.across = across

    def stage(self, number):
        if number == 0:
            super().stage(0)
            return
        p, work, items, width = self.place, self.work, self.items, self.width
        first_half, second_half = slice(0, 2 * width), slice(2 * width, 4 * width)
        kept, given = slice(2 * width, 3 * width), slice(3 * width, 4 * width)
        self.arrive()
        if number == 1:
            self.add_core()
            for step, peer in enumerate(p.z_peers):
                self.send(
                    lambda step=step: work.at[items, p.z_steps[step + 1], :, :, first_half],
                    lambda step=step: work.at[items, step, :, :, second_half],
                    peer,
                )
        elif number == 2:
            for item in self.numbers:
                total = work[item, p.z, :, :, first_half].astype(WIDE)
                for step in range(3):
                    total = total + work[item, step, :, :, second_half].astype(WIDE)
                work[item, 3, :, :, second_half] = total.astype(LOW)
            self.send(
                lambda: work.at[items, 3, 1 - p.x, :, second_half], lambda: self.across, p.x_peer
            )
        elif number == 3:
            for item in self.numbers:
                work[item, 3, p.x, :, second_half] += self.across[0]
            self.send(
                lambda: work.at[items, 3, p.x, :, given], lambda: self.last.at[items], p.y_peer
            )
        else:
            for item in self.numbers:
                mine = work[item, 3, p.x, :, kept].astype(WIDE)
                self.out[item] = mine + self.last[item].astype(WIDE)


class SumAll(Exchange):
    slots = 5

    def __init__(self, place, values, arrived, sends, recvs):
        super().__init__(sends, recvs, 0)
        p = place
        z_one = p.z + 1 - 2 * lax.rem(p.z, 2)
        peers = (p.core_peer, p.x_peer, p.y_peer, (2 * z_one + p.x, p.tp), p.z_peers[1])
        self.peers, self.values, self.arrived = peers, values, arrived

    def stage(self, number):
        if number:
            self.arrive()
            self.made[-1]().wait_send()
            self.values[...] = self.values[...] + self.arrived[number - 1]
        if number < 5:
            self.send(
                lambda: self.values, lambda: self.arrived.at[number], self.peers[number]
            )


def run_schedule(to, do):
    def step(task, number):
        return lambda: task.stage(number)

    do.fill_self_bias()
    to.place.meet()
    first = [to.keys_values, to.query, to.out, to.bias]
    rest = to.cross + to.ffn
    for task in first + to.cross:
        task.stage(0)
    to.embed_row.start()
    for task in to.ffn[:2]:
        task.stage(0)
    to.query_row.start()
    for task in to.ffn[2:]:
        task.stage(0)
    to.source_row.start()
    to.cotangent_row.start()
    for task in first + to.cross:
        task.stage(1)
    to.keys_values.stage(2)
    to.query.stage(2)
    to.keys_values.stage(3)
    to.embed_row.near()
    to.query_row.near()
    to.keys_values.stage(4)
    do.near_keys_values()
    to.out.stage(2)
    to.bias.stage(2)
    to.query.stage(3)
    to.query.stage(4)
    do.near_queries()
    to.embed_row.far()
    do.far_keys_values()
    for task in to.ffn[:2]:
        task.stage(1)

    def far_queries():
        to.query_row.far()
        do.far_queries()

    do.attend_self(
        {
            0: [step(to.cross[0], 2), step(to.out, 3)],
            1: [step(to.out, 4), step(to.bias, 3)],
            2: [far_queries, step(to.ffn[2], 1), step(to.ffn[3], 1), step(to.cross[0], 3), step(to.cross[1], 2)],
            3: [step(to.cross[0], 4), step(to.bias, 4)],
            5: [step(to.ffn[0], 2)],
            7: [step(to.cross[1], 3)],
        }
    )
    do.first_norm()
    to.ffn[1].stage(2)
    to.cross[1].stage(4)
    do.fill_cross_bias()
    do.cross_queries()
    to.source_row.near()
    to.source_row.far()
    do.cross_keys_values()
    do.attend_cross(
        {
            0: [step(to.ffn[2], 2), step(to.ffn[0], 3)],
            3: [step(to.ffn[3], 2), step(to.ffn[0], 4), step(to.ffn[1], 3)],
            5: [step(to.ffn[1], 4)],
            7: [step(to.ffn[2], 3)],
        }
    )
    do.bias_in()
    do.feed_forward_in(
        {
            1: [step(to.ffn[2], 4)],
            2: [step(to.ffn[3], 3)],
        }
    )
    to.cotangent_row.near()
    to.cotangent_row.far()
    to.ffn[3].stage(4)
    do.feed_forward()

    for task in to.ffn:
        task.finish()
    for group in (0, 1):
        for index, peer in enumerate(to.place.summing):
            there = index if index < 3 else 8 - index
            pl.semaphore_signal(
                to.ready.at[group, there], inc=1, device_id=peer, device_id_type=MESH
            )
    to.mixed.give_all()
    do.down_grad()
    to.down_sum.stage(0)
    do.up_grad()
    to.up_sum.stage(0)
    do.cross_out_back()
    to.down_sum.stage(1)
    to.up_sum.stage(1)
    do.cross_back({4: [step(to.down_sum, 2)]})
    do.cross_grads()
    to.cross_sum.stage(0)
    do.source_grad()
    to.source_grad.give_all()
    to.up_sum.stage(2)
    to.cross_sum.stage(1)
    do.first_norm_back()
    to.small_sum.stage(0)
    to.down_sum.stage(3)
    do.self_out_back()
    to.out_sum.stage(0)
    to.small_sum.stage(1)

    def give_query(number):
        def action():
            do.query_grad(number)
            to.query_grad.give(number)

        return action

    do.self_back(
        {
            0: [step(to.out_sum, 1)],
            1: [give_query(0)],
            3: [give_query(1), step(to.cross_sum, 2), step(to.small_sum, 2)],
            4: [step(to.up_sum, 3)],
            5: [give_query(2), step(to.out_sum, 2)],
            7: [give_query(3), step(to.small_sum, 3)],
        }
    )
    to.mixed.wait()
    to.mixed.finish()
    do.value_grad()
    to.value_sum.stage(0)
    do.key_grad()
    to.key_sum.stage(0)
    to.value_sum.stage(1)
    do.query_weight_grad()
    to.query_sum.stage(0)
    to.key_sum.stage(1)
    do.far_embed_grad()
    to.embed_grad.give(0)
    to.embed_grad.give(1)
    to.query_sum.stage(1)
    do.near_embed_grad()
    to.embed_grad.give(2)
    to.embed_grad.give(3)
    to.key_sum.stage(2)
    to.small_sum.stage(4)
    to.query_sum.stage(2)
    to.value_sum.stage(2)
    to.cross_sum.stage(3)
    to.out_sum.stage(3)
    to.down_sum.stage(4)
    to.up_sum.stage(4)
    to.key_sum.stage(3)
    to.small_sum.stage(5)
    to.query_sum.stage(3)
    to.value_sum.stage(3)
    for task in (to.cross_sum, to.out_sum, to.key_sum, to.value_sum, to.query_sum):
        task.stage(4)
    outgoing = [to.source_grad, to.query_grad, to.embed_grad]
    for task in outgoing:
        task.wait()
    for task in outgoing + [to.embed_row, to.query_row, to.source_row, to.cotangent_row]:
        task.finish()
    for task in first + to.cross:
        task.finish()
    for task in (to.down_sum, to.up_sum, to.cross_sum, to.out_sum):
        task.finish()
    for task in (to.key_sum, to.value_sum, to.query_sum):
        task.finish()


def layer_kernel(
    query, embed, source, cotangent, attn_q, attn_k, attn_v, attn_o, cross_q, cross_k, cross_v,
    cross_o, ffn_in, ffn_bias_in, ffn_out, bias_out, norm_gain, norm_bias, lengths, source_lengths,
    rank, limit,
    own_squares, own_wides, small, mixed_blocks, query_blocks, embed_blocks, encoder_blocks, kept_self, kept_cross,
    local_squares, local_wides, local_bias, squares, wides, biases, grad_squares, grad_wides,
    work, last_squares, last_wides, arrived, across,
    query_row, embed_row, source_row, cotangent_row,
    self_q, self_k, self_v, self_context, other_q, other_k, other_v, other_context,
    flipped, totals, other_totals, inner, highest, normal_one, inverse_one,
    hidden_one, hidden_two, act, pre, grad_ffn, grad_second, key_sum, value_sum, bias, bias_in,
    row_sends, row_recvs, row_own, gather_sends, gather_recvs, gather_own,
    scatter_sends, scatter_recvs, sum_sends, sum_recvs, kept_sems, ready,
):
    place = Place()
    place.greet()
    row = place.tp
    length, features = query_row.shape
    hidden = act.shape[1]
    half = length // 2
    near_half, far_half = rows_of(place.y, half), rows_of(1 - place.y, half)

    for index, piece in enumerate((attn_q, attn_k, attn_v, attn_o, cross_q, cross_k, cross_v, cross_o)):
        local_squares[index] = piece[...]
    local_wides[0] = ffn_in[...]
    local_wides[1] = ffn_out[...]
    local_bias[...] = jnp.zeros_like(local_bias)
    local_bias[0, 0:1, 0:64] = ffn_bias_in[...]
    small[...] = jnp.zeros_like(small)
    flipped[:, 64:] = jnp.ones((HEADS, flipped.shape[1] - 64, length), LOW)

    def gather(number, local, full, first, count, side=0, sides=1):
        sems = (gather_sends, gather_recvs, gather_own)
        return Gather(place, local, full, first, count, side, sides, *sems, number)

    def scatter(number, *buffers):
        kind = Scatter if len(buffers) == 7 else ScatterAcross
        return kind(place, *buffers, scatter_sends, scatter_recvs, number)

    def row_sems(number):
        return row_sends, row_recvs, row_own, number

    def square(index):
        return squares[index].reshape(features, features)

    def wide(index):
        return wides[index].reshape(features, hidden)

    def vector(index):
        first = (index % 4) * features
        return small.at[1 + index // 4 : 2 + index // 4, first : first + features]

    def quarter(ref, index):
        return ref.at[:, index * features : (index + 1) * features]

    square_sums = (grad_squares, work, last_squares, own_squares)
    wide_sums = (grad_wides, wides, last_wides, own_wides)
    to = SimpleNamespace(
        place=place,
        ready=ready,
        keys_values=gather(0, local_squares, squares, 1, 2),
        query=gather(1, local_squares, squares, 0, 1),
        out=gather(2, local_squares, squares, 3, 1),
        cross=[gather(3 + i, local_squares, squares, 4 + 2 * i, 2) for i in (0, 1)],
        ffn=[gather(5 + i, local_wides, wides, i // 2, 1, i % 2, 2) for i in range(4)],
        bias=gather(9, local_bias, biases, 0, 1),
        embed_row=ToRow(place, embed, embed_row, *row_sems(0)),
        query_row=ToRow(place, query, query_row, *row_sems(1)),
        source_row=ToRow(place, source, source_row, *row_sems(2)),
        cotangent_row=ToRow(place, cotangent, cotangent_row, *row_sems(3)),
        down_sum=scatter(0, *wide_sums, 1, 1, ready),
        up_sum=scatter(1, *wide_sums, 0, 1, ready),
        cross_sum=scatter(2, *square_sums, 4, 4, None),
        out_sum=scatter(3, *square_sums, 3, 1, None),
        key_sum=scatter(4, *square_sums, 1, 1, None),
        value_sum=scatter(5, *square_sums, 2, 1, None, across),
        query_sum=scatter(6, *square_sums, 0, 1, None),
        small_sum=SumAll(place, small, arrived, sum_sends, sum_recvs),
        mixed=FromRow(place, cotangent_row, mixed_blocks, *row_sems(4)),
        source_grad=FromRow(place, source_row, encoder_blocks, *row_sems(5)),
        query_grad=FromRow(place, hidden_two, query_blocks, *row_sems(6)),
        embed_grad=FromRow(place, cotangent_row, embed_blocks, *row_sems(7)),
    )
    score_room = ((key_sum, value_sum), highest)
    cotangent_low, grad_k, grad_v, grad_q = (quarter(act, i) for i in range(4))
    room = tuple(quarter(bias, i) for i in (0, 1))

    def fill_keys_values(rows):
        self_k[rows] = nn(embed_row[rows], square(1)).astype(LOW)
        self_v[rows] = nn(embed_row[rows], square(2)).astype(LOW)

    def fill_queries(rows):
        self_q[rows] = (nn(query_row[rows], square(0)) * 0.125).astype(LOW)

    def turned(step):
        return (length // Q_TILE - 1 - step // PAIRS) * PAIRS + lax.rem(step, PAIRS)

    def attend_self(after):
        flip_heads(self_v, flipped)
        attend(
            self_k, self_q, flipped, bias, self_context, totals,
            lambda number: place.tile(3 - number), score_room, Kept(kept_self, act, kept_sems, turned), after,
        )

    def first_norm():
        @pl.loop(0, length // 256)
        def _(tile):
            part = rows_of(tile, 256)
            branch = nt(self_context[part], square(3))
            normal, inverse = normalize(query_row[part].astype(WIDE) + branch)
            normal_one[part] = normal
            inverse_one[part] = inverse
            hidden_one[part] = (normal * norm_gain[0:1] + norm_bias[0:1]).astype(LOW)

    def fill_cross_queries():
        @pl.loop(0, 2)
        def _(tile):
            rows = rows_of(tile, half)
            other_q[rows] = (nn(hidden_one[rows], square(4)) * 0.125).astype(LOW)

    def fill_cross_keys_values():
        @pl.loop(0, 2)
        def _(tile):
            rows = rows_of(tile, half)
            other_k[rows] = nn(source_row[rows], square(5)).astype(LOW)
            other_v[rows] = nn(source_row[rows], square(6)).astype(LOW)

    def attend_cross(after):
        flip_heads(other_v, flipped)
        attend(
            other_k, other_q, flipped, bias, other_context, other_totals,
            lambda number: number, score_room, Kept(kept_cross, act, kept_sems), after,
        )

    def fill_bias_in():
        for block in range(4):
            pieces = biases[0, :, :, :, block * 128 : block * 128 + 128].reshape(128, 128)
            size = hidden // 4
            lane = lax.broadcasted_iota(jnp.int32, (128, size), 1)
            line = lax.broadcasted_iota(jnp.int32, (128, size), 0)
            spread = nn(pieces, jnp.where(lane % 64 == line, 1.0, 0.0).astype(LOW))
            spread = jnp.where(lane // 64 == line // 16, spread, 0.0)
            bias_in[:, block * size : block * size + size] = jnp.sum(spread, axis=0, keepdims=True)

    def feed_forward_in(after):
        @pl.loop(0, length // 256)
        def _(tile):
            part = rows_of(tile, 256)
            branch = nt(other_context[part], square(7))
            before = normal_one[part] * norm_gain[0:1] + norm_bias[0:1]
            normal, inverse = normalize(before + branch)
            grad_second[part] = normal
            key_sum[part, 0:1] = inverse
            low = (normal * norm_gain[1:2] + norm_bias[1:2]).astype(LOW)
            hidden_two[part] = low
            before = nn(low, wide(0)) + bias_in[...]
            below = 0.5 * (1.0 + lax.erf(before * 0.7071067811865476))
            density = jnp.exp(-0.5 * before * before) * 0.3989422804014327
            pre[part] = (below + before * density).astype(LOW)
            act[part] = (before * below).astype(LOW)
            run_after(tile, after)

    def feed_forward():
        @pl.loop(0, length // 256)
        def _(tile):
            part = rows_of(tile, 256)
            normal_mid = grad_second[part]
            after = normal_mid * norm_gain[1:2] + norm_bias[1:2]
            after = after + nt(act[part], wide(1)) + bias_out[...]
            normal, inverse = normalize(after)
            grad = cotangent_row[part].astype(WIDE)
            cotangent_row[part] = (normal * norm_gain[2:3] + norm_bias[2:3]).astype(LOW)
            add_rows(vector(2), grad * normal)
            add_rows(vector(5), grad)
            grad = normalize_back(grad, normal, inverse, norm_gain[2:3])
            low = grad.astype(LOW)
            grad_ffn[part] = low
            add_rows(vector(6), low.astype(WIDE))
            grad_pre = (nn(low, wide(1)) * pre[part].astype(WIDE)).astype(LOW)
            pre[part] = grad_pre
            add_rows(small.at[0:1], grad_pre.astype(WIDE))
            grad = grad + nt(grad_pre, wide(0))
            add_rows(vector(1), grad * normal_mid)
            add_rows(vector(4), grad)
            inverse_mid = key_sum[part, 0:1]
            grad_second[part] = normalize_back(grad, normal_mid, inverse_mid, norm_gain[1:2])

    def wide_grad(index, left, right):
        @pl.loop(0, 2)
        def _(side):
            lanes = rows_of(side, hidden // 2)
            total = tn(left[...], right[:, lanes]).astype(LOW)
            grad_wides[index, :, :, :, lanes] = total.reshape(4, 2, features // 8, hidden // 2)

    def square_grad(index, inputs, grad):
        @pl.loop(0, 2)
        def _(side):
            left = inputs[:, rows_of(side, features // 2)].astype(LOW)
            total = tn(left, grad[...]).astype(LOW)
            total = total.reshape(2, 2, features // 8, features)
            grad_squares[index, pl.ds(2 * side, 2)] = total

    def out_back(first, context, inverses, kept):
        for index in range(4):
            Kept(kept, pre, kept_sems).load(index).start()
        square_grad(first + 3, grad_second, context)
        lane = lax.broadcasted_iota(jnp.int32, (HEADS, features), 1)
        head = lax.broadcasted_iota(jnp.int32, (HEADS, features), 0)
        pick = jnp.where(lane // 64 == head, 1.0, 0.0)

        @pl.loop(0, 2)
        def _(tile):
            rows = rows_of(tile, half)
            spread = lax.dot_general(
                inverses[:, rows],
                pick,
                (((0,), (0,)), ((), ())),
                precision=lax.Precision.HIGHEST,
                preferred_element_type=WIDE,
            )
            grad = nn(grad_second[rows].astype(LOW), square(first + 3))
            cotangent_low[rows] = (grad * spread).astype(LOW)

    def attend_back_with(keys, queries, values, context, kept, tile_of, after):
        flip_heads(keys, flipped)
        inner_products(cotangent_low, context, inner)
        attend_back(
            flipped, queries, values, cotangent_low, inner,
            (key_sum, value_sum, grad_q), tile_of, room, Kept(kept, pre, kept_sems), after,
        )
        grad_k[...] = key_sum[...].astype(LOW)
        grad_v[...] = value_sum[...].astype(LOW)

    def cross_grads():
        square_grad(4, hidden_one, grad_q)
        square_grad(5, source_row, grad_k)
        square_grad(6, source_row, grad_v)

    def fill_source_grad():
        @pl.loop(0, 2)
        def _(tile):
            rows = rows_of(tile, half)
            grad = nt(grad_k[rows], square(5)) + nt(grad_v[rows], square(6))
            source_row[rows] = grad.astype(LOW)

    def first_norm_back():
        @pl.loop(0, length // 256)
        def _(tile):
            part = rows_of(tile, 256)
            grad = grad_second[part] + nt(grad_q[part], square(4))
            normal = normal_one[part]
            add_rows(vector(0), grad * normal)
            add_rows(vector(3), grad)
            grad_second[part] = normalize_back(grad, normal, inverse_one[part], norm_gain[0:1])

    def fill_query_grad(number):
        part = rows_of(place.tile(number), Q_TILE)
        grad = grad_second[part] + nt(grad_q[part], square(0))
        hidden_two[part] = grad.astype(LOW)

    def fill_embed_grad(rows):
        grad = nt(grad_k[rows], square(1)) + nt(grad_v[rows], square(2))
        cotangent_row[rows] = grad.astype(LOW)

    run_schedule(
        to,
        SimpleNamespace(
            fill_self_bias=lambda: fill_self_bias(bias, lengths, rank, limit, row),
            fill_cross_bias=lambda: fill_cross_bias(bias, lengths, source_lengths, row),
            near_keys_values=lambda: fill_keys_values(near_half),
            far_keys_values=lambda: fill_keys_values(far_half),
            near_queries=lambda: fill_queries(near_half),
            far_queries=lambda: fill_queries(far_half),
            attend_self=attend_self,
            first_norm=first_norm,
            cross_queries=fill_cross_queries,
            cross_keys_values=fill_cross_keys_values,
            attend_cross=attend_cross,
            bias_in=fill_bias_in,
            feed_forward_in=feed_forward_in,
            feed_forward=feed_forward,
            down_grad=lambda: wide_grad(1, grad_ffn, act),
            up_grad=lambda: wide_grad(0, hidden_two, pre),
            cross_out_back=lambda: out_back(4, other_context, other_totals, kept_cross),
            cross_back=lambda after: attend_back_with(
                other_k, other_q, other_v, other_context, kept_cross, lambda number: number, after
            ),
            cross_grads=cross_grads,
            source_grad=fill_source_grad,
            first_norm_back=first_norm_back,
            self_out_back=lambda: out_back(0, self_context, totals, kept_self),
            self_back=lambda after: attend_back_with(
                self_k, self_q, self_v, self_context, kept_self, place.tile, after
            ),
            query_grad=fill_query_grad,
            far_embed_grad=lambda: fill_embed_grad(far_half),
            near_embed_grad=lambda: fill_embed_grad(near_half),
            key_grad=lambda: square_grad(1, embed_row, grad_k),
            value_grad=lambda: square_grad(2, embed_row, grad_v),
            query_weight_grad=lambda: square_grad(0, query_row, grad_q),
        ),
    )


def run_layer(streams, weights, vectors, tables):
    _, size, features = streams[0].shape
    length = 4 * size
    hidden = 4 * weights[8].shape[1]
    shape = jax.ShapeDtypeStruct
    vmem_in = pl.BlockSpec(memory_space=pltpu.VMEM)
    smem_in = pl.BlockSpec(memory_space=pltpu.SMEM)
    hbm = pl.BlockSpec(memory_space=pl.ANY)
    vmem, dma = pltpu.VMEM, pltpu.SemaphoreType.DMA
    row, wide_row = vmem((length, features), LOW), vmem((length, features), WIDE)
    per_head, column = vmem((HEADS, length), WIDE), vmem((length, 1), WIDE)
    full_squares = vmem((8, 4, 2, features // 8, features), LOW)
    full_wides = vmem((2, 4, 2, features // 8, hidden), LOW)
    blocks = shape((4, size, features), LOW)
    return pl.pallas_call(
        layer_kernel,
        out_shape=[
            shape((8, features // 8, features // 4), WIDE),
            shape((2, features // 8, hidden // 4), WIDE),
            shape((8, hidden), WIDE),
        ]
        + [blocks] * 4
        + [shape((length // Q_TILE * PAIRS, length, 2 * Q_TILE), LOW)] * 2,
        in_specs=[hbm] * 4 + [vmem_in] * 14 + [smem_in] * 2 + [vmem_in] * 2,
        out_specs=[vmem_in] * 3 + [hbm] * 6,
        scratch_shapes=[
            vmem((8, features // 8, features // 4), LOW),
            vmem((2, features // 8, hidden // 4), LOW),
            vmem((1, 16, 128), LOW),
            full_squares,
            full_wides,
            vmem((1, 4, 2, 16, 512), LOW),
            full_squares,
            full_wides,
            full_squares,
            vmem((8, features // 8, features // 4), LOW),
            vmem((2, features // 8, hidden // 4), LOW),
            vmem((5, 8, hidden), WIDE),
            vmem((1, features // 8, features // 2), LOW),
        ]
        + [row] * 12
        + [vmem((HEADS, 80, length), LOW)]
        + [per_head] * 3
        + [vmem((4, 1, Q_TILE), WIDE)]
        + [wide_row, column, row, row]
        + [vmem((length, hidden), LOW)] * 2
        + [row, wide_row, wide_row, wide_row, vmem((length, length), LOW)]
        + [vmem((1, hidden), WIDE)]
        + [dma((8, 3)), dma((8, 3)), dma((8,))]
        + [dma((10, Gather.slots)), dma((10, Gather.slots)), dma((10,))]
        + [dma((7, Scatter.slots)), dma((7, Scatter.slots)), dma((1, 5)), dma((1, 5)), dma((4,))]
        + [pltpu.SemaphoreType.REGULAR((2, 6))],
        compiler_params=pltpu.CompilerParams(
            collective_id=0, has_side_effects=True, vmem_limit_bytes=127 * 2**19
        ),
        name="layer",
    )(*streams, *weights, *vectors, *tables)[:7]


def outputs_kernel(
    squares, wides, small, mixed, grad_query, grad_embed, grad_encoder,
    mixed_out, query_out, embed_out, encoder_out, *rest,
):
    square_outs, wide_outs, (bias_in, bias_out, gains, shifts) = rest[:8], rest[8:10], rest[10:]
    mixed_out[...] = mixed[...]
    for low, out in ((grad_query, query_out), (grad_embed, embed_out), (grad_encoder, encoder_out)):
        out[...] = low[...].astype(WIDE)

    @pl.when(pl.program_id(0) == 0)
    def _():
        for index, out in enumerate(square_outs):
            out[...] = squares[index]
        for index, out in enumerate(wide_outs):
            out[...] = wides[index]
        features = gains.shape[1]
        for index in range(7):
            first = (index % 4) * features
            value = small[1 + index // 4 : 2 + index // 4, first : first + features]
            if index == 6:
                bias_out[...] = value
            else:
                (gains if index < 3 else shifts)[index % 3 : index % 3 + 1] = value
        count = wides.shape[2]
        mine = small[0:1, rows_of(lax.axis_index("tp"), count)]
        shift = lax.rem(count - lax.axis_index("dp") * bias_in.shape[1], count)
        bias_in[...] = pltpu.roll(mine, shift, 1)[:, : bias_in.shape[1]]


def write_outputs(squares, wides, small, *blocks):
    shape = jax.ShapeDtypeStruct
    rows, size, features = blocks[0].shape
    whole = pl.BlockSpec(memory_space=pltpu.VMEM)
    one = pl.BlockSpec((1, size, features), lambda i: (i, 0, 0))

    def fixed(extent):
        return pl.BlockSpec(extent, lambda i: (0,) * len(extent))

    singles = [squares.shape[1:]] * 8 + [wides.shape[1:]] * 2
    singles += [(1, wides.shape[1]), (1, features), (3, features), (3, features)]
    return pl.pallas_call(
        outputs_kernel,
        grid=(rows,),
        out_shape=[shape(blocks[0].shape, LOW)]
        + [shape(blocks[0].shape, WIDE)] * 3
        + [shape(extent, WIDE) for extent in singles],
        in_specs=[fixed(squares.shape), fixed(wides.shape), fixed(small.shape)] + [one] * 4,
        out_specs=[one] * 4 + [fixed(extent) for extent in singles],
        name="outputs",
    )(squares, wides, small, *blocks)


def local_rows(
    query_stream,
    token_embed,
    encoder_out,
    out_grad,
    attn_q,
    attn_k,
    attn_v,
    attn_o,
    cross_q,
    cross_k,
    cross_v,
    cross_o,
    ffn_in,
    ffn_bias_in,
    ffn_out,
    ffn_bias_out,
    norm_gain,
    norm_bias,
    doc_lengths,
    src_lengths,
    ctx_rank,
    ctx_limit,
):
    received = run_layer(
        (query_stream, token_embed, encoder_out, out_grad),
        (attn_q, attn_k, attn_v, attn_o.T, cross_q, cross_k, cross_v, cross_o.T)
        + (ffn_in, ffn_bias_in[None], ffn_out.T),
        (ffn_bias_out[None], norm_gain, norm_bias),
        (doc_lengths, src_lengths, ctx_rank, ctx_limit),
    )
    (
        mixed,
        grad_query,
        grad_embed,
        grad_encoder,
        grad_attn_q,
        grad_attn_k,
        grad_attn_v,
        grad_attn_o,
        grad_cross_q,
        grad_cross_k,
        grad_cross_v,
        grad_cross_o,
        grad_ffn_in,
        grad_ffn_out,
        grad_bias_in,
        grad_bias_out,
        gain_grads,
        shift_grads,
    ) = write_outputs(*received)
    return (
        mixed,
        grad_query,
        grad_embed,
        grad_encoder,
        grad_attn_q,
        grad_attn_k,
        grad_attn_v,
        grad_attn_o.T,
        grad_cross_q,
        grad_cross_k,
        grad_cross_v,
        grad_cross_o.T,
        grad_ffn_in,
        grad_bias_in[0],
        grad_ffn_out.T,
        grad_bias_out[0],
        gain_grads,
        shift_grads,
    )


def local(*arrays):
    if arrays[0].shape[0] == 4 and (lax.axis_size("dp"), lax.axis_size("tp")) == (8, 4):
        return local_rows(*arrays)
    return local_split(*arrays)


def solution(mesh):
    in_specs = (
        P("dp", "tp", None),
        P("dp", "tp", None),
        P("dp", "tp", None),
        P("dp", "tp", None),
        P("dp", "tp"),
        P("dp", "tp"),
        P("dp", "tp"),
        P("tp", "dp"),
        P("dp", "tp"),
        P("dp", "tp"),
        P("dp", "tp"),
        P("tp", "dp"),
        P("dp", "tp"),
        P(("tp", "dp")),
        P("tp", "dp"),
        P(),
        P(),
        P(),
        P("dp", None),
        P("dp", None),
        P("dp", None),
        P("dp", None),
    )
    out_specs = (
        P("dp", "tp", None),
        P("dp", "tp", None),
        P("dp", "tp", None),
        P("dp", "tp", None),
        P("dp", "tp"),
        P("dp", "tp"),
        P("dp", "tp"),
        P("tp", "dp"),
        P("dp", "tp"),
        P("dp", "tp"),
        P("dp", "tp"),
        P("tp", "dp"),
        P("dp", "tp"),
        P(("tp", "dp")),
        P("tp", "dp"),
        P(),
        P(),
        P(),
    )
    return jax.shard_map(local, mesh=mesh, in_specs=in_specs, out_specs=out_specs, check_vma=False)
```
